32 devices in a mesh: dp: 2 (over core), pipe: 4 (over y, x), ctx: 4 (over z).
Axes of the slice: x: 2, y: 2, z: 4, core: 2. Of those that a mesh axis runs over, the one named last changes fastest.
Arguments:
- inputs: bfloat16 [4, 256, 768], P('dp', 'ctx'), may hold values from -6 to 6
- cotangent: bfloat16 [4, 256, 768], P('dp', 'ctx'), may hold values from -6 to 6
- dilated_kernel_weight: bfloat16 [4, 3, 768, 384], P('pipe'), may hold values from -0.125 to 0.125
- point_weight: bfloat16 [4, 384, 768], P('pipe'), may hold values from -0.3125 to 0.3125
Outputs:
- dilated_grad: float32 [4, 3, 768, 384], P('pipe', None, ('dp', 'ctx'))
The draws below stay inside these ranges and needn't reach their ends.
All inputs are finite; a program needn't handle non-finite values.
Results may differ from the reference program's by a relative error of at most 0.012.
Values may be sent and summed in bfloat16 or wider, within the bound.
No kernel may reach another device: no remote copies, remote signals or barrier semaphores. Data moves between devices by JAX's collectives and lax.ppermute only.
A program may use at most 64 MiB of HBM per device.

```python
import math
import jax
import jax.numpy as jnp
from jax import lax

C = 768
B = 384
BIN_DEV = 64
NBINS = 256
SEQS = 4
N_PIPE = 4


def spiked(result, rng, source, target, blocks, factor):
    def block_of(position):
        return (jnp.arange(result.shape[position]) // (result.shape[position] // blocks)).reshape((-1,) + (1,) * (result.ndim - 1 - position))

    first = jax.random.permutation(rng, blocks)[block_of(target)]
    other_side = (block_of(target) + blocks // 2) % blocks
    return jnp.where((block_of(source) == first) | (block_of(source) == other_side), factor * result, result)


def block_levels(key, dims, split, low, largest):
    loudness = 1.0
    for axis_at, parts in split:
        draws = jax.random.uniform(jax.random.fold_in(jax.random.fold_in(key, 6), axis_at), (parts,), jnp.float32, low / len(split), largest / len(split))
        loudness = loudness * jnp.repeat(jnp.exp(draws), dims[axis_at] // parts).reshape((-1,) + (1,) * (len(dims) - 1 - axis_at))
    return loudness


def scatter_about(stream_key, extent, scale, most, pieces=(), kind=jnp.bfloat16):
    result = scale * jax.random.normal(stream_key, extent, jnp.float32)
    if pieces:
        result = result * block_levels(stream_key, extent, pieces, -0.22, 0.18)
    return jnp.clip(result, -most, most).astype(kind)


def gaussian_with(key, dims, scale, bound, cuts, heavy, dtype=jnp.bfloat16):
    result = scale * jax.random.normal(key, dims, jnp.float32)
    if cuts:
        result = result * block_levels(key, dims, cuts, -0.22, 0.18)
    return jnp.clip(spiked(result, jax.random.fold_in(key, 3), *heavy), -bound, bound).astype(dtype)


def setup_inputs(seed: int = 0) -> dict:
    arg_keys = jax.random.split(jax.random.key(seed), 5)
    inputs = gaussian_with(arg_keys[0], (SEQS, NBINS, C), 1.0, 6.0, ((0, 2), (1, 4)), (1, 2, 4, 2.0))
    cotangent = scatter_about(arg_keys[1], (SEQS, NBINS, C), 1.0, 6.0, ((0, 2), (1, 4)))
    dilated_kernel_weight = scatter_about(arg_keys[2], (N_PIPE, 3, C, B), (3 * C) ** -0.5, 0.125, ((0, 4),))
    point_weight = scatter_about(arg_keys[3], (N_PIPE, B, C), B ** -0.5, 0.3125, ((0, 4),))
    return {"inputs": inputs, "cotangent": cotangent, "dilated_kernel_weight": dilated_kernel_weight, "point_weight": point_weight}


root_half = 0.7071067811865476
inv_root_two_pi = 0.3989422804014327

def gelu(value):
    return 0.5 * value * (1.0 + lax.erf(value * root_half))

def gelu_slope(value):
    return 0.5 * (1.0 + lax.erf(value * root_half)) + value * jnp.exp(-0.5 * value * value) * inv_root_two_pi

def reference(inputs, cotangent, dilated_kernel_weight, point_weight):
    layers = N_PIPE
    reach = BIN_DEV // 2
    length = NBINS
    scale = 1.0 / math.sqrt(SEQS * NBINS)
    trunk = inputs
    saved = []
    for layer in range(layers):
        spread = reach // 2 ** (layers - 1 - layer)
        act = gelu(trunk.astype(jnp.float32)).astype(jnp.bfloat16)
        padded = jnp.pad(act, ((0, 0), (spread, spread), (0, 0)))
        pre = jnp.zeros(act.shape[:2] + (dilated_kernel_weight.shape[3],), jnp.float32)
        for kernel_offset in range(3):
            receptive_span = padded[:, kernel_offset * spread:kernel_offset * spread + length]
            pre = pre + jnp.dot(receptive_span, dilated_kernel_weight[layer, kernel_offset], preferred_element_type=jnp.float32)
        inner = gelu(pre).astype(jnp.bfloat16)
        branch = jnp.dot(inner, point_weight[layer], preferred_element_type=jnp.float32)
        saved.append((trunk, padded, pre))
        trunk = (trunk.astype(jnp.float32) + branch).astype(jnp.bfloat16)
    upstream = (cotangent.astype(jnp.float32) * scale).astype(jnp.bfloat16)
    grads = [None] * layers
    for layer in reversed(range(layers)):
        spread = reach // 2 ** (layers - 1 - layer)
        trunk_in, padded, pre = saved[layer]
        inner_grad = jnp.dot(upstream, point_weight[layer].T, preferred_element_type=jnp.float32)
        dpre = (inner_grad * gelu_slope(pre)).astype(jnp.bfloat16)
        dpre_wide = dpre.astype(jnp.float32)
        taps = []
        for kernel_offset in range(3):
            receptive_span = padded[:, kernel_offset * spread:kernel_offset * spread + length].astype(jnp.float32)
            taps.append(jnp.einsum('snc,snb->cb', receptive_span, dpre_wide))
        grads[layer] = jnp.stack(taps)
        dpad = jnp.pad(dpre, ((0, 0), (spread, spread), (0, 0)))
        dact = jnp.zeros(trunk_in.shape, jnp.float32)
        for kernel_offset in range(3):
            receptive_span = dpad[:, (2 - kernel_offset) * spread:(2 - kernel_offset) * spread + length]
            dact = dact + jnp.dot(receptive_span, dilated_kernel_weight[layer, kernel_offset].T, preferred_element_type=jnp.float32)
        upstream = (upstream.astype(jnp.float32) + dact * gelu_slope(trunk_in.astype(jnp.float32))).astype(jnp.bfloat16)
    return jnp.stack(grads)
```

```python
import functools
import math

import jax
import jax.numpy as jnp
from jax import lax
from jax.experimental import pallas as pl
from jax.experimental.pallas import tpu as pltpu
from jax.sharding import PartitionSpec as P

root_half = 0.7071067811865476
inv_root_two_pi = 0.3989422804014327

contract_last = (((1,), (1,)), ((), ()))
contract_first = (((0,), (0,)), ((), ()))


def gelu(value):
    return 0.5 * value * (1.0 + lax.erf(value * root_half))


def gelu_slope(value):
    return (
        0.5 * (1.0 + lax.erf(value * root_half))
        + value * jnp.exp(-0.5 * value * value) * inv_root_two_pi
    )


def padded(cells, sides, width):
    for axis, dim in sides:
        count = lax.axis_size(axis)
        ends = count - 1
        head = lax.slice_in_dim(cells, 0, width, axis=dim)
        tail = lax.slice_in_dim(cells, cells.shape[dim] - width, cells.shape[dim], axis=dim)
        cells = jnp.concatenate(
            [
                lax.ppermute(tail, axis, [(i, (i + 1) % count) for i in range(ends)]),
                cells,
                lax.ppermute(head, axis, [((i + 1) % count, i) for i in range(ends)]),
            ],
            axis=dim,
        )
    return cells


def shifted(block, axis, distance):
    devices = range(lax.axis_size(axis))
    route = [(i - distance, i) for i in devices if i - distance in devices]
    return lax.ppermute(block, axis, route)


def edge_shards(inputs, cotangent, dilated_kernel_weight, point_weight):
    sections = lax.axis_size("pipe")
    section = lax.axis_index("pipe")
    seq_count, bins, chans = inputs.shape
    reach = bins // 2
    table = jnp.array(
        [reach // 2 ** (sections - 1 - level) for level in range(sections)], jnp.int32
    )
    spread = table[section]
    dilation_weight = dilated_kernel_weight[0]
    w_point = point_weight[0]
    inner_channel_count = dilation_weight.shape[2]
    scale = 1.0 / math.sqrt(seq_count * lax.axis_size("dp") * bins * lax.axis_size("ctx"))
    ticks = jnp.arange(seq_count + sections - 1, dtype=jnp.int32)

    def conv_fore(extended):
        running_total = jnp.zeros((bins, inner_channel_count), jnp.float32)
        for kernel_offset in range(3):
            receptive_span = lax.dynamic_slice_in_dim(
                extended, reach + (kernel_offset - 1) * spread, bins, 0
            )
            running_total = running_total + jnp.dot(
                receptive_span, dilation_weight[kernel_offset], preferred_element_type=jnp.float32
            )
        return running_total

    def put(store, slot, valid, item):
        current = lax.dynamic_index_in_dim(store, slot, 0, keepdims=False)
        return lax.dynamic_update_index_in_dim(store, jnp.where(valid, item, current), slot, 0)

    kept_x = jnp.zeros(inputs.shape, jnp.bfloat16)
    kept_ext = jnp.zeros((seq_count, bins + 2 * reach, chans), jnp.bfloat16)
    kept_pre = jnp.zeros((seq_count, bins, inner_channel_count), jnp.float32)

    def fore_tick(carry, tick):
        received, store_x, store_ext, store_pre = carry
        micro = tick - section
        valid = (micro >= 0) & (micro < seq_count)
        slot = jnp.clip(micro, 0, seq_count - 1)
        first = lax.dynamic_index_in_dim(inputs, slot, 0, keepdims=False)
        trunk_in = jnp.where(section == 0, first, received)
        act = gelu(trunk_in.astype(jnp.float32)).astype(jnp.bfloat16)
        extended = padded(act, (("ctx", 0),), reach)
        pre = conv_fore(extended)
        inner = gelu(pre).astype(jnp.bfloat16)
        out = (
            trunk_in.astype(jnp.float32)
            + jnp.dot(inner, w_point, preferred_element_type=jnp.float32)
        ).astype(jnp.bfloat16)
        sent = shifted(out, "pipe", 1)
        store_x = put(store_x, slot, valid, trunk_in)
        store_ext = put(store_ext, slot, valid, extended)
        store_pre = put(store_pre, slot, valid, pre)
        return ((sent, store_x, store_ext, store_pre), None)

    start_recv = jnp.zeros((bins, chans), jnp.bfloat16)
    (unused, kept_x, kept_ext, kept_pre), unused_out = lax.scan(
        fore_tick, (start_recv, kept_x, kept_ext, kept_pre), ticks
    )

    def back_tick(carry, tick):
        received, grad = carry
        micro = tick - (sections - 1 - section)
        valid = (micro >= 0) & (micro < seq_count)
        slot = jnp.clip(micro, 0, seq_count - 1)
        last = (
            lax.dynamic_index_in_dim(cotangent, slot, 0, keepdims=False).astype(jnp.float32) * scale
        ).astype(jnp.bfloat16)
        upstream = jnp.where(section == sections - 1, last, received)
        trunk_in = lax.dynamic_index_in_dim(kept_x, slot, 0, keepdims=False)
        extended = lax.dynamic_index_in_dim(kept_ext, slot, 0, keepdims=False)
        pre = lax.dynamic_index_in_dim(kept_pre, slot, 0, keepdims=False)
        inner_grad = lax.dot_general(
            upstream, w_point, contract_last, preferred_element_type=jnp.float32
        )
        dpre = (inner_grad * gelu_slope(pre) * valid.astype(jnp.float32)).astype(jnp.bfloat16)
        dpre_ext = padded(dpre, (("ctx", 0),), reach)
        dact = jnp.zeros((bins, chans), jnp.float32)
        taps = []
        for kernel_offset in range(3):
            receptive_span = lax.dynamic_slice_in_dim(
                dpre_ext, reach - (kernel_offset - 1) * spread, bins, 0
            )
            dact = dact + lax.dot_general(
                receptive_span,
                dilation_weight[kernel_offset],
                contract_last,
                preferred_element_type=jnp.float32,
            )
            source = lax.dynamic_slice_in_dim(
                extended, reach + (kernel_offset - 1) * spread, bins, 0
            )
            taps.append(
                lax.dot_general(source, dpre, contract_first, preferred_element_type=jnp.float32)
            )
        grad = grad + jnp.stack(taps)
        back = (
            upstream.astype(jnp.float32) + dact * gelu_slope(trunk_in.astype(jnp.float32))
        ).astype(jnp.bfloat16)
        sent = shifted(back, "pipe", -1)
        return ((sent, grad), None)

    start_grad = jnp.zeros((3, chans, inner_channel_count), jnp.float32)
    (unused_back, grad), unused_seq = lax.scan(back_tick, (start_recv, start_grad), ticks)
    term = grad[None]
    return lax.psum_scatter(term, ("dp", "ctx"), scatter_dimension=2, tiled=True)


def moved(value, by, bins):
    pieces = []
    for start in range(0, value.shape[0], bins):
        piece = value[start : start + bins]
        place = lax.broadcasted_iota(jnp.int32, piece.shape, 0)
        if by > 0:
            keep = place >= by
        else:
            keep = place < bins + by
        pieces.append(jnp.where(keep, pltpu.roll(piece, by % bins, 0), 0.0))
    return jnp.concatenate(pieces, axis=0)


def fore(x, weight_ref, spread, bins):
    act = gelu(x.astype(jnp.float32)).astype(jnp.bfloat16)
    terms = [
        jnp.dot(act, weight_ref[0, tap], preferred_element_type=jnp.float32) for tap in range(3)
    ]
    return terms[1] + moved(terms[0], spread, bins) + moved(terms[2], -spread, bins)


def back_pre(dy, pre, point_ref):
    inner_grad = lax.dot_general(
        dy, point_ref[0], contract_last, preferred_element_type=jnp.float32
    )
    return (inner_grad * gelu_slope(pre)).astype(jnp.bfloat16)


def back_trunk(dy, dpre, x, weight_ref, spread, bins):
    wide = dpre.astype(jnp.float32)
    spans = (
        moved(wide, -spread, bins).astype(jnp.bfloat16),
        dpre,
        moved(wide, spread, bins).astype(jnp.bfloat16),
    )
    dact = jnp.zeros(dy.shape, jnp.float32)
    for tap in range(3):
        dact = dact + lax.dot_general(
            spans[tap], weight_ref[0, tap], contract_last, preferred_element_type=jnp.float32
        )
    return (
        dy.astype(jnp.float32) + dact * gelu_slope(x.astype(jnp.float32))
    ).astype(jnp.bfloat16)


def split_kernel(last, inputs_ref, cotangent_ref, *out_refs):
    count = len(out_refs)
    seq_count, bins, chans = inputs_ref.shape
    part = bins // count
    section = lax.axis_index("pipe")
    place = lax.axis_index("ctx")

    def send(source_ref):
        source = source_ref[...].reshape(seq_count * bins, chans)
        for hop in range(count):
            residue = lax.rem(place + hop, count)
            rows = []
            for seq in range(seq_count):
                row = lax.broadcasted_iota(jnp.int32, (part, seq_count * bins), 0)
                col = lax.broadcasted_iota(jnp.int32, (part, seq_count * bins), 1)
                rows.append((col == seq * bins + count * row + residue).astype(jnp.float32))
            pick = jnp.concatenate(rows, axis=0).astype(jnp.bfloat16)
            out_refs[hop][...] = jnp.dot(
                pick, source, preferred_element_type=jnp.float32
            ).astype(jnp.bfloat16)

    @pl.when(section == 0)
    def first():
        send(inputs_ref)

    @pl.when(section == last)
    def final():
        send(cotangent_ref)


def first_kernel(last, count, bins, spread, *refs):
    parts = refs[:count]
    weight_ref, point_ref, whole_ref, out_ref, pre_ref = refs[count:]
    section = lax.axis_index("pipe")
    place = lax.axis_index("ctx")
    part = bins // count
    seq_count = whole_ref.shape[0] // bins

    @pl.when((section == 0) | (section == last))
    def gather():
        for hop in range(count):
            source = lax.rem(place - hop + count, count)
            for seq in range(seq_count):
                at = pl.multiple_of(seq * bins + source * part, part)
                whole_ref[pl.ds(at, part), :] = parts[hop][seq * part : (seq + 1) * part, :]

    @pl.when(section == 0)
    def layer():
        layer_body(whole_ref[...], weight_ref, point_ref, out_ref, pre_ref, spread, bins)


def layer_body(x, weight_ref, point_ref, out_ref, pre_ref, spread, bins):
    pre = fore(x, weight_ref, spread, bins)
    pre_ref[...] = pre
    branch = jnp.dot(
        gelu(pre).astype(jnp.bfloat16), point_ref[0], preferred_element_type=jnp.float32
    )
    out_ref[...] = (x.astype(jnp.float32) + branch).astype(jnp.bfloat16)


def fore_kernel(level, bins, spread, x_ref, weight_ref, point_ref, out_ref, pre_ref):
    @pl.when(lax.axis_index("pipe") == level)
    def layer():
        layer_body(x_ref[...], weight_ref, point_ref, out_ref, pre_ref, spread, bins)


def turn_kernel(level, bins, spread, scale, x_ref, cot_ref, weight_ref, point_ref, dy_ref, dpre_ref):
    @pl.when(lax.axis_index("pipe") == level)
    def layer():
        x = x_ref[...]
        pre = fore(x, weight_ref, spread, bins)
        dy = (cot_ref[...].astype(jnp.float32) * scale).astype(jnp.bfloat16)
        dpre = back_pre(dy, pre, point_ref)
        dpre_ref[...] = dpre
        dy_ref[...] = back_trunk(dy, dpre, x, weight_ref, spread, bins)


def back_kernel(level, bins, spread, dy_in_ref, x_ref, pre_ref, weight_ref, point_ref, dy_ref, dpre_ref):
    @pl.when(lax.axis_index("pipe") == level)
    def layer():
        dy = dy_in_ref[...]
        dpre = back_pre(dy, pre_ref[...], point_ref)
        dpre_ref[...] = dpre
        dy_ref[...] = back_trunk(dy, dpre, x_ref[...], weight_ref, spread, bins)


def head_kernel(sections, dy_in_ref, pre_ref, point_ref, *refs):
    others, out_ref = refs[:-1], refs[-1]
    section = lax.axis_index("pipe")

    @pl.when(section == 0)
    def layer():
        out_ref[...] = back_pre(dy_in_ref[...], pre_ref[...], point_ref)

    for level in range(1, sections):

        @pl.when(section == level)
        def keep(level=level):
            out_ref[...] = others[level - 1][...]


def columns_kernel(sections, groups, *refs):
    xs, out_refs = refs[:sections], refs[sections:]
    count = len(out_refs)
    section = lax.axis_index("pipe")
    place = lax.axis_index("ctx")
    core = lax.axis_index("dp")
    x = xs[0][...].astype(jnp.float32)
    for level in range(1, sections):
        x = jnp.where(section == level, xs[level][...].astype(jnp.float32), x)
    act = gelu(x).astype(jnp.bfloat16)
    chans = act.shape[1]
    width = chans // (groups * count)
    for hop in range(count):
        owner = lax.rem(place + hop, count)
        rows = []
        for step in range(groups):
            start = (lax.rem(core + step, groups) * count + owner) * width
            row = lax.broadcasted_iota(jnp.int32, (width, chans), 0)
            col = lax.broadcasted_iota(jnp.int32, (width, chans), 1)
            rows.append((col == start + row).astype(jnp.float32))
        pick = jnp.concatenate(rows, axis=0).astype(jnp.bfloat16)
        out_refs[hop][...] = lax.dot_general(
            pick, act, contract_last, preferred_element_type=jnp.float32
        ).astype(jnp.bfloat16)


def grad_kernel(sections, count, bins, *refs):
    columns, grads, outs = refs[:count], refs[count : 2 * count], refs[2 * count :]
    section = lax.axis_index("pipe")
    width = outs[0].shape[1]
    act = jnp.concatenate([ref[...] for ref in columns], axis=1)

    def taps(spread):
        dpre = jnp.concatenate([ref[...] for ref in grads], axis=0)
        wide = dpre.astype(jnp.float32)
        spans = (
            moved(wide, -spread, bins).astype(jnp.bfloat16),
            dpre,
            moved(wide, spread, bins).astype(jnp.bfloat16),
        )
        for tap in range(3):
            grad = jnp.dot(act, spans[tap], preferred_element_type=jnp.float32)
            for step, out_ref in enumerate(outs):
                out_ref[tap] = grad[step * width : (step + 1) * width]

    for level in range(sections):

        @pl.when(section == level)
        def run(level=level):
            taps(2**level)


def kernel_call(body, outs, flops, name):
    def call(*args):
        spec = pl.BlockSpec(memory_space=pltpu.VMEM)
        moved_bytes = sum(math.prod(a.shape) * a.dtype.itemsize for a in (*args, *outs))
        return pl.pallas_call(
            body,
            out_shape=list(outs),
            in_specs=[spec] * len(args),
            out_specs=[spec] * len(outs),
            compiler_params=pltpu.CompilerParams(vmem_limit_bytes=24 * 2**20),
            cost_estimate=pl.CostEstimate(
                flops=flops, bytes_accessed=moved_bytes, transcendentals=0
            ),
            name=name,
        )(*args)

    return call


def residue_shards(inputs, cotangent, weight, point):
    sections = lax.axis_size("pipe")
    count = lax.axis_size("ctx")
    groups = lax.axis_size("dp")
    seq_count, bins, chans = inputs.shape
    inner = weight.shape[3]
    rows = seq_count * bins
    scale = 1.0 / math.sqrt(seq_count * groups * bins * count)
    last = sections - 1
    layer_flops = 2 * rows * chans * inner * 4

    trunk = jax.ShapeDtypeStruct((rows, chans), jnp.bfloat16)
    inside = jax.ShapeDtypeStruct((rows, inner), jnp.bfloat16)
    inside_wide = jax.ShapeDtypeStruct((rows, inner), jnp.float32)
    part = jax.ShapeDtypeStruct((rows // count, chans), jnp.bfloat16)

    def hop(value, source, target):
        route = [(source * count + i, target * count + i) for i in range(count)]
        return lax.ppermute(value, ("pipe", "ctx"), route)

    parts = kernel_call(
        functools.partial(split_kernel, last), [part] * count, 2 * rows * rows * chans, "split"
    )(inputs, cotangent)
    stages = sorted({0, last})
    arrived = [parts[0]]
    for step in range(1, count):
        route = [
            (stage * count + i, stage * count + (i + step) % count)
            for stage in stages
            for i in range(count)
        ]
        arrived.append(lax.ppermute(parts[step], ("pipe", "ctx"), route))

    whole, out, pre = kernel_call(
        functools.partial(first_kernel, last, count, bins, 1),
        [trunk, trunk, inside_wide],
        layer_flops,
        "first",
    )(*arrived, weight, point)
    xs, pres = [whole], [pre]
    for level in range(1, last):
        x = hop(out, level - 1, level)
        out, pre = kernel_call(
            functools.partial(fore_kernel, level, bins, 2**level),
            [trunk, inside_wide],
            layer_flops,
            "fore",
        )(x, weight, point)
        xs.append(x)
        pres.append(pre)
    x = hop(out, last - 1, last)
    xs.append(x)
    dy, dpre = kernel_call(
        functools.partial(turn_kernel, last, bins, 2**last, scale),
        [trunk, inside],
        2 * layer_flops,
        "turn",
    )(x, whole, weight, point)
    dpres = [dpre]

    column = jax.ShapeDtypeStruct((chans // count, rows), jnp.bfloat16)
    columns = kernel_call(
        functools.partial(columns_kernel, sections, groups),
        [column] * count,
        2 * rows * chans * chans,
        "columns",
    )(*xs)

    def around(values):
        arrived = [values[0]]
        for step in range(1, count):
            route = [(i, (i + step) % count) for i in range(count)]
            arrived.append(lax.ppermute(values[step], "ctx", route))
        return arrived

    dy = hop(dy, last, last - 1)
    columns = around(columns)
    for level in range(last - 1, 0, -1):
        dy, dpre = kernel_call(
            functools.partial(back_kernel, level, bins, 2**level),
            [trunk, inside],
            layer_flops,
            "back",
        )(dy, xs[level], pres[level], weight, point)
        dpres.insert(0, dpre)
        dy = hop(dy, level, level - 1)
    (dpre,) = kernel_call(
        functools.partial(head_kernel, sections), [inside], layer_flops // 4, "head"
    )(dy, pres[0], point, *dpres)
    grads = around([dpre] * count)

    share = jax.ShapeDtypeStruct((3, chans // (count * groups), inner), jnp.float32)
    mine, *others = kernel_call(
        functools.partial(grad_kernel, sections, count, bins),
        [share] * groups,
        2 * 3 * rows * chans * inner,
        "grad",
    )(*columns, *grads)
    for step, other in enumerate(others, 1):
        route = [(i, (i + step) % groups) for i in range(groups)]
        mine = mine + lax.ppermute(other, "dp", route)
    return mine[None]


def solution(mesh):
    def shards(inputs, cotangent, dilated_kernel_weight, point_weight):
        bins = inputs.shape[1]
        first_spread = bins // 2 // 2 ** (mesh.shape["pipe"] - 1)
        count = mesh.shape["ctx"]
        residues = (
            first_spread == count
            and mesh.shape["pipe"] > 1
            and bins % (16 * count) == 0
            and inputs.shape[2] % (count * mesh.shape["dp"]) == 0
        )
        plan = residue_shards if residues else edge_shards
        return plan(inputs, cotangent, dilated_kernel_weight, point_weight)

    return jax.shard_map(
        shards,
        mesh=mesh,
        in_specs=(
            P("dp", "ctx", None),
            P("dp", "ctx", None),
            P("pipe", None, None, None),
            P("pipe", None, None),
        ),
        out_specs=P("pipe", None, ("dp", "ctx"), None),
        check_vma=False,
    )
```

```python
import functools
import math

import jax
import jax.numpy as jnp
from jax import lax
from jax.experimental import pallas as pl
from jax.experimental.pallas import tpu as pltpu
from jax.sharding import PartitionSpec as P

root_half = 0.7071067811865476
inv_root_two_pi = 0.3989422804014327

in_vmem = pl.BlockSpec(memory_space=pltpu.VMEM)
anywhere = pl.BlockSpec(memory_space=pl.ANY)
wide_grant = 56 * 2**20
contract_last = (((1,), (1,)), ((), ()))
contract_first = (((0,), (0,)), ((), ()))


def gelu(value):
    return 0.5 * value * (1.0 + lax.erf(value * root_half))


def gelu_slope(value):
    return (
        0.5 * (1.0 + lax.erf(value * root_half))
        + value * jnp.exp(-0.5 * value * value) * inv_root_two_pi
    )


def padded(cells, sides, width):
    for axis, dim in sides:
        count = lax.axis_size(axis)
        ends = count - 1
        head = lax.slice_in_dim(cells, 0, width, axis=dim)
        tail = lax.slice_in_dim(cells, cells.shape[dim] - width, cells.shape[dim], axis=dim)
        cells = jnp.concatenate(
            [
                lax.ppermute(tail, axis, [(i, (i + 1) % count) for i in range(ends)]),
                cells,
                lax.ppermute(head, axis, [((i + 1) % count, i) for i in range(ends)]),
            ],
            axis=dim,
        )
    return cells


def shifted(block, axis, distance):
    devices = range(lax.axis_size(axis))
    route = [(i - distance, i) for i in devices if i - distance in devices]
    return lax.ppermute(block, axis, route)


def edge_shards(inputs, cotangent, dilated_kernel_weight, point_weight):
    sections = lax.axis_size("pipe")
    section = lax.axis_index("pipe")
    seq_count, bins, chans = inputs.shape
    reach = bins // 2
    table = jnp.array(
        [reach // 2 ** (sections - 1 - level) for level in range(sections)], jnp.int32
    )
    spread = table[section]
    dilation_weight = dilated_kernel_weight[0]
    w_point = point_weight[0]
    inner_channel_count = dilation_weight.shape[2]
    scale = 1.0 / math.sqrt(seq_count * lax.axis_size("dp") * bins * lax.axis_size("ctx"))
    ticks = jnp.arange(seq_count + sections - 1, dtype=jnp.int32)

    def conv_fore(extended):
        running_total = jnp.zeros((bins, inner_channel_count), jnp.float32)
        for kernel_offset in range(3):
            receptive_span = lax.dynamic_slice_in_dim(
                extended, reach + (kernel_offset - 1) * spread, bins, 0
            )
            running_total = running_total + jnp.dot(
                receptive_span, dilation_weight[kernel_offset], preferred_element_type=jnp.float32
            )
        return running_total

    def put(store, slot, valid, item):
        current = lax.dynamic_index_in_dim(store, slot, 0, keepdims=False)
        return lax.dynamic_update_index_in_dim(store, jnp.where(valid, item, current), slot, 0)

    kept_x = jnp.zeros(inputs.shape, jnp.bfloat16)
    kept_ext = jnp.zeros((seq_count, bins + 2 * reach, chans), jnp.bfloat16)
    kept_pre = jnp.zeros((seq_count, bins, inner_channel_count), jnp.float32)

    def fore_tick(carry, tick):
        received, store_x, store_ext, store_pre = carry
        micro = tick - section
        valid = (micro >= 0) & (micro < seq_count)
        slot = jnp.clip(micro, 0, seq_count - 1)
        first = lax.dynamic_index_in_dim(inputs, slot, 0, keepdims=False)
        trunk_in = jnp.where(section == 0, first, received)
        act = gelu(trunk_in.astype(jnp.float32)).astype(jnp.bfloat16)
        extended = padded(act, (("ctx", 0),), reach)
        pre = conv_fore(extended)
        inner = gelu(pre).astype(jnp.bfloat16)
        out = (
            trunk_in.astype(jnp.float32)
            + jnp.dot(inner, w_point, preferred_element_type=jnp.float32)
        ).astype(jnp.bfloat16)
        sent = shifted(out, "pipe", 1)
        store_x = put(store_x, slot, valid, trunk_in)
        store_ext = put(store_ext, slot, valid, extended)
        store_pre = put(store_pre, slot, valid, pre)
        return ((sent, store_x, store_ext, store_pre), None)

    start_recv = jnp.zeros((bins, chans), jnp.bfloat16)
    (unused, kept_x, kept_ext, kept_pre), unused_out = lax.scan(
        fore_tick, (start_recv, kept_x, kept_ext, kept_pre), ticks
    )

    def back_tick(carry, tick):
        received, grad = carry
        micro = tick - (sections - 1 - section)
        valid = (micro >= 0) & (micro < seq_count)
        slot = jnp.clip(micro, 0, seq_count - 1)
        last = (
            lax.dynamic_index_in_dim(cotangent, slot, 0, keepdims=False).astype(jnp.float32) * scale
        ).astype(jnp.bfloat16)
        upstream = jnp.where(section == sections - 1, last, received)
        trunk_in = lax.dynamic_index_in_dim(kept_x, slot, 0, keepdims=False)
        extended = lax.dynamic_index_in_dim(kept_ext, slot, 0, keepdims=False)
        pre = lax.dynamic_index_in_dim(kept_pre, slot, 0, keepdims=False)
        inner_grad = lax.dot_general(
            upstream, w_point, contract_last, preferred_element_type=jnp.float32
        )
        dpre = (inner_grad * gelu_slope(pre) * valid.astype(jnp.float32)).astype(jnp.bfloat16)
        dpre_ext = padded(dpre, (("ctx", 0),), reach)
        dact = jnp.zeros((bins, chans), jnp.float32)
        taps = []
        for kernel_offset in range(3):
            receptive_span = lax.dynamic_slice_in_dim(
                dpre_ext, reach - (kernel_offset - 1) * spread, bins, 0
            )
            dact = dact + lax.dot_general(
                receptive_span,
                dilation_weight[kernel_offset],
                contract_last,
                preferred_element_type=jnp.float32,
            )
            source = lax.dynamic_slice_in_dim(
                extended, reach + (kernel_offset - 1) * spread, bins, 0
            )
            taps.append(
                lax.dot_general(source, dpre, contract_first, preferred_element_type=jnp.float32)
            )
        grad = grad + jnp.stack(taps)
        back = (
            upstream.astype(jnp.float32) + dact * gelu_slope(trunk_in.astype(jnp.float32))
        ).astype(jnp.bfloat16)
        sent = shifted(back, "pipe", -1)
        return ((sent, grad), None)

    start_grad = jnp.zeros((3, chans, inner_channel_count), jnp.float32)
    (unused_back, grad), unused_seq = lax.scan(back_tick, (start_recv, start_grad), ticks)
    term = grad[None]
    return lax.psum_scatter(term, ("dp", "ctx"), scatter_dimension=2, tiled=True)


def moved(value, by, bins):
    pieces = []
    for start in range(0, value.shape[0], bins):
        piece = value[start : start + bins]
        place = lax.broadcasted_iota(jnp.int32, piece.shape, 0)
        if by > 0:
            keep = place >= by
        else:
            keep = place < bins + by
        pieces.append(jnp.where(keep, pltpu.roll(piece, by % bins, 0), 0.0))
    return jnp.concatenate(pieces, axis=0)


def fore(x, weight_ref, spread, bins):
    return conv(gelu(x.astype(jnp.float32)).astype(jnp.bfloat16), weight_ref, spread, bins)


def conv(act, weight_ref, spread, bins):
    terms = [
        jnp.dot(act, weight_ref[0, tap], preferred_element_type=jnp.float32) for tap in range(3)
    ]
    return terms[1] + moved(terms[0], spread, bins) + moved(terms[2], -spread, bins)


def back_pre(dy, pre, point_ref):
    inner_grad = lax.dot_general(
        dy, point_ref[0], contract_last, preferred_element_type=jnp.float32
    )
    return (inner_grad * gelu_slope(pre)).astype(jnp.bfloat16)


def back_trunk(dy, dpre, x, weight_ref, spread, bins):
    wide = dpre.astype(jnp.float32)
    spans = (
        moved(wide, -spread, bins).astype(jnp.bfloat16),
        dpre,
        moved(wide, spread, bins).astype(jnp.bfloat16),
    )
    dact = jnp.zeros(dy.shape, jnp.float32)
    for tap in range(3):
        dact = dact + lax.dot_general(
            spans[tap], weight_ref[0, tap], contract_last, preferred_element_type=jnp.float32
        )
    return (
        dy.astype(jnp.float32) + dact * gelu_slope(x.astype(jnp.float32))
    ).astype(jnp.bfloat16)


def split_kernel(last, count, inputs_ref, cotangent_ref, parts_ref, held, sem):
    seq_count, bins, chans = inputs_ref.shape
    part = bins // count
    section = lax.axis_index("pipe")

    def send(source_ref):
        load = pltpu.make_async_copy(source_ref, held, sem)
        load.start()
        row = lax.broadcasted_iota(jnp.int32, (part, seq_count * bins), 0)
        col = lax.broadcasted_iota(jnp.int32, (part, seq_count * bins), 1)
        picks = [
            jnp.concatenate(
                [
                    (col == seq * bins + count * row + residue).astype(jnp.float32)
                    for seq in range(seq_count)
                ],
                axis=0,
            ).astype(jnp.bfloat16)
            for residue in range(count)
        ]
        load.wait()
        source = held[...].reshape(seq_count * bins, chans)
        for residue in range(count):
            parts_ref[residue] = jnp.dot(
                picks[residue], source, preferred_element_type=jnp.float32
            ).astype(jnp.bfloat16)

    @pl.when(section == 0)
    def first():
        send(inputs_ref)

    @pl.when(section == last)
    def final():
        send(cotangent_ref)


def first_kernel(
    last, bins, spread, parts_ref, weight_ref, point_ref, whole_ref, out_ref, pre_ref, weight_held, point_held, sems
):
    section = lax.axis_index("pipe")
    count = parts_ref.shape[0]
    part = bins // count
    seq_count = whole_ref.shape[0] // bins

    def gather():
        for source in range(count):
            for seq in range(seq_count):
                at = seq * bins + source * part
                whole_ref[at : at + part, :] = parts_ref[source, seq * part : (seq + 1) * part, :]

    @pl.when(section == 0)
    def layer():
        load_weight = pltpu.make_async_copy(weight_ref, weight_held, sems.at[0])
        load_point = pltpu.make_async_copy(point_ref, point_held, sems.at[1])
        load_weight.start()
        load_point.start()
        gather()
        x = whole_ref[...]
        act = gelu(x.astype(jnp.float32)).astype(jnp.bfloat16)
        load_weight.wait()
        pre = conv(act, weight_held, spread, bins)
        load_point.wait()
        finish(x, pre, point_held, out_ref, pre_ref)

    @pl.when(section == last)
    def turn():
        gather()


def finish(x, pre, point_ref, out_ref, pre_ref):
    pre_ref[...] = pre
    branch = jnp.dot(
        gelu(pre).astype(jnp.bfloat16), point_ref[0], preferred_element_type=jnp.float32
    )
    out_ref[...] = (x.astype(jnp.float32) + branch).astype(jnp.bfloat16)


def fore_kernel(level, bins, spread, x_ref, weight_ref, point_ref, out_ref, pre_ref):
    @pl.when(lax.axis_index("pipe") == level)
    def layer():
        x = x_ref[...]
        finish(x, fore(x, weight_ref, spread, bins), point_ref, out_ref, pre_ref)


def turn_kernel(level, bins, spread, scale, x_ref, cot_ref, weight_ref, point_ref, dy_ref, dpre_ref):
    @pl.when(lax.axis_index("pipe") == level)
    def layer():
        x = x_ref[...]
        pre = fore(x, weight_ref, spread, bins)
        dy = (cot_ref[...].astype(jnp.float32) * scale).astype(jnp.bfloat16)
        dpre = back_pre(dy, pre, point_ref)
        dpre_ref[...] = dpre
        dy_ref[...] = back_trunk(dy, dpre, x, weight_ref, spread, bins)


def back_kernel(level, bins, spread, dy_in_ref, x_ref, pre_ref, weight_ref, point_ref, dy_ref, dpre_ref):
    @pl.when(lax.axis_index("pipe") == level)
    def layer():
        dy = dy_in_ref[...]
        dpre = back_pre(dy, pre_ref[...], point_ref)
        dpre_ref[...] = dpre
        dy_ref[...] = back_trunk(dy, dpre, x_ref[...], weight_ref, spread, bins)


def head_kernel(sections, dy_in_ref, pre_ref, point_ref, *refs):
    others, out_ref = refs[:-1], refs[-1]
    section = lax.axis_index("pipe")

    @pl.when(section == 0)
    def layer():
        dpre = back_pre(dy_in_ref[...], pre_ref[...], point_ref)
        for copy in range(out_ref.shape[0]):
            out_ref[copy] = dpre

    for level in range(1, sections):

        @pl.when(section == level)
        def keep(level=level):
            for copy in range(out_ref.shape[0]):
                out_ref[copy] = others[level - 1][...]


def columns_kernel(sections, groups, *refs):
    xs, out_ref = refs[:sections], refs[sections]
    count = out_ref.shape[0]
    section = lax.axis_index("pipe")
    core = lax.axis_index("dp")
    x = xs[0][...].astype(jnp.float32)
    for level in range(1, sections):
        x = jnp.where(section == level, xs[level][...].astype(jnp.float32), x)
    act = gelu(x).astype(jnp.bfloat16)
    chans = act.shape[1]
    width = chans // (groups * count)
    row = lax.broadcasted_iota(jnp.int32, (width, chans), 0)
    col = lax.broadcasted_iota(jnp.int32, (width, chans), 1)
    for owner in range(count):
        rows = []
        for step in range(groups):
            start = (lax.rem(core + step, groups) * count + owner) * width
            rows.append((col == start + row).astype(jnp.float32))
        pick = jnp.concatenate(rows, axis=0).astype(jnp.bfloat16)
        out_ref[owner] = lax.dot_general(
            pick, act, contract_last, preferred_element_type=jnp.float32
        ).astype(jnp.bfloat16)


def grad_kernel(sections, bins, columns_ref, grads_ref, *outs):
    section = lax.axis_index("pipe")
    count, rows, inner = grads_ref.shape
    width = outs[0].shape[1]
    act = jnp.concatenate([columns_ref[source] for source in range(count)], axis=1)

    def taps(spread):
        dpre = grads_ref[...].reshape(count * rows, inner)
        wide = dpre.astype(jnp.float32)
        spans = (
            moved(wide, -spread, bins).astype(jnp.bfloat16),
            dpre,
            moved(wide, spread, bins).astype(jnp.bfloat16),
        )
        for tap in range(3):
            grad = jnp.dot(act, spans[tap], preferred_element_type=jnp.float32)
            for step, out_ref in enumerate(outs):
                out_ref[tap] = grad[step * width : (step + 1) * width]

    for level in range(sections):

        @pl.when(section == level)
        def run(level=level):
            taps(2**level)


def kernel_call(body, outs, flops, name, in_specs=None, scratch=(), limit=24 * 2**20):
    def call(*args):
        moved_bytes = sum(math.prod(a.shape) * a.dtype.itemsize for a in (*args, *outs))
        return pl.pallas_call(
            body,
            out_shape=list(outs),
            in_specs=in_specs or [in_vmem] * len(args),
            out_specs=[in_vmem] * len(outs),
            scratch_shapes=list(scratch),
            compiler_params=pltpu.CompilerParams(vmem_limit_bytes=limit),
            cost_estimate=pl.CostEstimate(
                flops=flops, bytes_accessed=moved_bytes, transcendentals=0
            ),
            name=name,
        )(*args)

    return call


def residue_shards(inputs, cotangent, weight, point):
    sections = lax.axis_size("pipe")
    count = lax.axis_size("ctx")
    groups = lax.axis_size("dp")
    seq_count, bins, chans = inputs.shape
    inner = weight.shape[3]
    rows = seq_count * bins
    scale = 1.0 / math.sqrt(seq_count * groups * bins * count)
    last = sections - 1
    layer_flops = 2 * rows * chans * inner * 4

    trunk = jax.ShapeDtypeStruct((rows, chans), jnp.bfloat16)
    inside = jax.ShapeDtypeStruct((rows, inner), jnp.bfloat16)
    inside_wide = jax.ShapeDtypeStruct((rows, inner), jnp.float32)
    parts = jax.ShapeDtypeStruct((count, rows // count, chans), jnp.bfloat16)

    def hop(value, source, target):
        route = [(source * count + i, target * count + i) for i in range(count)]
        return lax.ppermute(value, ("pipe", "ctx"), route)

    def exchange(blocks):
        return lax.all_to_all(blocks, "ctx", 0, 0)

    (parts,) = kernel_call(
        functools.partial(split_kernel, last, count),
        [parts],
        2 * rows * rows * chans,
        "split",
        in_specs=[anywhere] * 2,
        scratch=[pltpu.VMEM(inputs.shape, jnp.bfloat16), pltpu.SemaphoreType.DMA],
        limit=wide_grant,
    )(inputs, cotangent)

    whole, out, pre = kernel_call(
        functools.partial(first_kernel, last, bins, 1),
        [trunk, trunk, inside_wide],
        layer_flops,
        "first",
        in_specs=[in_vmem, anywhere, anywhere],
        scratch=[
            pltpu.VMEM(weight.shape, jnp.bfloat16),
            pltpu.VMEM(point.shape, jnp.bfloat16),
            pltpu.SemaphoreType.DMA((2,)),
        ],
        limit=wide_grant,
    )(exchange(parts), weight, point)
    xs, pres = [whole], [pre]
    for level in range(1, last):
        x = hop(out, level - 1, level)
        out, pre = kernel_call(
            functools.partial(fore_kernel, level, bins, 2**level),
            [trunk, inside_wide],
            layer_flops,
            "fore",
        )(x, weight, point)
        xs.append(x)
        pres.append(pre)
    x = hop(out, last - 1, last)
    xs.append(x)
    dy, dpre = kernel_call(
        functools.partial(turn_kernel, last, bins, 2**last, scale),
        [trunk, inside],
        2 * layer_flops,
        "turn",
    )(x, whole, weight, point)
    dpres = [dpre]

    dy = hop(dy, last, last - 1)
    columns = jax.ShapeDtypeStruct((count, chans // count, rows), jnp.bfloat16)
    (columns,) = kernel_call(
        functools.partial(columns_kernel, sections, groups),
        [columns],
        2 * rows * chans * chans,
        "columns",
    )(*xs)
    dy, columns = lax.optimization_barrier((dy, exchange(columns)))
    for level in range(last - 1, 0, -1):
        dy, dpre = kernel_call(
            functools.partial(back_kernel, level, bins, 2**level),
            [trunk, inside],
            layer_flops,
            "back",
        )(dy, xs[level], pres[level], weight, point)
        dpres.insert(0, dpre)
        dy = hop(dy, level, level - 1)
    copies = jax.ShapeDtypeStruct((count, rows, inner), jnp.bfloat16)
    (copies,) = kernel_call(
        functools.partial(head_kernel, sections), [copies], layer_flops // 4, "head"
    )(dy, pres[0], point, *dpres)
    grads = exchange(copies)

    share = jax.ShapeDtypeStruct((3, chans // (count * groups), inner), jnp.float32)
    mine, *others = kernel_call(
        functools.partial(grad_kernel, sections, bins),
        [share] * groups,
        2 * 3 * rows * chans * inner,
        "grad",
    )(columns, grads)
    for step, other in enumerate(others, 1):
        route = [(i, (i + step) % groups) for i in range(groups)]
        mine = mine + lax.ppermute(other, "dp", route)
    return mine[None]


def solution(mesh):
    def shards(inputs, cotangent, dilated_kernel_weight, point_weight):
        bins = inputs.shape[1]
        first_spread = bins // 2 // 2 ** (mesh.shape["pipe"] - 1)
        count = mesh.shape["ctx"]
        residues = (
            first_spread == count
            and mesh.shape["pipe"] > 1
            and bins % (16 * count) == 0
            and inputs.shape[2] % (count * mesh.shape["dp"]) == 0
        )
        plan = residue_shards if residues else edge_shards
        return plan(inputs, cotangent, dilated_kernel_weight, point_weight)

    return jax.shard_map(
        shards,
        mesh=mesh,
        in_specs=(
            P("dp", "ctx", None),
            P("dp", "ctx", None),
            P("pipe", None, None, None),
            P("pipe", None, None),
        ),
        out_specs=P("pipe", None, ("dp", "ctx"), None),
        check_vma=False,
    )
```

```python
import functools
import math

import jax
import jax.numpy as jnp
from jax import lax
from jax.experimental import pallas as pl
from jax.experimental.pallas import tpu as pltpu
from jax.sharding import PartitionSpec as P

root_half = 0.7071067811865476
inv_root_two_pi = 0.3989422804014327

contract_last = (((1,), (1,)), ((), ()))
contract_first = (((0,), (0,)), ((), ()))


def gelu(value):
    return 0.5 * value * (1.0 + lax.erf(value * root_half))


def gelu_slope(value):
    return (
        0.5 * (1.0 + lax.erf(value * root_half))
        + value * jnp.exp(-0.5 * value * value) * inv_root_two_pi
    )


def padded(cells, sides, width):
    for axis, dim in sides:
        count = lax.axis_size(axis)
        ends = count - 1
        head = lax.slice_in_dim(cells, 0, width, axis=dim)
        tail = lax.slice_in_dim(cells, cells.shape[dim] - width, cells.shape[dim], axis=dim)
        cells = jnp.concatenate(
            [
                lax.ppermute(tail, axis, [(i, (i + 1) % count) for i in range(ends)]),
                cells,
                lax.ppermute(head, axis, [((i + 1) % count, i) for i in range(ends)]),
            ],
            axis=dim,
        )
    return cells


def shifted(block, axis, distance):
    devices = range(lax.axis_size(axis))
    route = [(i - distance, i) for i in devices if i - distance in devices]
    return lax.ppermute(block, axis, route)


def edge_shards(inputs, cotangent, dilated_kernel_weight, point_weight):
    sections = lax.axis_size("pipe")
    section = lax.axis_index("pipe")
    seq_count, bins, chans = inputs.shape
    reach = bins // 2
    table = jnp.array(
        [reach // 2 ** (sections - 1 - level) for level in range(sections)], jnp.int32
    )
    spread = table[section]
    dilation_weight = dilated_kernel_weight[0]
    w_point = point_weight[0]
    inner_channel_count = dilation_weight.shape[2]
    scale = 1.0 / math.sqrt(seq_count * lax.axis_size("dp") * bins * lax.axis_size("ctx"))
    ticks = jnp.arange(seq_count + sections - 1, dtype=jnp.int32)

    def conv_fore(extended):
        running_total = jnp.zeros((bins, inner_channel_count), jnp.float32)
        for kernel_offset in range(3):
            receptive_span = lax.dynamic_slice_in_dim(
                extended, reach + (kernel_offset - 1) * spread, bins, 0
            )
            running_total = running_total + jnp.dot(
                receptive_span, dilation_weight[kernel_offset], preferred_element_type=jnp.float32
            )
        return running_total

    def put(store, slot, valid, item):
        current = lax.dynamic_index_in_dim(store, slot, 0, keepdims=False)
        return lax.dynamic_update_index_in_dim(store, jnp.where(valid, item, current), slot, 0)

    kept_x = jnp.zeros(inputs.shape, jnp.bfloat16)
    kept_ext = jnp.zeros((seq_count, bins + 2 * reach, chans), jnp.bfloat16)
    kept_pre = jnp.zeros((seq_count, bins, inner_channel_count), jnp.float32)

    def fore_tick(carry, tick):
        received, store_x, store_ext, store_pre = carry
        micro = tick - section
        valid = (micro >= 0) & (micro < seq_count)
        slot = jnp.clip(micro, 0, seq_count - 1)
        first = lax.dynamic_index_in_dim(inputs, slot, 0, keepdims=False)
        trunk_in = jnp.where(section == 0, first, received)
        act = gelu(trunk_in.astype(jnp.float32)).astype(jnp.bfloat16)
        extended = padded(act, (("ctx", 0),), reach)
        pre = conv_fore(extended)
        inner = gelu(pre).astype(jnp.bfloat16)
        out = (
            trunk_in.astype(jnp.float32)
            + jnp.dot(inner, w_point, preferred_element_type=jnp.float32)
        ).astype(jnp.bfloat16)
        sent = shifted(out, "pipe", 1)
        store_x = put(store_x, slot, valid, trunk_in)
        store_ext = put(store_ext, slot, valid, extended)
        store_pre = put(store_pre, slot, valid, pre)
        return ((sent, store_x, store_ext, store_pre), None)

    start_recv = jnp.zeros((bins, chans), jnp.bfloat16)
    (unused, kept_x, kept_ext, kept_pre), unused_out = lax.scan(
        fore_tick, (start_recv, kept_x, kept_ext, kept_pre), ticks
    )

    def back_tick(carry, tick):
        received, grad = carry
        micro = tick - (sections - 1 - section)
        valid = (micro >= 0) & (micro < seq_count)
        slot = jnp.clip(micro, 0, seq_count - 1)
        last = (
            lax.dynamic_index_in_dim(cotangent, slot, 0, keepdims=False).astype(jnp.float32) * scale
        ).astype(jnp.bfloat16)
        upstream = jnp.where(section == sections - 1, last, received)
        trunk_in = lax.dynamic_index_in_dim(kept_x, slot, 0, keepdims=False)
        extended = lax.dynamic_index_in_dim(kept_ext, slot, 0, keepdims=False)
        pre = lax.dynamic_index_in_dim(kept_pre, slot, 0, keepdims=False)
        inner_grad = lax.dot_general(
            upstream, w_point, contract_last, preferred_element_type=jnp.float32
        )
        dpre = (inner_grad * gelu_slope(pre) * valid.astype(jnp.float32)).astype(jnp.bfloat16)
        dpre_ext = padded(dpre, (("ctx", 0),), reach)
        dact = jnp.zeros((bins, chans), jnp.float32)
        taps = []
        for kernel_offset in range(3):
            receptive_span = lax.dynamic_slice_in_dim(
                dpre_ext, reach - (kernel_offset - 1) * spread, bins, 0
            )
            dact = dact + lax.dot_general(
                receptive_span,
                dilation_weight[kernel_offset],
                contract_last,
                preferred_element_type=jnp.float32,
            )
            source = lax.dynamic_slice_in_dim(
                extended, reach + (kernel_offset - 1) * spread, bins, 0
            )
            taps.append(
                lax.dot_general(source, dpre, contract_first, preferred_element_type=jnp.float32)
            )
        grad = grad + jnp.stack(taps)
        back = (
            upstream.astype(jnp.float32) + dact * gelu_slope(trunk_in.astype(jnp.float32))
        ).astype(jnp.bfloat16)
        sent = shifted(back, "pipe", -1)
        return ((sent, grad), None)

    start_grad = jnp.zeros((3, chans, inner_channel_count), jnp.float32)
    (unused_back, grad), unused_seq = lax.scan(back_tick, (start_recv, start_grad), ticks)
    term = grad[None]
    return lax.psum_scatter(term, ("dp", "ctx"), scatter_dimension=2, tiled=True)


def moved(value, by, bins):
    pieces = []
    for start in range(0, value.shape[0], bins):
        piece = value[start : start + bins]
        place = lax.broadcasted_iota(jnp.int32, piece.shape, 0)
        if by > 0:
            keep = place >= by
        else:
            keep = place < bins + by
        pieces.append(jnp.where(keep, pltpu.roll(piece, by % bins, 0), 0.0))
    return jnp.concatenate(pieces, axis=0)


def fore(x, weight_ref, spread, bins):
    act = gelu(x.astype(jnp.float32)).astype(jnp.bfloat16)
    terms = [
        jnp.dot(act, weight_ref[0, tap], preferred_element_type=jnp.float32) for tap in range(3)
    ]
    return terms[1] + moved(terms[0], spread, bins) + moved(terms[2], -spread, bins)


def back_pre(dy, pre, point_ref):
    inner_grad = lax.dot_general(
        dy, point_ref[0], contract_last, preferred_element_type=jnp.float32
    )
    return (inner_grad * gelu_slope(pre)).astype(jnp.bfloat16)


def back_trunk(dy, dpre, x, weight_ref, spread, bins):
    wide = dpre.astype(jnp.float32)
    spans = (
        moved(wide, -spread, bins).astype(jnp.bfloat16),
        dpre,
        moved(wide, spread, bins).astype(jnp.bfloat16),
    )
    dact = jnp.zeros(dy.shape, jnp.float32)
    for tap in range(3):
        dact = dact + lax.dot_general(
            spans[tap], weight_ref[0, tap], contract_last, preferred_element_type=jnp.float32
        )
    return (
        dy.astype(jnp.float32) + dact * gelu_slope(x.astype(jnp.float32))
    ).astype(jnp.bfloat16)


def split_kernel(last, payload_ref, *out_refs):
    count = len(out_refs)
    seq_count, bins, chans = payload_ref.shape
    part = bins // count
    section = lax.axis_index("pipe")
    place = lax.axis_index("ctx")

    @pl.when((section == 0) | (section == last))
    def send():
        source = payload_ref[...].reshape(seq_count * bins, chans)
        row = lax.broadcasted_iota(jnp.int32, (part, seq_count * bins), 0)
        col = lax.broadcasted_iota(jnp.int32, (part, seq_count * bins), 1)
        for hop in range(count):
            residue = lax.rem(place + hop, count)
            rows = [
                (col == seq * bins + count * row + residue).astype(jnp.float32)
                for seq in range(seq_count)
            ]
            pick = jnp.concatenate(rows, axis=0).astype(jnp.bfloat16)
            out_refs[hop][...] = jnp.dot(
                pick, source, preferred_element_type=jnp.float32
            ).astype(jnp.bfloat16)


def hold_kernel(part_ref, weight_ref, point_ref, out_ref):
    out_ref[...] = jnp.zeros(out_ref.shape, out_ref.dtype)


def gather_kernel(last, count, bins, *refs):
    parts, whole_refs = refs[:count], refs[count + 1 :]
    section = lax.axis_index("pipe")
    place = lax.axis_index("ctx")
    part = bins // count

    @pl.when((section == 0) | (section == last))
    def gather():
        for hop in range(count):
            source = lax.rem(place - hop + count, count)
            at = pl.multiple_of(source * part, part)
            for seq, whole_ref in enumerate(whole_refs):
                whole_ref[pl.ds(at, part), :] = parts[hop][seq * part : (seq + 1) * part, :]


def layer_body(x, weight_ref, point_ref, out_ref, pre_ref, spread, bins):
    pre = fore(x, weight_ref, spread, bins)
    pre_ref[...] = pre
    branch = jnp.dot(
        gelu(pre).astype(jnp.bfloat16), point_ref[0], preferred_element_type=jnp.float32
    )
    out_ref[...] = (x.astype(jnp.float32) + branch).astype(jnp.bfloat16)


def fore_kernel(level, bins, spread, x_ref, weight_ref, point_ref, out_ref, pre_ref):
    @pl.when(lax.axis_index("pipe") == level)
    def layer():
        layer_body(x_ref[...], weight_ref, point_ref, out_ref, pre_ref, spread, bins)


def turn_kernel(level, bins, spread, scale, x_ref, cot_ref, weight_ref, point_ref, dy_ref, dpre_ref):
    @pl.when(lax.axis_index("pipe") == level)
    def layer():
        x = x_ref[...]
        pre = fore(x, weight_ref, spread, bins)
        dy = (cot_ref[...].astype(jnp.float32) * scale).astype(jnp.bfloat16)
        dpre = back_pre(dy, pre, point_ref)
        dpre_ref[...] = dpre
        dy_ref[...] = back_trunk(dy, dpre, x, weight_ref, spread, bins)


def back_kernel(level, bins, spread, dy_in_ref, x_ref, pre_ref, weight_ref, point_ref, dy_ref, dpre_ref):
    @pl.when(lax.axis_index("pipe") == level)
    def layer():
        dy = dy_in_ref[...]
        dpre = back_pre(dy, pre_ref[...], point_ref)
        dpre_ref[...] = dpre
        dy_ref[...] = back_trunk(dy, dpre, x_ref[...], weight_ref, spread, bins)


def head_kernel(sections, dy_in_ref, pre_ref, point_ref, *refs):
    others, out_ref = refs[:-1], refs[-1]
    section = lax.axis_index("pipe")

    @pl.when(section == 0)
    def layer():
        out_ref[...] = back_pre(dy_in_ref[...], pre_ref[...], point_ref)

    for level in range(1, sections):

        @pl.when(section == level)
        def keep(level=level):
            out_ref[...] = others[level - 1][...]


def columns_kernel(sections, groups, seq_count, *refs):
    runs, out_refs = refs[: sections * seq_count], refs[sections * seq_count :]
    count = len(out_refs)
    section = lax.axis_index("pipe")
    place = lax.axis_index("ctx")
    core = lax.axis_index("dp")
    xs = [
        jnp.concatenate(
            [ref[...] for ref in runs[level * seq_count : (level + 1) * seq_count]], axis=0
        )
        for level in range(sections)
    ]
    x = xs[0].astype(jnp.float32)
    for level in range(1, sections):
        x = jnp.where(section == level, xs[level].astype(jnp.float32), x)
    act = gelu(x).astype(jnp.bfloat16)
    chans = act.shape[1]
    width = chans // (groups * count)
    for hop in range(count):
        owner = lax.rem(place + hop, count)
        rows = []
        for step in range(groups):
            start = (lax.rem(core + step, groups) * count + owner) * width
            row = lax.broadcasted_iota(jnp.int32, (width, chans), 0)
            col = lax.broadcasted_iota(jnp.int32, (width, chans), 1)
            rows.append((col == start + row).astype(jnp.float32))
        pick = jnp.concatenate(rows, axis=0).astype(jnp.bfloat16)
        out_refs[hop][...] = lax.dot_general(
            pick, act, contract_last, preferred_element_type=jnp.float32
        ).astype(jnp.bfloat16)


def grad_kernel(sections, count, seq_count, bins, *refs):
    columns, refs = refs[:count], refs[count:]
    grads, outs = refs[: count * seq_count], refs[count * seq_count :]
    section = lax.axis_index("pipe")
    width = outs[0].shape[1]
    act = jnp.concatenate([ref[...] for ref in columns], axis=1)

    def taps(spread):
        dpre = jnp.concatenate([ref[...] for ref in grads], axis=0)
        wide = dpre.astype(jnp.float32)
        spans = (
            moved(wide, -spread, bins).astype(jnp.bfloat16),
            dpre,
            moved(wide, spread, bins).astype(jnp.bfloat16),
        )
        for tap in range(3):
            grad = jnp.dot(act, spans[tap], preferred_element_type=jnp.float32)
            for step, out_ref in enumerate(outs):
                out_ref[tap] = grad[step * width : (step + 1) * width]

    for level in range(sections):

        @pl.when(section == level)
        def run(level=level):
            taps(2**level)


def kernel_call(body, outs, flops, name):
    def call(*args):
        spec = pl.BlockSpec(memory_space=pltpu.VMEM)
        moved_bytes = sum(math.prod(a.shape) * a.dtype.itemsize for a in (*args, *outs))
        return pl.pallas_call(
            body,
            out_shape=list(outs),
            in_specs=[spec] * len(args),
            out_specs=[spec] * len(outs),
            compiler_params=pltpu.CompilerParams(vmem_limit_bytes=24 * 2**20),
            cost_estimate=pl.CostEstimate(
                flops=flops, bytes_accessed=moved_bytes, transcendentals=0
            ),
            name=name,
        )(*args)

    return call


def residue_shards(inputs, cotangent, weight, point):
    sections = lax.axis_size("pipe")
    section = lax.axis_index("pipe")
    count = lax.axis_size("ctx")
    groups = lax.axis_size("dp")
    seq_count, bins, chans = inputs.shape
    inner = weight.shape[3]
    rows = seq_count * bins
    scale = 1.0 / math.sqrt(seq_count * groups * bins * count)
    last = sections - 1
    seqs = range(seq_count)
    layer_flops = 2 * bins * chans * inner * 4

    trunk = jax.ShapeDtypeStruct((bins, chans), jnp.bfloat16)
    inside = jax.ShapeDtypeStruct((bins, inner), jnp.bfloat16)
    inside_wide = jax.ShapeDtypeStruct((bins, inner), jnp.float32)
    part = jax.ShapeDtypeStruct((rows // count, chans), jnp.bfloat16)

    def hop(value, source, target):
        swap = {source: target, target: source}
        route = [
            (stage * count + i, swap.get(stage, stage) * count + i)
            for stage in range(sections)
            for i in range(count)
        ]
        return lax.ppermute(value, ("pipe", "ctx"), route)

    def around(values):
        arrived = [values[0]]
        for step in range(1, count):
            route = [(i, (i + step) % count) for i in range(count)]
            arrived.append(lax.ppermute(values[step], "ctx", route))
        return arrived

    def after(value, *others):
        return lax.optimization_barrier((value, *others))[0]

    payload = jnp.where(section == last, cotangent, inputs)
    parts = kernel_call(
        functools.partial(split_kernel, last), [part] * count, 2 * rows * rows * chans, "split"
    )(payload)
    (held,) = kernel_call(
        hold_kernel, [jax.ShapeDtypeStruct((8, 128), jnp.float32)], 0, "hold"
    )(parts[0], weight, point)
    arrived = around(parts)
    wholes = kernel_call(
        functools.partial(gather_kernel, last, count, bins),
        [trunk] * seq_count,
        0,
        "gather",
    )(*arrived, held)

    xs, pres = [wholes], []
    for level in range(last):
        outs, level_pres = [], []
        for seq in seqs:
            x = xs[level][seq]
            if seq == 0 and level > 0:
                x = after(x, *sent)
            out, pre = kernel_call(
                functools.partial(fore_kernel, level, bins, 2**level),
                [trunk, inside_wide],
                layer_flops,
                "fore",
            )(x, weight, point)
            outs.append(out)
            level_pres.append(pre)
        sent = outs
        pres.append(level_pres)
        xs.append([hop(out, level, level + 1) for out in outs])

    dys, dpres = [], [[] for level in range(sections)]
    for seq in seqs:
        x = xs[last][seq]
        if seq == 0:
            x = after(x, *sent)
        dy, dpre = kernel_call(
            functools.partial(turn_kernel, last, bins, 2**last, scale),
            [trunk, inside],
            2 * layer_flops,
            "turn",
        )(x, wholes[seq], weight, point)
        dys.append(dy)
        dpres[last].append(dpre)
    sent = dys
    dys = [hop(dy, last, last - 1) for dy in dys]

    column = jax.ShapeDtypeStruct((chans // count, rows), jnp.bfloat16)
    columns = kernel_call(
        functools.partial(columns_kernel, sections, groups, seq_count),
        [column] * count,
        2 * rows * chans * chans,
        "columns",
    )(*[after(x, *sent) if level == 0 else x for level in range(sections) for x in xs[level]])
    sent = [*sent, *columns]
    columns = around(columns)
    for level in range(last - 1, 0, -1):
        outs = []
        for seq in seqs:
            dy = dys[seq]
            if seq == 0:
                dy = after(dy, *sent)
            dy, dpre = kernel_call(
                functools.partial(back_kernel, level, bins, 2**level),
                [trunk, inside],
                layer_flops,
                "back",
            )(dy, xs[level][seq], pres[level][seq], weight, point)
            outs.append(dy)
            dpres[level].append(dpre)
        sent = outs if level < last - 1 else [*outs, *columns]
        dys = [hop(dy, level, level - 1) for dy in outs]
    grads = []
    for seq in seqs:
        dy = dys[seq]
        if seq == 0:
            dy = after(dy, *sent)
        (dpre,) = kernel_call(
            functools.partial(head_kernel, sections), [inside], layer_flops // 4, "head"
        )(dy, pres[0][seq], point, *[dpres[level][seq] for level in range(1, sections)])
        grads.append(around([dpre] * count))

    share = jax.ShapeDtypeStruct((3, chans // (count * groups), inner), jnp.float32)
    mine, *others = kernel_call(
        functools.partial(grad_kernel, sections, count, seq_count, bins),
        [share] * groups,
        2 * 3 * rows * chans * inner,
        "grad",
    )(*columns, *[grads[seq][hop] for hop in range(count) for seq in seqs])
    for step, other in enumerate(others, 1):
        route = [(i, (i + step) % groups) for i in range(groups)]
        mine = mine + lax.ppermute(other, "dp", route)
    return mine[None]


def solution(mesh):
    def shards(inputs, cotangent, dilated_kernel_weight, point_weight):
        bins = inputs.shape[1]
        first_spread = bins // 2 // 2 ** (mesh.shape["pipe"] - 1)
        count = mesh.shape["ctx"]
        residues = (
            first_spread == count
            and mesh.shape["pipe"] > 1
            and bins % (16 * count) == 0
            and inputs.shape[2] % (count * mesh.shape["dp"]) == 0
        )
        plan = residue_shards if residues else edge_shards
        return plan(inputs, cotangent, dilated_kernel_weight, point_weight)

    return jax.shard_map(
        shards,
        mesh=mesh,
        in_specs=(
            P("dp", "ctx", None),
            P("dp", "ctx", None),
            P("pipe", None, None, None),
            P("pipe", None, None),
        ),
        out_specs=P("pipe", None, ("dp", "ctx"), None),
        check_vma=False,
    )
```

```python
import functools
import math

import jax
import jax.numpy as jnp
from jax import lax
from jax.experimental import pallas as pl
from jax.experimental.pallas import tpu as pltpu
from jax.sharding import PartitionSpec as P

root_half = 0.7071067811865476
inv_root_two_pi = 0.3989422804014327

contract_last = (((1,), (1,)), ((), ()))
contract_first = (((0,), (0,)), ((), ()))


def gelu(value):
    return 0.5 * value * (1.0 + lax.erf(value * root_half))


def gelu_slope(value):
    return (
        0.5 * (1.0 + lax.erf(value * root_half))
        + value * jnp.exp(-0.5 * value * value) * inv_root_two_pi
    )


def padded(cells, sides, width):
    for axis, dim in sides:
        count = lax.axis_size(axis)
        ends = count - 1
        head = lax.slice_in_dim(cells, 0, width, axis=dim)
        tail = lax.slice_in_dim(cells, cells.shape[dim] - width, cells.shape[dim], axis=dim)
        cells = jnp.concatenate(
            [
                lax.ppermute(tail, axis, [(i, (i + 1) % count) for i in range(ends)]),
                cells,
                lax.ppermute(head, axis, [((i + 1) % count, i) for i in range(ends)]),
            ],
            axis=dim,
        )
    return cells


def shifted(block, axis, distance):
    devices = range(lax.axis_size(axis))
    route = [(i - distance, i) for i in devices if i - distance in devices]
    return lax.ppermute(block, axis, route)


def edge_shards(inputs, cotangent, dilated_kernel_weight, point_weight):
    sections = lax.axis_size("pipe")
    section = lax.axis_index("pipe")
    seq_count, bins, chans = inputs.shape
    reach = bins // 2
    table = jnp.array(
        [reach // 2 ** (sections - 1 - level) for level in range(sections)], jnp.int32
    )
    spread = table[section]
    dilation_weight = dilated_kernel_weight[0]
    w_point = point_weight[0]
    inner_channel_count = dilation_weight.shape[2]
    scale = 1.0 / math.sqrt(seq_count * lax.axis_size("dp") * bins * lax.axis_size("ctx"))
    ticks = jnp.arange(seq_count + sections - 1, dtype=jnp.int32)

    def conv_fore(extended):
        running_total = jnp.zeros((bins, inner_channel_count), jnp.float32)
        for kernel_offset in range(3):
            receptive_span = lax.dynamic_slice_in_dim(
                extended, reach + (kernel_offset - 1) * spread, bins, 0
            )
            running_total = running_total + jnp.dot(
                receptive_span, dilation_weight[kernel_offset], preferred_element_type=jnp.float32
            )
        return running_total

    def put(store, slot, valid, item):
        current = lax.dynamic_index_in_dim(store, slot, 0, keepdims=False)
        return lax.dynamic_update_index_in_dim(store, jnp.where(valid, item, current), slot, 0)

    kept_x = jnp.zeros(inputs.shape, jnp.bfloat16)
    kept_ext = jnp.zeros((seq_count, bins + 2 * reach, chans), jnp.bfloat16)
    kept_pre = jnp.zeros((seq_count, bins, inner_channel_count), jnp.float32)

    def fore_tick(carry, tick):
        received, store_x, store_ext, store_pre = carry
        micro = tick - section
        valid = (micro >= 0) & (micro < seq_count)
        slot = jnp.clip(micro, 0, seq_count - 1)
        first = lax.dynamic_index_in_dim(inputs, slot, 0, keepdims=False)
        trunk_in = jnp.where(section == 0, first, received)
        act = gelu(trunk_in.astype(jnp.float32)).astype(jnp.bfloat16)
        extended = padded(act, (("ctx", 0),), reach)
        pre = conv_fore(extended)
        inner = gelu(pre).astype(jnp.bfloat16)
        out = (
            trunk_in.astype(jnp.float32)
            + jnp.dot(inner, w_point, preferred_element_type=jnp.float32)
        ).astype(jnp.bfloat16)
        sent = shifted(out, "pipe", 1)
        store_x = put(store_x, slot, valid, trunk_in)
        store_ext = put(store_ext, slot, valid, extended)
        store_pre = put(store_pre, slot, valid, pre)
        return ((sent, store_x, store_ext, store_pre), None)

    start_recv = jnp.zeros((bins, chans), jnp.bfloat16)
    (unused, kept_x, kept_ext, kept_pre), unused_out = lax.scan(
        fore_tick, (start_recv, kept_x, kept_ext, kept_pre), ticks
    )

    def back_tick(carry, tick):
        received, grad = carry
        micro = tick - (sections - 1 - section)
        valid = (micro >= 0) & (micro < seq_count)
        slot = jnp.clip(micro, 0, seq_count - 1)
        last = (
            lax.dynamic_index_in_dim(cotangent, slot, 0, keepdims=False).astype(jnp.float32) * scale
        ).astype(jnp.bfloat16)
        upstream = jnp.where(section == sections - 1, last, received)
        trunk_in = lax.dynamic_index_in_dim(kept_x, slot, 0, keepdims=False)
        extended = lax.dynamic_index_in_dim(kept_ext, slot, 0, keepdims=False)
        pre = lax.dynamic_index_in_dim(kept_pre, slot, 0, keepdims=False)
        inner_grad = lax.dot_general(
            upstream, w_point, contract_last, preferred_element_type=jnp.float32
        )
        dpre = (inner_grad * gelu_slope(pre) * valid.astype(jnp.float32)).astype(jnp.bfloat16)
        dpre_ext = padded(dpre, (("ctx", 0),), reach)
        dact = jnp.zeros((bins, chans), jnp.float32)
        taps = []
        for kernel_offset in range(3):
            receptive_span = lax.dynamic_slice_in_dim(
                dpre_ext, reach - (kernel_offset - 1) * spread, bins, 0
            )
            dact = dact + lax.dot_general(
                receptive_span,
                dilation_weight[kernel_offset],
                contract_last,
                preferred_element_type=jnp.float32,
            )
            source = lax.dynamic_slice_in_dim(
                extended, reach + (kernel_offset - 1) * spread, bins, 0
            )
            taps.append(
                lax.dot_general(source, dpre, contract_first, preferred_element_type=jnp.float32)
            )
        grad = grad + jnp.stack(taps)
        back = (
            upstream.astype(jnp.float32) + dact * gelu_slope(trunk_in.astype(jnp.float32))
        ).astype(jnp.bfloat16)
        sent = shifted(back, "pipe", -1)
        return ((sent, grad), None)

    start_grad = jnp.zeros((3, chans, inner_channel_count), jnp.float32)
    (unused_back, grad), unused_seq = lax.scan(back_tick, (start_recv, start_grad), ticks)
    term = grad[None]
    return lax.psum_scatter(term, ("dp", "ctx"), scatter_dimension=2, tiled=True)


def moved(value, by, bins):
    pieces = []
    for start in range(0, value.shape[0], bins):
        piece = value[start : start + bins]
        place = lax.broadcasted_iota(jnp.int32, piece.shape, 0)
        if by > 0:
            keep = place >= by
        else:
            keep = place < bins + by
        pieces.append(jnp.where(keep, pltpu.roll(piece, by % bins, 0), 0.0))
    return jnp.concatenate(pieces, axis=0)


def fore(x, weight_ref, spread, bins):
    act = gelu(x.astype(jnp.float32)).astype(jnp.bfloat16)
    terms = [
        jnp.dot(act, weight_ref[0, tap], preferred_element_type=jnp.float32) for tap in range(3)
    ]
    return terms[1] + moved(terms[0], spread, bins) + moved(terms[2], -spread, bins)


def back_pre(dy, pre, point_ref):
    inner_grad = lax.dot_general(
        dy, point_ref[0], contract_last, preferred_element_type=jnp.float32
    )
    return (inner_grad * gelu_slope(pre)).astype(jnp.bfloat16)


def back_trunk(dy, dpre, x, weight_ref, spread, bins):
    wide = dpre.astype(jnp.float32)
    spans = (
        moved(wide, -spread, bins).astype(jnp.bfloat16),
        dpre,
        moved(wide, spread, bins).astype(jnp.bfloat16),
    )
    dact = jnp.zeros(dy.shape, jnp.float32)
    for tap in range(3):
        dact = dact + lax.dot_general(
            spans[tap], weight_ref[0, tap], contract_last, preferred_element_type=jnp.float32
        )
    return (
        dy.astype(jnp.float32) + dact * gelu_slope(x.astype(jnp.float32))
    ).astype(jnp.bfloat16)


def split_kernel(last, payload_ref, *out_refs):
    count = len(out_refs)
    seq_count, bins, chans = payload_ref.shape
    part = bins // count
    section = lax.axis_index("pipe")
    place = lax.axis_index("ctx")

    @pl.when((section == 0) | (section == last))
    def send():
        source = payload_ref[...].reshape(seq_count * bins, chans)
        row = lax.broadcasted_iota(jnp.int32, (part, seq_count * bins), 0)
        col = lax.broadcasted_iota(jnp.int32, (part, seq_count * bins), 1)
        for hop in range(count):
            residue = lax.rem(place + hop, count)
            rows = [
                (col == seq * bins + count * row + residue).astype(jnp.float32)
                for seq in range(seq_count)
            ]
            pick = jnp.concatenate(rows, axis=0).astype(jnp.bfloat16)
            out_refs[hop][...] = jnp.dot(
                pick, source, preferred_element_type=jnp.float32
            ).astype(jnp.bfloat16)


def hold_kernel(part_ref, weight_ref, point_ref, out_ref):
    out_ref[...] = jnp.zeros(out_ref.shape, out_ref.dtype)


def gather_kernel(last, count, bins, *refs):
    parts, whole_refs = refs[:count], refs[count + 1 :]
    section = lax.axis_index("pipe")
    place = lax.axis_index("ctx")
    part = bins // count

    @pl.when((section == 0) | (section == last))
    def gather():
        for hop in range(count):
            source = lax.rem(place - hop + count, count)
            at = pl.multiple_of(source * part, part)
            for seq, whole_ref in enumerate(whole_refs):
                whole_ref[pl.ds(at, part), :] = parts[hop][seq * part : (seq + 1) * part, :]


def layer_body(x, weight_ref, point_ref, out_ref, pre_ref, spread, bins):
    pre = fore(x, weight_ref, spread, bins)
    pre_ref[...] = pre
    branch = jnp.dot(
        gelu(pre).astype(jnp.bfloat16), point_ref[0], preferred_element_type=jnp.float32
    )
    out_ref[...] = (x.astype(jnp.float32) + branch).astype(jnp.bfloat16)


def fore_kernel(level, bins, spread, x_ref, weight_ref, point_ref, out_ref, pre_ref):
    @pl.when(lax.axis_index("pipe") == level)
    def layer():
        layer_body(x_ref[...], weight_ref, point_ref, out_ref, pre_ref, spread, bins)


def turn_kernel(level, bins, spread, scale, x_ref, cot_ref, weight_ref, point_ref, dy_ref, dpre_ref):
    @pl.when(lax.axis_index("pipe") == level)
    def layer():
        x = x_ref[...]
        pre = fore(x, weight_ref, spread, bins)
        dy = (cot_ref[...].astype(jnp.float32) * scale).astype(jnp.bfloat16)
        dpre = back_pre(dy, pre, point_ref)
        dpre_ref[...] = dpre
        dy_ref[...] = back_trunk(dy, dpre, x, weight_ref, spread, bins)


def back_kernel(level, bins, spread, dy_in_ref, x_ref, pre_ref, weight_ref, point_ref, dy_ref, dpre_ref):
    @pl.when(lax.axis_index("pipe") == level)
    def layer():
        dy = dy_in_ref[...]
        dpre = back_pre(dy, pre_ref[...], point_ref)
        dpre_ref[...] = dpre
        dy_ref[...] = back_trunk(dy, dpre, x_ref[...], weight_ref, spread, bins)


def head_kernel(sections, dy_in_ref, pre_ref, point_ref, *refs):
    others, out_ref = refs[:-1], refs[-1]
    section = lax.axis_index("pipe")

    @pl.when(section == 0)
    def layer():
        out_ref[...] = back_pre(dy_in_ref[...], pre_ref[...], point_ref)

    for level in range(1, sections):

        @pl.when(section == level)
        def keep(level=level):
            out_ref[...] = others[level - 1][...]


def columns_kernel(sections, groups, seq_count, *refs):
    runs, out_refs = refs[: sections * seq_count], refs[sections * seq_count :]
    count = len(out_refs)
    section = lax.axis_index("pipe")
    place = lax.axis_index("ctx")
    core = lax.axis_index("dp")
    xs = [
        jnp.concatenate(
            [ref[...] for ref in runs[level * seq_count : (level + 1) * seq_count]], axis=0
        )
        for level in range(sections)
    ]
    x = xs[0].astype(jnp.float32)
    for level in range(1, sections):
        x = jnp.where(section == level, xs[level].astype(jnp.float32), x)
    act = gelu(x).astype(jnp.bfloat16)
    chans = act.shape[1]
    width = chans // (groups * count)
    for hop in range(count):
        owner = lax.rem(place + hop, count)
        rows = []
        for step in range(groups):
            start = (lax.rem(core + step, groups) * count + owner) * width
            row = lax.broadcasted_iota(jnp.int32, (width, chans), 0)
            col = lax.broadcasted_iota(jnp.int32, (width, chans), 1)
            rows.append((col == start + row).astype(jnp.float32))
        pick = jnp.concatenate(rows, axis=0).astype(jnp.bfloat16)
        out_refs[hop][...] = lax.dot_general(
            pick, act, contract_last, preferred_element_type=jnp.float32
        ).astype(jnp.bfloat16)


def grad_kernel(sections, count, seq_count, bins, *refs):
    columns, refs = refs[:count], refs[count:]
    grads, outs = refs[: count * seq_count], refs[count * seq_count :]
    section = lax.axis_index("pipe")
    width = outs[0].shape[1]
    act = jnp.concatenate([ref[...] for ref in columns], axis=1)

    def taps(spread):
        dpre = jnp.concatenate([ref[...] for ref in grads], axis=0)
        wide = dpre.astype(jnp.float32)
        spans = (
            moved(wide, -spread, bins).astype(jnp.bfloat16),
            dpre,
            moved(wide, spread, bins).astype(jnp.bfloat16),
        )
        for tap in range(3):
            grad = jnp.dot(act, spans[tap], preferred_element_type=jnp.float32)
            for step, out_ref in enumerate(outs):
                out_ref[tap] = grad[step * width : (step + 1) * width]

    for level in range(sections):

        @pl.when(section == level)
        def run(level=level):
            taps(2**level)


def kernel_call(body, outs, flops, name):
    def call(*args):
        spec = pl.BlockSpec(memory_space=pltpu.VMEM)
        moved_bytes = sum(math.prod(a.shape) * a.dtype.itemsize for a in (*args, *outs))
        return pl.pallas_call(
            body,
            out_shape=list(outs),
            in_specs=[spec] * len(args),
            out_specs=[spec] * len(outs),
            compiler_params=pltpu.CompilerParams(vmem_limit_bytes=24 * 2**20),
            cost_estimate=pl.CostEstimate(
                flops=flops, bytes_accessed=moved_bytes, transcendentals=0
            ),
            name=name,
        )(*args)

    return call


def cycle_through(sections, source, target):
    ring = [0, 1, 3, 2] if sections == 4 else list(range(sections))
    here, there = ring.index(source), ring.index(target)
    step = (there - here) % sections
    if step in (1, sections - 1):
        return {ring[at]: ring[(at + step) % sections] for at in range(sections)}
    third = ring[(here - 1) % sections]
    cycle = {stage: stage for stage in ring}
    cycle.update({source: target, target: third, third: source})
    return cycle


def residue_shards(inputs, cotangent, weight, point):
    sections = lax.axis_size("pipe")
    section = lax.axis_index("pipe")
    count = lax.axis_size("ctx")
    groups = lax.axis_size("dp")
    seq_count, bins, chans = inputs.shape
    inner = weight.shape[3]
    rows = seq_count * bins
    scale = 1.0 / math.sqrt(seq_count * groups * bins * count)
    last = sections - 1
    seqs = range(seq_count)
    layer_flops = 2 * bins * chans * inner * 4

    trunk = jax.ShapeDtypeStruct((bins, chans), jnp.bfloat16)
    inside = jax.ShapeDtypeStruct((bins, inner), jnp.bfloat16)
    inside_wide = jax.ShapeDtypeStruct((bins, inner), jnp.float32)
    part = jax.ShapeDtypeStruct((rows // count, chans), jnp.bfloat16)

    def hop(value, source, target):
        cycle = cycle_through(sections, source, target)
        route = [
            (stage * count + i, cycle[stage] * count + i)
            for stage in range(sections)
            for i in range(count)
        ]
        return lax.ppermute(value, ("pipe", "ctx"), route)

    def around(values):
        arrived = [values[0]]
        for step in range(1, count):
            route = [(i, (i + step) % count) for i in range(count)]
            arrived.append(lax.ppermute(values[step], "ctx", route))
        return arrived

    def after(value, *others):
        return lax.optimization_barrier((value, *others))[0]

    payload = jnp.where(section == last, cotangent, inputs)
    parts = kernel_call(
        functools.partial(split_kernel, last), [part] * count, 2 * rows * rows * chans, "split"
    )(payload)
    (held,) = kernel_call(
        hold_kernel, [jax.ShapeDtypeStruct((8, 128), jnp.float32)], 0, "hold"
    )(parts[0], weight, point)
    arrived = around(parts)
    wholes = kernel_call(
        functools.partial(gather_kernel, last, count, bins),
        [trunk] * seq_count,
        0,
        "gather",
    )(*arrived, held)

    xs, pres = [wholes], []
    for level in range(last):
        outs, level_pres = [], []
        for seq in seqs:
            x = xs[level][seq]
            if seq == 0 and level > 0:
                x = after(x, *sent)
            out, pre = kernel_call(
                functools.partial(fore_kernel, level, bins, 2**level),
                [trunk, inside_wide],
                layer_flops,
                "fore",
            )(x, weight, point)
            outs.append(out)
            level_pres.append(pre)
        sent = outs
        pres.append(level_pres)
        xs.append([hop(out, level, level + 1) for out in outs])

    dys, dpres = [], [[] for level in range(sections)]
    for seq in seqs:
        x = xs[last][seq]
        if seq == 0:
            x = after(x, *sent)
        dy, dpre = kernel_call(
            functools.partial(turn_kernel, last, bins, 2**last, scale),
            [trunk, inside],
            2 * layer_flops,
            "turn",
        )(x, wholes[seq], weight, point)
        dys.append(dy)
        dpres[last].append(dpre)
    sent = dys
    dys = [hop(dy, last, last - 1) for dy in dys]

    column = jax.ShapeDtypeStruct((chans // count, rows), jnp.bfloat16)
    columns = kernel_call(
        functools.partial(columns_kernel, sections, groups, seq_count),
        [column] * count,
        2 * rows * chans * chans,
        "columns",
    )(*[after(x, *sent) if level == 0 else x for level in range(sections) for x in xs[level]])
    sent = [*sent, *columns]
    columns = around(columns)
    for level in range(last - 1, 0, -1):
        outs = []
        for seq in seqs:
            dy = dys[seq]
            if seq == 0:
                dy = after(dy, *sent)
            dy, dpre = kernel_call(
                functools.partial(back_kernel, level, bins, 2**level),
                [trunk, inside],
                layer_flops,
                "back",
            )(dy, xs[level][seq], pres[level][seq], weight, point)
            outs.append(dy)
            dpres[level].append(dpre)
        sent = outs if level < last - 1 else [*outs, *columns]
        dys = [hop(dy, level, level - 1) for dy in outs]
    grads = []
    for seq in seqs:
        dy = dys[seq]
        if seq == 0:
            dy = after(dy, *sent)
        (dpre,) = kernel_call(
            functools.partial(head_kernel, sections), [inside], layer_flops // 4, "head"
        )(dy, pres[0][seq], point, *[dpres[level][seq] for level in range(1, sections)])
        grads.append(around([dpre] * count))

    share = jax.ShapeDtypeStruct((3, chans // (count * groups), inner), jnp.float32)
    mine, *others = kernel_call(
        functools.partial(grad_kernel, sections, count, seq_count, bins),
        [share] * groups,
        2 * 3 * rows * chans * inner,
        "grad",
    )(*columns, *[grads[seq][hop] for hop in range(count) for seq in seqs])
    for step, other in enumerate(others, 1):
        route = [(i, (i + step) % groups) for i in range(groups)]
        mine = mine + lax.ppermute(other, "dp", route)
    return mine[None]


def solution(mesh):
    def shards(inputs, cotangent, dilated_kernel_weight, point_weight):
        bins = inputs.shape[1]
        first_spread = bins // 2 // 2 ** (mesh.shape["pipe"] - 1)
        count = mesh.shape["ctx"]
        residues = (
            first_spread == count
            and mesh.shape["pipe"] > 1
            and bins % (16 * count) == 0
            and inputs.shape[2] % (count * mesh.shape["dp"]) == 0
        )
        plan = residue_shards if residues else edge_shards
        return plan(inputs, cotangent, dilated_kernel_weight, point_weight)

    return jax.shard_map(
        shards,
        mesh=mesh,
        in_specs=(
            P("dp", "ctx", None),
            P("dp", "ctx", None),
            P("pipe", None, None, None),
            P("pipe", None, None),
        ),
        out_specs=P("pipe", None, ("dp", "ctx"), None),
        check_vma=False,
    )
```

```python
import functools
import math

import jax
import jax.numpy as jnp
from jax import lax
from jax.experimental import pallas as pl
from jax.experimental.pallas import tpu as pltpu
from jax.sharding import PartitionSpec as P

root_half = 0.7071067811865476
inv_root_two_pi = 0.3989422804014327

in_vmem = pl.BlockSpec(memory_space=pltpu.VMEM)
anywhere = pl.BlockSpec(memory_space=pl.ANY)
contract_last = (((1,), (1,)), ((), ()))
contract_first = (((0,), (0,)), ((), ()))


def gelu(value):
    return 0.5 * value * (1.0 + lax.erf(value * root_half))


def gelu_slope(value):
    return (
        0.5 * (1.0 + lax.erf(value * root_half))
        + value * jnp.exp(-0.5 * value * value) * inv_root_two_pi
    )


def padded(cells, sides, width):
    for axis, dim in sides:
        count = lax.axis_size(axis)
        ends = count - 1
        head = lax.slice_in_dim(cells, 0, width, axis=dim)
        tail = lax.slice_in_dim(cells, cells.shape[dim] - width, cells.shape[dim], axis=dim)
        cells = jnp.concatenate(
            [
                lax.ppermute(tail, axis, [(i, (i + 1) % count) for i in range(ends)]),
                cells,
                lax.ppermute(head, axis, [((i + 1) % count, i) for i in range(ends)]),
            ],
            axis=dim,
        )
    return cells


def shifted(block, axis, distance):
    devices = range(lax.axis_size(axis))
    route = [(i - distance, i) for i in devices if i - distance in devices]
    return lax.ppermute(block, axis, route)


def edge_shards(inputs, cotangent, dilated_kernel_weight, point_weight):
    sections = lax.axis_size("pipe")
    section = lax.axis_index("pipe")
    seq_count, bins, chans = inputs.shape
    reach = bins // 2
    table = jnp.array(
        [reach // 2 ** (sections - 1 - level) for level in range(sections)], jnp.int32
    )
    spread = table[section]
    dilation_weight = dilated_kernel_weight[0]
    w_point = point_weight[0]
    inner_channel_count = dilation_weight.shape[2]
    scale = 1.0 / math.sqrt(seq_count * lax.axis_size("dp") * bins * lax.axis_size("ctx"))
    ticks = jnp.arange(seq_count + sections - 1, dtype=jnp.int32)

    def conv_fore(extended):
        running_total = jnp.zeros((bins, inner_channel_count), jnp.float32)
        for kernel_offset in range(3):
            receptive_span = lax.dynamic_slice_in_dim(
                extended, reach + (kernel_offset - 1) * spread, bins, 0
            )
            running_total = running_total + jnp.dot(
                receptive_span, dilation_weight[kernel_offset], preferred_element_type=jnp.float32
            )
        return running_total

    def put(store, slot, valid, item):
        current = lax.dynamic_index_in_dim(store, slot, 0, keepdims=False)
        return lax.dynamic_update_index_in_dim(store, jnp.where(valid, item, current), slot, 0)

    kept_x = jnp.zeros(inputs.shape, jnp.bfloat16)
    kept_ext = jnp.zeros((seq_count, bins + 2 * reach, chans), jnp.bfloat16)
    kept_pre = jnp.zeros((seq_count, bins, inner_channel_count), jnp.float32)

    def fore_tick(carry, tick):
        received, store_x, store_ext, store_pre = carry
        micro = tick - section
        valid = (micro >= 0) & (micro < seq_count)
        slot = jnp.clip(micro, 0, seq_count - 1)
        first = lax.dynamic_index_in_dim(inputs, slot, 0, keepdims=False)
        trunk_in = jnp.where(section == 0, first, received)
        act = gelu(trunk_in.astype(jnp.float32)).astype(jnp.bfloat16)
        extended = padded(act, (("ctx", 0),), reach)
        pre = conv_fore(extended)
        inner = gelu(pre).astype(jnp.bfloat16)
        out = (
            trunk_in.astype(jnp.float32)
            + jnp.dot(inner, w_point, preferred_element_type=jnp.float32)
        ).astype(jnp.bfloat16)
        sent = shifted(out, "pipe", 1)
        store_x = put(store_x, slot, valid, trunk_in)
        store_ext = put(store_ext, slot, valid, extended)
        store_pre = put(store_pre, slot, valid, pre)
        return ((sent, store_x, store_ext, store_pre), None)

    start_recv = jnp.zeros((bins, chans), jnp.bfloat16)
    (unused, kept_x, kept_ext, kept_pre), unused_out = lax.scan(
        fore_tick, (start_recv, kept_x, kept_ext, kept_pre), ticks
    )

    def back_tick(carry, tick):
        received, grad = carry
        micro = tick - (sections - 1 - section)
        valid = (micro >= 0) & (micro < seq_count)
        slot = jnp.clip(micro, 0, seq_count - 1)
        last = (
            lax.dynamic_index_in_dim(cotangent, slot, 0, keepdims=False).astype(jnp.float32) * scale
        ).astype(jnp.bfloat16)
        upstream = jnp.where(section == sections - 1, last, received)
        trunk_in = lax.dynamic_index_in_dim(kept_x, slot, 0, keepdims=False)
        extended = lax.dynamic_index_in_dim(kept_ext, slot, 0, keepdims=False)
        pre = lax.dynamic_index_in_dim(kept_pre, slot, 0, keepdims=False)
        inner_grad = lax.dot_general(
            upstream, w_point, contract_last, preferred_element_type=jnp.float32
        )
        dpre = (inner_grad * gelu_slope(pre) * valid.astype(jnp.float32)).astype(jnp.bfloat16)
        dpre_ext = padded(dpre, (("ctx", 0),), reach)
        dact = jnp.zeros((bins, chans), jnp.float32)
        taps = []
        for kernel_offset in range(3):
            receptive_span = lax.dynamic_slice_in_dim(
                dpre_ext, reach - (kernel_offset - 1) * spread, bins, 0
            )
            dact = dact + lax.dot_general(
                receptive_span,
                dilation_weight[kernel_offset],
                contract_last,
                preferred_element_type=jnp.float32,
            )
            source = lax.dynamic_slice_in_dim(
                extended, reach + (kernel_offset - 1) * spread, bins, 0
            )
            taps.append(
                lax.dot_general(source, dpre, contract_first, preferred_element_type=jnp.float32)
            )
        grad = grad + jnp.stack(taps)
        back = (
            upstream.astype(jnp.float32) + dact * gelu_slope(trunk_in.astype(jnp.float32))
        ).astype(jnp.bfloat16)
        sent = shifted(back, "pipe", -1)
        return ((sent, grad), None)

    start_grad = jnp.zeros((3, chans, inner_channel_count), jnp.float32)
    (unused_back, grad), unused_seq = lax.scan(back_tick, (start_recv, start_grad), ticks)
    term = grad[None]
    return lax.psum_scatter(term, ("dp", "ctx"), scatter_dimension=2, tiled=True)


def moved(value, by, bins):
    pieces = []
    for start in range(0, value.shape[0], bins):
        piece = value[start : start + bins]
        place = lax.broadcasted_iota(jnp.int32, piece.shape, 0)
        if by > 0:
            keep = place >= by
        else:
            keep = place < bins + by
        pieces.append(jnp.where(keep, pltpu.roll(piece, by % bins, 0), 0.0))
    return jnp.concatenate(pieces, axis=0)


def fore(x, weight_ref, spread, bins):
    act = gelu(x.astype(jnp.float32)).astype(jnp.bfloat16)
    terms = [
        jnp.dot(act, weight_ref[0, tap], preferred_element_type=jnp.float32) for tap in range(3)
    ]
    return terms[1] + moved(terms[0], spread, bins) + moved(terms[2], -spread, bins)


def back_pre(dy, pre, point_ref):
    inner_grad = lax.dot_general(
        dy, point_ref[0], contract_last, preferred_element_type=jnp.float32
    )
    return (inner_grad * gelu_slope(pre)).astype(jnp.bfloat16)


def back_trunk(dy, dpre, x, weight_ref, spread, bins):
    wide = dpre.astype(jnp.float32)
    spans = (
        moved(wide, -spread, bins).astype(jnp.bfloat16),
        dpre,
        moved(wide, spread, bins).astype(jnp.bfloat16),
    )
    dact = jnp.zeros(dy.shape, jnp.float32)
    for tap in range(3):
        dact = dact + lax.dot_general(
            spans[tap], weight_ref[0, tap], contract_last, preferred_element_type=jnp.float32
        )
    return (
        dy.astype(jnp.float32) + dact * gelu_slope(x.astype(jnp.float32))
    ).astype(jnp.bfloat16)


def split_kernel(last, payload_ref, *out_refs):
    count = len(out_refs)
    seq_count, bins, chans = payload_ref.shape
    part = bins // count
    section = lax.axis_index("pipe")
    place = lax.axis_index("ctx")

    @pl.when((section == 0) | (section == last))
    def send():
        source = payload_ref[...].reshape(seq_count * bins, chans)
        row = lax.broadcasted_iota(jnp.int32, (part, seq_count * bins), 0)
        col = lax.broadcasted_iota(jnp.int32, (part, seq_count * bins), 1)
        for hop in range(count):
            residue = lax.rem(place + hop, count)
            rows = [
                (col == seq * bins + count * row + residue).astype(jnp.float32)
                for seq in range(seq_count)
            ]
            pick = jnp.concatenate(rows, axis=0).astype(jnp.bfloat16)
            out_refs[hop][...] = jnp.dot(
                pick, source, preferred_element_type=jnp.float32
            ).astype(jnp.bfloat16)


def hold_kernel(weight_ref, point_ref, weight_out, point_out, sems):
    loads = [
        pltpu.make_async_copy(weight_ref, weight_out, sems.at[0]),
        pltpu.make_async_copy(point_ref, point_out, sems.at[1]),
    ]
    for load in loads:
        load.start()
    for load in loads:
        load.wait()


def gather_kernel(last, count, bins, *refs):
    parts, whole_refs = refs[:count], refs[count:]
    section = lax.axis_index("pipe")
    place = lax.axis_index("ctx")
    part = bins // count

    @pl.when((section == 0) | (section == last))
    def gather():
        for hop in range(count):
            source = lax.rem(place - hop + count, count)
            at = pl.multiple_of(source * part, part)
            for seq, whole_ref in enumerate(whole_refs):
                whole_ref[pl.ds(at, part), :] = parts[hop][seq * part : (seq + 1) * part, :]


def layer_body(x, weight_ref, point_ref, out_ref, pre_ref, spread, bins):
    pre = fore(x, weight_ref, spread, bins)
    pre_ref[...] = pre
    branch = jnp.dot(
        gelu(pre).astype(jnp.bfloat16), point_ref[0], preferred_element_type=jnp.float32
    )
    out_ref[...] = (x.astype(jnp.float32) + branch).astype(jnp.bfloat16)


def fore_kernel(level, bins, spread, x_ref, weight_ref, point_ref, out_ref, pre_ref):
    @pl.when(lax.axis_index("pipe") == level)
    def layer():
        layer_body(x_ref[...], weight_ref, point_ref, out_ref, pre_ref, spread, bins)


def turn_kernel(level, bins, spread, scale, x_ref, cot_ref, weight_ref, point_ref, dy_ref, dpre_ref):
    @pl.when(lax.axis_index("pipe") == level)
    def layer():
        x = x_ref[...]
        pre = fore(x, weight_ref, spread, bins)
        dy = (cot_ref[...].astype(jnp.float32) * scale).astype(jnp.bfloat16)
        dpre = back_pre(dy, pre, point_ref)
        dpre_ref[...] = dpre
        dy_ref[...] = back_trunk(dy, dpre, x, weight_ref, spread, bins)


def back_kernel(level, bins, spread, dy_in_ref, x_ref, pre_ref, weight_ref, point_ref, dy_ref, dpre_ref):
    @pl.when(lax.axis_index("pipe") == level)
    def layer():
        dy = dy_in_ref[...]
        dpre = back_pre(dy, pre_ref[...], point_ref)
        dpre_ref[...] = dpre
        dy_ref[...] = back_trunk(dy, dpre, x_ref[...], weight_ref, spread, bins)


def head_kernel(sections, dy_in_ref, pre_ref, point_ref, *refs):
    others, out_ref = refs[:-1], refs[-1]
    section = lax.axis_index("pipe")

    @pl.when(section == 0)
    def layer():
        out_ref[...] = back_pre(dy_in_ref[...], pre_ref[...], point_ref)

    for level in range(1, sections):

        @pl.when(section == level)
        def keep(level=level):
            out_ref[...] = others[level - 1][...]


def columns_kernel(sections, groups, seq_count, *refs):
    runs, out_refs = refs[: sections * seq_count], refs[sections * seq_count :]
    count = len(out_refs)
    section = lax.axis_index("pipe")
    place = lax.axis_index("ctx")
    core = lax.axis_index("dp")
    xs = [
        jnp.concatenate(
            [ref[...] for ref in runs[level * seq_count : (level + 1) * seq_count]], axis=0
        )
        for level in range(sections)
    ]
    x = xs[0].astype(jnp.float32)
    for level in range(1, sections):
        x = jnp.where(section == level, xs[level].astype(jnp.float32), x)
    act = gelu(x).astype(jnp.bfloat16)
    chans = act.shape[1]
    width = chans // (groups * count)
    for hop in range(count):
        owner = lax.rem(place + hop, count)
        rows = []
        for step in range(groups):
            start = (lax.rem(core + step, groups) * count + owner) * width
            row = lax.broadcasted_iota(jnp.int32, (width, chans), 0)
            col = lax.broadcasted_iota(jnp.int32, (width, chans), 1)
            rows.append((col == start + row).astype(jnp.float32))
        pick = jnp.concatenate(rows, axis=0).astype(jnp.bfloat16)
        out_refs[hop][...] = lax.dot_general(
            pick, act, contract_last, preferred_element_type=jnp.float32
        ).astype(jnp.bfloat16)


def grad_kernel(sections, count, seq_count, bins, *refs):
    columns, refs = refs[:count], refs[count:]
    grads, outs = refs[: count * seq_count], refs[count * seq_count :]
    section = lax.axis_index("pipe")
    width = outs[0].shape[1]
    act = jnp.concatenate([ref[...] for ref in columns], axis=1)

    def taps(spread):
        dpre = jnp.concatenate([ref[...] for ref in grads], axis=0)
        wide = dpre.astype(jnp.float32)
        spans = (
            moved(wide, -spread, bins).astype(jnp.bfloat16),
            dpre,
            moved(wide, spread, bins).astype(jnp.bfloat16),
        )
        for tap in range(3):
            grad = jnp.dot(act, spans[tap], preferred_element_type=jnp.float32)
            for step, out_ref in enumerate(outs):
                out_ref[tap] = grad[step * width : (step + 1) * width]

    for level in range(sections):

        @pl.when(section == level)
        def run(level=level):
            taps(2**level)


def kernel_call(body, outs, flops, name, waits=(), in_spec=in_vmem, scratch=(), limit=24 * 2**20):
    def call(*args):
        def run(*refs):
            body(*refs[: len(args)], *refs[len(args) + len(waits) :])

        moved_bytes = sum(math.prod(a.shape) * a.dtype.itemsize for a in (*args, *outs))
        return pl.pallas_call(
            run,
            out_shape=list(outs),
            in_specs=[in_spec] * len(args) + [anywhere] * len(waits),
            out_specs=[in_vmem] * len(outs),
            scratch_shapes=list(scratch),
            compiler_params=pltpu.CompilerParams(vmem_limit_bytes=limit),
            cost_estimate=pl.CostEstimate(
                flops=flops, bytes_accessed=moved_bytes, transcendentals=0
            ),
            name=name,
        )(*args, *waits)

    return call


def hop_route(sections, source, target):
    step = target - source
    busy = (source, target, target + step)
    free = [stage for stage in range(sections) if stage not in busy]
    pairs = [(source, target)]
    if free:
        pairs.append((free[0] if step > 0 else free[-1], source))
    return pairs


def residue_shards(inputs, cotangent, weight, point):
    sections = lax.axis_size("pipe")
    section = lax.axis_index("pipe")
    count = lax.axis_size("ctx")
    groups = lax.axis_size("dp")
    seq_count, bins, chans = inputs.shape
    inner = weight.shape[3]
    rows = seq_count * bins
    scale = 1.0 / math.sqrt(seq_count * groups * bins * count)
    last = sections - 1
    seqs = range(seq_count)
    layer_flops = 2 * bins * chans * inner * 4

    trunk = jax.ShapeDtypeStruct((bins, chans), jnp.bfloat16)
    inside = jax.ShapeDtypeStruct((bins, inner), jnp.bfloat16)
    inside_wide = jax.ShapeDtypeStruct((bins, inner), jnp.float32)
    part = jax.ShapeDtypeStruct((rows // count, chans), jnp.bfloat16)

    def like(value):
        return jax.ShapeDtypeStruct(value.shape, value.dtype)

    def hop(value, source, target):
        route = [
            (giver * count + i, taker * count + i)
            for giver, taker in hop_route(sections, source, target)
            for i in range(count)
        ]
        return lax.ppermute(value, ("pipe", "ctx"), route)

    def around(values):
        arrived = [values[0]]
        for step in range(1, count):
            route = [(i, (i + step) % count) for i in range(count)]
            arrived.append(lax.ppermute(values[step], "ctx", route))
        return arrived

    payload = jnp.where(section == last, cotangent, inputs)
    parts = kernel_call(
        functools.partial(split_kernel, last), [part] * count, 2 * rows * rows * chans, "split"
    )(payload)
    weight, point = kernel_call(
        hold_kernel,
        [like(weight), like(point)],
        0,
        "hold",
        waits=[parts[0]],
        in_spec=anywhere,
        scratch=[pltpu.SemaphoreType.DMA((2,))],
    )(weight, point)
    arrived = around(parts)
    wholes = kernel_call(
        functools.partial(gather_kernel, last, count, bins),
        [trunk] * seq_count,
        0,
        "gather",
    )(*arrived)

    xs, pres, sent = [wholes], [], ()
    for level in range(last):
        outs, level_pres = [], []
        for seq in seqs:
            out, pre = kernel_call(
                functools.partial(fore_kernel, level, bins, 2**level),
                [trunk, inside_wide],
                layer_flops,
                "fore",
                waits=sent if seq == 0 else (),
            )(xs[level][seq], weight, point)
            outs.append(out)
            level_pres.append(pre)
        sent = outs
        pres.append(level_pres)
        xs.append([hop(out, level, level + 1) for out in outs])

    dys, dpres = [], [[] for level in range(sections)]
    for seq in seqs:
        dy, dpre = kernel_call(
            functools.partial(turn_kernel, last, bins, 2**last, scale),
            [trunk, inside],
            2 * layer_flops,
            "turn",
            waits=sent if seq == 0 else (),
        )(xs[last][seq], wholes[seq], weight, point)
        dys.append(dy)
        dpres[last].append(dpre)
    sent = dys
    dys = [hop(dy, last, last - 1) for dy in dys]

    column = jax.ShapeDtypeStruct((chans // count, rows), jnp.bfloat16)
    columns = kernel_call(
        functools.partial(columns_kernel, sections, groups, seq_count),
        [column] * count,
        2 * rows * chans * chans,
        "columns",
        waits=sent,
    )(*[x for level in range(sections) for x in xs[level]])
    columns = around(columns)
    sent = columns
    for level in range(last - 1, 0, -1):
        outs = []
        for seq in seqs:
            dy, dpre = kernel_call(
                functools.partial(back_kernel, level, bins, 2**level),
                [trunk, inside],
                layer_flops,
                "back",
                waits=sent if seq == 0 else (),
            )(dys[seq], xs[level][seq], pres[level][seq], weight, point)
            outs.append(dy)
            dpres[level].append(dpre)
        sent = outs
        dys = [hop(dy, level, level - 1) for dy in outs]
    grads = []
    for seq in seqs:
        (dpre,) = kernel_call(
            functools.partial(head_kernel, sections),
            [inside],
            layer_flops // 4,
            "head",
            waits=sent if seq == 0 else (),
        )(dys[seq], pres[0][seq], point, *[dpres[level][seq] for level in range(1, sections)])
        grads.append(around([dpre] * count))

    share = jax.ShapeDtypeStruct((3, chans // (count * groups), inner), jnp.float32)
    mine, *others = kernel_call(
        functools.partial(grad_kernel, sections, count, seq_count, bins),
        [share] * groups,
        2 * 3 * rows * chans * inner,
        "grad",
    )(*columns, *[grads[seq][hop] for hop in range(count) for seq in seqs])
    for step, other in enumerate(others, 1):
        route = [(i, (i + step) % groups) for i in range(groups)]
        mine = mine + lax.ppermute(other, "dp", route)
    return mine[None]


def solution(mesh):
    def shards(inputs, cotangent, dilated_kernel_weight, point_weight):
        bins = inputs.shape[1]
        first_spread = bins // 2 // 2 ** (mesh.shape["pipe"] - 1)
        count = mesh.shape["ctx"]
        residues = (
            first_spread == count
            and mesh.shape["pipe"] > 1
            and bins % (16 * count) == 0
            and inputs.shape[2] % (count * mesh.shape["dp"]) == 0
        )
        plan = residue_shards if residues else edge_shards
        return plan(inputs, cotangent, dilated_kernel_weight, point_weight)

    return jax.shard_map(
        shards,
        mesh=mesh,
        in_specs=(
            P("dp", "ctx", None),
            P("dp", "ctx", None),
            P("pipe", None, None, None),
            P("pipe", None, None),
        ),
        out_specs=P("pipe", None, ("dp", "ctx"), None),
        check_vma=False,
    )
```

```python
import functools
import math

import jax
import jax.numpy as jnp
from jax import lax
from jax.experimental import pallas as pl
from jax.experimental.pallas import tpu as pltpu
from jax.sharding import PartitionSpec as P

root_half = 0.7071067811865476
inv_root_two_pi = 0.3989422804014327

in_vmem = pl.BlockSpec(memory_space=pltpu.VMEM)
anywhere = pl.BlockSpec(memory_space=pl.ANY)
contract_last = (((1,), (1,)), ((), ()))
contract_first = (((0,), (0,)), ((), ()))


def gelu(value):
    return 0.5 * value * (1.0 + lax.erf(value * root_half))


def gelu_slope(value):
    return (
        0.5 * (1.0 + lax.erf(value * root_half))
        + value * jnp.exp(-0.5 * value * value) * inv_root_two_pi
    )


def padded(cells, sides, width):
    for axis, dim in sides:
        count = lax.axis_size(axis)
        ends = count - 1
        head = lax.slice_in_dim(cells, 0, width, axis=dim)
        tail = lax.slice_in_dim(cells, cells.shape[dim] - width, cells.shape[dim], axis=dim)
        cells = jnp.concatenate(
            [
                lax.ppermute(tail, axis, [(i, (i + 1) % count) for i in range(ends)]),
                cells,
                lax.ppermute(head, axis, [((i + 1) % count, i) for i in range(ends)]),
            ],
            axis=dim,
        )
    return cells


def shifted(block, axis, distance):
    devices = range(lax.axis_size(axis))
    route = [(i - distance, i) for i in devices if i - distance in devices]
    return lax.ppermute(block, axis, route)


def edge_shards(inputs, cotangent, dilated_kernel_weight, point_weight):
    sections = lax.axis_size("pipe")
    section = lax.axis_index("pipe")
    seq_count, bins, chans = inputs.shape
    reach = bins // 2
    table = jnp.array(
        [reach // 2 ** (sections - 1 - level) for level in range(sections)], jnp.int32
    )
    spread = table[section]
    dilation_weight = dilated_kernel_weight[0]
    w_point = point_weight[0]
    inner_channel_count = dilation_weight.shape[2]
    scale = 1.0 / math.sqrt(seq_count * lax.axis_size("dp") * bins * lax.axis_size("ctx"))
    ticks = jnp.arange(seq_count + sections - 1, dtype=jnp.int32)

    def conv_fore(extended):
        running_total = jnp.zeros((bins, inner_channel_count), jnp.float32)
        for kernel_offset in range(3):
            receptive_span = lax.dynamic_slice_in_dim(
                extended, reach + (kernel_offset - 1) * spread, bins, 0
            )
            running_total = running_total + jnp.dot(
                receptive_span, dilation_weight[kernel_offset], preferred_element_type=jnp.float32
            )
        return running_total

    def put(store, slot, valid, item):
        current = lax.dynamic_index_in_dim(store, slot, 0, keepdims=False)
        return lax.dynamic_update_index_in_dim(store, jnp.where(valid, item, current), slot, 0)

    kept_x = jnp.zeros(inputs.shape, jnp.bfloat16)
    kept_ext = jnp.zeros((seq_count, bins + 2 * reach, chans), jnp.bfloat16)
    kept_pre = jnp.zeros((seq_count, bins, inner_channel_count), jnp.float32)

    def fore_tick(carry, tick):
        received, store_x, store_ext, store_pre = carry
        micro = tick - section
        valid = (micro >= 0) & (micro < seq_count)
        slot = jnp.clip(micro, 0, seq_count - 1)
        first = lax.dynamic_index_in_dim(inputs, slot, 0, keepdims=False)
        trunk_in = jnp.where(section == 0, first, received)
        act = gelu(trunk_in.astype(jnp.float32)).astype(jnp.bfloat16)
        extended = padded(act, (("ctx", 0),), reach)
        pre = conv_fore(extended)
        inner = gelu(pre).astype(jnp.bfloat16)
        out = (
            trunk_in.astype(jnp.float32)
            + jnp.dot(inner, w_point, preferred_element_type=jnp.float32)
        ).astype(jnp.bfloat16)
        sent = shifted(out, "pipe", 1)
        store_x = put(store_x, slot, valid, trunk_in)
        store_ext = put(store_ext, slot, valid, extended)
        store_pre = put(store_pre, slot, valid, pre)
        return ((sent, store_x, store_ext, store_pre), None)

    start_recv = jnp.zeros((bins, chans), jnp.bfloat16)
    (unused, kept_x, kept_ext, kept_pre), unused_out = lax.scan(
        fore_tick, (start_recv, kept_x, kept_ext, kept_pre), ticks
    )

    def back_tick(carry, tick):
        received, grad = carry
        micro = tick - (sections - 1 - section)
        valid = (micro >= 0) & (micro < seq_count)
        slot = jnp.clip(micro, 0, seq_count - 1)
        last = (
            lax.dynamic_index_in_dim(cotangent, slot, 0, keepdims=False).astype(jnp.float32) * scale
        ).astype(jnp.bfloat16)
        upstream = jnp.where(section == sections - 1, last, received)
        trunk_in = lax.dynamic_index_in_dim(kept_x, slot, 0, keepdims=False)
        extended = lax.dynamic_index_in_dim(kept_ext, slot, 0, keepdims=False)
        pre = lax.dynamic_index_in_dim(kept_pre, slot, 0, keepdims=False)
        inner_grad = lax.dot_general(
            upstream, w_point, contract_last, preferred_element_type=jnp.float32
        )
        dpre = (inner_grad * gelu_slope(pre) * valid.astype(jnp.float32)).astype(jnp.bfloat16)
        dpre_ext = padded(dpre, (("ctx", 0),), reach)
        dact = jnp.zeros((bins, chans), jnp.float32)
        taps = []
        for kernel_offset in range(3):
            receptive_span = lax.dynamic_slice_in_dim(
                dpre_ext, reach - (kernel_offset - 1) * spread, bins, 0
            )
            dact = dact + lax.dot_general(
                receptive_span,
                dilation_weight[kernel_offset],
                contract_last,
                preferred_element_type=jnp.float32,
            )
            source = lax.dynamic_slice_in_dim(
                extended, reach + (kernel_offset - 1) * spread, bins, 0
            )
            taps.append(
                lax.dot_general(source, dpre, contract_first, preferred_element_type=jnp.float32)
            )
        grad = grad + jnp.stack(taps)
        back = (
            upstream.astype(jnp.float32) + dact * gelu_slope(trunk_in.astype(jnp.float32))
        ).astype(jnp.bfloat16)
        sent = shifted(back, "pipe", -1)
        return ((sent, grad), None)

    start_grad = jnp.zeros((3, chans, inner_channel_count), jnp.float32)
    (unused_back, grad), unused_seq = lax.scan(back_tick, (start_recv, start_grad), ticks)
    term = grad[None]
    return lax.psum_scatter(term, ("dp", "ctx"), scatter_dimension=2, tiled=True)


def moved(value, by, bins):
    pieces = []
    for start in range(0, value.shape[0], bins):
        piece = value[start : start + bins]
        place = lax.broadcasted_iota(jnp.int32, piece.shape, 0)
        if by > 0:
            keep = place >= by
        else:
            keep = place < bins + by
        pieces.append(jnp.where(keep, pltpu.roll(piece, by % bins, 0), 0.0))
    return jnp.concatenate(pieces, axis=0)


def fore(x, weight_ref, spread, bins):
    act = gelu(x.astype(jnp.float32)).astype(jnp.bfloat16)
    terms = [
        jnp.dot(act, weight_ref[0, tap], preferred_element_type=jnp.float32) for tap in range(3)
    ]
    return terms[1] + moved(terms[0], spread, bins) + moved(terms[2], -spread, bins)


def back_pre(dy, pre, point_ref):
    inner_grad = lax.dot_general(
        dy, point_ref[0], contract_last, preferred_element_type=jnp.float32
    )
    return (inner_grad * gelu_slope(pre)).astype(jnp.bfloat16)


def back_trunk(dy, dpre, x, weight_ref, spread, bins):
    wide = dpre.astype(jnp.float32)
    spans = (
        moved(wide, -spread, bins).astype(jnp.bfloat16),
        dpre,
        moved(wide, spread, bins).astype(jnp.bfloat16),
    )
    dact = jnp.zeros(dy.shape, jnp.float32)
    for tap in range(3):
        dact = dact + lax.dot_general(
            spans[tap], weight_ref[0, tap], contract_last, preferred_element_type=jnp.float32
        )
    return (
        dy.astype(jnp.float32) + dact * gelu_slope(x.astype(jnp.float32))
    ).astype(jnp.bfloat16)


def of_seq(ref, seq, bins):
    if ref.shape[0] == bins:
        return ref[...]
    return ref[seq * bins : (seq + 1) * bins, :]


def split_kernel(last, payload_ref, *out_refs):
    count = len(out_refs)
    seq_count, bins, chans = payload_ref.shape
    part = bins // count
    section = lax.axis_index("pipe")
    place = lax.axis_index("ctx")

    @pl.when((section == 0) | (section == last))
    def send():
        source = payload_ref[...].reshape(seq_count * bins, chans)
        row = lax.broadcasted_iota(jnp.int32, (part, seq_count * bins), 0)
        col = lax.broadcasted_iota(jnp.int32, (part, seq_count * bins), 1)
        for hop in range(count):
            residue = lax.rem(place + hop, count)
            rows = [
                (col == seq * bins + count * row + residue).astype(jnp.float32)
                for seq in range(seq_count)
            ]
            pick = jnp.concatenate(rows, axis=0).astype(jnp.bfloat16)
            out_refs[hop][...] = jnp.dot(
                pick, source, preferred_element_type=jnp.float32
            ).astype(jnp.bfloat16)


def hold_kernel(weight_ref, point_ref, weight_out, point_out, sems):
    loads = [
        pltpu.make_async_copy(weight_ref, weight_out, sems.at[0]),
        pltpu.make_async_copy(point_ref, point_out, sems.at[1]),
    ]
    for load in loads:
        load.start()
    for load in loads:
        load.wait()


def first_kernel(last, bins, *refs):
    parts, (weight_ref, point_ref, whole_ref, out_ref, pre_ref) = refs[:-5], refs[-5:]
    count = len(parts)
    section = lax.axis_index("pipe")
    place = lax.axis_index("ctx")
    part = bins // count
    seq_count = whole_ref.shape[0] // bins

    @pl.when((section == 0) | (section == last))
    def gather():
        for hop in range(count):
            source = lax.rem(place - hop + count, count)
            for seq in range(seq_count):
                at = pl.multiple_of(seq * bins + source * part, part)
                whole_ref[pl.ds(at, part), :] = parts[hop][seq * part : (seq + 1) * part, :]

    @pl.when(section == 0)
    def layer():
        x = whole_ref[...]
        finish(x, fore(x, weight_ref, 1, bins), point_ref, out_ref, pre_ref)


def finish(x, pre, point_ref, out_ref, pre_ref):
    pre_ref[...] = pre
    branch = jnp.dot(
        gelu(pre).astype(jnp.bfloat16), point_ref[0], preferred_element_type=jnp.float32
    )
    out_ref[...] = (x.astype(jnp.float32) + branch).astype(jnp.bfloat16)


def fore_kernel(level, seq, bins, x_ref, weight_ref, point_ref, out_ref, pre_ref):
    @pl.when(lax.axis_index("pipe") == level)
    def layer():
        x = of_seq(x_ref, seq, bins)
        finish(x, fore(x, weight_ref, 2**level, bins), point_ref, out_ref, pre_ref)


def turn_kernel(level, seq, bins, scale, x_ref, cot_ref, weight_ref, point_ref, dy_ref, dpre_ref):
    @pl.when(lax.axis_index("pipe") == level)
    def layer():
        x = of_seq(x_ref, seq, bins)
        pre = fore(x, weight_ref, 2**level, bins)
        cot = of_seq(cot_ref, seq, bins)
        dy = (cot.astype(jnp.float32) * scale).astype(jnp.bfloat16)
        dpre = back_pre(dy, pre, point_ref)
        dpre_ref[...] = dpre
        dy_ref[...] = back_trunk(dy, dpre, x, weight_ref, 2**level, bins)


def back_kernel(level, seq, bins, dy_in_ref, x_ref, pre_ref, weight_ref, point_ref, dy_ref, dpre_ref):
    @pl.when(lax.axis_index("pipe") == level)
    def layer():
        dy = dy_in_ref[...]
        x = of_seq(x_ref, seq, bins)
        dpre = back_pre(dy, of_seq(pre_ref, seq, bins), point_ref)
        dpre_ref[...] = dpre
        dy_ref[...] = back_trunk(dy, dpre, x, weight_ref, 2**level, bins)


def head_kernel(sections, seq, bins, dy_in_ref, pre_ref, point_ref, *refs):
    others, out_ref = refs[:-1], refs[-1]
    section = lax.axis_index("pipe")

    @pl.when(section == 0)
    def layer():
        out_ref[...] = back_pre(dy_in_ref[...], of_seq(pre_ref, seq, bins), point_ref)

    for level in range(1, sections):

        @pl.when(section == level)
        def keep(level=level):
            out_ref[...] = others[level - 1][...]


def columns_kernel(groups, runs, *refs):
    out_refs = refs[sum(runs) :]
    count = len(out_refs)
    section = lax.axis_index("pipe")
    core = lax.axis_index("dp")
    place = lax.axis_index("ctx")
    x, start = None, 0
    for level, run in enumerate(runs):
        pieces = [ref[...] for ref in refs[start : start + run]]
        start += run
        whole = jnp.concatenate(pieces, axis=0).astype(jnp.float32)
        x = whole if x is None else jnp.where(section == level, whole, x)
    act = gelu(x).astype(jnp.bfloat16)
    chans = act.shape[1]
    width = chans // (groups * count)
    row = lax.broadcasted_iota(jnp.int32, (width, chans), 0)
    col = lax.broadcasted_iota(jnp.int32, (width, chans), 1)
    for hop in range(count):
        owner = lax.rem(place + hop, count)
        rows = []
        for step in range(groups):
            first = (lax.rem(core + step, groups) * count + owner) * width
            rows.append((col == first + row).astype(jnp.float32))
        pick = jnp.concatenate(rows, axis=0).astype(jnp.bfloat16)
        out_refs[hop][...] = lax.dot_general(
            pick, act, contract_last, preferred_element_type=jnp.float32
        ).astype(jnp.bfloat16)


def grad_kernel(sections, count, seq_count, bins, *refs):
    columns, refs = refs[:count], refs[count:]
    grads, outs = refs[: count * seq_count], refs[count * seq_count :]
    section = lax.axis_index("pipe")
    width = outs[0].shape[1]
    act = jnp.concatenate([ref[...] for ref in columns], axis=1)

    def taps(spread):
        dpre = jnp.concatenate([ref[...] for ref in grads], axis=0)
        wide = dpre.astype(jnp.float32)
        spans = (
            moved(wide, -spread, bins).astype(jnp.bfloat16),
            dpre,
            moved(wide, spread, bins).astype(jnp.bfloat16),
        )
        for tap in range(3):
            grad = jnp.dot(act, spans[tap], preferred_element_type=jnp.float32)
            for step, out_ref in enumerate(outs):
                out_ref[tap] = grad[step * width : (step + 1) * width]

    for level in range(sections):

        @pl.when(section == level)
        def run(level=level):
            taps(2**level)


def kernel_call(body, outs, flops, name, waits=(), carries=(), in_spec=in_vmem, scratch=()):
    def call(*args):
        used, taken = len(args), len(args) + len(waits) + len(carries)

        def run(*refs):
            made = refs[taken : taken + len(outs)]
            body(*refs[:used], *made, *refs[taken + len(outs) + len(carries) :])

        moved_bytes = sum(math.prod(a.shape) * a.dtype.itemsize for a in (*args, *outs))
        return pl.pallas_call(
            run,
            out_shape=[*outs, *(jax.ShapeDtypeStruct(a.shape, a.dtype) for a in carries)],
            in_specs=[in_spec] * used + [anywhere] * (taken - used),
            out_specs=[in_vmem] * len(outs) + [anywhere] * len(carries),
            input_output_aliases={
                used + len(waits) + at: len(outs) + at for at in range(len(carries))
            },
            scratch_shapes=list(scratch),
            compiler_params=pltpu.CompilerParams(vmem_limit_bytes=24 * 2**20),
            cost_estimate=pl.CostEstimate(
                flops=flops, bytes_accessed=moved_bytes, transcendentals=0
            ),
            name=name,
        )(*args, *waits, *carries)

    return call


def cycle_through(sections, source, target):
    ring = [0, 1, 3, 2] if sections == 4 else list(range(sections))
    here, there = ring.index(source), ring.index(target)
    step = (there - here) % sections
    if step in (1, sections - 1):
        return {ring[at]: ring[(at + step) % sections] for at in range(sections)}
    third = ring[(here + 1) % sections]
    cycle = {stage: stage for stage in ring}
    cycle.update({source: target, target: third, third: source})
    return cycle


def residue_shards(inputs, cotangent, weight, point):
    sections = lax.axis_size("pipe")
    section = lax.axis_index("pipe")
    count = lax.axis_size("ctx")
    groups = lax.axis_size("dp")
    seq_count, bins, chans = inputs.shape
    inner = weight.shape[3]
    rows = seq_count * bins
    scale = 1.0 / math.sqrt(seq_count * groups * bins * count)
    last = sections - 1
    seqs = range(seq_count)
    layer_flops = 2 * bins * chans * inner * 4

    def shape(*dims, dtype=jnp.bfloat16):
        return jax.ShapeDtypeStruct(dims, dtype)

    def hop(value, source, target):
        cycle = cycle_through(sections, source, target)
        route = [
            (stage * count + i, cycle[stage] * count + i)
            for stage in range(sections)
            for i in range(count)
        ]
        return lax.ppermute(value, ("pipe", "ctx"), route)

    def onward(value, step):
        return lax.ppermute(value, "ctx", [(i, (i + step) % count) for i in range(count)])

    payload = jnp.where(section == last, cotangent, inputs)
    parts = kernel_call(
        functools.partial(split_kernel, last),
        [shape(rows // count, chans)] * count,
        2 * rows * rows * chans,
        "split",
    )(payload)
    weight, point = kernel_call(
        hold_kernel,
        [shape(*weight.shape), shape(*point.shape)],
        0,
        "hold",
        waits=[parts[0]],
        in_spec=anywhere,
        scratch=[pltpu.SemaphoreType.DMA((2,))],
    )(weight, point)
    parts = [parts[0], *(onward(parts[step], step) for step in range(1, count))]

    whole, out, pre = kernel_call(
        functools.partial(first_kernel, last, bins),
        [shape(rows, chans), shape(rows, chans), shape(rows, inner, dtype=jnp.float32)],
        seq_count * layer_flops,
        "first",
    )(*parts, weight, point)
    xs, pres, sent = [[whole]], [[pre]], ()
    xs.append([hop(out, 0, 1)])
    for level in range(1, last):
        outs = []
        pres.append([])
        for seq in seqs:
            out, pre = kernel_call(
                functools.partial(fore_kernel, level, seq, bins),
                [shape(bins, chans), shape(bins, inner, dtype=jnp.float32)],
                layer_flops,
                "fore",
                waits=outs[-1:] or sent,
            )(xs[level][min(seq, len(xs[level]) - 1)], weight, point)
            outs.append(out)
            pres[level].append(pre)
        sent = outs
        xs.append([hop(out, level, level + 1) for out in outs])

    dys, dpres = [], [[] for level in range(sections)]
    for seq in seqs:
        dy, dpre = kernel_call(
            functools.partial(turn_kernel, last, seq, bins, scale),
            [shape(bins, chans), shape(bins, inner)],
            2 * layer_flops,
            "turn",
            waits=dys[-1:] or sent,
        )(xs[last][min(seq, len(xs[last]) - 1)], whole, weight, point)
        dys.append(dy)
        dpres[last].append(dpre)
    columns = kernel_call(
        functools.partial(columns_kernel, groups, [len(x) for x in xs]),
        [shape(chans // count, rows)] * count,
        2 * rows * chans * chans,
        "columns",
        waits=dys,
    )(*[x for level in range(sections) for x in xs[level]])
    arrived, waiting = [columns[0]], list(columns[1:])
    sent = [columns[0]]
    dys = [hop(dy, last, last - 1) for dy in dys]

    for level in range(last - 1, 0, -1):
        outs = []
        for seq in seqs:
            final = seq == seq_count - 1
            dy, dpre, *carried = kernel_call(
                functools.partial(back_kernel, level, seq, bins),
                [shape(bins, chans), shape(bins, inner)],
                layer_flops,
                "back",
                waits=[*outs[-1:], *arrived[1:]] if final else outs[-1:] or sent,
                carries=waiting if final else (),
            )(
                dys[seq],
                xs[level][min(seq, len(xs[level]) - 1)],
                pres[level][min(seq, len(pres[level]) - 1)],
                weight,
                point,
            )
            outs.append(dy)
            dpres[level].append(dpre)
        sent = outs
        going = len(carried) if level == 1 else -(-len(carried) // (last - 1))
        waiting = carried[going:]
        for block in carried[:going]:
            arrived.append(onward(block, len(arrived)))
        dys = [hop(dy, level, level - 1) for dy in outs]

    grads = []
    for seq in seqs:
        (dpre,) = kernel_call(
            functools.partial(head_kernel, sections, seq, bins),
            [shape(bins, inner)],
            layer_flops // 4,
            "head",
            waits=sent if seq == 0 else [*arrived[1:], grads[-1][1]],
        )(dys[seq], pres[0][0], point, *[dpres[level][seq] for level in range(1, sections)])
        grads.append([dpre, *(onward(dpre, step) for step in range(1, count))])

    mine, *others = kernel_call(
        functools.partial(grad_kernel, sections, count, seq_count, bins),
        [shape(3, chans // (count * groups), inner, dtype=jnp.float32)] * groups,
        2 * 3 * rows * chans * inner,
        "grad",
    )(*arrived, *[grads[seq][step] for step in range(count) for seq in seqs])
    for step, other in enumerate(others, 1):
        route = [(i, (i + step) % groups) for i in range(groups)]
        mine = mine + lax.ppermute(other, "dp", route)
    return mine[None]


def solution(mesh):
    def shards(inputs, cotangent, dilated_kernel_weight, point_weight):
        bins = inputs.shape[1]
        first_spread = bins // 2 // 2 ** (mesh.shape["pipe"] - 1)
        count = mesh.shape["ctx"]
        residues = (
            first_spread == count
            and mesh.shape["pipe"] > 1
            and bins % (16 * count) == 0
            and inputs.shape[2] % (count * mesh.shape["dp"]) == 0
        )
        plan = residue_shards if residues else edge_shards
        return plan(inputs, cotangent, dilated_kernel_weight, point_weight)

    return jax.shard_map(
        shards,
        mesh=mesh,
        in_specs=(
            P("dp", "ctx", None),
            P("dp", "ctx", None),
            P("pipe", None, None, None),
            P("pipe", None, None),
        ),
        out_specs=P("pipe", None, ("dp", "ctx"), None),
        check_vma=False,
    )
```

```python
import functools
import math

import jax
import jax.numpy as jnp
from jax import lax
from jax.experimental import pallas as pl
from jax.experimental.pallas import tpu as pltpu
from jax.sharding import PartitionSpec as P

root_half = 0.7071067811865476
inv_root_two_pi = 0.3989422804014327

in_vmem = pl.BlockSpec(memory_space=pltpu.VMEM)
anywhere = pl.BlockSpec(memory_space=pl.ANY)
contract_last = (((1,), (1,)), ((), ()))
contract_first = (((0,), (0,)), ((), ()))


def gelu(value):
    return 0.5 * value * (1.0 + lax.erf(value * root_half))


def gelu_slope(value):
    return (
        0.5 * (1.0 + lax.erf(value * root_half))
        + value * jnp.exp(-0.5 * value * value) * inv_root_two_pi
    )


def padded(cells, sides, width):
    for axis, dim in sides:
        count = lax.axis_size(axis)
        ends = count - 1
        head = lax.slice_in_dim(cells, 0, width, axis=dim)
        tail = lax.slice_in_dim(cells, cells.shape[dim] - width, cells.shape[dim], axis=dim)
        cells = jnp.concatenate(
            [
                lax.ppermute(tail, axis, [(i, (i + 1) % count) for i in range(ends)]),
                cells,
                lax.ppermute(head, axis, [((i + 1) % count, i) for i in range(ends)]),
            ],
            axis=dim,
        )
    return cells


def shifted(block, axis, distance):
    devices = range(lax.axis_size(axis))
    route = [(i - distance, i) for i in devices if i - distance in devices]
    return lax.ppermute(block, axis, route)


def edge_shards(inputs, cotangent, dilated_kernel_weight, point_weight):
    sections = lax.axis_size("pipe")
    section = lax.axis_index("pipe")
    seq_count, bins, chans = inputs.shape
    reach = bins // 2
    table = jnp.array(
        [reach // 2 ** (sections - 1 - level) for level in range(sections)], jnp.int32
    )
    spread = table[section]
    dilation_weight = dilated_kernel_weight[0]
    w_point = point_weight[0]
    inner_channel_count = dilation_weight.shape[2]
    scale = 1.0 / math.sqrt(seq_count * lax.axis_size("dp") * bins * lax.axis_size("ctx"))
    ticks = jnp.arange(seq_count + sections - 1, dtype=jnp.int32)

    def conv_fore(extended):
        running_total = jnp.zeros((bins, inner_channel_count), jnp.float32)
        for kernel_offset in range(3):
            receptive_span = lax.dynamic_slice_in_dim(
                extended, reach + (kernel_offset - 1) * spread, bins, 0
            )
            running_total = running_total + jnp.dot(
                receptive_span, dilation_weight[kernel_offset], preferred_element_type=jnp.float32
            )
        return running_total

    def put(store, slot, valid, item):
        current = lax.dynamic_index_in_dim(store, slot, 0, keepdims=False)
        return lax.dynamic_update_index_in_dim(store, jnp.where(valid, item, current), slot, 0)

    kept_x = jnp.zeros(inputs.shape, jnp.bfloat16)
    kept_ext = jnp.zeros((seq_count, bins + 2 * reach, chans), jnp.bfloat16)
    kept_pre = jnp.zeros((seq_count, bins, inner_channel_count), jnp.float32)

    def fore_tick(carry, tick):
        received, store_x, store_ext, store_pre = carry
        micro = tick - section
        valid = (micro >= 0) & (micro < seq_count)
        slot = jnp.clip(micro, 0, seq_count - 1)
        first = lax.dynamic_index_in_dim(inputs, slot, 0, keepdims=False)
        trunk_in = jnp.where(section == 0, first, received)
        act = gelu(trunk_in.astype(jnp.float32)).astype(jnp.bfloat16)
        extended = padded(act, (("ctx", 0),), reach)
        pre = conv_fore(extended)
        inner = gelu(pre).astype(jnp.bfloat16)
        out = (
            trunk_in.astype(jnp.float32)
            + jnp.dot(inner, w_point, preferred_element_type=jnp.float32)
        ).astype(jnp.bfloat16)
        sent = shifted(out, "pipe", 1)
        store_x = put(store_x, slot, valid, trunk_in)
        store_ext = put(store_ext, slot, valid, extended)
        store_pre = put(store_pre, slot, valid, pre)
        return ((sent, store_x, store_ext, store_pre), None)

    start_recv = jnp.zeros((bins, chans), jnp.bfloat16)
    (unused, kept_x, kept_ext, kept_pre), unused_out = lax.scan(
        fore_tick, (start_recv, kept_x, kept_ext, kept_pre), ticks
    )

    def back_tick(carry, tick):
        received, grad = carry
        micro = tick - (sections - 1 - section)
        valid = (micro >= 0) & (micro < seq_count)
        slot = jnp.clip(micro, 0, seq_count - 1)
        last = (
            lax.dynamic_index_in_dim(cotangent, slot, 0, keepdims=False).astype(jnp.float32) * scale
        ).astype(jnp.bfloat16)
        upstream = jnp.where(section == sections - 1, last, received)
        trunk_in = lax.dynamic_index_in_dim(kept_x, slot, 0, keepdims=False)
        extended = lax.dynamic_index_in_dim(kept_ext, slot, 0, keepdims=False)
        pre = lax.dynamic_index_in_dim(kept_pre, slot, 0, keepdims=False)
        inner_grad = lax.dot_general(
            upstream, w_point, contract_last, preferred_element_type=jnp.float32
        )
        dpre = (inner_grad * gelu_slope(pre) * valid.astype(jnp.float32)).astype(jnp.bfloat16)
        dpre_ext = padded(dpre, (("ctx", 0),), reach)
        dact = jnp.zeros((bins, chans), jnp.float32)
        taps = []
        for kernel_offset in range(3):
            receptive_span = lax.dynamic_slice_in_dim(
                dpre_ext, reach - (kernel_offset - 1) * spread, bins, 0
            )
            dact = dact + lax.dot_general(
                receptive_span,
                dilation_weight[kernel_offset],
                contract_last,
                preferred_element_type=jnp.float32,
            )
            source = lax.dynamic_slice_in_dim(
                extended, reach + (kernel_offset - 1) * spread, bins, 0
            )
            taps.append(
                lax.dot_general(source, dpre, contract_first, preferred_element_type=jnp.float32)
            )
        grad = grad + jnp.stack(taps)
        back = (
            upstream.astype(jnp.float32) + dact * gelu_slope(trunk_in.astype(jnp.float32))
        ).astype(jnp.bfloat16)
        sent = shifted(back, "pipe", -1)
        return ((sent, grad), None)

    start_grad = jnp.zeros((3, chans, inner_channel_count), jnp.float32)
    (unused_back, grad), unused_seq = lax.scan(back_tick, (start_recv, start_grad), ticks)
    term = grad[None]
    return lax.psum_scatter(term, ("dp", "ctx"), scatter_dimension=2, tiled=True)


def moved(value, by, bins):
    pieces = []
    for start in range(0, value.shape[0], bins):
        piece = value[start : start + bins]
        place = lax.broadcasted_iota(jnp.int32, piece.shape, 0)
        if by > 0:
            keep = place >= by
        else:
            keep = place < bins + by
        pieces.append(jnp.where(keep, pltpu.roll(piece, by % bins, 0), 0.0))
    return jnp.concatenate(pieces, axis=0)


def fore(x, weight_ref, spread, bins):
    act = gelu(x.astype(jnp.float32)).astype(jnp.bfloat16)
    terms = [
        jnp.dot(act, weight_ref[0, tap], preferred_element_type=jnp.float32) for tap in range(3)
    ]
    return terms[1] + moved(terms[0], spread, bins) + moved(terms[2], -spread, bins)


def back_pre(dy, pre, point_ref):
    inner_grad = lax.dot_general(
        dy, point_ref[0], contract_last, preferred_element_type=jnp.float32
    )
    return (inner_grad * gelu_slope(pre)).astype(jnp.bfloat16)


def back_trunk(dy, dpre, x, weight_ref, spread, bins):
    wide = dpre.astype(jnp.float32)
    spans = (
        moved(wide, -spread, bins).astype(jnp.bfloat16),
        dpre,
        moved(wide, spread, bins).astype(jnp.bfloat16),
    )
    dact = jnp.zeros(dy.shape, jnp.float32)
    for tap in range(3):
        dact = dact + lax.dot_general(
            spans[tap], weight_ref[0, tap], contract_last, preferred_element_type=jnp.float32
        )
    return (
        dy.astype(jnp.float32) + dact * gelu_slope(x.astype(jnp.float32))
    ).astype(jnp.bfloat16)


def of_seq(ref, seq, bins):
    if ref.shape[0] == bins:
        return ref[...]
    return ref[seq * bins : (seq + 1) * bins, :]


def split_kernel(last, payload_ref, *out_refs):
    count = len(out_refs)
    seq_count, bins, chans = payload_ref.shape
    part = bins // count
    section = lax.axis_index("pipe")
    place = lax.axis_index("ctx")

    @pl.when((section == 0) | (section == last))
    def send():
        source = payload_ref[...].reshape(seq_count * bins, chans)
        row = lax.broadcasted_iota(jnp.int32, (part, seq_count * bins), 0)
        col = lax.broadcasted_iota(jnp.int32, (part, seq_count * bins), 1)
        for hop in range(count):
            residue = lax.bitwise_xor(place, hop)
            rows = [
                (col == seq * bins + count * row + residue).astype(jnp.float32)
                for seq in range(seq_count)
            ]
            pick = jnp.concatenate(rows, axis=0).astype(jnp.bfloat16)
            out_refs[hop][...] = jnp.dot(
                pick, source, preferred_element_type=jnp.float32
            ).astype(jnp.bfloat16)


def hold_kernel(weight_ref, point_ref, weight_out, point_out, sems):
    loads = [
        pltpu.make_async_copy(weight_ref, weight_out, sems.at[0]),
        pltpu.make_async_copy(point_ref, point_out, sems.at[1]),
    ]
    for load in loads:
        load.start()
    for load in loads:
        load.wait()


def first_kernel(last, bins, *refs):
    parts, (weight_ref, point_ref, whole_ref, out_ref, pre_ref) = refs[:-5], refs[-5:]
    count = len(parts)
    section = lax.axis_index("pipe")
    place = lax.axis_index("ctx")
    part = bins // count
    seq_count = whole_ref.shape[0] // bins

    @pl.when((section == 0) | (section == last))
    def gather():
        for hop in range(count):
            source = lax.bitwise_xor(place, hop)
            for seq in range(seq_count):
                at = pl.multiple_of(seq * bins + source * part, part)
                whole_ref[pl.ds(at, part), :] = parts[hop][seq * part : (seq + 1) * part, :]

    @pl.when(section == 0)
    def layer():
        x = whole_ref[...]
        finish(x, fore(x, weight_ref, 1, bins), point_ref, out_ref, pre_ref)


def finish(x, pre, point_ref, out_ref, pre_ref):
    pre_ref[...] = pre
    branch = jnp.dot(
        gelu(pre).astype(jnp.bfloat16), point_ref[0], preferred_element_type=jnp.float32
    )
    out_ref[...] = (x.astype(jnp.float32) + branch).astype(jnp.bfloat16)


def fore_kernel(level, seq, bins, x_ref, weight_ref, point_ref, out_ref, pre_ref):
    @pl.when(lax.axis_index("pipe") == level)
    def layer():
        x = of_seq(x_ref, seq, bins)
        finish(x, fore(x, weight_ref, 2**level, bins), point_ref, out_ref, pre_ref)


def turn_kernel(level, seq, bins, scale, x_ref, cot_ref, weight_ref, point_ref, dy_ref, dpre_ref):
    @pl.when(lax.axis_index("pipe") == level)
    def layer():
        x = of_seq(x_ref, seq, bins)
        pre = fore(x, weight_ref, 2**level, bins)
        cot = of_seq(cot_ref, seq, bins)
        dy = (cot.astype(jnp.float32) * scale).astype(jnp.bfloat16)
        dpre = back_pre(dy, pre, point_ref)
        dpre_ref[...] = dpre
        dy_ref[...] = back_trunk(dy, dpre, x, weight_ref, 2**level, bins)


def back_kernel(level, seq, bins, dy_in_ref, x_ref, pre_ref, weight_ref, point_ref, dy_ref, dpre_ref):
    @pl.when(lax.axis_index("pipe") == level)
    def layer():
        dy = dy_in_ref[...]
        x = of_seq(x_ref, seq, bins)
        dpre = back_pre(dy, of_seq(pre_ref, seq, bins), point_ref)
        dpre_ref[...] = dpre
        dy_ref[...] = back_trunk(dy, dpre, x, weight_ref, 2**level, bins)


def message_kernel(places, *refs):
    blocks, message_ref = refs[:-1], refs[-1]
    size = message_ref.shape[0] // len(places)
    for to, (ref, at) in enumerate(zip(blocks, places)):
        message_ref[to * size : (to + 1) * size, :] = ref[at * size : (at + 1) * size, :]


def head_kernel(sections, seq, bins, dy_in_ref, pre_ref, point_ref, *refs):
    others, out_ref = refs[:-1], refs[-1]
    section = lax.axis_index("pipe")

    @pl.when(section == 0)
    def layer():
        out_ref[...] = back_pre(dy_in_ref[...], of_seq(pre_ref, seq, bins), point_ref)

    for level in range(1, sections):

        @pl.when(section == level)
        def keep(level=level):
            out_ref[...] = others[level - 1][...]


def columns_kernel(groups, runs, kept, *refs):
    refs, (sent_ref,) = refs[:-1], refs[-1:]
    kept_refs = refs[sum(runs) :]
    count = 2 * len(kept)
    section = lax.axis_index("pipe")
    core = lax.axis_index("dp")
    place = lax.axis_index("ctx")
    x, start = None, 0
    for level, run in enumerate(runs):
        pieces = [ref[...] for ref in refs[start : start + run]]
        start += run
        whole = jnp.concatenate(pieces, axis=0).astype(jnp.float32)
        x = whole if x is None else jnp.where(section == level, whole, x)
    act = gelu(x).astype(jnp.bfloat16)
    chans = act.shape[1]
    width = chans // (groups * count)
    row = lax.broadcasted_iota(jnp.int32, (width, chans), 0)
    col = lax.broadcasted_iota(jnp.int32, (width, chans), 1)

    def block(offset):
        owner = lax.bitwise_xor(place, offset)
        rows = []
        for step in range(groups):
            first = (lax.rem(core + step, groups) * count + owner) * width
            rows.append((col == first + row).astype(jnp.float32))
        pick = jnp.concatenate(rows, axis=0).astype(jnp.bfloat16)
        return lax.dot_general(
            pick, act, contract_last, preferred_element_type=jnp.float32
        ).astype(jnp.bfloat16)

    size = groups * width
    for at, offset in enumerate(kept):
        kept_refs[at][...] = block(offset)
        sent_ref[at * size : (at + 1) * size, :] = block(offset ^ 1)


def grad_kernel(sections, seq, bins, blocks, *refs):
    columns, refs = refs[: len(blocks)], refs[len(blocks) :]
    grads, refs = refs[: len(blocks)], refs[len(blocks) :]
    made = len(refs) // 2
    section = lax.axis_index("pipe")

    def taps(spread, earlier, outs):
        width = outs[0].shape[1]
        size = len(outs) * width
        act = jnp.concatenate(
            [
                ref[at * size : (at + 1) * size, seq * bins : (seq + 1) * bins]
                for ref, at in zip(columns, blocks)
            ],
            axis=1,
        )
        dpre = jnp.concatenate([ref[...] for ref in grads], axis=0)
        wide = dpre.astype(jnp.float32)
        spans = (
            moved(wide, -spread, bins).astype(jnp.bfloat16),
            dpre,
            moved(wide, spread, bins).astype(jnp.bfloat16),
        )
        for tap in range(3):
            grad = jnp.dot(act, spans[tap], preferred_element_type=jnp.float32)
            for step, out_ref in enumerate(outs):
                term = grad[step * width : (step + 1) * width]
                out_ref[tap] = term if earlier is None else earlier[step][tap] + term

    if seq == 0:
        earlier, outs = None, refs
    else:
        earlier, outs = refs[:made], refs[made:]
    for level in range(sections):

        @pl.when(section == level)
        def run(level=level):
            taps(2**level, earlier, outs)


def kernel_call(body, outs, flops, name, waits=(), carries=(), in_spec=in_vmem, scratch=()):
    def call(*args):
        used, taken = len(args), len(args) + len(waits) + len(carries)

        def run(*refs):
            made = refs[taken : taken + len(outs)]
            body(*refs[:used], *made, *refs[taken + len(outs) + len(carries) :])

        moved_bytes = sum(math.prod(a.shape) * a.dtype.itemsize for a in (*args, *outs))
        return pl.pallas_call(
            run,
            out_shape=[*outs, *(jax.ShapeDtypeStruct(a.shape, a.dtype) for a in carries)],
            in_specs=[in_spec] * used + [anywhere] * (taken - used),
            out_specs=[in_vmem] * len(outs) + [anywhere] * len(carries),
            input_output_aliases={
                used + len(waits) + at: len(outs) + at for at in range(len(carries))
            },
            scratch_shapes=list(scratch),
            compiler_params=pltpu.CompilerParams(vmem_limit_bytes=24 * 2**20),
            cost_estimate=pl.CostEstimate(
                flops=flops, bytes_accessed=moved_bytes, transcendentals=0
            ),
            name=name,
        )(*args, *waits, *carries)

    return call


def cycle_through(sections, source, target):
    order = [0, 1, 3, 2] if sections == 4 else list(range(sections))
    step = (order.index(target) - order.index(source)) % sections
    if step not in (1, sections - 1):
        order, step = list(range(sections)), (target - source) % sections
    return {order[at]: order[(at + step) % sections] for at in range(sections)}


def residue_shards(inputs, cotangent, weight, point):
    sections = lax.axis_size("pipe")
    section = lax.axis_index("pipe")
    count = lax.axis_size("ctx")
    groups = lax.axis_size("dp")
    seq_count, bins, chans = inputs.shape
    inner = weight.shape[3]
    rows = seq_count * bins
    scale = 1.0 / math.sqrt(seq_count * groups * bins * count)
    last = sections - 1
    seqs = range(seq_count)
    layer_flops = 2 * bins * chans * inner * 4

    def shape(*dims, dtype=jnp.bfloat16):
        return jax.ShapeDtypeStruct(dims, dtype)

    def hop(value, source, target):
        cycle = cycle_through(sections, source, target)
        route = [
            (stage * count + i, cycle[stage] * count + i)
            for stage in range(sections)
            for i in range(count)
        ]
        return lax.ppermute(value, ("pipe", "ctx"), route)

    def exchange(value, offset):
        return lax.ppermute(value, "ctx", [(i, i ^ offset) for i in range(count)])

    payload = jnp.where(section == last, cotangent, inputs)
    parts = kernel_call(
        functools.partial(split_kernel, last),
        [shape(rows // count, chans)] * count,
        2 * rows * rows * chans,
        "split",
    )(payload)
    weight, point = kernel_call(
        hold_kernel,
        [shape(*weight.shape), shape(*point.shape)],
        0,
        "hold",
        waits=[parts[0]],
        in_spec=anywhere,
        scratch=[pltpu.SemaphoreType.DMA((2,))],
    )(weight, point)
    parts = [parts[0], *(exchange(parts[offset], offset) for offset in range(1, count))]

    whole, out, pre = kernel_call(
        functools.partial(first_kernel, last, bins),
        [shape(rows, chans), shape(rows, chans), shape(rows, inner, dtype=jnp.float32)],
        seq_count * layer_flops,
        "first",
    )(*parts, weight, point)
    xs, pres, sent = [[whole]], [[pre]], ()
    xs.append([hop(out, 0, 1)])
    for level in range(1, last):
        outs = []
        pres.append([])
        for seq in seqs:
            out, pre = kernel_call(
                functools.partial(fore_kernel, level, seq, bins),
                [shape(bins, chans), shape(bins, inner, dtype=jnp.float32)],
                layer_flops,
                "fore",
                waits=outs[-1:] or sent,
            )(xs[level][min(seq, len(xs[level]) - 1)], weight, point)
            outs.append(out)
            pres[level].append(pre)
        sent = outs
        xs.append([hop(out, level, level + 1) for out in outs])

    dys, dpres = [], [[] for level in range(sections)]
    for seq in seqs:
        dy, dpre = kernel_call(
            functools.partial(turn_kernel, last, seq, bins, scale),
            [shape(bins, chans), shape(bins, inner)],
            2 * layer_flops,
            "turn",
            waits=dys[-1:] or sent,
        )(xs[last][min(seq, len(xs[last]) - 1)], whole, weight, point)
        dys.append(dy)
        dpres[last].append(dpre)

    kept = list(range(0, count, 2))
    size = chans // count
    *owned, message = kernel_call(
        functools.partial(columns_kernel, groups, [len(x) for x in xs], kept),
        [shape(size, rows)] * len(kept) + [shape(size * len(kept), rows)],
        2 * rows * chans * chans,
        "columns",
        waits=dys,
    )(*[x for level in range(sections) for x in xs[level]])
    blocks = {(offset, 0): (array, 0) for offset, array in zip(kept, owned)}
    moving = [(offset, 0) for offset in kept]
    dys = [hop(dy, last, last - 1) for dy in dys]
    message, bit = exchange(message, 1), 1
    blocks.update({(to, start ^ bit): (message, at) for at, (to, start) in enumerate(moving)})
    sent = [owned[0]]

    late = []
    for level in range(last - 1, 0, -1):
        outs = []
        for seq in seqs:
            waits = outs[-1:] or sent
            if seq == seq_count - 1:
                waits, late = [*waits, *late], []
            dy, dpre = kernel_call(
                functools.partial(back_kernel, level, seq, bins),
                [shape(bins, chans), shape(bins, inner)],
                layer_flops,
                "back",
                waits=waits,
            )(
                dys[seq],
                xs[level][min(seq, len(xs[level]) - 1)],
                pres[level][min(seq, len(pres[level]) - 1)],
                weight,
                point,
            )
            outs.append(dy)
            dpres[level].append(dpre)
        dys = [hop(dy, level, level - 1) for dy in outs]
        sent = outs
        if 2 * bit < count:
            bit *= 2
            moving = sorted(key for key in blocks if key[0] & bit)
            (message,) = kernel_call(
                functools.partial(message_kernel, [blocks[key][1] for key in moving]),
                [shape(size * len(moving), rows)],
                0,
                "message",
                waits=outs,
            )(*[blocks[key][0] for key in moving])
            message = exchange(message, bit)
            for at, (to, start) in enumerate(moving):
                del blocks[to, start]
                blocks[to ^ bit, start ^ bit] = (message, at)
            late = [message]

    columns = [blocks[0, offset] for offset in range(count)]
    shares = [shape(3, chans // (count * groups), inner, dtype=jnp.float32)] * groups
    parts, grads = [], []
    for seq in seqs:
        (dpre,) = kernel_call(
            functools.partial(head_kernel, sections, seq, bins),
            [shape(bins, inner)],
            layer_flops // 4,
            "head",
            waits=sent if seq == 0 else (),
        )(dys[seq], pres[0][0], point, *[dpres[level][seq] for level in range(1, sections)])
        grads.append([dpre, *(exchange(dpre, offset) for offset in range(1, count))])
    for seq in seqs:
        parts = kernel_call(
            functools.partial(grad_kernel, sections, seq, bins, [at for array, at in columns]),
            shares,
            2 * 3 * bins * count * chans * inner // count,
            "grad",
        )(*[array for array, at in columns], *grads[seq], *parts)
    mine, *others = parts
    for step, other in enumerate(others, 1):
        route = [(i, (i + step) % groups) for i in range(groups)]
        mine = mine + lax.ppermute(other, "dp", route)
    return mine[None]


def solution(mesh):
    def shards(inputs, cotangent, dilated_kernel_weight, point_weight):
        bins = inputs.shape[1]
        first_spread = bins // 2 // 2 ** (mesh.shape["pipe"] - 1)
        count = mesh.shape["ctx"]
        residues = (
            first_spread == count
            and mesh.shape["pipe"] > 1
            and bins % (16 * count) == 0
            and 1 < count == 1 << (count.bit_length() - 1) <= 1 << (mesh.shape["pipe"] - 1)
            and inputs.shape[2] % (count * mesh.shape["dp"]) == 0
        )
        plan = residue_shards if residues else edge_shards
        return plan(inputs, cotangent, dilated_kernel_weight, point_weight)

    return jax.shard_map(
        shards,
        mesh=mesh,
        in_specs=(
            P("dp", "ctx", None),
            P("dp", "ctx", None),
            P("pipe", None, None, None),
            P("pipe", None, None),
        ),
        out_specs=P("pipe", None, ("dp", "ctx"), None),
        check_vma=False,
    )
```

```python
import functools
import math

import jax
import jax.numpy as jnp
from jax import lax
from jax.experimental import pallas as pl
from jax.experimental.pallas import tpu as pltpu
from jax.sharding import PartitionSpec as P

root_half = 0.7071067811865476
inv_root_two_pi = 0.3989422804014327

in_vmem = pl.BlockSpec(memory_space=pltpu.VMEM)
anywhere = pl.BlockSpec(memory_space=pl.ANY)
contract_last = (((1,), (1,)), ((), ()))
contract_first = (((0,), (0,)), ((), ()))


def gelu(value):
    return 0.5 * value * (1.0 + lax.erf(value * root_half))


def gelu_slope(value):
    return (
        0.5 * (1.0 + lax.erf(value * root_half))
        + value * jnp.exp(-0.5 * value * value) * inv_root_two_pi
    )


def padded(cells, sides, width):
    for axis, dim in sides:
        count = lax.axis_size(axis)
        ends = count - 1
        head = lax.slice_in_dim(cells, 0, width, axis=dim)
        tail = lax.slice_in_dim(cells, cells.shape[dim] - width, cells.shape[dim], axis=dim)
        cells = jnp.concatenate(
            [
                lax.ppermute(tail, axis, [(i, (i + 1) % count) for i in range(ends)]),
                cells,
                lax.ppermute(head, axis, [((i + 1) % count, i) for i in range(ends)]),
            ],
            axis=dim,
        )
    return cells


def shifted(block, axis, distance):
    devices = range(lax.axis_size(axis))
    route = [(i - distance, i) for i in devices if i - distance in devices]
    return lax.ppermute(block, axis, route)


def edge_shards(inputs, cotangent, dilated_kernel_weight, point_weight):
    sections = lax.axis_size("pipe")
    section = lax.axis_index("pipe")
    seq_count, bins, chans = inputs.shape
    reach = bins // 2
    table = jnp.array(
        [reach // 2 ** (sections - 1 - level) for level in range(sections)], jnp.int32
    )
    spread = table[section]
    dilation_weight = dilated_kernel_weight[0]
    w_point = point_weight[0]
    inner_channel_count = dilation_weight.shape[2]
    scale = 1.0 / math.sqrt(seq_count * lax.axis_size("dp") * bins * lax.axis_size("ctx"))
    ticks = jnp.arange(seq_count + sections - 1, dtype=jnp.int32)

    def conv_fore(extended):
        running_total = jnp.zeros((bins, inner_channel_count), jnp.float32)
        for kernel_offset in range(3):
            receptive_span = lax.dynamic_slice_in_dim(
                extended, reach + (kernel_offset - 1) * spread, bins, 0
            )
            running_total = running_total + jnp.dot(
                receptive_span, dilation_weight[kernel_offset], preferred_element_type=jnp.float32
            )
        return running_total

    def put(store, slot, valid, item):
        current = lax.dynamic_index_in_dim(store, slot, 0, keepdims=False)
        return lax.dynamic_update_index_in_dim(store, jnp.where(valid, item, current), slot, 0)

    kept_x = jnp.zeros(inputs.shape, jnp.bfloat16)
    kept_ext = jnp.zeros((seq_count, bins + 2 * reach, chans), jnp.bfloat16)
    kept_pre = jnp.zeros((seq_count, bins, inner_channel_count), jnp.float32)

    def fore_tick(carry, tick):
        received, store_x, store_ext, store_pre = carry
        micro = tick - section
        valid = (micro >= 0) & (micro < seq_count)
        slot = jnp.clip(micro, 0, seq_count - 1)
        first = lax.dynamic_index_in_dim(inputs, slot, 0, keepdims=False)
        trunk_in = jnp.where(section == 0, first, received)
        act = gelu(trunk_in.astype(jnp.float32)).astype(jnp.bfloat16)
        extended = padded(act, (("ctx", 0),), reach)
        pre = conv_fore(extended)
        inner = gelu(pre).astype(jnp.bfloat16)
        out = (
            trunk_in.astype(jnp.float32)
            + jnp.dot(inner, w_point, preferred_element_type=jnp.float32)
        ).astype(jnp.bfloat16)
        sent = shifted(out, "pipe", 1)
        store_x = put(store_x, slot, valid, trunk_in)
        store_ext = put(store_ext, slot, valid, extended)
        store_pre = put(store_pre, slot, valid, pre)
        return ((sent, store_x, store_ext, store_pre), None)

    start_recv = jnp.zeros((bins, chans), jnp.bfloat16)
    (unused, kept_x, kept_ext, kept_pre), unused_out = lax.scan(
        fore_tick, (start_recv, kept_x, kept_ext, kept_pre), ticks
    )

    def back_tick(carry, tick):
        received, grad = carry
        micro = tick - (sections - 1 - section)
        valid = (micro >= 0) & (micro < seq_count)
        slot = jnp.clip(micro, 0, seq_count - 1)
        last = (
            lax.dynamic_index_in_dim(cotangent, slot, 0, keepdims=False).astype(jnp.float32) * scale
        ).astype(jnp.bfloat16)
        upstream = jnp.where(section == sections - 1, last, received)
        trunk_in = lax.dynamic_index_in_dim(kept_x, slot, 0, keepdims=False)
        extended = lax.dynamic_index_in_dim(kept_ext, slot, 0, keepdims=False)
        pre = lax.dynamic_index_in_dim(kept_pre, slot, 0, keepdims=False)
        inner_grad = lax.dot_general(
            upstream, w_point, contract_last, preferred_element_type=jnp.float32
        )
        dpre = (inner_grad * gelu_slope(pre) * valid.astype(jnp.float32)).astype(jnp.bfloat16)
        dpre_ext = padded(dpre, (("ctx", 0),), reach)
        dact = jnp.zeros((bins, chans), jnp.float32)
        taps = []
        for kernel_offset in range(3):
            receptive_span = lax.dynamic_slice_in_dim(
                dpre_ext, reach - (kernel_offset - 1) * spread, bins, 0
            )
            dact = dact + lax.dot_general(
                receptive_span,
                dilation_weight[kernel_offset],
                contract_last,
                preferred_element_type=jnp.float32,
            )
            source = lax.dynamic_slice_in_dim(
                extended, reach + (kernel_offset - 1) * spread, bins, 0
            )
            taps.append(
                lax.dot_general(source, dpre, contract_first, preferred_element_type=jnp.float32)
            )
        grad = grad + jnp.stack(taps)
        back = (
            upstream.astype(jnp.float32) + dact * gelu_slope(trunk_in.astype(jnp.float32))
        ).astype(jnp.bfloat16)
        sent = shifted(back, "pipe", -1)
        return ((sent, grad), None)

    start_grad = jnp.zeros((3, chans, inner_channel_count), jnp.float32)
    (unused_back, grad), unused_seq = lax.scan(back_tick, (start_recv, start_grad), ticks)
    term = grad[None]
    return lax.psum_scatter(term, ("dp", "ctx"), scatter_dimension=2, tiled=True)


def moved(value, by, bins):
    pieces = []
    for start in range(0, value.shape[0], bins):
        piece = value[start : start + bins]
        place = lax.broadcasted_iota(jnp.int32, piece.shape, 0)
        if by > 0:
            keep = place >= by
        else:
            keep = place < bins + by
        pieces.append(jnp.where(keep, pltpu.roll(piece, by % bins, 0), 0.0))
    return jnp.concatenate(pieces, axis=0)


def fore(x, weight_ref, spread, bins):
    act = gelu(x.astype(jnp.float32)).astype(jnp.bfloat16)
    terms = [
        jnp.dot(act, weight_ref[0, tap], preferred_element_type=jnp.float32) for tap in range(3)
    ]
    return terms[1] + moved(terms[0], spread, bins) + moved(terms[2], -spread, bins)


def back_pre(dy, pre, point_ref):
    inner_grad = lax.dot_general(
        dy, point_ref[0], contract_last, preferred_element_type=jnp.float32
    )
    return (inner_grad * gelu_slope(pre)).astype(jnp.bfloat16)


def back_trunk(dy, dpre, x, weight_ref, spread, bins):
    wide = dpre.astype(jnp.float32)
    spans = (
        moved(wide, -spread, bins).astype(jnp.bfloat16),
        dpre,
        moved(wide, spread, bins).astype(jnp.bfloat16),
    )
    dact = jnp.zeros(dy.shape, jnp.float32)
    for tap in range(3):
        dact = dact + lax.dot_general(
            spans[tap], weight_ref[0, tap], contract_last, preferred_element_type=jnp.float32
        )
    return (
        dy.astype(jnp.float32) + dact * gelu_slope(x.astype(jnp.float32))
    ).astype(jnp.bfloat16)


def of_seq(ref, seq, bins):
    if ref.shape[0] == bins:
        return ref[...]
    return ref[seq * bins : (seq + 1) * bins, :]


def split_kernel(last, payload_ref, *out_refs):
    count = len(out_refs)
    seq_count, bins, chans = payload_ref.shape
    part = bins // count
    section = lax.axis_index("pipe")
    place = lax.axis_index("ctx")

    @pl.when((section == 0) | (section == last))
    def send():
        source = payload_ref[...].reshape(seq_count * bins, chans)
        row = lax.broadcasted_iota(jnp.int32, (part, seq_count * bins), 0)
        col = lax.broadcasted_iota(jnp.int32, (part, seq_count * bins), 1)
        for hop in range(count):
            residue = lax.rem(place + hop, count)
            rows = [
                (col == seq * bins + count * row + residue).astype(jnp.float32)
                for seq in range(seq_count)
            ]
            pick = jnp.concatenate(rows, axis=0).astype(jnp.bfloat16)
            out_refs[hop][...] = jnp.dot(
                pick, source, preferred_element_type=jnp.float32
            ).astype(jnp.bfloat16)


def hold_kernel(weight_ref, point_ref, weight_out, point_out, sems):
    loads = [
        pltpu.make_async_copy(weight_ref, weight_out, sems.at[0]),
        pltpu.make_async_copy(point_ref, point_out, sems.at[1]),
    ]
    for load in loads:
        load.start()
    for load in loads:
        load.wait()


def first_kernel(last, bins, *refs):
    parts, (weight_ref, point_ref, whole_ref, out_ref, pre_ref) = refs[:-5], refs[-5:]
    count = len(parts)
    section = lax.axis_index("pipe")
    place = lax.axis_index("ctx")
    part = bins // count
    seq_count = whole_ref.shape[0] // bins

    @pl.when((section == 0) | (section == last))
    def gather():
        for hop in range(count):
            source = lax.rem(place - hop + count, count)
            for seq in range(seq_count):
                at = pl.multiple_of(seq * bins + source * part, part)
                whole_ref[pl.ds(at, part), :] = parts[hop][seq * part : (seq + 1) * part, :]

    @pl.when(section == 0)
    def layer():
        x = whole_ref[...]
        finish(x, fore(x, weight_ref, 1, bins), point_ref, out_ref, pre_ref)


def finish(x, pre, point_ref, out_ref, pre_ref):
    pre_ref[...] = pre
    branch = jnp.dot(
        gelu(pre).astype(jnp.bfloat16), point_ref[0], preferred_element_type=jnp.float32
    )
    out_ref[...] = (x.astype(jnp.float32) + branch).astype(jnp.bfloat16)


def fore_kernel(level, seq, bins, x_ref, weight_ref, point_ref, out_ref, pre_ref):
    @pl.when(lax.axis_index("pipe") == level)
    def layer():
        x = of_seq(x_ref, seq, bins)
        finish(x, fore(x, weight_ref, 2**level, bins), point_ref, out_ref, pre_ref)


def turn_kernel(level, seq, bins, scale, x_ref, cot_ref, weight_ref, point_ref, dy_ref, dpre_ref):
    @pl.when(lax.axis_index("pipe") == level)
    def layer():
        x = of_seq(x_ref, seq, bins)
        pre = fore(x, weight_ref, 2**level, bins)
        cot = of_seq(cot_ref, seq, bins)
        dy = (cot.astype(jnp.float32) * scale).astype(jnp.bfloat16)
        dpre = back_pre(dy, pre, point_ref)
        dpre_ref[...] = dpre
        dy_ref[...] = back_trunk(dy, dpre, x, weight_ref, 2**level, bins)


def back_kernel(level, seq, bins, dy_in_ref, x_ref, pre_ref, weight_ref, point_ref, dy_ref, dpre_ref):
    @pl.when(lax.axis_index("pipe") == level)
    def layer():
        dy = dy_in_ref[...]
        x = of_seq(x_ref, seq, bins)
        dpre = back_pre(dy, of_seq(pre_ref, seq, bins), point_ref)
        dpre_ref[...] = dpre
        dy_ref[...] = back_trunk(dy, dpre, x, weight_ref, 2**level, bins)


def message_kernel(places, *refs):
    blocks, message_ref = refs[:-1], refs[-1]
    size = message_ref.shape[0] // len(places)
    for to, (ref, at) in enumerate(zip(blocks, places)):
        message_ref[to * size : (to + 1) * size, :] = ref[at * size : (at + 1) * size, :]


def head_kernel(sections, seq, bins, dy_in_ref, pre_ref, point_ref, *refs):
    others, out_ref = refs[:-1], refs[-1]
    section = lax.axis_index("pipe")

    @pl.when(section == 0)
    def layer():
        out_ref[...] = back_pre(dy_in_ref[...], of_seq(pre_ref, seq, bins), point_ref)

    for level in range(1, sections):

        @pl.when(section == level)
        def keep(level=level):
            out_ref[...] = others[level - 1][...]


def columns_kernel(groups, runs, kept, *refs):
    refs, (sent_ref,) = refs[:-1], refs[-1:]
    kept_refs = refs[sum(runs) :]
    count = 2 * len(kept)
    section = lax.axis_index("pipe")
    core = lax.axis_index("dp")
    place = lax.axis_index("ctx")
    x, start = None, 0
    for level, run in enumerate(runs):
        pieces = [ref[...] for ref in refs[start : start + run]]
        start += run
        whole = jnp.concatenate(pieces, axis=0).astype(jnp.float32)
        x = whole if x is None else jnp.where(section == level, whole, x)
    act = gelu(x).astype(jnp.bfloat16)
    chans = act.shape[1]
    width = chans // (groups * count)
    row = lax.broadcasted_iota(jnp.int32, (width, chans), 0)
    col = lax.broadcasted_iota(jnp.int32, (width, chans), 1)

    def block(offset):
        owner = lax.bitwise_xor(place, offset)
        rows = []
        for step in range(groups):
            first = (lax.rem(core + step, groups) * count + owner) * width
            rows.append((col == first + row).astype(jnp.float32))
        pick = jnp.concatenate(rows, axis=0).astype(jnp.bfloat16)
        return lax.dot_general(
            pick, act, contract_last, preferred_element_type=jnp.float32
        ).astype(jnp.bfloat16)

    size = groups * width
    for at, offset in enumerate(kept):
        kept_refs[at][...] = block(offset)
        sent_ref[at * size : (at + 1) * size, :] = block(offset ^ 1)


def grad_kernel(sections, seq, bins, blocks, *refs):
    columns, refs = refs[: len(blocks)], refs[len(blocks) :]
    grads, refs = refs[: len(blocks)], refs[len(blocks) :]
    made = len(refs) // 2
    section = lax.axis_index("pipe")

    def taps(spread, earlier, outs):
        width = outs[0].shape[1]
        size = len(outs) * width
        act = jnp.concatenate(
            [
                ref[at * size : (at + 1) * size, seq * bins : (seq + 1) * bins]
                for ref, at in zip(columns, blocks)
            ],
            axis=1,
        )
        dpre = jnp.concatenate([ref[...] for ref in grads], axis=0)
        wide = dpre.astype(jnp.float32)
        spans = (
            moved(wide, -spread, bins).astype(jnp.bfloat16),
            dpre,
            moved(wide, spread, bins).astype(jnp.bfloat16),
        )
        for tap in range(3):
            grad = jnp.dot(act, spans[tap], preferred_element_type=jnp.float32)
            for step, out_ref in enumerate(outs):
                term = grad[step * width : (step + 1) * width]
                if earlier is not None:
                    term = earlier[step][tap] + term
                out_ref[tap] = term.astype(out_ref.dtype)

    if seq == 0:
        earlier, outs = None, refs
    else:
        earlier, outs = refs[:made], refs[made:]
    for level in range(sections):

        @pl.when(section == level)
        def run(level=level):
            taps(2**level, earlier, outs)


def kernel_call(body, outs, flops, name, waits=(), carries=(), in_spec=in_vmem, scratch=()):
    def call(*args):
        used, taken = len(args), len(args) + len(waits) + len(carries)

        def run(*refs):
            made = refs[taken : taken + len(outs)]
            body(*refs[:used], *made, *refs[taken + len(outs) + len(carries) :])

        moved_bytes = sum(math.prod(a.shape) * a.dtype.itemsize for a in (*args, *outs))
        return pl.pallas_call(
            run,
            out_shape=[*outs, *(jax.ShapeDtypeStruct(a.shape, a.dtype) for a in carries)],
            in_specs=[in_spec] * used + [anywhere] * (taken - used),
            out_specs=[in_vmem] * len(outs) + [anywhere] * len(carries),
            input_output_aliases={
                used + len(waits) + at: len(outs) + at for at in range(len(carries))
            },
            scratch_shapes=list(scratch),
            compiler_params=pltpu.CompilerParams(vmem_limit_bytes=24 * 2**20),
            cost_estimate=pl.CostEstimate(
                flops=flops, bytes_accessed=moved_bytes, transcendentals=0
            ),
            name=name,
        )(*args, *waits, *carries)

    return call


def cycle_through(sections, source, target):
    order = [0, 1, 3, 2] if sections == 4 else list(range(sections))
    step = (order.index(target) - order.index(source)) % sections
    if step not in (1, sections - 1):
        order, step = list(range(sections)), (target - source) % sections
    return {order[at]: order[(at + step) % sections] for at in range(sections)}


def residue_shards(inputs, cotangent, weight, point):
    sections = lax.axis_size("pipe")
    section = lax.axis_index("pipe")
    count = lax.axis_size("ctx")
    groups = lax.axis_size("dp")
    seq_count, bins, chans = inputs.shape
    inner = weight.shape[3]
    rows = seq_count * bins
    scale = 1.0 / math.sqrt(seq_count * groups * bins * count)
    last = sections - 1
    seqs = range(seq_count)
    layer_flops = 2 * bins * chans * inner * 4

    def shape(*dims, dtype=jnp.bfloat16):
        return jax.ShapeDtypeStruct(dims, dtype)

    def hop(value, source, target):
        cycle = cycle_through(sections, source, target)
        route = [
            (stage * count + i, cycle[stage] * count + i)
            for stage in range(sections)
            for i in range(count)
        ]
        return lax.ppermute(value, ("pipe", "ctx"), route)

    def onward(value, step):
        return lax.ppermute(value, "ctx", [(i, (i + step) % count) for i in range(count)])

    def exchange(value, offset):
        return lax.ppermute(value, "ctx", [(i, i ^ offset) for i in range(count)])

    payload = jnp.where(section == last, cotangent, inputs)
    parts = kernel_call(
        functools.partial(split_kernel, last),
        [shape(rows // count, chans)] * count,
        10 * seq_count * layer_flops,
        "split",
    )(payload)
    weight, point = kernel_call(
        hold_kernel,
        [shape(*weight.shape), shape(*point.shape)],
        0,
        "hold",
        waits=[parts[0]],
        in_spec=anywhere,
        scratch=[pltpu.SemaphoreType.DMA((2,))],
    )(weight, point)
    parts = [parts[0], *(onward(parts[step], step) for step in range(1, count))]

    whole, out, pre = kernel_call(
        functools.partial(first_kernel, last, bins),
        [shape(rows, chans), shape(rows, chans), shape(rows, inner, dtype=jnp.float32)],
        seq_count * layer_flops,
        "first",
    )(*parts, weight, point)
    xs, pres, sent = [[whole]], [[pre]], ()
    xs.append([hop(out, 0, 1)])
    for level in range(1, last):
        outs = []
        pres.append([])
        for seq in seqs:
            out, pre = kernel_call(
                functools.partial(fore_kernel, level, seq, bins),
                [shape(bins, chans), shape(bins, inner, dtype=jnp.float32)],
                layer_flops,
                "fore",
                waits=outs[-1:] or sent,
            )(xs[level][min(seq, len(xs[level]) - 1)], weight, point)
            outs.append(out)
            pres[level].append(pre)
        sent = outs
        xs.append([hop(out, level, level + 1) for out in outs])

    dys, dpres = [], [[] for level in range(sections)]
    for seq in seqs:
        dy, dpre = kernel_call(
            functools.partial(turn_kernel, last, seq, bins, scale),
            [shape(bins, chans), shape(bins, inner)],
            2 * layer_flops,
            "turn",
            waits=dys[-1:] or sent,
        )(xs[last][min(seq, len(xs[last]) - 1)], whole, weight, point)
        dys.append(dy)
        dpres[last].append(dpre)

    kept = list(range(0, count, 2))
    size = chans // count
    *owned, message = kernel_call(
        functools.partial(columns_kernel, groups, [len(x) for x in xs], kept),
        [shape(size, rows)] * len(kept) + [shape(size * len(kept), rows)],
        2 * rows * chans * chans,
        "columns",
        waits=dys,
    )(*[x for level in range(sections) for x in xs[level]])
    blocks = {(offset, 0): (array, 0) for offset, array in zip(kept, owned)}
    moving = [(offset, 0) for offset in kept]
    dys = [hop(dy, last, last - 1) for dy in dys]
    message, bit = exchange(message, 1), 1
    blocks.update({(to, start ^ bit): (message, at) for at, (to, start) in enumerate(moving)})
    sent = [owned[0]]

    late = []
    for level in range(last - 1, 0, -1):
        outs = []
        for seq in seqs:
            waits = outs[-1:] or sent
            dy, dpre = kernel_call(
                functools.partial(back_kernel, level, seq, bins),
                [shape(bins, chans), shape(bins, inner)],
                layer_flops,
                "back",
                waits=waits,
            )(
                dys[seq],
                xs[level][min(seq, len(xs[level]) - 1)],
                pres[level][min(seq, len(pres[level]) - 1)],
                weight,
                point,
            )
            outs.append(dy)
            dpres[level].append(dpre)
        dys = [hop(dy, level, level - 1) for dy in outs]
        sent = outs
        if 2 * bit < count:
            bit *= 2
            moving = sorted(key for key in blocks if key[0] & bit)
            (message,) = kernel_call(
                functools.partial(message_kernel, [blocks[key][1] for key in moving]),
                [shape(size * len(moving), rows)],
                0,
                "message",
                waits=outs,
            )(*[blocks[key][0] for key in moving])
            message = exchange(message, bit)
            for at, (to, start) in enumerate(moving):
                del blocks[to, start]
                blocks[to ^ bit, start ^ bit] = (message, at)
            late = [message]

    columns = [blocks[0, offset] for offset in range(count)]
    shares = [shape(3, chans // (count * groups), inner, dtype=jnp.float32)] * groups
    sent_shares = [shares[0], *(shape(*share.shape) for share in shares[1:])]
    far_first = [*range(count // 2, count), *range(1, count // 2)]
    parts, grads = [], []
    for seq in seqs:
        (dpre,) = kernel_call(
            functools.partial(head_kernel, sections, seq, bins),
            [shape(bins, inner)],
            layer_flops // 4,
            "head",
            waits=sent if seq == 0 else late,
        )(dys[seq], pres[0][0], point, *[dpres[level][seq] for level in range(1, sections)])
        gathered = {offset: exchange(dpre, offset) for offset in far_first}
        grads.append([dpre, *(gathered[offset] for offset in range(1, count))])
    for seq in seqs:
        parts = kernel_call(
            functools.partial(grad_kernel, sections, seq, bins, [at for array, at in columns]),
            sent_shares if seq == seq_count - 1 else shares,
            2 * 3 * bins * chans * inner,
            "grad",
        )(*[array for array, at in columns], *grads[seq], *parts)
    mine, *others = parts
    for step, other in enumerate(others, 1):
        route = [(i, (i + step) % groups) for i in range(groups)]
        mine = mine + lax.ppermute(other, "dp", route).astype(jnp.float32)
    return mine[None]


def solution(mesh):
    def shards(inputs, cotangent, dilated_kernel_weight, point_weight):
        bins = inputs.shape[1]
        first_spread = bins // 2 // 2 ** (mesh.shape["pipe"] - 1)
        count = mesh.shape["ctx"]
        residues = (
            first_spread == count
            and mesh.shape["pipe"] > 1
            and bins % (16 * count) == 0
            and 1 < count == 1 << (count.bit_length() - 1) <= 1 << (mesh.shape["pipe"] - 1)
            and inputs.shape[2] % (count * mesh.shape["dp"]) == 0
        )
        plan = residue_shards if residues else edge_shards
        return plan(inputs, cotangent, dilated_kernel_weight, point_weight)

    return jax.shard_map(
        shards,
        mesh=mesh,
        in_specs=(
            P("dp", "ctx", None),
            P("dp", "ctx", None),
            P("pipe", None, None, None),
            P("pipe", None, None),
        ),
        out_specs=P("pipe", None, ("dp", "ctx"), None),
        check_vma=False,
    )
```

```python
import functools
import math

import jax
import jax.numpy as jnp
from jax import lax
from jax.experimental import pallas as pl
from jax.experimental.pallas import tpu as pltpu
from jax.sharding import PartitionSpec as P

root_half = 0.7071067811865476
inv_root_two_pi = 0.3989422804014327

in_vmem = pl.BlockSpec(memory_space=pltpu.VMEM)
anywhere = pl.BlockSpec(memory_space=pl.ANY)
contract_last = (((1,), (1,)), ((), ()))
contract_first = (((0,), (0,)), ((), ()))


def gelu(value):
    return 0.5 * value * (1.0 + lax.erf(value * root_half))


def gelu_slope(value):
    return (
        0.5 * (1.0 + lax.erf(value * root_half))
        + value * jnp.exp(-0.5 * value * value) * inv_root_two_pi
    )


def padded(cells, sides, width):
    for axis, dim in sides:
        count = lax.axis_size(axis)
        ends = count - 1
        head = lax.slice_in_dim(cells, 0, width, axis=dim)
        tail = lax.slice_in_dim(cells, cells.shape[dim] - width, cells.shape[dim], axis=dim)
        cells = jnp.concatenate(
            [
                lax.ppermute(tail, axis, [(i, (i + 1) % count) for i in range(ends)]),
                cells,
                lax.ppermute(head, axis, [((i + 1) % count, i) for i in range(ends)]),
            ],
            axis=dim,
        )
    return cells


def shifted(block, axis, distance):
    devices = range(lax.axis_size(axis))
    route = [(i - distance, i) for i in devices if i - distance in devices]
    return lax.ppermute(block, axis, route)


def edge_shards(inputs, cotangent, dilated_kernel_weight, point_weight):
    sections = lax.axis_size("pipe")
    section = lax.axis_index("pipe")
    seq_count, bins, chans = inputs.shape
    reach = bins // 2
    table = jnp.array(
        [reach // 2 ** (sections - 1 - level) for level in range(sections)], jnp.int32
    )
    spread = table[section]
    dilation_weight = dilated_kernel_weight[0]
    w_point = point_weight[0]
    inner_channel_count = dilation_weight.shape[2]
    scale = 1.0 / math.sqrt(seq_count * lax.axis_size("dp") * bins * lax.axis_size("ctx"))
    ticks = jnp.arange(seq_count + sections - 1, dtype=jnp.int32)

    def conv_fore(extended):
        running_total = jnp.zeros((bins, inner_channel_count), jnp.float32)
        for kernel_offset in range(3):
            receptive_span = lax.dynamic_slice_in_dim(
                extended, reach + (kernel_offset - 1) * spread, bins, 0
            )
            running_total = running_total + jnp.dot(
                receptive_span, dilation_weight[kernel_offset], preferred_element_type=jnp.float32
            )
        return running_total

    def put(store, slot, valid, item):
        current = lax.dynamic_index_in_dim(store, slot, 0, keepdims=False)
        return lax.dynamic_update_index_in_dim(store, jnp.where(valid, item, current), slot, 0)

    kept_x = jnp.zeros(inputs.shape, jnp.bfloat16)
    kept_ext = jnp.zeros((seq_count, bins + 2 * reach, chans), jnp.bfloat16)
    kept_pre = jnp.zeros((seq_count, bins, inner_channel_count), jnp.float32)

    def fore_tick(carry, tick):
        received, store_x, store_ext, store_pre = carry
        micro = tick - section
        valid = (micro >= 0) & (micro < seq_count)
        slot = jnp.clip(micro, 0, seq_count - 1)
        first = lax.dynamic_index_in_dim(inputs, slot, 0, keepdims=False)
        trunk_in = jnp.where(section == 0, first, received)
        act = gelu(trunk_in.astype(jnp.float32)).astype(jnp.bfloat16)
        extended = padded(act, (("ctx", 0),), reach)
        pre = conv_fore(extended)
        inner = gelu(pre).astype(jnp.bfloat16)
        out = (
            trunk_in.astype(jnp.float32)
            + jnp.dot(inner, w_point, preferred_element_type=jnp.float32)
        ).astype(jnp.bfloat16)
        sent = shifted(out, "pipe", 1)
        store_x = put(store_x, slot, valid, trunk_in)
        store_ext = put(store_ext, slot, valid, extended)
        store_pre = put(store_pre, slot, valid, pre)
        return ((sent, store_x, store_ext, store_pre), None)

    start_recv = jnp.zeros((bins, chans), jnp.bfloat16)
    (unused, kept_x, kept_ext, kept_pre), unused_out = lax.scan(
        fore_tick, (start_recv, kept_x, kept_ext, kept_pre), ticks
    )

    def back_tick(carry, tick):
        received, grad = carry
        micro = tick - (sections - 1 - section)
        valid = (micro >= 0) & (micro < seq_count)
        slot = jnp.clip(micro, 0, seq_count - 1)
        last = (
            lax.dynamic_index_in_dim(cotangent, slot, 0, keepdims=False).astype(jnp.float32) * scale
        ).astype(jnp.bfloat16)
        upstream = jnp.where(section == sections - 1, last, received)
        trunk_in = lax.dynamic_index_in_dim(kept_x, slot, 0, keepdims=False)
        extended = lax.dynamic_index_in_dim(kept_ext, slot, 0, keepdims=False)
        pre = lax.dynamic_index_in_dim(kept_pre, slot, 0, keepdims=False)
        inner_grad = lax.dot_general(
            upstream, w_point, contract_last, preferred_element_type=jnp.float32
        )
        dpre = (inner_grad * gelu_slope(pre) * valid.astype(jnp.float32)).astype(jnp.bfloat16)
        dpre_ext = padded(dpre, (("ctx", 0),), reach)
        dact = jnp.zeros((bins, chans), jnp.float32)
        taps = []
        for kernel_offset in range(3):
            receptive_span = lax.dynamic_slice_in_dim(
                dpre_ext, reach - (kernel_offset - 1) * spread, bins, 0
            )
            dact = dact + lax.dot_general(
                receptive_span,
                dilation_weight[kernel_offset],
                contract_last,
                preferred_element_type=jnp.float32,
            )
            source = lax.dynamic_slice_in_dim(
                extended, reach + (kernel_offset - 1) * spread, bins, 0
            )
            taps.append(
                lax.dot_general(source, dpre, contract_first, preferred_element_type=jnp.float32)
            )
        grad = grad + jnp.stack(taps)
        back = (
            upstream.astype(jnp.float32) + dact * gelu_slope(trunk_in.astype(jnp.float32))
        ).astype(jnp.bfloat16)
        sent = shifted(back, "pipe", -1)
        return ((sent, grad), None)

    start_grad = jnp.zeros((3, chans, inner_channel_count), jnp.float32)
    (unused_back, grad), unused_seq = lax.scan(back_tick, (start_recv, start_grad), ticks)
    term = grad[None]
    return lax.psum_scatter(term, ("dp", "ctx"), scatter_dimension=2, tiled=True)


def moved(value, by, bins):
    pieces = []
    for start in range(0, value.shape[0], bins):
        piece = value[start : start + bins]
        place = lax.broadcasted_iota(jnp.int32, piece.shape, 0)
        if by > 0:
            keep = place >= by
        else:
            keep = place < bins + by
        pieces.append(jnp.where(keep, pltpu.roll(piece, by % bins, 0), 0.0))
    return jnp.concatenate(pieces, axis=0)


def fore(x, weight_ref, spread, bins):
    act = gelu(x.astype(jnp.float32)).astype(jnp.bfloat16)
    terms = [
        jnp.dot(act, weight_ref[0, tap], preferred_element_type=jnp.float32) for tap in range(3)
    ]
    return terms[1] + moved(terms[0], spread, bins) + moved(terms[2], -spread, bins)


def back_pre(dy, pre, point_ref):
    inner_grad = lax.dot_general(
        dy, point_ref[0], contract_last, preferred_element_type=jnp.float32
    )
    return (inner_grad * gelu_slope(pre)).astype(jnp.bfloat16)


def back_trunk(dy, dpre, x, weight_ref, spread, bins):
    wide = dpre.astype(jnp.float32)
    spans = (
        moved(wide, -spread, bins).astype(jnp.bfloat16),
        dpre,
        moved(wide, spread, bins).astype(jnp.bfloat16),
    )
    dact = jnp.zeros(dy.shape, jnp.float32)
    for tap in range(3):
        dact = dact + lax.dot_general(
            spans[tap], weight_ref[0, tap], contract_last, preferred_element_type=jnp.float32
        )
    return (
        dy.astype(jnp.float32) + dact * gelu_slope(x.astype(jnp.float32))
    ).astype(jnp.bfloat16)


def split_kernel(last, payload_ref, *out_refs):
    count = len(out_refs)
    seq_count, bins, chans = payload_ref.shape
    part = bins // count
    section = lax.axis_index("pipe")
    place = lax.axis_index("ctx")

    @pl.when((section == 0) | (section == last))
    def send():
        source = payload_ref[...].reshape(seq_count * bins, chans)
        row = lax.broadcasted_iota(jnp.int32, (part, seq_count * bins), 0)
        col = lax.broadcasted_iota(jnp.int32, (part, seq_count * bins), 1)
        for hop in range(count):
            residue = lax.rem(place + hop, count)
            rows = [
                (col == seq * bins + count * row + residue).astype(jnp.float32)
                for seq in range(seq_count)
            ]
            pick = jnp.concatenate(rows, axis=0).astype(jnp.bfloat16)
            out_refs[hop][...] = jnp.dot(
                pick, source, preferred_element_type=jnp.float32
            ).astype(jnp.bfloat16)


def hold_kernel(weight_ref, point_ref, weight_out, point_out, sems):
    loads = [
        pltpu.make_async_copy(weight_ref, weight_out, sems.at[0]),
        pltpu.make_async_copy(point_ref, point_out, sems.at[1]),
    ]
    for load in loads:
        load.start()
    for load in loads:
        load.wait()


def first_kernel(last, bins, *refs):
    parts, (weight_ref, point_ref, whole_ref, out_ref, pre_ref) = refs[:-5], refs[-5:]
    count = len(parts)
    section = lax.axis_index("pipe")
    place = lax.axis_index("ctx")
    part = bins // count
    seq_count = whole_ref.shape[0] // bins

    @pl.when((section == 0) | (section == last))
    def gather():
        for hop in range(count):
            source = lax.rem(place - hop + count, count)
            for seq in range(seq_count):
                at = pl.multiple_of(seq * bins + source * part, part)
                whole_ref[pl.ds(at, part), :] = parts[hop][seq * part : (seq + 1) * part, :]

    @pl.when(section == 0)
    def layer():
        x = whole_ref[...]
        finish(x, fore(x, weight_ref, 1, bins), point_ref, out_ref, pre_ref)


def finish(x, pre, point_ref, out_ref, pre_ref):
    pre_ref[...] = pre
    branch = jnp.dot(
        gelu(pre).astype(jnp.bfloat16), point_ref[0], preferred_element_type=jnp.float32
    )
    out_ref[...] = (x.astype(jnp.float32) + branch).astype(jnp.bfloat16)


def fore_kernel(level, bins, x_ref, weight_ref, point_ref, out_ref, pre_ref):
    @pl.when(lax.axis_index("pipe") == level)
    def layer():
        x = x_ref[...]
        finish(x, fore(x, weight_ref, 2**level, bins), point_ref, out_ref, pre_ref)


def turn_kernel(level, bins, scale, x_ref, cot_ref, weight_ref, point_ref, dy_ref, dpre_ref):
    @pl.when(lax.axis_index("pipe") == level)
    def layer():
        x = x_ref[...]
        pre = fore(x, weight_ref, 2**level, bins)
        dy = (cot_ref[...].astype(jnp.float32) * scale).astype(jnp.bfloat16)
        dpre = back_pre(dy, pre, point_ref)
        dpre_ref[...] = dpre
        dy_ref[...] = back_trunk(dy, dpre, x, weight_ref, 2**level, bins)


def back_kernel(level, bins, dy_in_ref, x_ref, pre_ref, weight_ref, point_ref, dy_ref, dpre_ref):
    @pl.when(lax.axis_index("pipe") == level)
    def layer():
        dy = dy_in_ref[...]
        dpre = back_pre(dy, pre_ref[...], point_ref)
        dpre_ref[...] = dpre
        dy_ref[...] = back_trunk(dy, dpre, x_ref[...], weight_ref, 2**level, bins)


def message_kernel(places, *refs):
    blocks, message_ref = refs[:-1], refs[-1]
    size = message_ref.shape[0] // len(places)
    for to, (ref, at) in enumerate(zip(blocks, places)):
        message_ref[to * size : (to + 1) * size, :] = ref[at * size : (at + 1) * size, :]


def head_kernel(sections, dy_in_ref, pre_ref, point_ref, *refs):
    others, out_ref = refs[:-1], refs[-1]
    section = lax.axis_index("pipe")

    @pl.when(section == 0)
    def layer():
        out_ref[...] = back_pre(dy_in_ref[...], pre_ref[...], point_ref)

    for level in range(1, sections):

        @pl.when(section == level)
        def keep(level=level):
            out_ref[...] = others[level - 1][...]


def columns_kernel(groups, sections, kept, *refs):
    xs, kept_refs, sent_ref = refs[:sections], refs[sections:-1], refs[-1]
    count = 2 * len(kept)
    section = lax.axis_index("pipe")
    core = lax.axis_index("dp")
    place = lax.axis_index("ctx")
    x = xs[0][...].astype(jnp.float32)
    for level in range(1, sections):
        x = jnp.where(section == level, xs[level][...].astype(jnp.float32), x)
    act = gelu(x).astype(jnp.bfloat16)
    chans = act.shape[1]
    width = chans // (groups * count)
    row = lax.broadcasted_iota(jnp.int32, (width, chans), 0)
    col = lax.broadcasted_iota(jnp.int32, (width, chans), 1)

    def block(offset):
        owner = lax.bitwise_xor(place, offset)
        rows = []
        for step in range(groups):
            first = (lax.rem(core + step, groups) * count + owner) * width
            rows.append((col == first + row).astype(jnp.float32))
        pick = jnp.concatenate(rows, axis=0).astype(jnp.bfloat16)
        return lax.dot_general(
            pick, act, contract_last, preferred_element_type=jnp.float32
        ).astype(jnp.bfloat16)

    size = groups * width
    for at, offset in enumerate(kept):
        kept_refs[at][...] = block(offset)
        sent_ref[at * size : (at + 1) * size, :] = block(offset ^ 1)


def grad_kernel(sections, bins, places, *refs):
    columns, refs = refs[: len(places)], refs[len(places) :]
    grads, outs = refs[: len(places)], refs[len(places) :]
    section = lax.axis_index("pipe")
    width = outs[0].shape[1]
    size = len(outs) * width

    def taps(spread):
        act = jnp.concatenate(
            [ref[at * size : (at + 1) * size, :] for ref, at in zip(columns, places)], axis=1
        )
        dpre = jnp.concatenate([ref[...] for ref in grads], axis=0)
        wide = dpre.astype(jnp.float32)
        spans = (
            moved(wide, -spread, bins).astype(jnp.bfloat16),
            dpre,
            moved(wide, spread, bins).astype(jnp.bfloat16),
        )
        for tap in range(3):
            grad = jnp.dot(act, spans[tap], preferred_element_type=jnp.float32)
            for step, out_ref in enumerate(outs):
                out_ref[tap] = grad[step * width : (step + 1) * width].astype(out_ref.dtype)

    for level in range(sections):

        @pl.when(section == level)
        def run(level=level):
            taps(2**level)


def kernel_call(body, outs, flops, name, waits=(), carries=(), in_spec=in_vmem, scratch=()):
    def call(*args):
        used, taken = len(args), len(args) + len(waits) + len(carries)

        def run(*refs):
            made = refs[taken : taken + len(outs)]
            body(*refs[:used], *made, *refs[taken + len(outs) + len(carries) :])

        moved_bytes = sum(math.prod(a.shape) * a.dtype.itemsize for a in (*args, *outs))
        return pl.pallas_call(
            run,
            out_shape=[*outs, *(jax.ShapeDtypeStruct(a.shape, a.dtype) for a in carries)],
            in_specs=[in_spec] * used + [anywhere] * (taken - used),
            out_specs=[in_vmem] * len(outs) + [anywhere] * len(carries),
            input_output_aliases={
                used + len(waits) + at: len(outs) + at for at in range(len(carries))
            },
            scratch_shapes=list(scratch),
            compiler_params=pltpu.CompilerParams(vmem_limit_bytes=24 * 2**20),
            cost_estimate=pl.CostEstimate(
                flops=flops, bytes_accessed=moved_bytes, transcendentals=0
            ),
            name=name,
        )(*args, *waits, *carries)

    return call


def cycle_through(sections, source, target):
    order = [0, 1, 3, 2] if sections == 4 else list(range(sections))
    step = (order.index(target) - order.index(source)) % sections
    if step not in (1, sections - 1):
        order, step = list(range(sections)), (target - source) % sections
    return {order[at]: order[(at + step) % sections] for at in range(sections)}


def residue_shards(inputs, cotangent, weight, point):
    sections = lax.axis_size("pipe")
    section = lax.axis_index("pipe")
    count = lax.axis_size("ctx")
    groups = lax.axis_size("dp")
    seq_count, bins, chans = inputs.shape
    inner = weight.shape[3]
    rows = seq_count * bins
    scale = 1.0 / math.sqrt(seq_count * groups * bins * count)
    last = sections - 1
    layer_flops = 2 * rows * chans * inner * 4

    def shape(*dims, dtype=jnp.bfloat16):
        return jax.ShapeDtypeStruct(dims, dtype)

    def hop(value, source, target):
        cycle = cycle_through(sections, source, target)
        route = [
            (stage * count + i, cycle[stage] * count + i)
            for stage in range(sections)
            for i in range(count)
        ]
        return lax.ppermute(value, ("pipe", "ctx"), route)

    def onward(value, step):
        return lax.ppermute(value, "ctx", [(i, (i + step) % count) for i in range(count)])

    def exchange(value, offset):
        return lax.ppermute(value, "ctx", [(i, i ^ offset) for i in range(count)])

    payload = jnp.where(section == last, cotangent, inputs)
    parts = kernel_call(
        functools.partial(split_kernel, last),
        [shape(rows // count, chans)] * count,
        10 * layer_flops,
        "split",
    )(payload)
    weight, point = kernel_call(
        hold_kernel,
        [shape(*weight.shape), shape(*point.shape)],
        0,
        "hold",
        waits=[parts[0]],
        in_spec=anywhere,
        scratch=[pltpu.SemaphoreType.DMA((2,))],
    )(weight, point)
    parts = [parts[0], *(onward(parts[step], step) for step in range(1, count))]

    trunk, inside = shape(rows, chans), shape(rows, inner)
    inside_wide = shape(rows, inner, dtype=jnp.float32)
    whole, out, pre = kernel_call(
        functools.partial(first_kernel, last, bins),
        [trunk, trunk, inside_wide],
        layer_flops,
        "first",
    )(*parts, weight, point)
    xs, pres = [whole], [pre]
    for level in range(1, last):
        xs.append(hop(out, level - 1, level))
        out, pre = kernel_call(
            functools.partial(fore_kernel, level, bins),
            [trunk, inside_wide],
            layer_flops,
            "fore",
        )(xs[level], weight, point)
        pres.append(pre)
    xs.append(hop(out, last - 1, last))
    dy, dpre = kernel_call(
        functools.partial(turn_kernel, last, bins, scale),
        [trunk, inside],
        2 * layer_flops,
        "turn",
    )(xs[last], whole, weight, point)
    dpres = [dpre]

    kept = list(range(0, count, 2))
    size = chans // count
    *owned, message = kernel_call(
        functools.partial(columns_kernel, groups, sections, kept),
        [shape(size, rows)] * len(kept) + [shape(size * len(kept), rows)],
        2 * rows * chans * chans,
        "columns",
        waits=[dy],
    )(*xs)
    blocks = {(offset, 0): (array, 0) for offset, array in zip(kept, owned)}
    moving = [(offset, 0) for offset in kept]
    dy = hop(dy, last, last - 1)
    message, bit = exchange(message, 1), 1
    blocks.update({(to, start ^ bit): (message, at) for at, (to, start) in enumerate(moving)})
    late = [owned[0]]

    for level in range(last - 1, 0, -1):
        bit *= 2
        moving = sorted(key for key in blocks if key[0] & bit)
        if moving:
            (message,) = kernel_call(
                functools.partial(message_kernel, [blocks[key][1] for key in moving]),
                [shape(size * len(moving), rows)],
                0,
                "message",
            )(*[blocks[key][0] for key in moving])
            late = [message]
        out, dpre = kernel_call(
            functools.partial(back_kernel, level, bins),
            [trunk, inside],
            layer_flops,
            "back",
            waits=late,
        )(dy, xs[level], pres[level], weight, point)
        dpres.insert(0, dpre)
        dy, late = hop(out, level, level - 1), []
        if moving:
            message = exchange(message, bit)
            for at, (to, start) in enumerate(moving):
                del blocks[to, start]
                blocks[to ^ bit, start ^ bit] = (message, at)

    columns = [blocks[0, offset] for offset in range(count)]
    (dpre,) = kernel_call(
        functools.partial(head_kernel, sections), [inside], layer_flops // 4, "head", waits=late
    )(dy, pres[0], point, *dpres)
    gathered = {offset: exchange(dpre, offset) for offset in range(1, count)}
    share = shape(3, chans // (count * groups), inner, dtype=jnp.float32)
    mine, *others = kernel_call(
        functools.partial(grad_kernel, sections, bins, [at for array, at in columns]),
        [share, *[shape(*share.shape)] * (groups - 1)],
        2 * 3 * rows * chans * inner,
        "grad",
    )(*[array for array, at in columns], dpre, *[gathered[offset] for offset in range(1, count)])
    for step, other in enumerate(others, 1):
        route = [(i, (i + step) % groups) for i in range(groups)]
        mine = mine + lax.ppermute(other, "dp", route).astype(jnp.float32)
    return mine[None]


def solution(mesh):
    def shards(inputs, cotangent, dilated_kernel_weight, point_weight):
        bins = inputs.shape[1]
        first_spread = bins // 2 // 2 ** (mesh.shape["pipe"] - 1)
        count = mesh.shape["ctx"]
        residues = (
            first_spread == count
            and mesh.shape["pipe"] > 1
            and bins % (16 * count) == 0
            and 1 < count == 1 << (count.bit_length() - 1) <= 1 << (mesh.shape["pipe"] - 1)
            and inputs.shape[2] % (count * mesh.shape["dp"]) == 0
        )
        plan = residue_shards if residues else edge_shards
        return plan(inputs, cotangent, dilated_kernel_weight, point_weight)

    return jax.shard_map(
        shards,
        mesh=mesh,
        in_specs=(
            P("dp", "ctx", None),
            P("dp", "ctx", None),
            P("pipe", None, None, None),
            P("pipe", None, None),
        ),
        out_specs=P("pipe", None, ("dp", "ctx"), None),
        check_vma=False,
    )
```

```python
import functools
import math

import jax
import jax.numpy as jnp
from jax import lax
from jax.experimental import pallas as pl
from jax.experimental.pallas import tpu as pltpu
from jax.sharding import PartitionSpec as P

root_half = 0.7071067811865476
inv_root_two_pi = 0.3989422804014327

in_vmem = pl.BlockSpec(memory_space=pltpu.VMEM)
anywhere = pl.BlockSpec(memory_space=pl.ANY)
contract_last = (((1,), (1,)), ((), ()))
contract_first = (((0,), (0,)), ((), ()))


def gelu(value):
    return 0.5 * value * (1.0 + lax.erf(value * root_half))


def gelu_slope(value):
    return (
        0.5 * (1.0 + lax.erf(value * root_half))
        + value * jnp.exp(-0.5 * value * value) * inv_root_two_pi
    )


def padded(cells, sides, width):
    for axis, dim in sides:
        count = lax.axis_size(axis)
        ends = count - 1
        head = lax.slice_in_dim(cells, 0, width, axis=dim)
        tail = lax.slice_in_dim(cells, cells.shape[dim] - width, cells.shape[dim], axis=dim)
        cells = jnp.concatenate(
            [
                lax.ppermute(tail, axis, [(i, (i + 1) % count) for i in range(ends)]),
                cells,
                lax.ppermute(head, axis, [((i + 1) % count, i) for i in range(ends)]),
            ],
            axis=dim,
        )
    return cells


def shifted(block, axis, distance):
    devices = range(lax.axis_size(axis))
    route = [(i - distance, i) for i in devices if i - distance in devices]
    return lax.ppermute(block, axis, route)


def edge_shards(inputs, cotangent, dilated_kernel_weight, point_weight):
    sections = lax.axis_size("pipe")
    section = lax.axis_index("pipe")
    seq_count, bins, chans = inputs.shape
    reach = bins // 2
    table = jnp.array(
        [reach // 2 ** (sections - 1 - level) for level in range(sections)], jnp.int32
    )
    spread = table[section]
    dilation_weight = dilated_kernel_weight[0]
    w_point = point_weight[0]
    inner_channel_count = dilation_weight.shape[2]
    scale = 1.0 / math.sqrt(seq_count * lax.axis_size("dp") * bins * lax.axis_size("ctx"))
    ticks = jnp.arange(seq_count + sections - 1, dtype=jnp.int32)

    def conv_fore(extended):
        running_total = jnp.zeros((bins, inner_channel_count), jnp.float32)
        for kernel_offset in range(3):
            receptive_span = lax.dynamic_slice_in_dim(
                extended, reach + (kernel_offset - 1) * spread, bins, 0
            )
            running_total = running_total + jnp.dot(
                receptive_span, dilation_weight[kernel_offset], preferred_element_type=jnp.float32
            )
        return running_total

    def put(store, slot, valid, item):
        current = lax.dynamic_index_in_dim(store, slot, 0, keepdims=False)
        return lax.dynamic_update_index_in_dim(store, jnp.where(valid, item, current), slot, 0)

    kept_x = jnp.zeros(inputs.shape, jnp.bfloat16)
    kept_ext = jnp.zeros((seq_count, bins + 2 * reach, chans), jnp.bfloat16)
    kept_pre = jnp.zeros((seq_count, bins, inner_channel_count), jnp.float32)

    def fore_tick(carry, tick):
        received, store_x, store_ext, store_pre = carry
        micro = tick - section
        valid = (micro >= 0) & (micro < seq_count)
        slot = jnp.clip(micro, 0, seq_count - 1)
        first = lax.dynamic_index_in_dim(inputs, slot, 0, keepdims=False)
        trunk_in = jnp.where(section == 0, first, received)
        act = gelu(trunk_in.astype(jnp.float32)).astype(jnp.bfloat16)
        extended = padded(act, (("ctx", 0),), reach)
        pre = conv_fore(extended)
        inner = gelu(pre).astype(jnp.bfloat16)
        out = (
            trunk_in.astype(jnp.float32)
            + jnp.dot(inner, w_point, preferred_element_type=jnp.float32)
        ).astype(jnp.bfloat16)
        sent = shifted(out, "pipe", 1)
        store_x = put(store_x, slot, valid, trunk_in)
        store_ext = put(store_ext, slot, valid, extended)
        store_pre = put(store_pre, slot, valid, pre)
        return ((sent, store_x, store_ext, store_pre), None)

    start_recv = jnp.zeros((bins, chans), jnp.bfloat16)
    (unused, kept_x, kept_ext, kept_pre), unused_out = lax.scan(
        fore_tick, (start_recv, kept_x, kept_ext, kept_pre), ticks
    )

    def back_tick(carry, tick):
        received, grad = carry
        micro = tick - (sections - 1 - section)
        valid = (micro >= 0) & (micro < seq_count)
        slot = jnp.clip(micro, 0, seq_count - 1)
        last = (
            lax.dynamic_index_in_dim(cotangent, slot, 0, keepdims=False).astype(jnp.float32) * scale
        ).astype(jnp.bfloat16)
        upstream = jnp.where(section == sections - 1, last, received)
        trunk_in = lax.dynamic_index_in_dim(kept_x, slot, 0, keepdims=False)
        extended = lax.dynamic_index_in_dim(kept_ext, slot, 0, keepdims=False)
        pre = lax.dynamic_index_in_dim(kept_pre, slot, 0, keepdims=False)
        inner_grad = lax.dot_general(
            upstream, w_point, contract_last, preferred_element_type=jnp.float32
        )
        dpre = (inner_grad * gelu_slope(pre) * valid.astype(jnp.float32)).astype(jnp.bfloat16)
        dpre_ext = padded(dpre, (("ctx", 0),), reach)
        dact = jnp.zeros((bins, chans), jnp.float32)
        taps = []
        for kernel_offset in range(3):
            receptive_span = lax.dynamic_slice_in_dim(
                dpre_ext, reach - (kernel_offset - 1) * spread, bins, 0
            )
            dact = dact + lax.dot_general(
                receptive_span,
                dilation_weight[kernel_offset],
                contract_last,
                preferred_element_type=jnp.float32,
            )
            source = lax.dynamic_slice_in_dim(
                extended, reach + (kernel_offset - 1) * spread, bins, 0
            )
            taps.append(
                lax.dot_general(source, dpre, contract_first, preferred_element_type=jnp.float32)
            )
        grad = grad + jnp.stack(taps)
        back = (
            upstream.astype(jnp.float32) + dact * gelu_slope(trunk_in.astype(jnp.float32))
        ).astype(jnp.bfloat16)
        sent = shifted(back, "pipe", -1)
        return ((sent, grad), None)

    start_grad = jnp.zeros((3, chans, inner_channel_count), jnp.float32)
    (unused_back, grad), unused_seq = lax.scan(back_tick, (start_recv, start_grad), ticks)
    term = grad[None]
    return lax.psum_scatter(term, ("dp", "ctx"), scatter_dimension=2, tiled=True)


def moved(value, by, bins):
    pieces = []
    for start in range(0, value.shape[0], bins):
        piece = value[start : start + bins]
        place = lax.broadcasted_iota(jnp.int32, piece.shape, 0)
        if by > 0:
            keep = place >= by
        else:
            keep = place < bins + by
        pieces.append(jnp.where(keep, pltpu.roll(piece, by % bins, 0), 0.0))
    return jnp.concatenate(pieces, axis=0)


def fore(x, weight_ref, spread, bins):
    act = gelu(x.astype(jnp.float32)).astype(jnp.bfloat16)
    terms = [
        jnp.dot(act, weight_ref[0, tap], preferred_element_type=jnp.float32) for tap in range(3)
    ]
    return terms[1] + moved(terms[0], spread, bins) + moved(terms[2], -spread, bins)


def back_pre(dy, pre, point_ref):
    inner_grad = lax.dot_general(
        dy, point_ref[0], contract_last, preferred_element_type=jnp.float32
    )
    return (inner_grad * gelu_slope(pre)).astype(jnp.bfloat16)


def back_trunk(dy, dpre, x, weight_ref, spread, bins):
    wide = dpre.astype(jnp.float32)
    spans = (
        moved(wide, -spread, bins).astype(jnp.bfloat16),
        dpre,
        moved(wide, spread, bins).astype(jnp.bfloat16),
    )
    dact = jnp.zeros(dy.shape, jnp.float32)
    for tap in range(3):
        dact = dact + lax.dot_general(
            spans[tap], weight_ref[0, tap], contract_last, preferred_element_type=jnp.float32
        )
    return (
        dy.astype(jnp.float32) + dact * gelu_slope(x.astype(jnp.float32))
    ).astype(jnp.bfloat16)


def split_kernel(last, payload_ref, *out_refs):
    count = len(out_refs)
    seq_count, bins, chans = payload_ref.shape
    part = bins // count
    section = lax.axis_index("pipe")
    place = lax.axis_index("ctx")

    @pl.when((section == 0) | (section == last))
    def send():
        source = payload_ref[...].reshape(seq_count * bins, chans)
        row = lax.broadcasted_iota(jnp.int32, (part, seq_count * bins), 0)
        col = lax.broadcasted_iota(jnp.int32, (part, seq_count * bins), 1)
        for hop in range(count):
            residue = lax.rem(place + hop, count)
            rows = [
                (col == seq * bins + count * row + residue).astype(jnp.float32)
                for seq in range(seq_count)
            ]
            pick = jnp.concatenate(rows, axis=0).astype(jnp.bfloat16)
            out_refs[hop][...] = jnp.dot(
                pick, source, preferred_element_type=jnp.float32
            ).astype(jnp.bfloat16)


def hold_kernel(weight_ref, point_ref, weight_out, point_out, sems):
    loads = [
        pltpu.make_async_copy(weight_ref, weight_out, sems.at[0]),
        pltpu.make_async_copy(point_ref, point_out, sems.at[1]),
    ]
    for load in loads:
        load.start()
    for load in loads:
        load.wait()


def first_kernel(last, bins, *refs):
    parts, (weight_ref, point_ref, whole_ref, out_ref, pre_ref) = refs[:-5], refs[-5:]
    count = len(parts)
    section = lax.axis_index("pipe")
    place = lax.axis_index("ctx")
    part = bins // count
    seq_count = whole_ref.shape[0] // bins

    @pl.when((section == 0) | (section == last))
    def gather():
        for hop in range(count):
            source = lax.rem(place - hop + count, count)
            for seq in range(seq_count):
                at = pl.multiple_of(seq * bins + source * part, part)
                whole_ref[pl.ds(at, part), :] = parts[hop][seq * part : (seq + 1) * part, :]

    @pl.when(section == 0)
    def layer():
        x = whole_ref[...]
        finish(x, fore(x, weight_ref, 1, bins), point_ref, out_ref, pre_ref)


def finish(x, pre, point_ref, out_ref, pre_ref):
    pre_ref[...] = pre
    branch = jnp.dot(
        gelu(pre).astype(jnp.bfloat16), point_ref[0], preferred_element_type=jnp.float32
    )
    out_ref[...] = (x.astype(jnp.float32) + branch).astype(jnp.bfloat16)


def fore_kernel(level, bins, x_ref, weight_ref, point_ref, out_ref, pre_ref):
    @pl.when(lax.axis_index("pipe") == level)
    def layer():
        x = x_ref[...]
        finish(x, fore(x, weight_ref, 2**level, bins), point_ref, out_ref, pre_ref)


def turn_kernel(level, bins, scale, x_ref, cot_ref, weight_ref, point_ref, dy_ref, dpre_ref):
    @pl.when(lax.axis_index("pipe") == level)
    def layer():
        x = x_ref[...]
        pre = fore(x, weight_ref, 2**level, bins)
        dy = (cot_ref[...].astype(jnp.float32) * scale).astype(jnp.bfloat16)
        dpre = back_pre(dy, pre, point_ref)
        dpre_ref[...] = dpre
        dy_ref[...] = back_trunk(dy, dpre, x, weight_ref, 2**level, bins)


def back_kernel(level, bins, dy_in_ref, x_ref, pre_ref, weight_ref, point_ref, dy_ref, dpre_ref):
    @pl.when(lax.axis_index("pipe") == level)
    def layer():
        dy = dy_in_ref[...]
        dpre = back_pre(dy, pre_ref[...], point_ref)
        dpre_ref[...] = dpre
        dy_ref[...] = back_trunk(dy, dpre, x_ref[...], weight_ref, 2**level, bins)


def message_kernel(places, *refs):
    blocks, message_ref = refs[:-1], refs[-1]
    size = message_ref.shape[0] // len(places)
    for to, (ref, at) in enumerate(zip(blocks, places)):
        message_ref[to * size : (to + 1) * size, :] = ref[at * size : (at + 1) * size, :]


def head_kernel(sections, dy_in_ref, pre_ref, point_ref, *refs):
    others, out_ref = refs[:-1], refs[-1]
    section = lax.axis_index("pipe")

    @pl.when(section == 0)
    def layer():
        out_ref[...] = back_pre(dy_in_ref[...], pre_ref[...], point_ref)

    for level in range(1, sections):

        @pl.when(section == level)
        def keep(level=level):
            out_ref[...] = others[level - 1][...]


def columns_kernel(groups, sections, kept, *refs):
    xs, kept_refs, sent_ref = refs[:sections], refs[sections:-1], refs[-1]
    count = 2 * len(kept)
    section = lax.axis_index("pipe")
    core = lax.axis_index("dp")
    place = lax.axis_index("ctx")
    x = xs[0][...].astype(jnp.float32)
    for level in range(1, sections):
        x = jnp.where(section == level, xs[level][...].astype(jnp.float32), x)
    act = gelu(x).astype(jnp.bfloat16)
    chans = act.shape[1]
    width = chans // (groups * count)
    row = lax.broadcasted_iota(jnp.int32, (width, chans), 0)
    col = lax.broadcasted_iota(jnp.int32, (width, chans), 1)

    def block(offset):
        owner = lax.bitwise_xor(place, offset)
        rows = []
        for step in range(groups):
            first = (lax.rem(core + step, groups) * count + owner) * width
            rows.append((col == first + row).astype(jnp.float32))
        pick = jnp.concatenate(rows, axis=0).astype(jnp.bfloat16)
        return lax.dot_general(
            pick, act, contract_last, preferred_element_type=jnp.float32
        ).astype(jnp.bfloat16)

    size = groups * width
    for at, offset in enumerate(kept):
        kept_refs[at][...] = block(offset)
        sent_ref[at * size : (at + 1) * size, :] = block(offset ^ 1)


def grad_kernel(sections, bins, places, *refs):
    columns, refs = refs[: len(places)], refs[len(places) :]
    grads, outs = refs[: len(places)], refs[len(places) :]
    section = lax.axis_index("pipe")
    width = outs[0].shape[1]
    size = len(outs) * width

    def taps(spread):
        act = jnp.concatenate(
            [ref[at * size : (at + 1) * size, :] for ref, at in zip(columns, places)], axis=1
        )
        dpre = jnp.concatenate([ref[...] for ref in grads], axis=0)
        wide = dpre.astype(jnp.float32)
        spans = (
            moved(wide, -spread, bins).astype(jnp.bfloat16),
            dpre,
            moved(wide, spread, bins).astype(jnp.bfloat16),
        )
        for tap in range(3):
            grad = jnp.dot(act, spans[tap], preferred_element_type=jnp.float32)
            for step, out_ref in enumerate(outs):
                out_ref[tap] = grad[step * width : (step + 1) * width].astype(out_ref.dtype)

    for level in range(sections):

        @pl.when(section == level)
        def run(level=level):
            taps(2**level)


def kernel_call(body, outs, flops, name, waits=(), carries=(), in_spec=in_vmem, scratch=()):
    def call(*args):
        used, taken = len(args), len(args) + len(waits) + len(carries)

        def run(*refs):
            made = refs[taken : taken + len(outs)]
            body(*refs[:used], *made, *refs[taken + len(outs) + len(carries) :])

        moved_bytes = sum(math.prod(a.shape) * a.dtype.itemsize for a in (*args, *outs))
        return pl.pallas_call(
            run,
            out_shape=[*outs, *(jax.ShapeDtypeStruct(a.shape, a.dtype) for a in carries)],
            in_specs=[in_spec] * used + [anywhere] * (taken - used),
            out_specs=[in_vmem] * len(outs) + [anywhere] * len(carries),
            input_output_aliases={
                used + len(waits) + at: len(outs) + at for at in range(len(carries))
            },
            scratch_shapes=list(scratch),
            compiler_params=pltpu.CompilerParams(vmem_limit_bytes=24 * 2**20),
            cost_estimate=pl.CostEstimate(
                flops=flops, bytes_accessed=moved_bytes, transcendentals=0
            ),
            name=name,
        )(*args, *waits, *carries)

    return call


def residue_shards(inputs, cotangent, weight, point):
    sections = lax.axis_size("pipe")
    section = lax.axis_index("pipe")
    count = lax.axis_size("ctx")
    groups = lax.axis_size("dp")
    seq_count, bins, chans = inputs.shape
    inner = weight.shape[3]
    rows = seq_count * bins
    scale = 1.0 / math.sqrt(seq_count * groups * bins * count)
    last = sections - 1
    layer_flops = 2 * rows * chans * inner * 4

    def shape(*dims, dtype=jnp.bfloat16):
        return jax.ShapeDtypeStruct(dims, dtype)

    def hop(value, source, target):
        swap = {source: target, target: source}
        route = []
        for core in range(groups):
            for stage in range(sections):
                taker = core if stage in swap else (core + 1) % groups
                for i in range(count):
                    giver = (core * sections + stage) * count + i
                    route.append((giver, (taker * sections + swap.get(stage, stage)) * count + i))
        return lax.ppermute(value, ("dp", "pipe", "ctx"), route)

    def onward(value, step):
        return lax.ppermute(value, "ctx", [(i, (i + step) % count) for i in range(count)])

    def exchange(value, offset):
        return lax.ppermute(value, "ctx", [(i, i ^ offset) for i in range(count)])

    payload = jnp.where(section == last, cotangent, inputs)
    parts = kernel_call(
        functools.partial(split_kernel, last),
        [shape(rows // count, chans)] * count,
        10 * layer_flops,
        "split",
    )(payload)
    weight, point = kernel_call(
        hold_kernel,
        [shape(*weight.shape), shape(*point.shape)],
        0,
        "hold",
        waits=[parts[0]],
        in_spec=anywhere,
        scratch=[pltpu.SemaphoreType.DMA((2,))],
    )(weight, point)
    parts = [parts[0], *(onward(parts[step], step) for step in range(1, count))]

    trunk, inside = shape(rows, chans), shape(rows, inner)
    inside_wide = shape(rows, inner, dtype=jnp.float32)
    whole, out, pre = kernel_call(
        functools.partial(first_kernel, last, bins),
        [trunk, trunk, inside_wide],
        layer_flops,
        "first",
    )(*parts, weight, point)
    xs, pres = [whole], [pre]
    for level in range(1, last):
        xs.append(hop(out, level - 1, level))
        out, pre = kernel_call(
            functools.partial(fore_kernel, level, bins),
            [trunk, inside_wide],
            layer_flops,
            "fore",
        )(xs[level], weight, point)
        pres.append(pre)
    xs.append(hop(out, last - 1, last))
    dy, dpre = kernel_call(
        functools.partial(turn_kernel, last, bins, scale),
        [trunk, inside],
        2 * layer_flops,
        "turn",
    )(xs[last], whole, weight, point)
    dpres = [dpre]

    kept = list(range(0, count, 2))
    size = chans // count
    *owned, message = kernel_call(
        functools.partial(columns_kernel, groups, sections, kept),
        [shape(size, rows)] * len(kept) + [shape(size * len(kept), rows)],
        2 * rows * chans * chans,
        "columns",
        waits=[dy],
    )(*xs)
    blocks = {(offset, 0): (array, 0) for offset, array in zip(kept, owned)}
    moving = [(offset, 0) for offset in kept]
    dy = hop(dy, last, last - 1)
    message, bit = exchange(message, 1), 1
    blocks.update({(to, start ^ bit): (message, at) for at, (to, start) in enumerate(moving)})
    late = [owned[0]]

    for level in range(last - 1, 0, -1):
        bit *= 2
        moving = sorted(key for key in blocks if key[0] & bit)
        if moving:
            (message,) = kernel_call(
                functools.partial(message_kernel, [blocks[key][1] for key in moving]),
                [shape(size * len(moving), rows)],
                0,
                "message",
            )(*[blocks[key][0] for key in moving])
            late = [message]
        out, dpre = kernel_call(
            functools.partial(back_kernel, level, bins),
            [trunk, inside],
            layer_flops,
            "back",
            waits=late,
        )(dy, xs[level], pres[level], weight, point)
        dpres.insert(0, dpre)
        dy, late = hop(out, level, level - 1), []
        if moving:
            message = exchange(message, bit)
            for at, (to, start) in enumerate(moving):
                del blocks[to, start]
                blocks[to ^ bit, start ^ bit] = (message, at)

    columns = [blocks[0, offset] for offset in range(count)]
    (dpre,) = kernel_call(
        functools.partial(head_kernel, sections), [inside], layer_flops // 4, "head", waits=late
    )(dy, pres[0], point, *dpres)
    gathered = {offset: exchange(dpre, offset) for offset in range(1, count)}
    share = shape(3, chans // (count * groups), inner, dtype=jnp.float32)
    mine, *others = kernel_call(
        functools.partial(grad_kernel, sections, bins, [at for array, at in columns]),
        [share, *[shape(*share.shape)] * (groups - 1)],
        2 * 3 * rows * chans * inner,
        "grad",
    )(*[array for array, at in columns], dpre, *[gathered[offset] for offset in range(1, count)])
    for step, other in enumerate(others, 1):
        route = [(i, (i + step) % groups) for i in range(groups)]
        mine = mine + lax.ppermute(other, "dp", route).astype(jnp.float32)
    return mine[None]


def solution(mesh):
    def shards(inputs, cotangent, dilated_kernel_weight, point_weight):
        bins = inputs.shape[1]
        first_spread = bins // 2 // 2 ** (mesh.shape["pipe"] - 1)
        count = mesh.shape["ctx"]
        residues = (
            first_spread == count
            and mesh.shape["pipe"] > 1
            and bins % (16 * count) == 0
            and 1 < count == 1 << (count.bit_length() - 1) <= 1 << (mesh.shape["pipe"] - 1)
            and inputs.shape[2] % (count * mesh.shape["dp"]) == 0
        )
        plan = residue_shards if residues else edge_shards
        return plan(inputs, cotangent, dilated_kernel_weight, point_weight)

    return jax.shard_map(
        shards,
        mesh=mesh,
        in_specs=(
            P("dp", "ctx", None),
            P("dp", "ctx", None),
            P("pipe", None, None, None),
            P("pipe", None, None),
        ),
        out_specs=P("pipe", None, ("dp", "ctx"), None),
        check_vma=False,
    )
```

```python
import functools
import math

import jax
import jax.numpy as jnp
from jax import lax
from jax.experimental import pallas as pl
from jax.experimental.pallas import tpu as pltpu
from jax.sharding import PartitionSpec as P

root_half = 0.7071067811865476
inv_root_two_pi = 0.3989422804014327

in_vmem = pl.BlockSpec(memory_space=pltpu.VMEM)
anywhere = pl.BlockSpec(memory_space=pl.ANY)
contract_last = (((1,), (1,)), ((), ()))
contract_first = (((0,), (0,)), ((), ()))


def gelu(value):
    return 0.5 * value * (1.0 + lax.erf(value * root_half))


def gelu_slope(value):
    return (
        0.5 * (1.0 + lax.erf(value * root_half))
        + value * jnp.exp(-0.5 * value * value) * inv_root_two_pi
    )


def padded(cells, sides, width):
    for axis, dim in sides:
        count = lax.axis_size(axis)
        ends = count - 1
        head = lax.slice_in_dim(cells, 0, width, axis=dim)
        tail = lax.slice_in_dim(cells, cells.shape[dim] - width, cells.shape[dim], axis=dim)
        cells = jnp.concatenate(
            [
                lax.ppermute(tail, axis, [(i, (i + 1) % count) for i in range(ends)]),
                cells,
                lax.ppermute(head, axis, [((i + 1) % count, i) for i in range(ends)]),
            ],
            axis=dim,
        )
    return cells


def shifted(block, axis, distance):
    devices = range(lax.axis_size(axis))
    route = [(i - distance, i) for i in devices if i - distance in devices]
    return lax.ppermute(block, axis, route)


def edge_shards(inputs, cotangent, dilated_kernel_weight, point_weight):
    sections = lax.axis_size("pipe")
    section = lax.axis_index("pipe")
    seq_count, bins, chans = inputs.shape
    reach = bins // 2
    table = jnp.array(
        [reach // 2 ** (sections - 1 - level) for level in range(sections)], jnp.int32
    )
    spread = table[section]
    dilation_weight = dilated_kernel_weight[0]
    w_point = point_weight[0]
    inner_channel_count = dilation_weight.shape[2]
    scale = 1.0 / math.sqrt(seq_count * lax.axis_size("dp") * bins * lax.axis_size("ctx"))
    ticks = jnp.arange(seq_count + sections - 1, dtype=jnp.int32)

    def conv_fore(extended):
        running_total = jnp.zeros((bins, inner_channel_count), jnp.float32)
        for kernel_offset in range(3):
            receptive_span = lax.dynamic_slice_in_dim(
                extended, reach + (kernel_offset - 1) * spread, bins, 0
            )
            running_total = running_total + jnp.dot(
                receptive_span, dilation_weight[kernel_offset], preferred_element_type=jnp.float32
            )
        return running_total

    def put(store, slot, valid, item):
        current = lax.dynamic_index_in_dim(store, slot, 0, keepdims=False)
        return lax.dynamic_update_index_in_dim(store, jnp.where(valid, item, current), slot, 0)

    kept_x = jnp.zeros(inputs.shape, jnp.bfloat16)
    kept_ext = jnp.zeros((seq_count, bins + 2 * reach, chans), jnp.bfloat16)
    kept_pre = jnp.zeros((seq_count, bins, inner_channel_count), jnp.float32)

    def fore_tick(carry, tick):
        received, store_x, store_ext, store_pre = carry
        micro = tick - section
        valid = (micro >= 0) & (micro < seq_count)
        slot = jnp.clip(micro, 0, seq_count - 1)
        first = lax.dynamic_index_in_dim(inputs, slot, 0, keepdims=False)
        trunk_in = jnp.where(section == 0, first, received)
        act = gelu(trunk_in.astype(jnp.float32)).astype(jnp.bfloat16)
        extended = padded(act, (("ctx", 0),), reach)
        pre = conv_fore(extended)
        inner = gelu(pre).astype(jnp.bfloat16)
        out = (
            trunk_in.astype(jnp.float32)
            + jnp.dot(inner, w_point, preferred_element_type=jnp.float32)
        ).astype(jnp.bfloat16)
        sent = shifted(out, "pipe", 1)
        store_x = put(store_x, slot, valid, trunk_in)
        store_ext = put(store_ext, slot, valid, extended)
        store_pre = put(store_pre, slot, valid, pre)
        return ((sent, store_x, store_ext, store_pre), None)

    start_recv = jnp.zeros((bins, chans), jnp.bfloat16)
    (unused, kept_x, kept_ext, kept_pre), unused_out = lax.scan(
        fore_tick, (start_recv, kept_x, kept_ext, kept_pre), ticks
    )

    def back_tick(carry, tick):
        received, grad = carry
        micro = tick - (sections - 1 - section)
        valid = (micro >= 0) & (micro < seq_count)
        slot = jnp.clip(micro, 0, seq_count - 1)
        last = (
            lax.dynamic_index_in_dim(cotangent, slot, 0, keepdims=False).astype(jnp.float32) * scale
        ).astype(jnp.bfloat16)
        upstream = jnp.where(section == sections - 1, last, received)
        trunk_in = lax.dynamic_index_in_dim(kept_x, slot, 0, keepdims=False)
        extended = lax.dynamic_index_in_dim(kept_ext, slot, 0, keepdims=False)
        pre = lax.dynamic_index_in_dim(kept_pre, slot, 0, keepdims=False)
        inner_grad = lax.dot_general(
            upstream, w_point, contract_last, preferred_element_type=jnp.float32
        )
        dpre = (inner_grad * gelu_slope(pre) * valid.astype(jnp.float32)).astype(jnp.bfloat16)
        dpre_ext = padded(dpre, (("ctx", 0),), reach)
        dact = jnp.zeros((bins, chans), jnp.float32)
        taps = []
        for kernel_offset in range(3):
            receptive_span = lax.dynamic_slice_in_dim(
                dpre_ext, reach - (kernel_offset - 1) * spread, bins, 0
            )
            dact = dact + lax.dot_general(
                receptive_span,
                dilation_weight[kernel_offset],
                contract_last,
                preferred_element_type=jnp.float32,
            )
            source = lax.dynamic_slice_in_dim(
                extended, reach + (kernel_offset - 1) * spread, bins, 0
            )
            taps.append(
                lax.dot_general(source, dpre, contract_first, preferred_element_type=jnp.float32)
            )
        grad = grad + jnp.stack(taps)
        back = (
            upstream.astype(jnp.float32) + dact * gelu_slope(trunk_in.astype(jnp.float32))
        ).astype(jnp.bfloat16)
        sent = shifted(back, "pipe", -1)
        return ((sent, grad), None)

    start_grad = jnp.zeros((3, chans, inner_channel_count), jnp.float32)
    (unused_back, grad), unused_seq = lax.scan(back_tick, (start_recv, start_grad), ticks)
    term = grad[None]
    return lax.psum_scatter(term, ("dp", "ctx"), scatter_dimension=2, tiled=True)


def moved(value, by, bins):
    pieces = []
    for start in range(0, value.shape[0], bins):
        piece = value[start : start + bins]
        place = lax.broadcasted_iota(jnp.int32, piece.shape, 0)
        if by > 0:
            keep = place >= by
        else:
            keep = place < bins + by
        pieces.append(jnp.where(keep, pltpu.roll(piece, by % bins, 0), 0.0))
    return jnp.concatenate(pieces, axis=0)


def fore(x, weight_ref, spread, bins):
    act = gelu(x.astype(jnp.float32)).astype(jnp.bfloat16)
    terms = [
        jnp.dot(act, weight_ref[0, tap], preferred_element_type=jnp.float32) for tap in range(3)
    ]
    return terms[1] + moved(terms[0], spread, bins) + moved(terms[2], -spread, bins)


def back_pre(dy, pre, point_ref):
    inner_grad = lax.dot_general(
        dy, point_ref[0], contract_last, preferred_element_type=jnp.float32
    )
    return (inner_grad * gelu_slope(pre)).astype(jnp.bfloat16)


def back_trunk(dy, dpre, x, weight_ref, spread, bins):
    wide = dpre.astype(jnp.float32)
    spans = (
        moved(wide, -spread, bins).astype(jnp.bfloat16),
        dpre,
        moved(wide, spread, bins).astype(jnp.bfloat16),
    )
    dact = jnp.zeros(dy.shape, jnp.float32)
    for tap in range(3):
        dact = dact + lax.dot_general(
            spans[tap], weight_ref[0, tap], contract_last, preferred_element_type=jnp.float32
        )
    return (
        dy.astype(jnp.float32) + dact * gelu_slope(x.astype(jnp.float32))
    ).astype(jnp.bfloat16)


def of_seq(ref, seq, bins):
    if ref.shape[0] == bins:
        return ref[...]
    return ref[seq * bins : (seq + 1) * bins, :]


def split_kernel(last, payload_ref, *out_refs):
    count = len(out_refs)
    seq_count, bins, chans = payload_ref.shape
    part = bins // count
    section = lax.axis_index("pipe")
    place = lax.axis_index("ctx")

    @pl.when((section == 0) | (section == last))
    def send():
        source = payload_ref[...].reshape(seq_count * bins, chans)
        row = lax.broadcasted_iota(jnp.int32, (part, seq_count * bins), 0)
        col = lax.broadcasted_iota(jnp.int32, (part, seq_count * bins), 1)
        for hop in range(count):
            residue = lax.rem(place + hop, count)
            rows = [
                (col == seq * bins + count * row + residue).astype(jnp.float32)
                for seq in range(seq_count)
            ]
            pick = jnp.concatenate(rows, axis=0).astype(jnp.bfloat16)
            out_refs[hop][...] = jnp.dot(
                pick, source, preferred_element_type=jnp.float32
            ).astype(jnp.bfloat16)


def hold_kernel(weight_ref, point_ref, weight_out, point_out, sems):
    loads = [
        pltpu.make_async_copy(weight_ref, weight_out, sems.at[0]),
        pltpu.make_async_copy(point_ref, point_out, sems.at[1]),
    ]
    for load in loads:
        load.start()
    for load in loads:
        load.wait()


def first_kernel(last, bins, *refs):
    parts, (weight_ref, point_ref, whole_ref, out_ref, pre_ref) = refs[:-5], refs[-5:]
    count = len(parts)
    section = lax.axis_index("pipe")
    place = lax.axis_index("ctx")
    part = bins // count
    seq_count = whole_ref.shape[0] // bins

    @pl.when((section == 0) | (section == last))
    def gather():
        for hop in range(count):
            source = lax.rem(place - hop + count, count)
            for seq in range(seq_count):
                at = pl.multiple_of(seq * bins + source * part, part)
                whole_ref[pl.ds(at, part), :] = parts[hop][seq * part : (seq + 1) * part, :]

    @pl.when(section == 0)
    def layer():
        x = whole_ref[:bins, :]
        finish(x, fore(x, weight_ref, 1, bins), point_ref, out_ref, pre_ref)


def finish(x, pre, point_ref, out_ref, pre_ref):
    pre_ref[...] = pre
    branch = jnp.dot(
        gelu(pre).astype(jnp.bfloat16), point_ref[0], preferred_element_type=jnp.float32
    )
    out_ref[...] = (x.astype(jnp.float32) + branch).astype(jnp.bfloat16)


def fore_kernel(level, seq, bins, x_ref, weight_ref, point_ref, out_ref, pre_ref):
    @pl.when(lax.axis_index("pipe") == level)
    def layer():
        x = of_seq(x_ref, seq, bins)
        finish(x, fore(x, weight_ref, 2**level, bins), point_ref, out_ref, pre_ref)


def turn_kernel(level, seq, bins, scale, x_ref, cot_ref, weight_ref, point_ref, dy_ref, dpre_ref):
    @pl.when(lax.axis_index("pipe") == level)
    def layer():
        x = of_seq(x_ref, seq, bins)
        pre = fore(x, weight_ref, 2**level, bins)
        cot = of_seq(cot_ref, seq, bins)
        dy = (cot.astype(jnp.float32) * scale).astype(jnp.bfloat16)
        dpre = back_pre(dy, pre, point_ref)
        dpre_ref[...] = dpre
        dy_ref[...] = back_trunk(dy, dpre, x, weight_ref, 2**level, bins)


def back_kernel(level, seq, bins, dy_in_ref, x_ref, pre_ref, weight_ref, point_ref, dy_ref, dpre_ref):
    @pl.when(lax.axis_index("pipe") == level)
    def layer():
        dy = dy_in_ref[...]
        x = of_seq(x_ref, seq, bins)
        dpre = back_pre(dy, of_seq(pre_ref, seq, bins), point_ref)
        dpre_ref[...] = dpre
        dy_ref[...] = back_trunk(dy, dpre, x, weight_ref, 2**level, bins)


def message_kernel(places, *refs):
    blocks, message_ref = refs[:-1], refs[-1]
    size = message_ref.shape[0] // len(places)
    for to, (ref, at) in enumerate(zip(blocks, places)):
        message_ref[to * size : (to + 1) * size, :] = ref[at * size : (at + 1) * size, :]


def head_kernel(sections, earlier, dy_in_ref, pre_ref, point_ref, *refs):
    others, before, out_ref = refs[: sections - 1], refs[sections - 1 : -1], refs[-1]
    section = lax.axis_index("pipe")
    bins = dy_in_ref.shape[0]
    for ref in before:
        out_ref[:earlier, :] = ref[...]

    @pl.when(section == 0)
    def layer():
        out_ref[earlier : earlier + bins, :] = back_pre(dy_in_ref[...], pre_ref[...], point_ref)

    for level in range(1, sections):

        @pl.when(section == level)
        def keep(level=level):
            out_ref[earlier : earlier + bins, :] = others[level - 1][...]


def columns_kernel(groups, runs, kept, *refs):
    refs, (sent_ref,) = refs[:-1], refs[-1:]
    kept_refs = refs[sum(runs) :]
    count = 2 * len(kept)
    section = lax.axis_index("pipe")
    core = lax.axis_index("dp")
    place = lax.axis_index("ctx")
    x, start = None, 0
    for level, run in enumerate(runs):
        pieces = [ref[...] for ref in refs[start : start + run]]
        start += run
        whole = jnp.concatenate(pieces, axis=0).astype(jnp.float32)
        x = whole if x is None else jnp.where(section == level, whole, x)
    act = gelu(x).astype(jnp.bfloat16)
    chans = act.shape[1]
    width = chans // (groups * count)
    row = lax.broadcasted_iota(jnp.int32, (width, chans), 0)
    col = lax.broadcasted_iota(jnp.int32, (width, chans), 1)

    def block(offset):
        owner = lax.bitwise_xor(place, offset)
        rows = []
        for step in range(groups):
            first = (lax.rem(core + step, groups) * count + owner) * width
            rows.append((col == first + row).astype(jnp.float32))
        pick = jnp.concatenate(rows, axis=0).astype(jnp.bfloat16)
        return lax.dot_general(
            pick, act, contract_last, preferred_element_type=jnp.float32
        ).astype(jnp.bfloat16)

    size = groups * width
    for at, offset in enumerate(kept):
        kept_refs[at][...] = block(offset)
        sent_ref[at * size : (at + 1) * size, :] = block(offset ^ 1)


def grad_kernel(sections, bins, places, *refs):
    columns, refs = refs[: len(places)], refs[len(places) :]
    grads, outs = refs[: len(places)], refs[len(places) :]
    section = lax.axis_index("pipe")
    width = outs[0].shape[1]
    size = len(outs) * width

    def taps(spread):
        act = jnp.concatenate(
            [ref[at * size : (at + 1) * size, :] for ref, at in zip(columns, places)], axis=1
        )
        dpre = jnp.concatenate([ref[...] for ref in grads], axis=0)
        wide = dpre.astype(jnp.float32)
        spans = (
            moved(wide, -spread, bins).astype(jnp.bfloat16),
            dpre,
            moved(wide, spread, bins).astype(jnp.bfloat16),
        )
        for tap in range(3):
            grad = jnp.dot(act, spans[tap], preferred_element_type=jnp.float32)
            for step, out_ref in enumerate(outs):
                out_ref[tap] = grad[step * width : (step + 1) * width].astype(out_ref.dtype)

    for level in range(sections):

        @pl.when(section == level)
        def run(level=level):
            taps(2**level)


def kernel_call(body, outs, flops, name, waits=(), carries=(), in_spec=in_vmem, scratch=()):
    def call(*args):
        used, taken = len(args), len(args) + len(waits) + len(carries)

        def run(*refs):
            made = refs[taken : taken + len(outs)]
            body(*refs[:used], *made, *refs[taken + len(outs) + len(carries) :])

        moved_bytes = sum(math.prod(a.shape) * a.dtype.itemsize for a in (*args, *outs))
        return pl.pallas_call(
            run,
            out_shape=[*outs, *(jax.ShapeDtypeStruct(a.shape, a.dtype) for a in carries)],
            in_specs=[in_spec] * used + [anywhere] * (taken - used),
            out_specs=[in_vmem] * len(outs) + [anywhere] * len(carries),
            input_output_aliases={
                used + len(waits) + at: len(outs) + at for at in range(len(carries))
            },
            scratch_shapes=list(scratch),
            compiler_params=pltpu.CompilerParams(vmem_limit_bytes=24 * 2**20),
            cost_estimate=pl.CostEstimate(
                flops=flops, bytes_accessed=moved_bytes, transcendentals=0
            ),
            name=name,
        )(*args, *waits, *carries)

    return call


def residue_shards(inputs, cotangent, weight, point):
    sections = lax.axis_size("pipe")
    section = lax.axis_index("pipe")
    count = lax.axis_size("ctx")
    groups = lax.axis_size("dp")
    seq_count, bins, chans = inputs.shape
    inner = weight.shape[3]
    rows = seq_count * bins
    scale = 1.0 / math.sqrt(seq_count * groups * bins * count)
    last = sections - 1
    seqs = range(seq_count)
    layer_flops = 2 * bins * chans * inner * 4

    def shape(*dims, dtype=jnp.bfloat16):
        return jax.ShapeDtypeStruct(dims, dtype)

    def hop(value, source, target):
        swap = {source: target, target: source}
        route = []
        for core in range(groups):
            for stage in range(sections):
                taker = core if stage in swap else (core + 1) % groups
                for i in range(count):
                    giver = (core * sections + stage) * count + i
                    route.append((giver, (taker * sections + swap.get(stage, stage)) * count + i))
        return lax.ppermute(value, ("dp", "pipe", "ctx"), route)

    def onward(value, step):
        return lax.ppermute(value, "ctx", [(i, (i + step) % count) for i in range(count)])

    def exchange(value, offset):
        return lax.ppermute(value, "ctx", [(i, i ^ offset) for i in range(count)])

    payload = jnp.where(section == last, cotangent, inputs)
    parts = kernel_call(
        functools.partial(split_kernel, last),
        [shape(rows // count, chans)] * count,
        10 * seq_count * layer_flops,
        "split",
    )(payload)
    weight, point = kernel_call(
        hold_kernel,
        [shape(*weight.shape), shape(*point.shape)],
        0,
        "hold",
        waits=[parts[0]],
        in_spec=anywhere,
        scratch=[pltpu.SemaphoreType.DMA((2,))],
    )(weight, point)
    parts = [parts[0], *(onward(parts[step], step) for step in range(1, count))]

    trunk, inside = shape(bins, chans), shape(bins, inner)
    inside_wide = shape(bins, inner, dtype=jnp.float32)
    whole, out, pre = kernel_call(
        functools.partial(first_kernel, last, bins),
        [shape(rows, chans), trunk, inside_wide],
        layer_flops,
        "first",
    )(*parts, weight, point)
    outs, pres, xs, sent = [out], [[pre]], [[whole]], ()
    for level in range(last):
        if level > 0:
            xs.append([hop(out, level - 1, level) for out in outs])
            outs = []
            pres.append([])
        for seq in range(len(outs), seq_count):
            out, pre = kernel_call(
                functools.partial(fore_kernel, level, seq, bins),
                [trunk, inside_wide],
                layer_flops,
                "fore",
                waits=outs[-1:] or sent,
            )(xs[level][seq if level else 0], weight, point)
            outs.append(out)
            pres[level].append(pre)
        sent = outs
    xs.append([hop(out, last - 1, last) for out in outs])

    dys, dpres = [], [[] for level in range(sections)]
    for seq in seqs:
        dy, dpre = kernel_call(
            functools.partial(turn_kernel, last, seq, bins, scale),
            [trunk, inside],
            2 * layer_flops,
            "turn",
            waits=dys[-1:] or sent,
        )(xs[last][seq], whole, weight, point)
        dys.append(dy)
        dpres[last].append(dpre)
    sent = dys
    dys = [hop(dy, last, last - 1) for dy in dys]

    size = chans // count
    blocks, bit = {}, 1
    for level in range(last - 1, 0, -1):
        outs = []
        for seq in seqs:
            dy, dpre = kernel_call(
                functools.partial(back_kernel, level, seq, bins),
                [trunk, inside],
                layer_flops,
                "back",
                waits=outs[-1:] or sent,
            )(dys[seq], xs[level][seq], pres[level][seq], weight, point)
            outs.append(dy)
            dpres[level].append(dpre)
        sent = outs
        dys = [hop(dy, level, level - 1) for dy in outs]
        if level == last - 1:
            kept = list(range(0, count, 2))
            moving = [(offset, 0) for offset in range(1, count, 2)]
            *owned, message = kernel_call(
                functools.partial(columns_kernel, groups, [len(x) for x in xs], kept),
                [shape(size, rows)] * len(kept) + [shape(size * len(kept), rows)],
                2 * rows * chans * chans,
                "columns",
                waits=outs,
            )(*[x for some in xs for x in some])
            blocks = {(offset, 0): (array, 0) for offset, array in zip(kept, owned)}
        else:
            bit *= 2
            moving = sorted(key for key in blocks if key[0] & bit)
            if not moving:
                continue
            (message,) = kernel_call(
                functools.partial(message_kernel, [blocks[key][1] for key in moving]),
                [shape(size * len(moving), rows)],
                0,
                "message",
                waits=outs,
            )(*[blocks[key][0] for key in moving])
        message = exchange(message, bit)
        for at, (to, start) in enumerate(moving):
            blocks[to ^ bit, start ^ bit] = (message, at)

    dpre = []
    for seq in seqs:
        dpre = kernel_call(
            functools.partial(head_kernel, sections, seq * bins),
            [shape((seq + 1) * bins, inner)],
            layer_flops // 4,
            "head",
            waits=dpre or sent,
        )(dys[seq], pres[0][seq], point, *[dpres[level][seq] for level in range(1, sections)], *dpre)
    (dpre,) = dpre
    gathered = {offset: exchange(dpre, offset) for offset in range(1, count)}
    columns = [blocks[0, offset] for offset in range(count)]
    share = shape(3, chans // (count * groups), inner, dtype=jnp.float32)
    mine, *others = kernel_call(
        functools.partial(grad_kernel, sections, bins, [at for array, at in columns]),
        [share, *[shape(*share.shape)] * (groups - 1)],
        2 * 3 * rows * chans * inner,
        "grad",
    )(*[array for array, at in columns], dpre, *[gathered[offset] for offset in range(1, count)])
    for step, other in enumerate(others, 1):
        route = [(i, (i + step) % groups) for i in range(groups)]
        mine = mine + lax.ppermute(other, "dp", route).astype(jnp.float32)
    return mine[None]


def solution(mesh):
    def shards(inputs, cotangent, dilated_kernel_weight, point_weight):
        bins = inputs.shape[1]
        first_spread = bins // 2 // 2 ** (mesh.shape["pipe"] - 1)
        count = mesh.shape["ctx"]
        residues = (
            first_spread == count
            and mesh.shape["pipe"] > 1
            and bins % (16 * count) == 0
            and 1 < count == 1 << (count.bit_length() - 1) <= 1 << (mesh.shape["pipe"] - 2)
            and inputs.shape[2] % (count * mesh.shape["dp"]) == 0
        )
        plan = residue_shards if residues else edge_shards
        return plan(inputs, cotangent, dilated_kernel_weight, point_weight)

    return jax.shard_map(
        shards,
        mesh=mesh,
        in_specs=(
            P("dp", "ctx", None),
            P("dp", "ctx", None),
            P("pipe", None, None, None),
            P("pipe", None, None),
        ),
        out_specs=P("pipe", None, ("dp", "ctx"), None),
        check_vma=False,
    )
```

```python
import functools
import math

import jax
import jax.numpy as jnp
from jax import lax
from jax.experimental import pallas as pl
from jax.experimental.pallas import tpu as pltpu
from jax.sharding import PartitionSpec as P

root_half = 0.7071067811865476
inv_root_two_pi = 0.3989422804014327

in_vmem = pl.BlockSpec(memory_space=pltpu.VMEM)
anywhere = pl.BlockSpec(memory_space=pl.ANY)
contract_last = (((1,), (1,)), ((), ()))
contract_first = (((0,), (0,)), ((), ()))


def gelu(value):
    return 0.5 * value * (1.0 + lax.erf(value * root_half))


def gelu_slope(value):
    return (
        0.5 * (1.0 + lax.erf(value * root_half))
        + value * jnp.exp(-0.5 * value * value) * inv_root_two_pi
    )


def padded(cells, sides, width):
    for axis, dim in sides:
        count = lax.axis_size(axis)
        ends = count - 1
        head = lax.slice_in_dim(cells, 0, width, axis=dim)
        tail = lax.slice_in_dim(cells, cells.shape[dim] - width, cells.shape[dim], axis=dim)
        cells = jnp.concatenate(
            [
                lax.ppermute(tail, axis, [(i, (i + 1) % count) for i in range(ends)]),
                cells,
                lax.ppermute(head, axis, [((i + 1) % count, i) for i in range(ends)]),
            ],
            axis=dim,
        )
    return cells


def shifted(block, axis, distance):
    devices = range(lax.axis_size(axis))
    route = [(i - distance, i) for i in devices if i - distance in devices]
    return lax.ppermute(block, axis, route)


def edge_shards(inputs, cotangent, dilated_kernel_weight, point_weight):
    sections = lax.axis_size("pipe")
    section = lax.axis_index("pipe")
    seq_count, bins, chans = inputs.shape
    reach = bins // 2
    table = jnp.array(
        [reach // 2 ** (sections - 1 - level) for level in range(sections)], jnp.int32
    )
    spread = table[section]
    dilation_weight = dilated_kernel_weight[0]
    w_point = point_weight[0]
    inner_channel_count = dilation_weight.shape[2]
    scale = 1.0 / math.sqrt(seq_count * lax.axis_size("dp") * bins * lax.axis_size("ctx"))
    ticks = jnp.arange(seq_count + sections - 1, dtype=jnp.int32)

    def conv_fore(extended):
        running_total = jnp.zeros((bins, inner_channel_count), jnp.float32)
        for kernel_offset in range(3):
            receptive_span = lax.dynamic_slice_in_dim(
                extended, reach + (kernel_offset - 1) * spread, bins, 0
            )
            running_total = running_total + jnp.dot(
                receptive_span, dilation_weight[kernel_offset], preferred_element_type=jnp.float32
            )
        return running_total

    def put(store, slot, valid, item):
        current = lax.dynamic_index_in_dim(store, slot, 0, keepdims=False)
        return lax.dynamic_update_index_in_dim(store, jnp.where(valid, item, current), slot, 0)

    kept_x = jnp.zeros(inputs.shape, jnp.bfloat16)
    kept_ext = jnp.zeros((seq_count, bins + 2 * reach, chans), jnp.bfloat16)
    kept_pre = jnp.zeros((seq_count, bins, inner_channel_count), jnp.float32)

    def fore_tick(carry, tick):
        received, store_x, store_ext, store_pre = carry
        micro = tick - section
        valid = (micro >= 0) & (micro < seq_count)
        slot = jnp.clip(micro, 0, seq_count - 1)
        first = lax.dynamic_index_in_dim(inputs, slot, 0, keepdims=False)
        trunk_in = jnp.where(section == 0, first, received)
        act = gelu(trunk_in.astype(jnp.float32)).astype(jnp.bfloat16)
        extended = padded(act, (("ctx", 0),), reach)
        pre = conv_fore(extended)
        inner = gelu(pre).astype(jnp.bfloat16)
        out = (
            trunk_in.astype(jnp.float32)
            + jnp.dot(inner, w_point, preferred_element_type=jnp.float32)
        ).astype(jnp.bfloat16)
        sent = shifted(out, "pipe", 1)
        store_x = put(store_x, slot, valid, trunk_in)
        store_ext = put(store_ext, slot, valid, extended)
        store_pre = put(store_pre, slot, valid, pre)
        return ((sent, store_x, store_ext, store_pre), None)

    start_recv = jnp.zeros((bins, chans), jnp.bfloat16)
    (unused, kept_x, kept_ext, kept_pre), unused_out = lax.scan(
        fore_tick, (start_recv, kept_x, kept_ext, kept_pre), ticks
    )

    def back_tick(carry, tick):
        received, grad = carry
        micro = tick - (sections - 1 - section)
        valid = (micro >= 0) & (micro < seq_count)
        slot = jnp.clip(micro, 0, seq_count - 1)
        last = (
            lax.dynamic_index_in_dim(cotangent, slot, 0, keepdims=False).astype(jnp.float32) * scale
        ).astype(jnp.bfloat16)
        upstream = jnp.where(section == sections - 1, last, received)
        trunk_in = lax.dynamic_index_in_dim(kept_x, slot, 0, keepdims=False)
        extended = lax.dynamic_index_in_dim(kept_ext, slot, 0, keepdims=False)
        pre = lax.dynamic_index_in_dim(kept_pre, slot, 0, keepdims=False)
        inner_grad = lax.dot_general(
            upstream, w_point, contract_last, preferred_element_type=jnp.float32
        )
        dpre = (inner_grad * gelu_slope(pre) * valid.astype(jnp.float32)).astype(jnp.bfloat16)
        dpre_ext = padded(dpre, (("ctx", 0),), reach)
        dact = jnp.zeros((bins, chans), jnp.float32)
        taps = []
        for kernel_offset in range(3):
            receptive_span = lax.dynamic_slice_in_dim(
                dpre_ext, reach - (kernel_offset - 1) * spread, bins, 0
            )
            dact = dact + lax.dot_general(
                receptive_span,
                dilation_weight[kernel_offset],
                contract_last,
                preferred_element_type=jnp.float32,
            )
            source = lax.dynamic_slice_in_dim(
                extended, reach + (kernel_offset - 1) * spread, bins, 0
            )
            taps.append(
                lax.dot_general(source, dpre, contract_first, preferred_element_type=jnp.float32)
            )
        grad = grad + jnp.stack(taps)
        back = (
            upstream.astype(jnp.float32) + dact * gelu_slope(trunk_in.astype(jnp.float32))
        ).astype(jnp.bfloat16)
        sent = shifted(back, "pipe", -1)
        return ((sent, grad), None)

    start_grad = jnp.zeros((3, chans, inner_channel_count), jnp.float32)
    (unused_back, grad), unused_seq = lax.scan(back_tick, (start_recv, start_grad), ticks)
    term = grad[None]
    return lax.psum_scatter(term, ("dp", "ctx"), scatter_dimension=2, tiled=True)


def moved(value, by, bins):
    pieces = []
    for start in range(0, value.shape[0], bins):
        piece = value[start : start + bins]
        place = lax.broadcasted_iota(jnp.int32, piece.shape, 0)
        if by > 0:
            keep = place >= by
        else:
            keep = place < bins + by
        pieces.append(jnp.where(keep, pltpu.roll(piece, by % bins, 0), 0.0))
    return jnp.concatenate(pieces, axis=0)


def fore(x, weight_ref, spread, bins):
    act = gelu(x.astype(jnp.float32)).astype(jnp.bfloat16)
    terms = [
        jnp.dot(act, weight_ref[0, tap], preferred_element_type=jnp.float32) for tap in range(3)
    ]
    return terms[1] + moved(terms[0], spread, bins) + moved(terms[2], -spread, bins)


def back_pre(dy, pre, point_ref):
    inner_grad = lax.dot_general(
        dy, point_ref[0], contract_last, preferred_element_type=jnp.float32
    )
    return (inner_grad * gelu_slope(pre)).astype(jnp.bfloat16)


def back_trunk(dy, dpre, x, weight_ref, spread, bins):
    wide = dpre.astype(jnp.float32)
    spans = (
        moved(wide, -spread, bins).astype(jnp.bfloat16),
        dpre,
        moved(wide, spread, bins).astype(jnp.bfloat16),
    )
    dact = jnp.zeros(dy.shape, jnp.float32)
    for tap in range(3):
        dact = dact + lax.dot_general(
            spans[tap], weight_ref[0, tap], contract_last, preferred_element_type=jnp.float32
        )
    return (
        dy.astype(jnp.float32) + dact * gelu_slope(x.astype(jnp.float32))
    ).astype(jnp.bfloat16)


def of_seq(ref, seq, bins):
    if ref.shape[0] == bins:
        return ref[...]
    return ref[seq * bins : (seq + 1) * bins, :]


def split_kernel(last, payload_ref, *out_refs):
    count = len(out_refs)
    seq_count, bins, chans = payload_ref.shape
    part = bins // count
    section = lax.axis_index("pipe")
    place = lax.axis_index("ctx")

    @pl.when((section == 0) | (section == last))
    def send():
        source = payload_ref[...].reshape(seq_count * bins, chans)
        row = lax.broadcasted_iota(jnp.int32, (part, seq_count * bins), 0)
        col = lax.broadcasted_iota(jnp.int32, (part, seq_count * bins), 1)
        for hop in range(count):
            residue = lax.rem(place + hop, count)
            rows = [
                (col == seq * bins + count * row + residue).astype(jnp.float32)
                for seq in range(seq_count)
            ]
            pick = jnp.concatenate(rows, axis=0).astype(jnp.bfloat16)
            out_refs[hop][...] = jnp.dot(
                pick, source, preferred_element_type=jnp.float32
            ).astype(jnp.bfloat16)


def hold_kernel(weight_ref, point_ref, weight_out, point_out, sems):
    loads = [
        pltpu.make_async_copy(weight_ref, weight_out, sems.at[0]),
        pltpu.make_async_copy(point_ref, point_out, sems.at[1]),
    ]
    for load in loads:
        load.start()
    for load in loads:
        load.wait()


def first_kernel(last, bins, *refs):
    parts, (weight_ref, point_ref, whole_ref, out_ref, pre_ref) = refs[:-5], refs[-5:]
    count = len(parts)
    section = lax.axis_index("pipe")
    place = lax.axis_index("ctx")
    part = bins // count
    seq_count = whole_ref.shape[0] // bins

    @pl.when((section == 0) | (section == last))
    def gather():
        for hop in range(count):
            source = lax.rem(place - hop + count, count)
            for seq in range(seq_count):
                at = pl.multiple_of(seq * bins + source * part, part)
                whole_ref[pl.ds(at, part), :] = parts[hop][seq * part : (seq + 1) * part, :]

    @pl.when(section == 0)
    def layer():
        x = whole_ref[:bins, :]
        finish(x, fore(x, weight_ref, 1, bins), point_ref, out_ref, pre_ref)


def finish(x, pre, point_ref, out_ref, pre_ref):
    pre_ref[...] = pre
    branch = jnp.dot(
        gelu(pre).astype(jnp.bfloat16), point_ref[0], preferred_element_type=jnp.float32
    )
    out_ref[...] = (x.astype(jnp.float32) + branch).astype(jnp.bfloat16)


def fore_kernel(level, seq, bins, x_ref, weight_ref, point_ref, out_ref, pre_ref):
    @pl.when(lax.axis_index("pipe") == level)
    def layer():
        x = of_seq(x_ref, seq, bins)
        finish(x, fore(x, weight_ref, 2**level, bins), point_ref, out_ref, pre_ref)


def turn_kernel(level, seq, bins, scale, x_ref, cot_ref, weight_ref, point_ref, dy_ref, dpre_ref):
    @pl.when(lax.axis_index("pipe") == level)
    def layer():
        x = of_seq(x_ref, seq, bins)
        pre = fore(x, weight_ref, 2**level, bins)
        cot = of_seq(cot_ref, seq, bins)
        dy = (cot.astype(jnp.float32) * scale).astype(jnp.bfloat16)
        dpre = back_pre(dy, pre, point_ref)
        dpre_ref[...] = dpre
        dy_ref[...] = back_trunk(dy, dpre, x, weight_ref, 2**level, bins)


def back_kernel(level, seq, bins, dy_in_ref, x_ref, pre_ref, weight_ref, point_ref, dy_ref, dpre_ref):
    @pl.when(lax.axis_index("pipe") == level)
    def layer():
        dy = dy_in_ref[...]
        x = of_seq(x_ref, seq, bins)
        dpre = back_pre(dy, of_seq(pre_ref, seq, bins), point_ref)
        dpre_ref[...] = dpre
        dy_ref[...] = back_trunk(dy, dpre, x, weight_ref, 2**level, bins)


def message_kernel(places, *refs):
    blocks, message_ref = refs[:-1], refs[-1]
    size = message_ref.shape[0] // len(places)
    for to, (ref, at) in enumerate(zip(blocks, places)):
        message_ref[to * size : (to + 1) * size, :] = ref[at * size : (at + 1) * size, :]


def head_kernel(sections, earlier, dy_in_ref, pre_ref, point_ref, *refs):
    others, before, out_ref = refs[: sections - 1], refs[sections - 1 : -1], refs[-1]
    section = lax.axis_index("pipe")
    bins = dy_in_ref.shape[0]
    for ref in before:
        out_ref[:earlier, :] = ref[...]

    @pl.when(section == 0)
    def layer():
        out_ref[earlier : earlier + bins, :] = back_pre(dy_in_ref[...], pre_ref[...], point_ref)

    for level in range(1, sections):

        @pl.when(section == level)
        def keep(level=level):
            out_ref[earlier : earlier + bins, :] = others[level - 1][...]


def columns_kernel(groups, runs, kept, *refs):
    refs, (sent_ref,) = refs[:-1], refs[-1:]
    kept_refs = refs[sum(runs) :]
    count = 2 * len(kept)
    section = lax.axis_index("pipe")
    core = lax.axis_index("dp")
    place = lax.axis_index("ctx")
    x, start = None, 0
    for level, run in enumerate(runs):
        pieces = [ref[...] for ref in refs[start : start + run]]
        start += run
        whole = jnp.concatenate(pieces, axis=0).astype(jnp.float32)
        x = whole if x is None else jnp.where(section == level, whole, x)
    act = gelu(x).astype(jnp.bfloat16)
    chans = act.shape[1]
    width = chans // (groups * count)
    row = lax.broadcasted_iota(jnp.int32, (width, chans), 0)
    col = lax.broadcasted_iota(jnp.int32, (width, chans), 1)

    def block(offset):
        owner = lax.bitwise_xor(place, offset)
        rows = []
        for step in range(groups):
            first = (lax.rem(core + step, groups) * count + owner) * width
            rows.append((col == first + row).astype(jnp.float32))
        pick = jnp.concatenate(rows, axis=0).astype(jnp.bfloat16)
        return lax.dot_general(
            pick, act, contract_last, preferred_element_type=jnp.float32
        ).astype(jnp.bfloat16)

    size = groups * width
    for at, offset in enumerate(kept):
        kept_refs[at][...] = block(offset)
        sent_ref[at * size : (at + 1) * size, :] = block(offset ^ 1)


def grad_kernel(sections, bins, places, *refs):
    columns, refs = refs[: len(places)], refs[len(places) :]
    grads, outs = refs[: len(places)], refs[len(places) :]
    section = lax.axis_index("pipe")
    width = outs[0].shape[1]
    size = len(outs) * width

    def taps(spread):
        act = jnp.concatenate(
            [ref[at * size : (at + 1) * size, :] for ref, at in zip(columns, places)], axis=1
        )
        dpre = jnp.concatenate([ref[...] for ref in grads], axis=0)
        wide = dpre.astype(jnp.float32)
        spans = (
            moved(wide, -spread, bins).astype(jnp.bfloat16),
            dpre,
            moved(wide, spread, bins).astype(jnp.bfloat16),
        )
        for tap in range(3):
            grad = jnp.dot(act, spans[tap], preferred_element_type=jnp.float32)
            for step, out_ref in enumerate(outs):
                out_ref[tap] = grad[step * width : (step + 1) * width].astype(out_ref.dtype)

    for level in range(sections):

        @pl.when(section == level)
        def run(level=level):
            taps(2**level)


def kernel_call(body, outs, flops, name, waits=(), carries=(), in_spec=in_vmem, scratch=()):
    def call(*args):
        used, taken = len(args), len(args) + len(waits) + len(carries)

        def run(*refs):
            made = refs[taken : taken + len(outs)]
            body(*refs[:used], *made, *refs[taken + len(outs) + len(carries) :])

        moved_bytes = sum(math.prod(a.shape) * a.dtype.itemsize for a in (*args, *outs))
        return pl.pallas_call(
            run,
            out_shape=[*outs, *(jax.ShapeDtypeStruct(a.shape, a.dtype) for a in carries)],
            in_specs=[in_spec] * used + [anywhere] * (taken - used),
            out_specs=[in_vmem] * len(outs) + [anywhere] * len(carries),
            input_output_aliases={
                used + len(waits) + at: len(outs) + at for at in range(len(carries))
            },
            scratch_shapes=list(scratch),
            compiler_params=pltpu.CompilerParams(vmem_limit_bytes=24 * 2**20),
            cost_estimate=pl.CostEstimate(
                flops=flops, bytes_accessed=moved_bytes, transcendentals=0
            ),
            name=name,
        )(*args, *waits, *carries)

    return call


def residue_shards(inputs, cotangent, weight, point):
    sections = lax.axis_size("pipe")
    section = lax.axis_index("pipe")
    count = lax.axis_size("ctx")
    groups = lax.axis_size("dp")
    seq_count, bins, chans = inputs.shape
    inner = weight.shape[3]
    rows = seq_count * bins
    scale = 1.0 / math.sqrt(seq_count * groups * bins * count)
    last = sections - 1
    seqs = range(seq_count)
    layer_flops = 2 * bins * chans * inner * 4

    def shape(*dims, dtype=jnp.bfloat16):
        return jax.ShapeDtypeStruct(dims, dtype)

    def hop(value, source, target):
        step = target - source
        free = [s for s in range(sections) if s not in (source, target, target + step)]
        third = free[0 if step > 0 else -1] if free else source
        sends = {source: target, target: third, third: source} if free else {source: target, target: source}
        route = []
        for core in range(groups):
            for stage in range(sections):
                taker = core if stage in sends else (core + 1) % groups
                for i in range(count):
                    giver = (core * sections + stage) * count + i
                    route.append((giver, (taker * sections + sends.get(stage, stage)) * count + i))
        return lax.ppermute(value, ("dp", "pipe", "ctx"), route)

    def onward(value, step):
        return lax.ppermute(value, "ctx", [(i, (i + step) % count) for i in range(count)])

    def exchange(value, offset):
        return lax.ppermute(value, "ctx", [(i, i ^ offset) for i in range(count)])

    payload = jnp.where(section == last, cotangent, inputs)
    parts = kernel_call(
        functools.partial(split_kernel, last),
        [shape(rows // count, chans)] * count,
        10 * seq_count * layer_flops,
        "split",
    )(payload)
    weight, point = kernel_call(
        hold_kernel,
        [shape(*weight.shape), shape(*point.shape)],
        0,
        "hold",
        waits=[parts[0]],
        in_spec=anywhere,
        scratch=[pltpu.SemaphoreType.DMA((2,))],
    )(weight, point)
    moved_parts = {step: onward(parts[step], step) for step in range(count - 1, 0, -1)}
    parts = [parts[0], *(moved_parts[step] for step in range(1, count))]

    trunk, inside = shape(bins, chans), shape(bins, inner)
    inside_wide = shape(bins, inner, dtype=jnp.float32)
    whole, out, pre = kernel_call(
        functools.partial(first_kernel, last, bins),
        [shape(rows, chans), trunk, inside_wide],
        layer_flops,
        "first",
    )(*parts, weight, point)
    outs, pres, xs, sent = [out], [[pre]], [[whole]], ()
    for level in range(last):
        if level > 0:
            xs.append([hop(out, level - 1, level) for out in outs])
            outs = []
            pres.append([])
        for seq in range(len(outs), seq_count):
            out, pre = kernel_call(
                functools.partial(fore_kernel, level, seq, bins),
                [trunk, inside_wide],
                layer_flops,
                "fore",
                waits=outs[-1:] or sent,
            )(xs[level][seq if level else 0], weight, point)
            outs.append(out)
            pres[level].append(pre)
        sent = outs
    xs.append([hop(out, last - 1, last) for out in outs])

    dys, dpres = [], [[] for level in range(sections)]
    for seq in seqs:
        dy, dpre = kernel_call(
            functools.partial(turn_kernel, last, seq, bins, scale),
            [trunk, inside],
            2 * layer_flops,
            "turn",
            waits=dys[-1:] or sent,
        )(xs[last][seq], whole, weight, point)
        dys.append(dy)
        dpres[last].append(dpre)
    kept = list(range(0, count, 2))
    moving = [(offset, 0) for offset in range(1, count, 2)]
    size = chans // count
    *owned, message = kernel_call(
        functools.partial(columns_kernel, groups, [len(x) for x in xs], kept),
        [shape(size, rows)] * len(kept) + [shape(size * len(kept), rows)],
        2 * rows * chans * chans,
        "columns",
        waits=dys,
    )(*[x for some in xs for x in some])
    blocks = {(offset, 0): (array, 0) for offset, array in zip(kept, owned)}
    sent = [owned[0]]
    dys = [hop(dy, last, last - 1) for dy in dys]

    bit = 1
    for level in range(last - 1, 0, -1):
        outs = []
        for seq in seqs:
            carries = [message] if level == last - 1 and seq == seq_count - 1 else []
            dy, dpre, *carried = kernel_call(
                functools.partial(back_kernel, level, seq, bins),
                [trunk, inside],
                layer_flops,
                "back",
                waits=outs[-1:] or sent,
                carries=carries,
            )(dys[seq], xs[level][seq], pres[level][seq], weight, point)
            outs.append(dy)
            dpres[level].append(dpre)
        sent = outs
        dys = [hop(dy, level, level - 1) for dy in outs]
        if level == last - 1:
            (message,) = carried
        else:
            bit *= 2
            moving = sorted(key for key in blocks if key[0] & bit)
            if not moving:
                continue
            (message,) = kernel_call(
                functools.partial(message_kernel, [blocks[key][1] for key in moving]),
                [shape(size * len(moving), rows)],
                0,
                "message",
                waits=outs,
            )(*[blocks[key][0] for key in moving])
        message = exchange(message, bit)
        for at, (to, start) in enumerate(moving):
            blocks[to ^ bit, start ^ bit] = (message, at)

    dpre = []
    for seq in seqs:
        dpre = kernel_call(
            functools.partial(head_kernel, sections, seq * bins),
            [shape((seq + 1) * bins, inner)],
            layer_flops // 4,
            "head",
            waits=dpre or sent,
        )(dys[seq], pres[0][seq], point, *[dpres[level][seq] for level in range(1, sections)], *dpre)
    (dpre,) = dpre
    gathered = {offset: exchange(dpre, offset) for offset in range(1, count)}
    columns = [blocks[0, offset] for offset in range(count)]
    share = shape(3, chans // (count * groups), inner, dtype=jnp.float32)
    mine, *others = kernel_call(
        functools.partial(grad_kernel, sections, bins, [at for array, at in columns]),
        [share, *[shape(*share.shape)] * (groups - 1)],
        2 * 3 * rows * chans * inner,
        "grad",
    )(*[array for array, at in columns], dpre, *[gathered[offset] for offset in range(1, count)])
    for step, other in enumerate(others, 1):
        route = [(i, (i + step) % groups) for i in range(groups)]
        mine = mine + lax.ppermute(other, "dp", route).astype(jnp.float32)
    return mine[None]


def solution(mesh):
    def shards(inputs, cotangent, dilated_kernel_weight, point_weight):
        bins = inputs.shape[1]
        first_spread = bins // 2 // 2 ** (mesh.shape["pipe"] - 1)
        count = mesh.shape["ctx"]
        residues = (
            first_spread == count
            and mesh.shape["pipe"] > 1
            and bins % (16 * count) == 0
            and 1 < count == 1 << (count.bit_length() - 1) <= 1 << (mesh.shape["pipe"] - 2)
            and inputs.shape[2] % (count * mesh.shape["dp"]) == 0
        )
        plan = residue_shards if residues else edge_shards
        return plan(inputs, cotangent, dilated_kernel_weight, point_weight)

    return jax.shard_map(
        shards,
        mesh=mesh,
        in_specs=(
            P("dp", "ctx", None),
            P("dp", "ctx", None),
            P("pipe", None, None, None),
            P("pipe", None, None),
        ),
        out_specs=P("pipe", None, ("dp", "ctx"), None),
        check_vma=False,
    )
```

```python
import functools
import math

import jax
import jax.numpy as jnp
from jax import lax
from jax.experimental import pallas as pl
from jax.experimental.pallas import tpu as pltpu
from jax.sharding import PartitionSpec as P

root_half = 0.7071067811865476
inv_root_two_pi = 0.3989422804014327

in_vmem = pl.BlockSpec(memory_space=pltpu.VMEM)
anywhere = pl.BlockSpec(memory_space=pl.ANY)
contract_last = (((1,), (1,)), ((), ()))
contract_first = (((0,), (0,)), ((), ()))


def gelu(value):
    return 0.5 * value * (1.0 + lax.erf(value * root_half))


def gelu_slope(value):
    return (
        0.5 * (1.0 + lax.erf(value * root_half))
        + value * jnp.exp(-0.5 * value * value) * inv_root_two_pi
    )


def padded(cells, sides, width):
    for axis, dim in sides:
        count = lax.axis_size(axis)
        ends = count - 1
        head = lax.slice_in_dim(cells, 0, width, axis=dim)
        tail = lax.slice_in_dim(cells, cells.shape[dim] - width, cells.shape[dim], axis=dim)
        cells = jnp.concatenate(
            [
                lax.ppermute(tail, axis, [(i, (i + 1) % count) for i in range(ends)]),
                cells,
                lax.ppermute(head, axis, [((i + 1) % count, i) for i in range(ends)]),
            ],
            axis=dim,
        )
    return cells


def shifted(block, axis, distance):
    devices = range(lax.axis_size(axis))
    route = [(i - distance, i) for i in devices if i - distance in devices]
    return lax.ppermute(block, axis, route)


def edge_shards(inputs, cotangent, dilated_kernel_weight, point_weight):
    sections = lax.axis_size("pipe")
    section = lax.axis_index("pipe")
    seq_count, bins, chans = inputs.shape
    reach = bins // 2
    table = jnp.array(
        [reach // 2 ** (sections - 1 - level) for level in range(sections)], jnp.int32
    )
    spread = table[section]
    dilation_weight = dilated_kernel_weight[0]
    w_point = point_weight[0]
    inner_channel_count = dilation_weight.shape[2]
    scale = 1.0 / math.sqrt(seq_count * lax.axis_size("dp") * bins * lax.axis_size("ctx"))
    ticks = jnp.arange(seq_count + sections - 1, dtype=jnp.int32)

    def conv_fore(extended):
        running_total = jnp.zeros((bins, inner_channel_count), jnp.float32)
        for kernel_offset in range(3):
            receptive_span = lax.dynamic_slice_in_dim(
                extended, reach + (kernel_offset - 1) * spread, bins, 0
            )
            running_total = running_total + jnp.dot(
                receptive_span, dilation_weight[kernel_offset], preferred_element_type=jnp.float32
            )
        return running_total

    def put(store, slot, valid, item):
        current = lax.dynamic_index_in_dim(store, slot, 0, keepdims=False)
        return lax.dynamic_update_index_in_dim(store, jnp.where(valid, item, current), slot, 0)

    kept_x = jnp.zeros(inputs.shape, jnp.bfloat16)
    kept_ext = jnp.zeros((seq_count, bins + 2 * reach, chans), jnp.bfloat16)
    kept_pre = jnp.zeros((seq_count, bins, inner_channel_count), jnp.float32)

    def fore_tick(carry, tick):
        received, store_x, store_ext, store_pre = carry
        micro = tick - section
        valid = (micro >= 0) & (micro < seq_count)
        slot = jnp.clip(micro, 0, seq_count - 1)
        first = lax.dynamic_index_in_dim(inputs, slot, 0, keepdims=False)
        trunk_in = jnp.where(section == 0, first, received)
        act = gelu(trunk_in.astype(jnp.float32)).astype(jnp.bfloat16)
        extended = padded(act, (("ctx", 0),), reach)
        pre = conv_fore(extended)
        inner = gelu(pre).astype(jnp.bfloat16)
        out = (
            trunk_in.astype(jnp.float32)
            + jnp.dot(inner, w_point, preferred_element_type=jnp.float32)
        ).astype(jnp.bfloat16)
        sent = shifted(out, "pipe", 1)
        store_x = put(store_x, slot, valid, trunk_in)
        store_ext = put(store_ext, slot, valid, extended)
        store_pre = put(store_pre, slot, valid, pre)
        return ((sent, store_x, store_ext, store_pre), None)

    start_recv = jnp.zeros((bins, chans), jnp.bfloat16)
    (unused, kept_x, kept_ext, kept_pre), unused_out = lax.scan(
        fore_tick, (start_recv, kept_x, kept_ext, kept_pre), ticks
    )

    def back_tick(carry, tick):
        received, grad = carry
        micro = tick - (sections - 1 - section)
        valid = (micro >= 0) & (micro < seq_count)
        slot = jnp.clip(micro, 0, seq_count - 1)
        last = (
            lax.dynamic_index_in_dim(cotangent, slot, 0, keepdims=False).astype(jnp.float32) * scale
        ).astype(jnp.bfloat16)
        upstream = jnp.where(section == sections - 1, last, received)
        trunk_in = lax.dynamic_index_in_dim(kept_x, slot, 0, keepdims=False)
        extended = lax.dynamic_index_in_dim(kept_ext, slot, 0, keepdims=False)
        pre = lax.dynamic_index_in_dim(kept_pre, slot, 0, keepdims=False)
        inner_grad = lax.dot_general(
            upstream, w_point, contract_last, preferred_element_type=jnp.float32
        )
        dpre = (inner_grad * gelu_slope(pre) * valid.astype(jnp.float32)).astype(jnp.bfloat16)
        dpre_ext = padded(dpre, (("ctx", 0),), reach)
        dact = jnp.zeros((bins, chans), jnp.float32)
        taps = []
        for kernel_offset in range(3):
            receptive_span = lax.dynamic_slice_in_dim(
                dpre_ext, reach - (kernel_offset - 1) * spread, bins, 0
            )
            dact = dact + lax.dot_general(
                receptive_span,
                dilation_weight[kernel_offset],
                contract_last,
                preferred_element_type=jnp.float32,
            )
            source = lax.dynamic_slice_in_dim(
                extended, reach + (kernel_offset - 1) * spread, bins, 0
            )
            taps.append(
                lax.dot_general(source, dpre, contract_first, preferred_element_type=jnp.float32)
            )
        grad = grad + jnp.stack(taps)
        back = (
            upstream.astype(jnp.float32) + dact * gelu_slope(trunk_in.astype(jnp.float32))
        ).astype(jnp.bfloat16)
        sent = shifted(back, "pipe", -1)
        return ((sent, grad), None)

    start_grad = jnp.zeros((3, chans, inner_channel_count), jnp.float32)
    (unused_back, grad), unused_seq = lax.scan(back_tick, (start_recv, start_grad), ticks)
    term = grad[None]
    return lax.psum_scatter(term, ("dp", "ctx"), scatter_dimension=2, tiled=True)


def moved(value, by, bins):
    pieces = []
    for start in range(0, value.shape[0], bins):
        piece = value[start : start + bins]
        place = lax.broadcasted_iota(jnp.int32, piece.shape, 0)
        if by > 0:
            keep = place >= by
        else:
            keep = place < bins + by
        pieces.append(jnp.where(keep, pltpu.roll(piece, by % bins, 0), 0.0))
    return jnp.concatenate(pieces, axis=0)


def fore(x, weight_ref, spread, bins):
    act = gelu(x.astype(jnp.float32)).astype(jnp.bfloat16)
    terms = [
        jnp.dot(act, weight_ref[0, tap], preferred_element_type=jnp.float32) for tap in range(3)
    ]
    return terms[1] + moved(terms[0], spread, bins) + moved(terms[2], -spread, bins)


def back_pre(dy, pre, point_ref):
    inner_grad = lax.dot_general(
        dy, point_ref[0], contract_last, preferred_element_type=jnp.float32
    )
    return (inner_grad * gelu_slope(pre)).astype(jnp.bfloat16)


def back_trunk(dy, dpre, x, weight_ref, spread, bins):
    wide = dpre.astype(jnp.float32)
    spans = (
        moved(wide, -spread, bins).astype(jnp.bfloat16),
        dpre,
        moved(wide, spread, bins).astype(jnp.bfloat16),
    )
    dact = jnp.zeros(dy.shape, jnp.float32)
    for tap in range(3):
        dact = dact + lax.dot_general(
            spans[tap], weight_ref[0, tap], contract_last, preferred_element_type=jnp.float32
        )
    return (
        dy.astype(jnp.float32) + dact * gelu_slope(x.astype(jnp.float32))
    ).astype(jnp.bfloat16)


def of_seq(ref, seq, bins):
    if ref.shape[0] == bins:
        return ref[...]
    return ref[seq * bins : (seq + 1) * bins, :]


def split_kernel(last, payload_ref, *out_refs):
    count = len(out_refs)
    seq_count, bins, chans = payload_ref.shape
    part = bins // count
    section = lax.axis_index("pipe")
    place = lax.axis_index("ctx")

    @pl.when((section == 0) | (section == last))
    def send():
        source = payload_ref[...].reshape(seq_count * bins, chans)
        row = lax.broadcasted_iota(jnp.int32, (part, seq_count * bins), 0)
        col = lax.broadcasted_iota(jnp.int32, (part, seq_count * bins), 1)
        for hop in range(count):
            residue = lax.rem(place + hop, count)
            rows = [
                (col == seq * bins + count * row + residue).astype(jnp.float32)
                for seq in range(seq_count)
            ]
            pick = jnp.concatenate(rows, axis=0).astype(jnp.bfloat16)
            out_refs[hop][...] = jnp.dot(
                pick, source, preferred_element_type=jnp.float32
            ).astype(jnp.bfloat16)


def hold_kernel(weight_ref, point_ref, weight_out, point_out, sems):
    loads = [
        pltpu.make_async_copy(weight_ref, weight_out, sems.at[0]),
        pltpu.make_async_copy(point_ref, point_out, sems.at[1]),
    ]
    for load in loads:
        load.start()
    for load in loads:
        load.wait()


def first_kernel(last, bins, *refs):
    parts, (weight_ref, point_ref, whole_ref, out_ref, pre_ref) = refs[:-5], refs[-5:]
    count = len(parts)
    section = lax.axis_index("pipe")
    place = lax.axis_index("ctx")
    part = bins // count
    seq_count = whole_ref.shape[0] // bins

    @pl.when((section == 0) | (section == last))
    def gather():
        for back, part_ref in enumerate(parts, 1):
            source = lax.rem(place + back, count)
            for seq in range(seq_count):
                at = pl.multiple_of(seq * bins + source * part, part)
                whole_ref[pl.ds(at, part), :] = part_ref[seq * part : (seq + 1) * part, :]

    @pl.when(section == 0)
    def layer():
        x = whole_ref[:bins, :]
        finish(x, fore(x, weight_ref, 1, bins), point_ref, out_ref, pre_ref)


def finish(x, pre, point_ref, out_ref, pre_ref):
    pre_ref[...] = pre
    branch = jnp.dot(
        gelu(pre).astype(jnp.bfloat16), point_ref[0], preferred_element_type=jnp.float32
    )
    out_ref[...] = (x.astype(jnp.float32) + branch).astype(jnp.bfloat16)


def fore_kernel(level, seq, bins, x_ref, weight_ref, point_ref, out_ref, pre_ref):
    @pl.when(lax.axis_index("pipe") == level)
    def layer():
        x = of_seq(x_ref, seq, bins)
        finish(x, fore(x, weight_ref, 2**level, bins), point_ref, out_ref, pre_ref)


def turn_kernel(level, seq, bins, scale, x_ref, cot_ref, weight_ref, point_ref, dy_ref, dpre_ref):
    @pl.when(lax.axis_index("pipe") == level)
    def layer():
        x = of_seq(x_ref, seq, bins)
        pre = fore(x, weight_ref, 2**level, bins)
        cot = of_seq(cot_ref, seq, bins)
        dy = (cot.astype(jnp.float32) * scale).astype(jnp.bfloat16)
        dpre = back_pre(dy, pre, point_ref)
        dpre_ref[...] = dpre
        dy_ref[...] = back_trunk(dy, dpre, x, weight_ref, 2**level, bins)


def back_kernel(level, seq, bins, dy_in_ref, x_ref, pre_ref, weight_ref, point_ref, dy_ref, dpre_ref):
    @pl.when(lax.axis_index("pipe") == level)
    def layer():
        dy = dy_in_ref[...]
        x = of_seq(x_ref, seq, bins)
        dpre = back_pre(dy, of_seq(pre_ref, seq, bins), point_ref)
        dpre_ref[...] = dpre
        dy_ref[...] = back_trunk(dy, dpre, x, weight_ref, 2**level, bins)


def message_kernel(places, *refs):
    blocks, message_ref = refs[:-1], refs[-1]
    size = message_ref.shape[0] // len(places)
    for to, (ref, at) in enumerate(zip(blocks, places)):
        message_ref[to * size : (to + 1) * size, :] = ref[at * size : (at + 1) * size, :]


def head_kernel(sections, earlier, dy_in_ref, pre_ref, point_ref, *refs):
    others, before, out_ref = refs[: sections - 1], refs[sections - 1 : -1], refs[-1]
    section = lax.axis_index("pipe")
    bins = dy_in_ref.shape[0]
    for ref in before:
        out_ref[:earlier, :] = ref[...]

    @pl.when(section == 0)
    def layer():
        out_ref[earlier : earlier + bins, :] = back_pre(dy_in_ref[...], pre_ref[...], point_ref)

    for level in range(1, sections):

        @pl.when(section == level)
        def keep(level=level):
            out_ref[earlier : earlier + bins, :] = others[level - 1][...]


def columns_kernel(groups, runs, kept, *refs):
    refs, (sent_ref,) = refs[:-1], refs[-1:]
    kept_refs = refs[sum(runs) :]
    count = 2 * len(kept)
    section = lax.axis_index("pipe")
    core = lax.axis_index("dp")
    place = lax.axis_index("ctx")
    x, start = None, 0
    for level, run in enumerate(runs):
        pieces = [ref[...] for ref in refs[start : start + run]]
        start += run
        whole = jnp.concatenate(pieces, axis=0).astype(jnp.float32)
        x = whole if x is None else jnp.where(section == level, whole, x)
    act = gelu(x).astype(jnp.bfloat16)
    chans = act.shape[1]
    width = chans // (groups * count)
    row = lax.broadcasted_iota(jnp.int32, (width, chans), 0)
    col = lax.broadcasted_iota(jnp.int32, (width, chans), 1)

    def block(offset):
        owner = lax.bitwise_xor(place, offset)
        rows = []
        for step in range(groups):
            first = (lax.rem(core + step, groups) * count + owner) * width
            rows.append((col == first + row).astype(jnp.float32))
        pick = jnp.concatenate(rows, axis=0).astype(jnp.bfloat16)
        return lax.dot_general(
            pick, act, contract_last, preferred_element_type=jnp.float32
        ).astype(jnp.bfloat16)

    size = groups * width
    for at, offset in enumerate(kept):
        kept_refs[at][...] = block(offset)
        sent_ref[at * size : (at + 1) * size, :] = block(offset ^ 1)


def grad_kernel(sections, bins, places, *refs):
    columns, refs = refs[: len(places)], refs[len(places) :]
    grads, outs = refs[: len(places)], refs[len(places) :]
    section = lax.axis_index("pipe")
    width = outs[0].shape[1]
    size = len(outs) * width

    def taps(spread):
        act = jnp.concatenate(
            [ref[at * size : (at + 1) * size, :] for ref, at in zip(columns, places)], axis=1
        )
        dpre = jnp.concatenate([ref[...] for ref in grads], axis=0)
        wide = dpre.astype(jnp.float32)
        spans = (
            moved(wide, -spread, bins).astype(jnp.bfloat16),
            dpre,
            moved(wide, spread, bins).astype(jnp.bfloat16),
        )
        for tap in range(3):
            grad = jnp.dot(act, spans[tap], preferred_element_type=jnp.float32)
            for step, out_ref in enumerate(outs):
                out_ref[tap] = grad[step * width : (step + 1) * width].astype(out_ref.dtype)

    for level in range(sections):

        @pl.when(section == level)
        def run(level=level):
            taps(2**level)


def kernel_call(body, outs, flops, name, waits=(), carries=(), in_spec=in_vmem, scratch=()):
    def call(*args):
        used, taken = len(args), len(args) + len(waits) + len(carries)

        def run(*refs):
            made = refs[taken : taken + len(outs)]
            body(*refs[:used], *made, *refs[taken + len(outs) + len(carries) :])

        moved_bytes = sum(math.prod(a.shape) * a.dtype.itemsize for a in (*args, *outs))
        return pl.pallas_call(
            run,
            out_shape=[*outs, *(jax.ShapeDtypeStruct(a.shape, a.dtype) for a in carries)],
            in_specs=[in_spec] * used + [anywhere] * (taken - used),
            out_specs=[in_vmem] * len(outs) + [anywhere] * len(carries),
            input_output_aliases={
                used + len(waits) + at: len(outs) + at for at in range(len(carries))
            },
            scratch_shapes=list(scratch),
            compiler_params=pltpu.CompilerParams(vmem_limit_bytes=24 * 2**20),
            cost_estimate=pl.CostEstimate(
                flops=flops, bytes_accessed=moved_bytes, transcendentals=0
            ),
            name=name,
        )(*args, *waits, *carries)

    return call


def residue_shards(inputs, cotangent, weight, point):
    sections = lax.axis_size("pipe")
    section = lax.axis_index("pipe")
    count = lax.axis_size("ctx")
    groups = lax.axis_size("dp")
    seq_count, bins, chans = inputs.shape
    inner = weight.shape[3]
    rows = seq_count * bins
    scale = 1.0 / math.sqrt(seq_count * groups * bins * count)
    last = sections - 1
    seqs = range(seq_count)
    layer_flops = 2 * bins * chans * inner * 4

    def shape(*dims, dtype=jnp.bfloat16):
        return jax.ShapeDtypeStruct(dims, dtype)

    def hop(value, source, target, third=None):
        sends = {source: target, target: source}
        if third not in (None, source, target):
            sends.update({target: third, third: source})
        route = []
        for core in range(groups):
            for stage in range(sections):
                taker = core if stage in sends else (core + 1) % groups
                for i in range(count):
                    giver = (core * sections + stage) * count + i
                    route.append((giver, (taker * sections + sends.get(stage, stage)) * count + i))
        return lax.ppermute(value, ("dp", "pipe", "ctx"), route)

    def onward(value, step):
        return lax.ppermute(value, "ctx", [(i, (i + step) % count) for i in range(count)])

    def exchange(value, offset):
        return lax.ppermute(value, "ctx", [(i, i ^ offset) for i in range(count)])

    payload = jnp.where(section == last, cotangent, inputs)
    parts = kernel_call(
        functools.partial(split_kernel, last),
        [shape(rows // count, chans)] * count,
        10 * seq_count * layer_flops,
        "split",
    )(payload)
    weight, point = kernel_call(
        hold_kernel,
        [shape(*weight.shape), shape(*point.shape)],
        0,
        "hold",
        waits=[parts[0]],
        in_spec=anywhere,
        scratch=[pltpu.SemaphoreType.DMA((2,))],
    )(weight, point)
    parts = [*(onward(parts[step], step) for step in range(count - 1, 0, -1)), parts[0]]

    trunk, inside = shape(bins, chans), shape(bins, inner)
    inside_wide = shape(bins, inner, dtype=jnp.float32)
    whole, out, pre = kernel_call(
        functools.partial(first_kernel, last, bins),
        [shape(rows, chans), trunk, inside_wide],
        layer_flops,
        "first",
    )(*parts, weight, point)
    outs, pres, xs, sent = [out], [[pre]], [[whole]], ()
    for level in range(last):
        if level > 0:
            xs.append([hop(out, level - 1, level, 0) for out in outs])
            outs = []
            pres.append([])
        for seq in range(len(outs), seq_count):
            out, pre = kernel_call(
                functools.partial(fore_kernel, level, seq, bins),
                [trunk, inside_wide],
                layer_flops,
                "fore",
                waits=outs[-1:] or sent,
            )(xs[level][seq if level else 0], weight, point)
            outs.append(out)
            pres[level].append(pre)
        sent = outs
    xs.append([hop(out, last - 1, last, 0) for out in outs])

    dys, dpres = [], [[] for level in range(sections)]
    for seq in seqs:
        dy, dpre = kernel_call(
            functools.partial(turn_kernel, last, seq, bins, scale),
            [trunk, inside],
            2 * layer_flops,
            "turn",
            waits=dys[-1:] or sent,
        )(xs[last][seq], whole, weight, point)
        dys.append(dy)
        dpres[last].append(dpre)
    kept = list(range(0, count, 2))
    moving = [(offset, 0) for offset in range(1, count, 2)]
    size = chans // count
    *owned, message = kernel_call(
        functools.partial(columns_kernel, groups, [len(x) for x in xs], kept),
        [shape(size, rows)] * len(kept) + [shape(size * len(kept), rows)],
        2 * rows * chans * chans,
        "columns",
        waits=dys,
    )(*[x for some in xs for x in some])
    blocks = {(offset, 0): (array, 0) for offset, array in zip(kept, owned)}
    sent = [owned[0]]
    dys = [hop(dy, last, last - 1) for dy in dys]

    bit = 1
    for level in range(last - 1, 0, -1):
        outs = []
        for seq in seqs:
            carries = [message] if level == last - 1 and seq == seq_count - 1 else []
            dy, dpre, *carried = kernel_call(
                functools.partial(back_kernel, level, seq, bins),
                [trunk, inside],
                layer_flops,
                "back",
                waits=outs[-1:] or sent,
                carries=carries,
            )(dys[seq], xs[level][seq], pres[level][seq], weight, point)
            outs.append(dy)
            dpres[level].append(dpre)
        sent = outs
        dys = [hop(dy, level, level - 1, None if level > 1 else last) for dy in outs]
        if level == last - 1:
            (message,) = carried
        else:
            bit *= 2
            moving = sorted(key for key in blocks if key[0] & bit)
            if not moving:
                continue
            (message,) = kernel_call(
                functools.partial(message_kernel, [blocks[key][1] for key in moving]),
                [shape(size * len(moving), rows)],
                0,
                "message",
                waits=outs,
            )(*[blocks[key][0] for key in moving])
        message = exchange(message, bit)
        for at, (to, start) in enumerate(moving):
            blocks[to ^ bit, start ^ bit] = (message, at)

    dpre = []
    for seq in seqs:
        dpre = kernel_call(
            functools.partial(head_kernel, sections, seq * bins),
            [shape((seq + 1) * bins, inner)],
            layer_flops // 4,
            "head",
            waits=dpre or sent,
        )(dys[seq], pres[0][seq], point, *[dpres[level][seq] for level in range(1, sections)], *dpre)
    (dpre,) = dpre
    far_first = range(count - 1, 0, -1)
    gathered = [*(exchange(dpre, offset) for offset in far_first), dpre]
    columns = [blocks[0, offset] for offset in [*far_first, 0]]
    share = shape(3, chans // (count * groups), inner, dtype=jnp.float32)
    mine, *others = kernel_call(
        functools.partial(grad_kernel, sections, bins, [at for array, at in columns]),
        [share, *[shape(*share.shape)] * (groups - 1)],
        2 * 3 * rows * chans * inner,
        "grad",
    )(*[array for array, at in columns], *gathered)
    for step, other in enumerate(others, 1):
        route = [(i, (i + step) % groups) for i in range(groups)]
        mine = mine + lax.ppermute(other, "dp", route).astype(jnp.float32)
    return mine[None]


def solution(mesh):
    def shards(inputs, cotangent, dilated_kernel_weight, point_weight):
        bins = inputs.shape[1]
        first_spread = bins // 2 // 2 ** (mesh.shape["pipe"] - 1)
        count = mesh.shape["ctx"]
        residues = (
            first_spread == count
            and mesh.shape["pipe"] > 1
            and bins % (16 * count) == 0
            and 1 < count == 1 << (count.bit_length() - 1) <= 1 << (mesh.shape["pipe"] - 2)
            and inputs.shape[2] % (count * mesh.shape["dp"]) == 0
        )
        plan = residue_shards if residues else edge_shards
        return plan(inputs, cotangent, dilated_kernel_weight, point_weight)

    return jax.shard_map(
        shards,
        mesh=mesh,
        in_specs=(
            P("dp", "ctx", None),
            P("dp", "ctx", None),
            P("pipe", None, None, None),
            P("pipe", None, None),
        ),
        out_specs=P("pipe", None, ("dp", "ctx"), None),
        check_vma=False,
    )
```

```python
import functools
import math

import jax
import jax.numpy as jnp
from jax import lax
from jax.experimental import pallas as pl
from jax.experimental.pallas import tpu as pltpu
from jax.sharding import PartitionSpec as P

root_half = 0.7071067811865476
inv_root_two_pi = 0.3989422804014327

in_vmem = pl.BlockSpec(memory_space=pltpu.VMEM)
anywhere = pl.BlockSpec(memory_space=pl.ANY)
contract_last = (((1,), (1,)), ((), ()))
contract_first = (((0,), (0,)), ((), ()))


def gelu(value):
    return 0.5 * value * (1.0 + lax.erf(value * root_half))


def gelu_slope(value):
    return (
        0.5 * (1.0 + lax.erf(value * root_half))
        + value * jnp.exp(-0.5 * value * value) * inv_root_two_pi
    )


def padded(cells, sides, width):
    for axis, dim in sides:
        count = lax.axis_size(axis)
        ends = count - 1
        head = lax.slice_in_dim(cells, 0, width, axis=dim)
        tail = lax.slice_in_dim(cells, cells.shape[dim] - width, cells.shape[dim], axis=dim)
        cells = jnp.concatenate(
            [
                lax.ppermute(tail, axis, [(i, (i + 1) % count) for i in range(ends)]),
                cells,
                lax.ppermute(head, axis, [((i + 1) % count, i) for i in range(ends)]),
            ],
            axis=dim,
        )
    return cells


def shifted(block, axis, distance):
    devices = range(lax.axis_size(axis))
    route = [(i - distance, i) for i in devices if i - distance in devices]
    return lax.ppermute(block, axis, route)


def edge_shards(inputs, cotangent, dilated_kernel_weight, point_weight):
    sections = lax.axis_size("pipe")
    section = lax.axis_index("pipe")
    seq_count, bins, chans = inputs.shape
    reach = bins // 2
    table = jnp.array(
        [reach // 2 ** (sections - 1 - level) for level in range(sections)], jnp.int32
    )
    spread = table[section]
    dilation_weight = dilated_kernel_weight[0]
    w_point = point_weight[0]
    inner_channel_count = dilation_weight.shape[2]
    scale = 1.0 / math.sqrt(seq_count * lax.axis_size("dp") * bins * lax.axis_size("ctx"))
    ticks = jnp.arange(seq_count + sections - 1, dtype=jnp.int32)

    def conv_fore(extended):
        running_total = jnp.zeros((bins, inner_channel_count), jnp.float32)
        for kernel_offset in range(3):
            receptive_span = lax.dynamic_slice_in_dim(
                extended, reach + (kernel_offset - 1) * spread, bins, 0
            )
            running_total = running_total + jnp.dot(
                receptive_span, dilation_weight[kernel_offset], preferred_element_type=jnp.float32
            )
        return running_total

    def put(store, slot, valid, item):
        current = lax.dynamic_index_in_dim(store, slot, 0, keepdims=False)
        return lax.dynamic_update_index_in_dim(store, jnp.where(valid, item, current), slot, 0)

    kept_x = jnp.zeros(inputs.shape, jnp.bfloat16)
    kept_ext = jnp.zeros((seq_count, bins + 2 * reach, chans), jnp.bfloat16)
    kept_pre = jnp.zeros((seq_count, bins, inner_channel_count), jnp.float32)

    def fore_tick(carry, tick):
        received, store_x, store_ext, store_pre = carry
        micro = tick - section
        valid = (micro >= 0) & (micro < seq_count)
        slot = jnp.clip(micro, 0, seq_count - 1)
        first = lax.dynamic_index_in_dim(inputs, slot, 0, keepdims=False)
        trunk_in = jnp.where(section == 0, first, received)
        act = gelu(trunk_in.astype(jnp.float32)).astype(jnp.bfloat16)
        extended = padded(act, (("ctx", 0),), reach)
        pre = conv_fore(extended)
        inner = gelu(pre).astype(jnp.bfloat16)
        out = (
            trunk_in.astype(jnp.float32)
            + jnp.dot(inner, w_point, preferred_element_type=jnp.float32)
        ).astype(jnp.bfloat16)
        sent = shifted(out, "pipe", 1)
        store_x = put(store_x, slot, valid, trunk_in)
        store_ext = put(store_ext, slot, valid, extended)
        store_pre = put(store_pre, slot, valid, pre)
        return ((sent, store_x, store_ext, store_pre), None)

    start_recv = jnp.zeros((bins, chans), jnp.bfloat16)
    (unused, kept_x, kept_ext, kept_pre), unused_out = lax.scan(
        fore_tick, (start_recv, kept_x, kept_ext, kept_pre), ticks
    )

    def back_tick(carry, tick):
        received, grad = carry
        micro = tick - (sections - 1 - section)
        valid = (micro >= 0) & (micro < seq_count)
        slot = jnp.clip(micro, 0, seq_count - 1)
        last = (
            lax.dynamic_index_in_dim(cotangent, slot, 0, keepdims=False).astype(jnp.float32) * scale
        ).astype(jnp.bfloat16)
        upstream = jnp.where(section == sections - 1, last, received)
        trunk_in = lax.dynamic_index_in_dim(kept_x, slot, 0, keepdims=False)
        extended = lax.dynamic_index_in_dim(kept_ext, slot, 0, keepdims=False)
        pre = lax.dynamic_index_in_dim(kept_pre, slot, 0, keepdims=False)
        inner_grad = lax.dot_general(
            upstream, w_point, contract_last, preferred_element_type=jnp.float32
        )
        dpre = (inner_grad * gelu_slope(pre) * valid.astype(jnp.float32)).astype(jnp.bfloat16)
        dpre_ext = padded(dpre, (("ctx", 0),), reach)
        dact = jnp.zeros((bins, chans), jnp.float32)
        taps = []
        for kernel_offset in range(3):
            receptive_span = lax.dynamic_slice_in_dim(
                dpre_ext, reach - (kernel_offset - 1) * spread, bins, 0
            )
            dact = dact + lax.dot_general(
                receptive_span,
                dilation_weight[kernel_offset],
                contract_last,
                preferred_element_type=jnp.float32,
            )
            source = lax.dynamic_slice_in_dim(
                extended, reach + (kernel_offset - 1) * spread, bins, 0
            )
            taps.append(
                lax.dot_general(source, dpre, contract_first, preferred_element_type=jnp.float32)
            )
        grad = grad + jnp.stack(taps)
        back = (
            upstream.astype(jnp.float32) + dact * gelu_slope(trunk_in.astype(jnp.float32))
        ).astype(jnp.bfloat16)
        sent = shifted(back, "pipe", -1)
        return ((sent, grad), None)

    start_grad = jnp.zeros((3, chans, inner_channel_count), jnp.float32)
    (unused_back, grad), unused_seq = lax.scan(back_tick, (start_recv, start_grad), ticks)
    term = grad[None]
    return lax.psum_scatter(term, ("dp", "ctx"), scatter_dimension=2, tiled=True)


def moved(value, by, bins):
    pieces = []
    for start in range(0, value.shape[0], bins):
        piece = value[start : start + bins]
        place = lax.broadcasted_iota(jnp.int32, piece.shape, 0)
        if by > 0:
            keep = place >= by
        else:
            keep = place < bins + by
        pieces.append(jnp.where(keep, pltpu.roll(piece, by % bins, 0), 0.0))
    return jnp.concatenate(pieces, axis=0)


def fore(x, weight_ref, spread, bins):
    act = gelu(x.astype(jnp.float32)).astype(jnp.bfloat16)
    terms = [
        jnp.dot(act, weight_ref[0, tap], preferred_element_type=jnp.float32) for tap in range(3)
    ]
    return terms[1] + moved(terms[0], spread, bins) + moved(terms[2], -spread, bins)


def back_pre(dy, pre, point_ref):
    inner_grad = lax.dot_general(
        dy, point_ref[0], contract_last, preferred_element_type=jnp.float32
    )
    return (inner_grad * gelu_slope(pre)).astype(jnp.bfloat16)


def back_trunk(dy, dpre, x, weight_ref, spread, bins):
    wide = dpre.astype(jnp.float32)
    spans = (
        moved(wide, -spread, bins).astype(jnp.bfloat16),
        dpre,
        moved(wide, spread, bins).astype(jnp.bfloat16),
    )
    dact = jnp.zeros(dy.shape, jnp.float32)
    for tap in range(3):
        dact = dact + lax.dot_general(
            spans[tap], weight_ref[0, tap], contract_last, preferred_element_type=jnp.float32
        )
    return (
        dy.astype(jnp.float32) + dact * gelu_slope(x.astype(jnp.float32))
    ).astype(jnp.bfloat16)


def of_seq(ref, seq, bins):
    if ref.shape[0] == bins:
        return ref[...]
    return ref[seq * bins : (seq + 1) * bins, :]


def split_kernel(last, payload_ref, *out_refs):
    count = len(out_refs)
    seq_count, bins, chans = payload_ref.shape
    part = bins // count
    section = lax.axis_index("pipe")
    place = lax.axis_index("ctx")

    @pl.when((section == 0) | (section == last))
    def send():
        source = payload_ref[...].reshape(seq_count * bins, chans)
        row = lax.broadcasted_iota(jnp.int32, (part, seq_count * bins), 0)
        col = lax.broadcasted_iota(jnp.int32, (part, seq_count * bins), 1)
        for hop in range(count):
            residue = lax.rem(place + hop, count)
            rows = [
                (col == seq * bins + count * row + residue).astype(jnp.float32)
                for seq in range(seq_count)
            ]
            pick = jnp.concatenate(rows, axis=0).astype(jnp.bfloat16)
            out_refs[hop][...] = jnp.dot(
                pick, source, preferred_element_type=jnp.float32
            ).astype(jnp.bfloat16)


def hold_kernel(weight_ref, point_ref, weight_out, point_out, sems):
    loads = [
        pltpu.make_async_copy(weight_ref, weight_out, sems.at[0]),
        pltpu.make_async_copy(point_ref, point_out, sems.at[1]),
    ]
    for load in loads:
        load.start()
    for load in loads:
        load.wait()


def first_kernel(last, bins, *refs):
    parts, (weight_ref, point_ref, whole_ref, out_ref, pre_ref) = refs[:-5], refs[-5:]
    count = len(parts)
    section = lax.axis_index("pipe")
    place = lax.axis_index("ctx")
    part = bins // count
    seq_count = whole_ref.shape[0] // bins

    @pl.when((section == 0) | (section == last))
    def gather():
        for back, part_ref in enumerate(parts, 1):
            source = lax.rem(place + back, count)
            for seq in range(seq_count):
                at = pl.multiple_of(seq * bins + source * part, part)
                whole_ref[pl.ds(at, part), :] = part_ref[seq * part : (seq + 1) * part, :]

    @pl.when(section == 0)
    def layer():
        x = whole_ref[:bins, :]
        finish(x, fore(x, weight_ref, 1, bins), point_ref, out_ref, pre_ref)


def finish(x, pre, point_ref, out_ref, pre_ref):
    pre_ref[...] = pre
    branch = jnp.dot(
        gelu(pre).astype(jnp.bfloat16), point_ref[0], preferred_element_type=jnp.float32
    )
    out_ref[...] = (x.astype(jnp.float32) + branch).astype(jnp.bfloat16)


def fore_kernel(level, seq, bins, x_ref, weight_ref, point_ref, out_ref, pre_ref):
    @pl.when(lax.axis_index("pipe") == level)
    def layer():
        x = of_seq(x_ref, seq, bins)
        finish(x, fore(x, weight_ref, 2**level, bins), point_ref, out_ref, pre_ref)


def turn_kernel(level, seq, bins, scale, x_ref, cot_ref, weight_ref, point_ref, dy_ref, dpre_ref):
    @pl.when(lax.axis_index("pipe") == level)
    def layer():
        x = of_seq(x_ref, seq, bins)
        pre = fore(x, weight_ref, 2**level, bins)
        cot = of_seq(cot_ref, seq, bins)
        dy = (cot.astype(jnp.float32) * scale).astype(jnp.bfloat16)
        dpre = back_pre(dy, pre, point_ref)
        dpre_ref[...] = dpre
        dy_ref[...] = back_trunk(dy, dpre, x, weight_ref, 2**level, bins)


def back_kernel(level, seq, bins, dy_in_ref, x_ref, pre_ref, weight_ref, point_ref, dy_ref, dpre_ref):
    @pl.when(lax.axis_index("pipe") == level)
    def layer():
        dy = dy_in_ref[...]
        x = of_seq(x_ref, seq, bins)
        dpre = back_pre(dy, of_seq(pre_ref, seq, bins), point_ref)
        dpre_ref[...] = dpre
        dy_ref[...] = back_trunk(dy, dpre, x, weight_ref, 2**level, bins)


def message_kernel(places, *refs):
    blocks, message_ref = refs[:-1], refs[-1]
    size = message_ref.shape[0] // len(places)
    for to, (ref, at) in enumerate(zip(blocks, places)):
        message_ref[to * size : (to + 1) * size, :] = ref[at * size : (at + 1) * size, :]


def head_kernel(sections, earlier, dy_in_ref, pre_ref, point_ref, *refs):
    others, before, out_ref = refs[: sections - 1], refs[sections - 1 : -1], refs[-1]
    section = lax.axis_index("pipe")
    bins = dy_in_ref.shape[0]
    for ref in before:
        out_ref[:earlier, :] = ref[...]

    @pl.when(section == 0)
    def layer():
        out_ref[earlier : earlier + bins, :] = back_pre(dy_in_ref[...], pre_ref[...], point_ref)

    for level in range(1, sections):

        @pl.when(section == level)
        def keep(level=level):
            out_ref[earlier : earlier + bins, :] = others[level - 1][...]


def columns_kernel(groups, runs, kept, *refs):
    refs, (sent_ref,) = refs[:-1], refs[-1:]
    kept_refs = refs[sum(runs) :]
    count = 2 * len(kept)
    section = lax.axis_index("pipe")
    core = lax.axis_index("dp")
    place = lax.axis_index("ctx")
    x, start = None, 0
    for level, run in enumerate(runs):
        pieces = [ref[...] for ref in refs[start : start + run]]
        start += run
        whole = jnp.concatenate(pieces, axis=0).astype(jnp.float32)
        x = whole if x is None else jnp.where(section == level, whole, x)
    act = gelu(x).astype(jnp.bfloat16)
    chans = act.shape[1]
    width = chans // (groups * count)
    row = lax.broadcasted_iota(jnp.int32, (width, chans), 0)
    col = lax.broadcasted_iota(jnp.int32, (width, chans), 1)

    def block(offset):
        owner = lax.bitwise_xor(place, offset)
        rows = []
        for step in range(groups):
            first = (lax.rem(core + step, groups) * count + owner) * width
            rows.append((col == first + row).astype(jnp.float32))
        pick = jnp.concatenate(rows, axis=0).astype(jnp.bfloat16)
        return lax.dot_general(
            pick, act, contract_last, preferred_element_type=jnp.float32
        ).astype(jnp.bfloat16)

    size = groups * width
    for at, offset in enumerate(kept):
        kept_refs[at][...] = block(offset)
        sent_ref[at * size : (at + 1) * size, :] = block(offset ^ 1)


def grad_kernel(sections, bins, places, *refs):
    columns, refs = refs[: len(places)], refs[len(places) :]
    grads, outs = refs[: len(places)], refs[len(places) :]
    section = lax.axis_index("pipe")
    width = outs[0].shape[1]
    size = len(outs) * width

    def taps(spread):
        act = jnp.concatenate(
            [ref[at * size : (at + 1) * size, :] for ref, at in zip(columns, places)], axis=1
        )
        dpre = jnp.concatenate([ref[...] for ref in grads], axis=0)
        wide = dpre.astype(jnp.float32)
        spans = (
            moved(wide, -spread, bins).astype(jnp.bfloat16),
            dpre,
            moved(wide, spread, bins).astype(jnp.bfloat16),
        )
        for tap in range(3):
            grad = jnp.dot(act, spans[tap], preferred_element_type=jnp.float32)
            for step, out_ref in enumerate(outs):
                out_ref[tap] = grad[step * width : (step + 1) * width].astype(out_ref.dtype)

    for level in range(sections):

        @pl.when(section == level)
        def run(level=level):
            taps(2**level)


def kernel_call(body, outs, flops, name, waits=(), carries=(), in_spec=in_vmem, scratch=()):
    def call(*args):
        used, taken = len(args), len(args) + len(waits) + len(carries)

        def run(*refs):
            made = refs[taken : taken + len(outs)]
            body(*refs[:used], *made, *refs[taken + len(outs) + len(carries) :])

        moved_bytes = sum(math.prod(a.shape) * a.dtype.itemsize for a in (*args, *outs))
        return pl.pallas_call(
            run,
            out_shape=[*outs, *(jax.ShapeDtypeStruct(a.shape, a.dtype) for a in carries)],
            in_specs=[in_spec] * used + [anywhere] * (taken - used),
            out_specs=[in_vmem] * len(outs) + [anywhere] * len(carries),
            input_output_aliases={
                used + len(waits) + at: len(outs) + at for at in range(len(carries))
            },
            scratch_shapes=list(scratch),
            compiler_params=pltpu.CompilerParams(vmem_limit_bytes=24 * 2**20),
            cost_estimate=pl.CostEstimate(
                flops=flops, bytes_accessed=moved_bytes, transcendentals=0
            ),
            name=name,
        )(*args, *waits, *carries)

    return call


def residue_shards(inputs, cotangent, weight, point):
    sections = lax.axis_size("pipe")
    section = lax.axis_index("pipe")
    count = lax.axis_size("ctx")
    groups = lax.axis_size("dp")
    seq_count, bins, chans = inputs.shape
    inner = weight.shape[3]
    rows = seq_count * bins
    scale = 1.0 / math.sqrt(seq_count * groups * bins * count)
    last = sections - 1
    seqs = range(seq_count)
    layer_flops = 2 * bins * chans * inner * 4

    def shape(*dims, dtype=jnp.bfloat16):
        return jax.ShapeDtypeStruct(dims, dtype)

    def hop(value, source, target, third=None):
        sends = {source: target, target: source}
        if third not in (None, source, target):
            sends.update({target: third, third: source})
        route = []
        for core in range(groups):
            for stage in range(sections):
                taker = core if stage in sends else (core + 1) % groups
                for i in range(count):
                    giver = (core * sections + stage) * count + i
                    route.append((giver, (taker * sections + sends.get(stage, stage)) * count + i))
        return lax.ppermute(value, ("dp", "pipe", "ctx"), route)

    def onward(value, step):
        return lax.ppermute(value, "ctx", [(i, (i + step) % count) for i in range(count)])

    def exchange(value, offset):
        return lax.ppermute(value, "ctx", [(i, i ^ offset) for i in range(count)])

    payload = jnp.where(section == last, cotangent, inputs)
    parts = kernel_call(
        functools.partial(split_kernel, last),
        [shape(rows // count, chans)] * count,
        10 * seq_count * layer_flops,
        "split",
    )(payload)
    weight, point = kernel_call(
        hold_kernel,
        [shape(*weight.shape), shape(*point.shape)],
        0,
        "hold",
        waits=[parts[0]],
        in_spec=anywhere,
        scratch=[pltpu.SemaphoreType.DMA((2,))],
    )(weight, point)
    parts = [*(onward(parts[step], step) for step in range(count - 1, 0, -1)), parts[0]]

    trunk, inside = shape(bins, chans), shape(bins, inner)
    inside_wide = shape(bins, inner, dtype=jnp.float32)
    whole, out, pre = kernel_call(
        functools.partial(first_kernel, last, bins),
        [shape(rows, chans), trunk, inside_wide],
        layer_flops,
        "first",
    )(*parts, weight, point)
    outs, pres, xs, sent = [out], [[pre]], [[whole]], ()
    for level in range(last):
        if level > 0:
            xs.append([hop(out, level - 1, level, 0) for out in outs])
            outs = []
            pres.append([])
        for seq in range(len(outs), seq_count):
            out, pre = kernel_call(
                functools.partial(fore_kernel, level, seq, bins),
                [trunk, inside_wide],
                layer_flops,
                "fore",
                waits=outs[-1:] or sent,
            )(xs[level][seq if level else 0], weight, point)
            outs.append(out)
            pres[level].append(pre)
        sent = outs
    xs.append([hop(out, last - 1, last, 0) for out in outs])

    dys, dpres = [], [[] for level in range(sections)]
    for seq in seqs:
        dy, dpre = kernel_call(
            functools.partial(turn_kernel, last, seq, bins, scale),
            [trunk, inside],
            2 * layer_flops,
            "turn",
            waits=dys[-1:] or sent,
        )(xs[last][seq], whole, weight, point)
        dys.append(dy)
        dpres[last].append(dpre)
    kept = list(range(0, count, 2))
    moving = [(offset, 0) for offset in range(1, count, 2)]
    size = chans // count
    *owned, message = kernel_call(
        functools.partial(columns_kernel, groups, [len(x) for x in xs], kept),
        [shape(size, rows)] * len(kept) + [shape(size * len(kept), rows)],
        2 * rows * chans * chans,
        "columns",
        waits=dys,
    )(*[x for some in xs for x in some])
    blocks = {(offset, 0): (array, 0) for offset, array in zip(kept, owned)}
    sent = [owned[0]]
    dys = [hop(dy, last, last - 1) for dy in dys]
    message, bit = exchange(message, 1), 1
    blocks.update({(to ^ 1, start ^ 1): (message, at) for at, (to, start) in enumerate(moving)})

    for level in range(last - 1, 0, -1):
        outs = []
        for seq in seqs:
            dy, dpre = kernel_call(
                functools.partial(back_kernel, level, seq, bins),
                [trunk, inside],
                layer_flops,
                "back",
                waits=outs[-1:] or sent,
            )(dys[seq], xs[level][seq], pres[level][seq], weight, point)
            outs.append(dy)
            dpres[level].append(dpre)
        sent = outs
        dys = [hop(dy, level, level - 1, None if level > 1 else last) for dy in outs]
        bit *= 2
        moving = sorted(key for key in blocks if key[0] & bit)
        if moving:
            (message,) = kernel_call(
                functools.partial(message_kernel, [blocks[key][1] for key in moving]),
                [shape(size * len(moving), rows)],
                0,
                "message",
                waits=outs,
            )(*[blocks[key][0] for key in moving])
            sent = [*outs, message]
            message = exchange(message, bit)
            for at, (to, start) in enumerate(moving):
                blocks[to ^ bit, start ^ bit] = (message, at)

    sent = [*sent, message]
    dpre = []
    for seq in seqs:
        dpre = kernel_call(
            functools.partial(head_kernel, sections, seq * bins),
            [shape((seq + 1) * bins, inner)],
            layer_flops // 4,
            "head",
            waits=dpre or sent,
        )(dys[seq], pres[0][seq], point, *[dpres[level][seq] for level in range(1, sections)], *dpre)
    (dpre,) = dpre
    far_first = range(count - 1, 0, -1)
    gathered = [*(exchange(dpre, offset) for offset in far_first), dpre]
    columns = [blocks[0, offset] for offset in [*far_first, 0]]
    share = shape(3, chans // (count * groups), inner, dtype=jnp.float32)
    mine, *others = kernel_call(
        functools.partial(grad_kernel, sections, bins, [at for array, at in columns]),
        [share, *[shape(*share.shape)] * (groups - 1)],
        2 * 3 * rows * chans * inner,
        "grad",
    )(*[array for array, at in columns], *gathered)
    for step, other in enumerate(others, 1):
        route = [(i, (i + step) % groups) for i in range(groups)]
        mine = mine + lax.ppermute(other, "dp", route).astype(jnp.float32)
    return mine[None]


def solution(mesh):
    def shards(inputs, cotangent, dilated_kernel_weight, point_weight):
        bins = inputs.shape[1]
        first_spread = bins // 2 // 2 ** (mesh.shape["pipe"] - 1)
        count = mesh.shape["ctx"]
        residues = (
            first_spread == count
            and mesh.shape["pipe"] > 1
            and bins % (16 * count) == 0
            and 1 < count == 1 << (count.bit_length() - 1) <= 1 << (mesh.shape["pipe"] - 2)
            and inputs.shape[2] % (count * mesh.shape["dp"]) == 0
        )
        plan = residue_shards if residues else edge_shards
        return plan(inputs, cotangent, dilated_kernel_weight, point_weight)

    return jax.shard_map(
        shards,
        mesh=mesh,
        in_specs=(
            P("dp", "ctx", None),
            P("dp", "ctx", None),
            P("pipe", None, None, None),
            P("pipe", None, None),
        ),
        out_specs=P("pipe", None, ("dp", "ctx"), None),
        check_vma=False,
    )
```

```python
import functools
import math

import jax
import jax.numpy as jnp
from jax import lax
from jax.experimental import pallas as pl
from jax.experimental.pallas import tpu as pltpu
from jax.sharding import PartitionSpec as P

root_half = 0.7071067811865476
inv_root_two_pi = 0.3989422804014327

in_vmem = pl.BlockSpec(memory_space=pltpu.VMEM)
anywhere = pl.BlockSpec(memory_space=pl.ANY)
contract_last = (((1,), (1,)), ((), ()))
contract_first = (((0,), (0,)), ((), ()))


def gelu(value):
    return 0.5 * value * (1.0 + lax.erf(value * root_half))


def gelu_slope(value):
    return (
        0.5 * (1.0 + lax.erf(value * root_half))
        + value * jnp.exp(-0.5 * value * value) * inv_root_two_pi
    )


def padded(cells, sides, width):
    for axis, dim in sides:
        count = lax.axis_size(axis)
        ends = count - 1
        head = lax.slice_in_dim(cells, 0, width, axis=dim)
        tail = lax.slice_in_dim(cells, cells.shape[dim] - width, cells.shape[dim], axis=dim)
        cells = jnp.concatenate(
            [
                lax.ppermute(tail, axis, [(i, (i + 1) % count) for i in range(ends)]),
                cells,
                lax.ppermute(head, axis, [((i + 1) % count, i) for i in range(ends)]),
            ],
            axis=dim,
        )
    return cells


def shifted(block, axis, distance):
    devices = range(lax.axis_size(axis))
    route = [(i - distance, i) for i in devices if i - distance in devices]
    return lax.ppermute(block, axis, route)


def edge_shards(inputs, cotangent, dilated_kernel_weight, point_weight):
    sections = lax.axis_size("pipe")
    section = lax.axis_index("pipe")
    seq_count, bins, chans = inputs.shape
    reach = bins // 2
    table = jnp.array(
        [reach // 2 ** (sections - 1 - level) for level in range(sections)], jnp.int32
    )
    spread = table[section]
    dilation_weight = dilated_kernel_weight[0]
    w_point = point_weight[0]
    inner_channel_count = dilation_weight.shape[2]
    scale = 1.0 / math.sqrt(seq_count * lax.axis_size("dp") * bins * lax.axis_size("ctx"))
    ticks = jnp.arange(seq_count + sections - 1, dtype=jnp.int32)

    def conv_fore(extended):
        running_total = jnp.zeros((bins, inner_channel_count), jnp.float32)
        for kernel_offset in range(3):
            receptive_span = lax.dynamic_slice_in_dim(
                extended, reach + (kernel_offset - 1) * spread, bins, 0
            )
            running_total = running_total + jnp.dot(
                receptive_span, dilation_weight[kernel_offset], preferred_element_type=jnp.float32
            )
        return running_total

    def put(store, slot, valid, item):
        current = lax.dynamic_index_in_dim(store, slot, 0, keepdims=False)
        return lax.dynamic_update_index_in_dim(store, jnp.where(valid, item, current), slot, 0)

    kept_x = jnp.zeros(inputs.shape, jnp.bfloat16)
    kept_ext = jnp.zeros((seq_count, bins + 2 * reach, chans), jnp.bfloat16)
    kept_pre = jnp.zeros((seq_count, bins, inner_channel_count), jnp.float32)

    def fore_tick(carry, tick):
        received, store_x, store_ext, store_pre = carry
        micro = tick - section
        valid = (micro >= 0) & (micro < seq_count)
        slot = jnp.clip(micro, 0, seq_count - 1)
        first = lax.dynamic_index_in_dim(inputs, slot, 0, keepdims=False)
        trunk_in = jnp.where(section == 0, first, received)
        act = gelu(trunk_in.astype(jnp.float32)).astype(jnp.bfloat16)
        extended = padded(act, (("ctx", 0),), reach)
        pre = conv_fore(extended)
        inner = gelu(pre).astype(jnp.bfloat16)
        out = (
            trunk_in.astype(jnp.float32)
            + jnp.dot(inner, w_point, preferred_element_type=jnp.float32)
        ).astype(jnp.bfloat16)
        sent = shifted(out, "pipe", 1)
        store_x = put(store_x, slot, valid, trunk_in)
        store_ext = put(store_ext, slot, valid, extended)
        store_pre = put(store_pre, slot, valid, pre)
        return ((sent, store_x, store_ext, store_pre), None)

    start_recv = jnp.zeros((bins, chans), jnp.bfloat16)
    (unused, kept_x, kept_ext, kept_pre), unused_out = lax.scan(
        fore_tick, (start_recv, kept_x, kept_ext, kept_pre), ticks
    )

    def back_tick(carry, tick):
        received, grad = carry
        micro = tick - (sections - 1 - section)
        valid = (micro >= 0) & (micro < seq_count)
        slot = jnp.clip(micro, 0, seq_count - 1)
        last = (
            lax.dynamic_index_in_dim(cotangent, slot, 0, keepdims=False).astype(jnp.float32) * scale
        ).astype(jnp.bfloat16)
        upstream = jnp.where(section == sections - 1, last, received)
        trunk_in = lax.dynamic_index_in_dim(kept_x, slot, 0, keepdims=False)
        extended = lax.dynamic_index_in_dim(kept_ext, slot, 0, keepdims=False)
        pre = lax.dynamic_index_in_dim(kept_pre, slot, 0, keepdims=False)
        inner_grad = lax.dot_general(
            upstream, w_point, contract_last, preferred_element_type=jnp.float32
        )
        dpre = (inner_grad * gelu_slope(pre) * valid.astype(jnp.float32)).astype(jnp.bfloat16)
        dpre_ext = padded(dpre, (("ctx", 0),), reach)
        dact = jnp.zeros((bins, chans), jnp.float32)
        taps = []
        for kernel_offset in range(3):
            receptive_span = lax.dynamic_slice_in_dim(
                dpre_ext, reach - (kernel_offset - 1) * spread, bins, 0
            )
            dact = dact + lax.dot_general(
                receptive_span,
                dilation_weight[kernel_offset],
                contract_last,
                preferred_element_type=jnp.float32,
            )
            source = lax.dynamic_slice_in_dim(
                extended, reach + (kernel_offset - 1) * spread, bins, 0
            )
            taps.append(
                lax.dot_general(source, dpre, contract_first, preferred_element_type=jnp.float32)
            )
        grad = grad + jnp.stack(taps)
        back = (
            upstream.astype(jnp.float32) + dact * gelu_slope(trunk_in.astype(jnp.float32))
        ).astype(jnp.bfloat16)
        sent = shifted(back, "pipe", -1)
        return ((sent, grad), None)

    start_grad = jnp.zeros((3, chans, inner_channel_count), jnp.float32)
    (unused_back, grad), unused_seq = lax.scan(back_tick, (start_recv, start_grad), ticks)
    term = grad[None]
    return lax.psum_scatter(term, ("dp", "ctx"), scatter_dimension=2, tiled=True)


def moved(value, by, bins):
    pieces = []
    for start in range(0, value.shape[0], bins):
        piece = value[start : start + bins]
        place = lax.broadcasted_iota(jnp.int32, piece.shape, 0)
        if by > 0:
            keep = place >= by
        else:
            keep = place < bins + by
        pieces.append(jnp.where(keep, pltpu.roll(piece, by % bins, 0), 0.0))
    return jnp.concatenate(pieces, axis=0)


def fore(x, weight_ref, spread, bins):
    act = gelu(x.astype(jnp.float32)).astype(jnp.bfloat16)
    terms = [
        jnp.dot(act, weight_ref[0, tap], preferred_element_type=jnp.float32) for tap in range(3)
    ]
    return terms[1] + moved(terms[0], spread, bins) + moved(terms[2], -spread, bins)


def back_pre(dy, pre, point_ref):
    inner_grad = lax.dot_general(
        dy, point_ref[0], contract_last, preferred_element_type=jnp.float32
    )
    return (inner_grad * gelu_slope(pre)).astype(jnp.bfloat16)


def back_trunk(dy, dpre, x, weight_ref, spread, bins):
    wide = dpre.astype(jnp.float32)
    spans = (
        moved(wide, -spread, bins).astype(jnp.bfloat16),
        dpre,
        moved(wide, spread, bins).astype(jnp.bfloat16),
    )
    dact = jnp.zeros(dy.shape, jnp.float32)
    for tap in range(3):
        dact = dact + lax.dot_general(
            spans[tap], weight_ref[0, tap], contract_last, preferred_element_type=jnp.float32
        )
    return (
        dy.astype(jnp.float32) + dact * gelu_slope(x.astype(jnp.float32))
    ).astype(jnp.bfloat16)


def of_seq(ref, seq, bins):
    if ref.shape[0] == bins:
        return ref[...]
    return ref[seq * bins : (seq + 1) * bins, :]


def split_kernel(last, payload_ref, *out_refs):
    count = len(out_refs)
    seq_count, bins, chans = payload_ref.shape
    part = bins // count
    section = lax.axis_index("pipe")
    place = lax.axis_index("ctx")

    @pl.when((section == 0) | (section == last))
    def send():
        source = payload_ref[...].reshape(seq_count * bins, chans)
        row = lax.broadcasted_iota(jnp.int32, (part, seq_count * bins), 0)
        col = lax.broadcasted_iota(jnp.int32, (part, seq_count * bins), 1)
        for hop in range(count):
            residue = lax.rem(place + hop, count)
            rows = [
                (col == seq * bins + count * row + residue).astype(jnp.float32)
                for seq in range(seq_count)
            ]
            pick = jnp.concatenate(rows, axis=0).astype(jnp.bfloat16)
            out_refs[hop][...] = jnp.dot(
                pick, source, preferred_element_type=jnp.float32
            ).astype(jnp.bfloat16)


def hold_kernel(weight_ref, point_ref, weight_out, point_out, sems):
    loads = [
        pltpu.make_async_copy(weight_ref, weight_out, sems.at[0]),
        pltpu.make_async_copy(point_ref, point_out, sems.at[1]),
    ]
    for load in loads:
        load.start()
    for load in loads:
        load.wait()


def first_kernel(last, bins, *refs):
    parts, (weight_ref, point_ref, whole_ref, out_ref, pre_ref) = refs[:-5], refs[-5:]
    count = len(parts)
    section = lax.axis_index("pipe")
    place = lax.axis_index("ctx")
    part = bins // count
    seq_count = whole_ref.shape[0] // bins

    @pl.when((section == 0) | (section == last))
    def gather():
        for back, part_ref in enumerate(parts, 1):
            source = lax.rem(place + back, count)
            for seq in range(seq_count):
                at = pl.multiple_of(seq * bins + source * part, part)
                whole_ref[pl.ds(at, part), :] = part_ref[seq * part : (seq + 1) * part, :]

    @pl.when(section == 0)
    def layer():
        x = whole_ref[:bins, :]
        finish(x, fore(x, weight_ref, 1, bins), point_ref, out_ref, pre_ref)


def finish(x, pre, point_ref, out_ref, pre_ref):
    pre_ref[...] = pre
    branch = jnp.dot(
        gelu(pre).astype(jnp.bfloat16), point_ref[0], preferred_element_type=jnp.float32
    )
    out_ref[...] = (x.astype(jnp.float32) + branch).astype(jnp.bfloat16)


def fore_kernel(level, seq, bins, x_ref, weight_ref, point_ref, out_ref, pre_ref):
    @pl.when(lax.axis_index("pipe") == level)
    def layer():
        x = of_seq(x_ref, seq, bins)
        finish(x, fore(x, weight_ref, 2**level, bins), point_ref, out_ref, pre_ref)


def turn_kernel(level, seq, bins, scale, x_ref, cot_ref, weight_ref, point_ref, dy_ref, dpre_ref):
    @pl.when(lax.axis_index("pipe") == level)
    def layer():
        x = of_seq(x_ref, seq, bins)
        pre = fore(x, weight_ref, 2**level, bins)
        cot = of_seq(cot_ref, seq, bins)
        dy = (cot.astype(jnp.float32) * scale).astype(jnp.bfloat16)
        dpre = back_pre(dy, pre, point_ref)
        dpre_ref[...] = dpre
        dy_ref[...] = back_trunk(dy, dpre, x, weight_ref, 2**level, bins)


def back_kernel(level, seq, bins, dy_in_ref, x_ref, pre_ref, weight_ref, point_ref, dy_ref, dpre_ref):
    @pl.when(lax.axis_index("pipe") == level)
    def layer():
        dy = dy_in_ref[...]
        x = of_seq(x_ref, seq, bins)
        dpre = back_pre(dy, of_seq(pre_ref, seq, bins), point_ref)
        dpre_ref[...] = dpre
        dy_ref[...] = back_trunk(dy, dpre, x, weight_ref, 2**level, bins)


def message_kernel(places, *refs):
    blocks, message_ref = refs[:-1], refs[-1]
    size = message_ref.shape[0] // len(places)
    for to, (ref, at) in enumerate(zip(blocks, places)):
        message_ref[to * size : (to + 1) * size, :] = ref[at * size : (at + 1) * size, :]


def head_kernel(sections, earlier, dy_in_ref, pre_ref, point_ref, *refs):
    others, before, out_ref = refs[: sections - 1], refs[sections - 1 : -1], refs[-1]
    section = lax.axis_index("pipe")
    bins = dy_in_ref.shape[0]
    for ref in before:
        out_ref[:earlier, :] = ref[...]

    @pl.when(section == 0)
    def layer():
        out_ref[earlier : earlier + bins, :] = back_pre(dy_in_ref[...], pre_ref[...], point_ref)

    for level in range(1, sections):

        @pl.when(section == level)
        def keep(level=level):
            out_ref[earlier : earlier + bins, :] = others[level - 1][...]


def columns_kernel(groups, runs, kept, *refs):
    refs, (sent_ref,) = refs[:-1], refs[-1:]
    kept_refs = refs[sum(runs) :]
    count = 2 * len(kept)
    section = lax.axis_index("pipe")
    core = lax.axis_index("dp")
    place = lax.axis_index("ctx")
    x, start = None, 0
    for level, run in enumerate(runs):
        pieces = [ref[...] for ref in refs[start : start + run]]
        start += run
        whole = jnp.concatenate(pieces, axis=0).astype(jnp.float32)
        x = whole if x is None else jnp.where(section == level, whole, x)
    act = gelu(x).astype(jnp.bfloat16)
    chans = act.shape[1]
    width = chans // (groups * count)
    row = lax.broadcasted_iota(jnp.int32, (width, chans), 0)
    col = lax.broadcasted_iota(jnp.int32, (width, chans), 1)

    def block(offset):
        owner = lax.bitwise_xor(place, offset)
        rows = []
        for step in range(groups):
            first = (lax.rem(core + step, groups) * count + owner) * width
            rows.append((col == first + row).astype(jnp.float32))
        pick = jnp.concatenate(rows, axis=0).astype(jnp.bfloat16)
        return lax.dot_general(
            pick, act, contract_last, preferred_element_type=jnp.float32
        ).astype(jnp.bfloat16)

    size = groups * width
    for at, offset in enumerate(kept):
        kept_refs[at][...] = block(offset)
        sent_ref[at * size : (at + 1) * size, :] = block(offset ^ 1)


def grad_kernel(sections, bins, places, *refs):
    columns, refs = refs[: len(places)], refs[len(places) :]
    grads, outs = refs[: len(places)], refs[len(places) :]
    section = lax.axis_index("pipe")
    width = outs[0].shape[1]
    size = len(outs) * width

    def taps(spread):
        act = jnp.concatenate(
            [ref[at * size : (at + 1) * size, :] for ref, at in zip(columns, places)], axis=1
        )
        dpre = jnp.concatenate([ref[...] for ref in grads], axis=0)
        wide = dpre.astype(jnp.float32)
        spans = (
            moved(wide, -spread, bins).astype(jnp.bfloat16),
            dpre,
            moved(wide, spread, bins).astype(jnp.bfloat16),
        )
        for tap in range(3):
            grad = jnp.dot(act, spans[tap], preferred_element_type=jnp.float32)
            for step, out_ref in enumerate(outs):
                out_ref[tap] = grad[step * width : (step + 1) * width].astype(out_ref.dtype)

    for level in range(sections):

        @pl.when(section == level)
        def run(level=level):
            taps(2**level)


def kernel_call(body, outs, flops, name, waits=(), carries=(), in_spec=in_vmem, scratch=()):
    def call(*args):
        used, taken = len(args), len(args) + len(waits) + len(carries)

        def run(*refs):
            made = refs[taken : taken + len(outs)]
            body(*refs[:used], *made, *refs[taken + len(outs) + len(carries) :])

        moved_bytes = sum(math.prod(a.shape) * a.dtype.itemsize for a in (*args, *outs))
        return pl.pallas_call(
            run,
            out_shape=[*outs, *(jax.ShapeDtypeStruct(a.shape, a.dtype) for a in carries)],
            in_specs=[in_spec] * used + [anywhere] * (taken - used),
            out_specs=[in_vmem] * len(outs) + [anywhere] * len(carries),
            input_output_aliases={
                used + len(waits) + at: len(outs) + at for at in range(len(carries))
            },
            scratch_shapes=list(scratch),
            compiler_params=pltpu.CompilerParams(vmem_limit_bytes=24 * 2**20),
            cost_estimate=pl.CostEstimate(
                flops=flops, bytes_accessed=moved_bytes, transcendentals=0
            ),
            name=name,
        )(*args, *waits, *carries)

    return call


def residue_shards(inputs, cotangent, weight, point):
    sections = lax.axis_size("pipe")
    section = lax.axis_index("pipe")
    count = lax.axis_size("ctx")
    groups = lax.axis_size("dp")
    seq_count, bins, chans = inputs.shape
    inner = weight.shape[3]
    rows = seq_count * bins
    scale = 1.0 / math.sqrt(seq_count * groups * bins * count)
    last = sections - 1
    seqs = range(seq_count)
    layer_flops = 2 * bins * chans * inner * 4

    def shape(*dims, dtype=jnp.bfloat16):
        return jax.ShapeDtypeStruct(dims, dtype)

    def hop(value, source, target, third=None):
        sends = {source: target, target: source}
        if third is not None and third % sections not in sends:
            sends.update({target: third % sections, third % sections: source})
        route = []
        for core in range(groups):
            for stage in range(sections):
                taker = core if stage in sends else (core + 1) % groups
                for i in range(count):
                    giver = (core * sections + stage) * count + i
                    route.append((giver, (taker * sections + sends.get(stage, stage)) * count + i))
        return lax.ppermute(value, ("dp", "pipe", "ctx"), route)

    def onward(value, step):
        return lax.ppermute(value, "ctx", [(i, (i + step) % count) for i in range(count)])

    def exchange(value, offset):
        return lax.ppermute(value, "ctx", [(i, i ^ offset) for i in range(count)])

    payload = jnp.where(section == last, cotangent, inputs)
    parts = kernel_call(
        functools.partial(split_kernel, last),
        [shape(rows // count, chans)] * count,
        10 * seq_count * layer_flops,
        "split",
    )(payload)
    weight, point = kernel_call(
        hold_kernel,
        [shape(*weight.shape), shape(*point.shape)],
        0,
        "hold",
        waits=[parts[0]],
        in_spec=anywhere,
        scratch=[pltpu.SemaphoreType.DMA((2,))],
    )(weight, point)
    parts = [*(onward(parts[step], step) for step in range(count - 1, 0, -1)), parts[0]]

    trunk, inside = shape(bins, chans), shape(bins, inner)
    inside_wide = shape(bins, inner, dtype=jnp.float32)
    whole, out, pre = kernel_call(
        functools.partial(first_kernel, last, bins),
        [shape(rows, chans), trunk, inside_wide],
        layer_flops,
        "first",
    )(*parts, weight, point)
    outs, pres, xs, sent = [out], [[pre]], [[whole]], ()
    for level in range(last):
        if level > 0:
            third = level - 2 if level > 1 else None
            xs.append([hop(out, level - 1, level, third) for out in outs])
            outs = []
            pres.append([])
        for seq in range(len(outs), seq_count):
            out, pre = kernel_call(
                functools.partial(fore_kernel, level, seq, bins),
                [trunk, inside_wide],
                layer_flops,
                "fore",
                waits=outs[-1:] or sent,
            )(xs[level][seq if level else 0], weight, point)
            outs.append(out)
            pres[level].append(pre)
        sent = outs
    xs.append([hop(out, last - 1, last, last - 2) for out in outs])

    dys, dpres = [], [[] for level in range(sections)]
    for seq in seqs:
        dy, dpre = kernel_call(
            functools.partial(turn_kernel, last, seq, bins, scale),
            [trunk, inside],
            2 * layer_flops,
            "turn",
            waits=dys[-1:] or sent,
        )(xs[last][seq], whole, weight, point)
        dys.append(dy)
        dpres[last].append(dpre)
    kept = list(range(0, count, 2))
    moving = [(offset, 0) for offset in range(1, count, 2)]
    size = chans // count
    *owned, message = kernel_call(
        functools.partial(columns_kernel, groups, [len(x) for x in xs], kept),
        [shape(size, rows)] * len(kept) + [shape(size * len(kept), rows)],
        2 * rows * chans * chans,
        "columns",
        waits=dys,
    )(*[x for some in xs for x in some])
    blocks = {(offset, 0): (array, 0) for offset, array in zip(kept, owned)}
    sent = [owned[0]]
    dys = [hop(dy, last, last - 1) for dy in dys]
    message, bit = exchange(message, 1), 1
    blocks.update({(to ^ 1, start ^ 1): (message, at) for at, (to, start) in enumerate(moving)})

    for level in range(last - 1, 0, -1):
        outs = []
        for seq in seqs:
            dy, dpre = kernel_call(
                functools.partial(back_kernel, level, seq, bins),
                [trunk, inside],
                layer_flops,
                "back",
                waits=outs[-1:] or sent,
            )(dys[seq], xs[level][seq], pres[level][seq], weight, point)
            outs.append(dy)
            dpres[level].append(dpre)
        sent = outs
        dys = [hop(dy, level, level - 1, level - 2) for dy in outs]
        bit *= 2
        moving = sorted(key for key in blocks if key[0] & bit)
        if moving:
            (message,) = kernel_call(
                functools.partial(message_kernel, [blocks[key][1] for key in moving]),
                [shape(size * len(moving), rows)],
                0,
                "message",
                waits=outs,
            )(*[blocks[key][0] for key in moving])
            sent = [*outs, message]
            message = exchange(message, bit)
            for at, (to, start) in enumerate(moving):
                blocks[to ^ bit, start ^ bit] = (message, at)

    sent = [*sent, message]
    dpre = []
    for seq in seqs:
        dpre = kernel_call(
            functools.partial(head_kernel, sections, seq * bins),
            [shape((seq + 1) * bins, inner)],
            layer_flops // 4,
            "head",
            waits=dpre or sent,
        )(dys[seq], pres[0][seq], point, *[dpres[level][seq] for level in range(1, sections)], *dpre)
    (dpre,) = dpre
    far_first = range(count - 1, 0, -1)
    gathered = [*(exchange(dpre, offset) for offset in far_first), dpre]
    columns = [blocks[0, offset] for offset in [*far_first, 0]]
    share = shape(3, chans // (count * groups), inner, dtype=jnp.float32)
    mine, *others = kernel_call(
        functools.partial(grad_kernel, sections, bins, [at for array, at in columns]),
        [share, *[shape(*share.shape)] * (groups - 1)],
        2 * 3 * rows * chans * inner,
        "grad",
    )(*[array for array, at in columns], *gathered)
    for step, other in enumerate(others, 1):
        route = [(i, (i + step) % groups) for i in range(groups)]
        mine = mine + lax.ppermute(other, "dp", route).astype(jnp.float32)
    return mine[None]


def solution(mesh):
    def shards(inputs, cotangent, dilated_kernel_weight, point_weight):
        bins = inputs.shape[1]
        first_spread = bins // 2 // 2 ** (mesh.shape["pipe"] - 1)
        count = mesh.shape["ctx"]
        residues = (
            first_spread == count
            and mesh.shape["pipe"] > 1
            and bins % (16 * count) == 0
            and 1 < count == 1 << (count.bit_length() - 1) <= 1 << (mesh.shape["pipe"] - 2)
            and inputs.shape[2] % (count * mesh.shape["dp"]) == 0
        )
        plan = residue_shards if residues else edge_shards
        return plan(inputs, cotangent, dilated_kernel_weight, point_weight)

    return jax.shard_map(
        shards,
        mesh=mesh,
        in_specs=(
            P("dp", "ctx", None),
            P("dp", "ctx", None),
            P("pipe", None, None, None),
            P("pipe", None, None),
        ),
        out_specs=P("pipe", None, ("dp", "ctx"), None),
        check_vma=False,
    )
```

```python
import functools
import math

import jax
import jax.numpy as jnp
from jax import lax
from jax.experimental import pallas as pl
from jax.experimental.pallas import tpu as pltpu
from jax.sharding import PartitionSpec as P

root_half = 0.7071067811865476
inv_root_two_pi = 0.3989422804014327

in_vmem = pl.BlockSpec(memory_space=pltpu.VMEM)
anywhere = pl.BlockSpec(memory_space=pl.ANY)
contract_last = (((1,), (1,)), ((), ()))
contract_first = (((0,), (0,)), ((), ()))


def gelu(value):
    return 0.5 * value * (1.0 + lax.erf(value * root_half))


def gelu_slope(value):
    return (
        0.5 * (1.0 + lax.erf(value * root_half))
        + value * jnp.exp(-0.5 * value * value) * inv_root_two_pi
    )


def padded(cells, sides, width):
    for axis, dim in sides:
        count = lax.axis_size(axis)
        ends = count - 1
        head = lax.slice_in_dim(cells, 0, width, axis=dim)
        tail = lax.slice_in_dim(cells, cells.shape[dim] - width, cells.shape[dim], axis=dim)
        cells = jnp.concatenate(
            [
                lax.ppermute(tail, axis, [(i, (i + 1) % count) for i in range(ends)]),
                cells,
                lax.ppermute(head, axis, [((i + 1) % count, i) for i in range(ends)]),
            ],
            axis=dim,
        )
    return cells


def shifted(block, axis, distance):
    devices = range(lax.axis_size(axis))
    route = [(i - distance, i) for i in devices if i - distance in devices]
    return lax.ppermute(block, axis, route)


def edge_shards(inputs, cotangent, dilated_kernel_weight, point_weight):
    sections = lax.axis_size("pipe")
    section = lax.axis_index("pipe")
    seq_count, bins, chans = inputs.shape
    reach = bins // 2
    table = jnp.array(
        [reach // 2 ** (sections - 1 - level) for level in range(sections)], jnp.int32
    )
    spread = table[section]
    dilation_weight = dilated_kernel_weight[0]
    w_point = point_weight[0]
    inner_channel_count = dilation_weight.shape[2]
    scale = 1.0 / math.sqrt(seq_count * lax.axis_size("dp") * bins * lax.axis_size("ctx"))
    ticks = jnp.arange(seq_count + sections - 1, dtype=jnp.int32)

    def conv_fore(extended):
        running_total = jnp.zeros((bins, inner_channel_count), jnp.float32)
        for kernel_offset in range(3):
            receptive_span = lax.dynamic_slice_in_dim(
                extended, reach + (kernel_offset - 1) * spread, bins, 0
            )
            running_total = running_total + jnp.dot(
                receptive_span, dilation_weight[kernel_offset], preferred_element_type=jnp.float32
            )
        return running_total

    def put(store, slot, valid, item):
        current = lax.dynamic_index_in_dim(store, slot, 0, keepdims=False)
        return lax.dynamic_update_index_in_dim(store, jnp.where(valid, item, current), slot, 0)

    kept_x = jnp.zeros(inputs.shape, jnp.bfloat16)
    kept_ext = jnp.zeros((seq_count, bins + 2 * reach, chans), jnp.bfloat16)
    kept_pre = jnp.zeros((seq_count, bins, inner_channel_count), jnp.float32)

    def fore_tick(carry, tick):
        received, store_x, store_ext, store_pre = carry
        micro = tick - section
        valid = (micro >= 0) & (micro < seq_count)
        slot = jnp.clip(micro, 0, seq_count - 1)
        first = lax.dynamic_index_in_dim(inputs, slot, 0, keepdims=False)
        trunk_in = jnp.where(section == 0, first, received)
        act = gelu(trunk_in.astype(jnp.float32)).astype(jnp.bfloat16)
        extended = padded(act, (("ctx", 0),), reach)
        pre = conv_fore(extended)
        inner = gelu(pre).astype(jnp.bfloat16)
        out = (
            trunk_in.astype(jnp.float32)
            + jnp.dot(inner, w_point, preferred_element_type=jnp.float32)
        ).astype(jnp.bfloat16)
        sent = shifted(out, "pipe", 1)
        store_x = put(store_x, slot, valid, trunk_in)
        store_ext = put(store_ext, slot, valid, extended)
        store_pre = put(store_pre, slot, valid, pre)
        return ((sent, store_x, store_ext, store_pre), None)

    start_recv = jnp.zeros((bins, chans), jnp.bfloat16)
    (unused, kept_x, kept_ext, kept_pre), unused_out = lax.scan(
        fore_tick, (start_recv, kept_x, kept_ext, kept_pre), ticks
    )

    def back_tick(carry, tick):
        received, grad = carry
        micro = tick - (sections - 1 - section)
        valid = (micro >= 0) & (micro < seq_count)
        slot = jnp.clip(micro, 0, seq_count - 1)
        last = (
            lax.dynamic_index_in_dim(cotangent, slot, 0, keepdims=False).astype(jnp.float32) * scale
        ).astype(jnp.bfloat16)
        upstream = jnp.where(section == sections - 1, last, received)
        trunk_in = lax.dynamic_index_in_dim(kept_x, slot, 0, keepdims=False)
        extended = lax.dynamic_index_in_dim(kept_ext, slot, 0, keepdims=False)
        pre = lax.dynamic_index_in_dim(kept_pre, slot, 0, keepdims=False)
        inner_grad = lax.dot_general(
            upstream, w_point, contract_last, preferred_element_type=jnp.float32
        )
        dpre = (inner_grad * gelu_slope(pre) * valid.astype(jnp.float32)).astype(jnp.bfloat16)
        dpre_ext = padded(dpre, (("ctx", 0),), reach)
        dact = jnp.zeros((bins, chans), jnp.float32)
        taps = []
        for kernel_offset in range(3):
            receptive_span = lax.dynamic_slice_in_dim(
                dpre_ext, reach - (kernel_offset - 1) * spread, bins, 0
            )
            dact = dact + lax.dot_general(
                receptive_span,
                dilation_weight[kernel_offset],
                contract_last,
                preferred_element_type=jnp.float32,
            )
            source = lax.dynamic_slice_in_dim(
                extended, reach + (kernel_offset - 1) * spread, bins, 0
            )
            taps.append(
                lax.dot_general(source, dpre, contract_first, preferred_element_type=jnp.float32)
            )
        grad = grad + jnp.stack(taps)
        back = (
            upstream.astype(jnp.float32) + dact * gelu_slope(trunk_in.astype(jnp.float32))
        ).astype(jnp.bfloat16)
        sent = shifted(back, "pipe", -1)
        return ((sent, grad), None)

    start_grad = jnp.zeros((3, chans, inner_channel_count), jnp.float32)
    (unused_back, grad), unused_seq = lax.scan(back_tick, (start_recv, start_grad), ticks)
    term = grad[None]
    return lax.psum_scatter(term, ("dp", "ctx"), scatter_dimension=2, tiled=True)


def moved(value, by, bins):
    pieces = []
    for start in range(0, value.shape[0], bins):
        piece = value[start : start + bins]
        place = lax.broadcasted_iota(jnp.int32, piece.shape, 0)
        if by > 0:
            keep = place >= by
        else:
            keep = place < bins + by
        pieces.append(jnp.where(keep, pltpu.roll(piece, by % bins, 0), 0.0))
    return jnp.concatenate(pieces, axis=0)


def fore(x, weight_ref, spread, bins):
    act = gelu(x.astype(jnp.float32)).astype(jnp.bfloat16)
    terms = [
        jnp.dot(act, weight_ref[0, tap], preferred_element_type=jnp.float32) for tap in range(3)
    ]
    return terms[1] + moved(terms[0], spread, bins) + moved(terms[2], -spread, bins)


def back_pre(dy, pre_slope, point_ref):
    inner_grad = lax.dot_general(
        dy, point_ref[0], contract_last, preferred_element_type=jnp.float32
    )
    return (inner_grad * pre_slope).astype(jnp.bfloat16)


def back_trunk(dy, dpre, x_slope, weight_ref, spread, bins):
    wide = dpre.astype(jnp.float32)
    spans = (
        moved(wide, -spread, bins).astype(jnp.bfloat16),
        dpre,
        moved(wide, spread, bins).astype(jnp.bfloat16),
    )
    dact = jnp.zeros(dy.shape, jnp.float32)
    for tap in range(3):
        dact = dact + lax.dot_general(
            spans[tap], weight_ref[0, tap], contract_last, preferred_element_type=jnp.float32
        )
    return (dy.astype(jnp.float32) + dact * x_slope).astype(jnp.bfloat16)


def of_seq(ref, seq, bins):
    if ref.shape[0] == bins:
        return ref[...]
    return ref[seq * bins : (seq + 1) * bins, :]


def split_kernel(last, payload_ref, *out_refs):
    count = len(out_refs)
    seq_count, bins, chans = payload_ref.shape
    part = bins // count
    section = lax.axis_index("pipe")
    place = lax.axis_index("ctx")

    @pl.when((section == 0) | (section == last))
    def send():
        source = payload_ref[...].reshape(seq_count * bins, chans)
        row = lax.broadcasted_iota(jnp.int32, (part, seq_count * bins), 0)
        col = lax.broadcasted_iota(jnp.int32, (part, seq_count * bins), 1)
        for hop in range(count):
            residue = lax.rem(place + hop, count)
            rows = [
                (col == seq * bins + count * row + residue).astype(jnp.float32)
                for seq in range(seq_count)
            ]
            pick = jnp.concatenate(rows, axis=0).astype(jnp.bfloat16)
            out_refs[hop][...] = jnp.dot(
                pick, source, preferred_element_type=jnp.float32
            ).astype(jnp.bfloat16)


def hold_kernel(weight_ref, point_ref, weight_out, point_out, sems):
    loads = [
        pltpu.make_async_copy(weight_ref, weight_out, sems.at[0]),
        pltpu.make_async_copy(point_ref, point_out, sems.at[1]),
    ]
    for load in loads:
        load.start()
    for load in loads:
        load.wait()


def first_kernel(last, bins, steps, *refs):
    parts, (weight_ref, point_ref, whole_ref, out_ref, pre_ref) = refs[:-5], refs[-5:]
    count = len(parts)
    section = lax.axis_index("pipe")
    place = lax.axis_index("ctx")
    part = bins // count
    seq_count = whole_ref.shape[0] // bins

    @pl.when((section == 0) | (section == last))
    def gather():
        for step, part_ref in zip(steps, parts):
            source = lax.rem(place + count - step, count)
            for seq in range(seq_count):
                at = pl.multiple_of(seq * bins + source * part, part)
                whole_ref[pl.ds(at, part), :] = part_ref[seq * part : (seq + 1) * part, :]

    @pl.when(section == 0)
    def layer():
        x = whole_ref[:bins, :]
        finish(x, fore(x, weight_ref, 1, bins), point_ref, out_ref, pre_ref)


def finish(x, pre, point_ref, out_ref, pre_ref):
    pre_ref[...] = pre
    branch = jnp.dot(
        gelu(pre).astype(jnp.bfloat16), point_ref[0], preferred_element_type=jnp.float32
    )
    out_ref[...] = (x.astype(jnp.float32) + branch).astype(jnp.bfloat16)


def fore_kernel(level, seq, bins, x_ref, weight_ref, point_ref, out_ref, pre_ref):
    @pl.when(lax.axis_index("pipe") == level)
    def layer():
        x = of_seq(x_ref, seq, bins)
        finish(x, fore(x, weight_ref, 2**level, bins), point_ref, out_ref, pre_ref)


def turn_kernel(level, seq, bins, scale, x_ref, cot_ref, weight_ref, point_ref, dy_ref, dpre_ref):
    @pl.when(lax.axis_index("pipe") == level)
    def layer():
        x = of_seq(x_ref, seq, bins)
        pre = fore(x, weight_ref, 2**level, bins)
        cot = of_seq(cot_ref, seq, bins)
        dy = (cot.astype(jnp.float32) * scale).astype(jnp.bfloat16)
        dpre = back_pre(dy, gelu_slope(pre), point_ref)
        dpre_ref[...] = dpre
        x_slope = gelu_slope(x.astype(jnp.float32))
        dy_ref[...] = back_trunk(dy, dpre, x_slope, weight_ref, 2**level, bins)


def slope_kernel(levels, seq_count, bins, *refs):
    xs, pres = refs[: levels * seq_count], refs[levels * seq_count : 2 * levels * seq_count]
    outs = refs[2 * levels * seq_count :]
    for level in range(levels):

        @pl.when(lax.axis_index("pipe") == level)
        def layer(level=level):
            for seq in range(seq_count):
                x = of_seq(xs[level * seq_count + seq], seq, bins)
                outs[2 * seq][...] = gelu_slope(x.astype(jnp.float32))
                outs[2 * seq + 1][...] = gelu_slope(pres[level * seq_count + seq][...])


def back_kernel(level, bins, dy_in_ref, x_slope_ref, pre_slope_ref, weight_ref, point_ref, dy_ref, dpre_ref):
    @pl.when(lax.axis_index("pipe") == level)
    def layer():
        dy = dy_in_ref[...]
        dpre = back_pre(dy, pre_slope_ref[...], point_ref)
        dpre_ref[...] = dpre
        dy_ref[...] = back_trunk(dy, dpre, x_slope_ref[...], weight_ref, 2**level, bins)


def message_kernel(places, *refs):
    blocks, message_ref = refs[:-1], refs[-1]
    size = message_ref.shape[0] // len(places)
    for to, (ref, at) in enumerate(zip(blocks, places)):
        message_ref[to * size : (to + 1) * size, :] = ref[at * size : (at + 1) * size, :]


def head_kernel(sections, earlier, dy_in_ref, slope_ref, point_ref, *refs):
    others, before, out_ref = refs[: sections - 1], refs[sections - 1 : -1], refs[-1]
    section = lax.axis_index("pipe")
    bins = dy_in_ref.shape[0]
    for ref in before:
        out_ref[:earlier, :] = ref[...]

    @pl.when(section == 0)
    def layer():
        out_ref[earlier : earlier + bins, :] = back_pre(dy_in_ref[...], slope_ref[...], point_ref)

    for level in range(1, sections):

        @pl.when(section == level)
        def keep(level=level):
            out_ref[earlier : earlier + bins, :] = others[level - 1][...]


def columns_kernel(groups, runs, kept, *refs):
    refs, (sent_ref,) = refs[:-1], refs[-1:]
    kept_refs = refs[sum(runs) :]
    count = 2 * len(kept)
    section = lax.axis_index("pipe")
    core = lax.axis_index("dp")
    place = lax.axis_index("ctx")
    x, start = None, 0
    for level, run in enumerate(runs):
        pieces = [ref[...] for ref in refs[start : start + run]]
        start += run
        whole = jnp.concatenate(pieces, axis=0).astype(jnp.float32)
        x = whole if x is None else jnp.where(section == level, whole, x)
    act = gelu(x).astype(jnp.bfloat16)
    chans = act.shape[1]
    width = chans // (groups * count)
    row = lax.broadcasted_iota(jnp.int32, (width, chans), 0)
    col = lax.broadcasted_iota(jnp.int32, (width, chans), 1)

    def block(offset):
        owner = lax.bitwise_xor(place, offset)
        rows = []
        for step in range(groups):
            first = (lax.rem(core + step, groups) * count + owner) * width
            rows.append((col == first + row).astype(jnp.float32))
        pick = jnp.concatenate(rows, axis=0).astype(jnp.bfloat16)
        return lax.dot_general(
            pick, act, contract_last, preferred_element_type=jnp.float32
        ).astype(jnp.bfloat16)

    size = groups * width
    for at, offset in enumerate(kept):
        kept_refs[at][...] = block(offset)
        sent_ref[at * size : (at + 1) * size, :] = block(offset ^ 1)


def grad_kernel(sections, bins, places, *refs):
    columns, refs = refs[: len(places)], refs[len(places) :]
    grads, out_ref = refs[:-1], refs[-1]
    section = lax.axis_index("pipe")
    width = out_ref.shape[1]

    def taps(spread):
        act = jnp.concatenate(
            [ref[at : at + width, :] for ref, at in zip(columns, places)], axis=1
        )
        dpre = jnp.concatenate([ref[...] for ref in grads], axis=0)
        wide = dpre.astype(jnp.float32)
        spans = (
            moved(wide, -spread, bins).astype(jnp.bfloat16),
            dpre,
            moved(wide, spread, bins).astype(jnp.bfloat16),
        )
        for tap in range(3):
            out_ref[tap] = jnp.dot(
                act, spans[tap], preferred_element_type=jnp.float32
            ).astype(out_ref.dtype)

    for level in range(sections):

        @pl.when(section == level)
        def run(level=level):
            taps(2**level)


def kernel_call(body, outs, flops, name, waits=(), carries=(), in_spec=in_vmem, scratch=()):
    def call(*args):
        used, taken = len(args), len(args) + len(waits) + len(carries)

        def run(*refs):
            made = refs[taken : taken + len(outs)]
            body(*refs[:used], *made, *refs[taken + len(outs) + len(carries) :])

        moved_bytes = sum(math.prod(a.shape) * a.dtype.itemsize for a in (*args, *outs))
        return pl.pallas_call(
            run,
            out_shape=[*outs, *(jax.ShapeDtypeStruct(a.shape, a.dtype) for a in carries)],
            in_specs=[in_spec] * used + [anywhere] * (taken - used),
            out_specs=[in_vmem] * len(outs) + [anywhere] * len(carries),
            input_output_aliases={
                used + len(waits) + at: len(outs) + at for at in range(len(carries))
            },
            scratch_shapes=list(scratch),
            compiler_params=pltpu.CompilerParams(vmem_limit_bytes=24 * 2**20),
            cost_estimate=pl.CostEstimate(
                flops=flops, bytes_accessed=moved_bytes, transcendentals=0
            ),
            name=name,
        )(*args, *waits, *carries)

    return call


def residue_shards(inputs, cotangent, weight, point):
    sections = lax.axis_size("pipe")
    section = lax.axis_index("pipe")
    count = lax.axis_size("ctx")
    groups = lax.axis_size("dp")
    seq_count, bins, chans = inputs.shape
    inner = weight.shape[3]
    rows = seq_count * bins
    scale = 1.0 / math.sqrt(seq_count * groups * bins * count)
    last = sections - 1
    seqs = range(seq_count)
    layer_flops = 2 * bins * chans * inner * 4

    def shape(*dims, dtype=jnp.bfloat16):
        return jax.ShapeDtypeStruct(dims, dtype)

    def hop(value, source, target, third=None):
        sends = {source: target, target: source}
        if third is not None and third not in sends:
            sends.update({target: third, third: source})
        route = []
        for core in range(groups):
            for stage in range(sections):
                taker = core if stage in sends else (core + 1) % groups
                for i in range(count):
                    giver = (core * sections + stage) * count + i
                    route.append((giver, (taker * sections + sends.get(stage, stage)) * count + i))
        return lax.ppermute(value, ("dp", "pipe", "ctx"), route)

    def onward(value, step):
        return lax.ppermute(value, "ctx", [(i, (i + step) % count) for i in range(count)])

    def exchange(value, offset):
        return lax.ppermute(value, "ctx", [(i, i ^ offset) for i in range(count)])

    payload = jnp.where(section == last, cotangent, inputs)
    parts = kernel_call(
        functools.partial(split_kernel, last),
        [shape(rows // count, chans)] * count,
        10 * seq_count * layer_flops,
        "split",
    )(payload)
    weight, point = kernel_call(
        hold_kernel,
        [shape(*weight.shape), shape(*point.shape)],
        0,
        "hold",
        waits=[parts[0]],
        in_spec=anywhere,
        scratch=[pltpu.SemaphoreType.DMA((2,))],
    )(weight, point)
    steps = [1, *range(count - 1, 1, -1)]
    parts = [*(onward(parts[step], step) for step in steps), parts[0]]

    trunk, inside = shape(bins, chans), shape(bins, inner)
    inside_wide = shape(bins, inner, dtype=jnp.float32)
    whole, out, pre = kernel_call(
        functools.partial(first_kernel, last, bins, [*steps, 0]),
        [shape(rows, chans), trunk, inside_wide],
        layer_flops,
        "first",
    )(*parts, weight, point)
    outs, pres, xs, sent = [out], [[pre]], [[whole]], ()
    for level in range(last):
        if level > 0:
            third = last if level > 1 else None
            xs.append([hop(out, level - 1, level, third) for out in outs])
            outs = []
            pres.append([])
        for seq in range(len(outs), seq_count):
            out, pre = kernel_call(
                functools.partial(fore_kernel, level, seq, bins),
                [trunk, inside_wide],
                layer_flops,
                "fore",
                waits=outs[-1:] or sent,
            )(xs[level][seq if level else 0], weight, point)
            outs.append(out)
            pres[level].append(pre)
        sent = outs
    slopes = kernel_call(
        functools.partial(slope_kernel, last, seq_count, bins),
        [shape(bins, chans, dtype=jnp.float32), inside_wide] * seq_count,
        0,
        "slopes",
        waits=outs,
    )(
        *[xs[level][seq if level else 0] for level in range(last) for seq in seqs],
        *[pre for some in pres for pre in some],
    )
    sent = [*sent, *slopes]
    xs.append([hop(out, last - 1, last, 0) for out in outs])

    dys, dpres = [], [[] for level in range(sections)]
    for seq in seqs:
        dy, dpre = kernel_call(
            functools.partial(turn_kernel, last, seq, bins, scale),
            [trunk, inside],
            2 * layer_flops,
            "turn",
            waits=dys[-1:] or sent,
        )(xs[last][seq], whole, weight, point)
        dys.append(dy)
        dpres[last].append(dpre)
    kept = list(range(0, count, 2))
    moving = [(offset, 0) for offset in range(1, count, 2)]
    size = chans // count
    *owned, message = kernel_call(
        functools.partial(columns_kernel, groups, [len(x) for x in xs], kept),
        [shape(size, rows)] * len(kept) + [shape(size * len(kept), rows)],
        2 * rows * chans * chans,
        "columns",
        waits=dys,
    )(*[x for some in xs for x in some])
    blocks = {(offset, 0): (array, 0) for offset, array in zip(kept, owned)}
    sent = [owned[0]]
    dys = [hop(dy, last, last - 1) for dy in dys]
    message, bit = exchange(message, 1), 1
    blocks.update({(to ^ 1, start ^ 1): (message, at) for at, (to, start) in enumerate(moving)})

    for level in range(last - 1, 0, -1):
        outs = []
        for seq in seqs:
            dy, dpre = kernel_call(
                functools.partial(back_kernel, level, bins),
                [trunk, inside],
                layer_flops,
                "back",
                waits=outs[-1:] or sent,
            )(dys[seq], *slopes[2 * seq : 2 * seq + 2], weight, point)
            outs.append(dy)
            dpres[level].append(dpre)
        sent = outs
        dys = [hop(dy, level, level - 1, None if level > 1 else last) for dy in outs]
        bit *= 2
        moving = sorted(key for key in blocks if key[0] & bit)
        if moving:
            (message,) = kernel_call(
                functools.partial(message_kernel, [blocks[key][1] for key in moving]),
                [shape(size * len(moving), rows)],
                0,
                "message",
                waits=outs,
            )(*[blocks[key][0] for key in moving])
            sent = [*outs, message]
            message = exchange(message, bit)
            for at, (to, start) in enumerate(moving):
                blocks[to ^ bit, start ^ bit] = (message, at)

    sent = [*sent, message]
    dpre = []
    for seq in seqs:
        dpre = kernel_call(
            functools.partial(head_kernel, sections, seq * bins),
            [shape((seq + 1) * bins, inner)],
            layer_flops // 4,
            "head",
            waits=dpre or sent,
        )(dys[seq], slopes[2 * seq + 1], point, *[dpres[level][seq] for level in range(1, sections)], *dpre)
    (dpre,) = dpre
    far_first = range(count - 1, 0, -1)
    gathered = [*(exchange(dpre, offset) for offset in far_first), dpre]
    columns = [blocks[0, offset] for offset in [*far_first, 0]]
    width = size // groups

    def gradient(step, dtype, waits=()):
        places = [at * size + step * width for array, at in columns]
        (part,) = kernel_call(
            functools.partial(grad_kernel, sections, bins, places),
            [shape(3, width, inner, dtype=dtype)],
            2 * 3 * rows * count * width * inner,
            "grad",
            waits=waits,
        )(*[array for array, at in columns], *gathered)
        return part

    others = [gradient(step, jnp.bfloat16) for step in range(1, groups)]
    mine = gradient(0, jnp.float32, waits=others)
    for step, other in enumerate(others, 1):
        route = [(i, (i + step) % groups) for i in range(groups)]
        mine = mine + lax.ppermute(other, "dp", route).astype(jnp.float32)
    return mine[None]


def solution(mesh):
    def shards(inputs, cotangent, dilated_kernel_weight, point_weight):
        bins = inputs.shape[1]
        first_spread = bins // 2 // 2 ** (mesh.shape["pipe"] - 1)
        count = mesh.shape["ctx"]
        residues = (
            first_spread == count
            and mesh.shape["pipe"] > 1
            and bins % (16 * count) == 0
            and 1 < count == 1 << (count.bit_length() - 1) <= 1 << (mesh.shape["pipe"] - 2)
            and inputs.shape[2] % (count * mesh.shape["dp"]) == 0
        )
        plan = residue_shards if residues else edge_shards
        return plan(inputs, cotangent, dilated_kernel_weight, point_weight)

    return jax.shard_map(
        shards,
        mesh=mesh,
        in_specs=(
            P("dp", "ctx", None),
            P("dp", "ctx", None),
            P("pipe", None, None, None),
            P("pipe", None, None),
        ),
        out_specs=P("pipe", None, ("dp", "ctx"), None),
        check_vma=False,
    )
```

```python
import functools
import math

import jax
import jax.numpy as jnp
from jax import lax
from jax.experimental import pallas as pl
from jax.experimental.pallas import tpu as pltpu
from jax.sharding import PartitionSpec as P

root_half = 0.7071067811865476
inv_root_two_pi = 0.3989422804014327

in_vmem = pl.BlockSpec(memory_space=pltpu.VMEM)
anywhere = pl.BlockSpec(memory_space=pl.ANY)
contract_last = (((1,), (1,)), ((), ()))
contract_first = (((0,), (0,)), ((), ()))


def gelu(value):
    return 0.5 * value * (1.0 + lax.erf(value * root_half))


def gelu_slope(value):
    return (
        0.5 * (1.0 + lax.erf(value * root_half))
        + value * jnp.exp(-0.5 * value * value) * inv_root_two_pi
    )


def padded(cells, sides, width):
    for axis, dim in sides:
        count = lax.axis_size(axis)
        ends = count - 1
        head = lax.slice_in_dim(cells, 0, width, axis=dim)
        tail = lax.slice_in_dim(cells, cells.shape[dim] - width, cells.shape[dim], axis=dim)
        cells = jnp.concatenate(
            [
                lax.ppermute(tail, axis, [(i, (i + 1) % count) for i in range(ends)]),
                cells,
                lax.ppermute(head, axis, [((i + 1) % count, i) for i in range(ends)]),
            ],
            axis=dim,
        )
    return cells


def shifted(block, axis, distance):
    devices = range(lax.axis_size(axis))
    route = [(i - distance, i) for i in devices if i - distance in devices]
    return lax.ppermute(block, axis, route)


def edge_shards(inputs, cotangent, dilated_kernel_weight, point_weight):
    sections = lax.axis_size("pipe")
    section = lax.axis_index("pipe")
    seq_count, bins, chans = inputs.shape
    reach = bins // 2
    table = jnp.array(
        [reach // 2 ** (sections - 1 - level) for level in range(sections)], jnp.int32
    )
    spread = table[section]
    dilation_weight = dilated_kernel_weight[0]
    w_point = point_weight[0]
    inner_channel_count = dilation_weight.shape[2]
    scale = 1.0 / math.sqrt(seq_count * lax.axis_size("dp") * bins * lax.axis_size("ctx"))
    ticks = jnp.arange(seq_count + sections - 1, dtype=jnp.int32)

    def conv_fore(extended):
        running_total = jnp.zeros((bins, inner_channel_count), jnp.float32)
        for kernel_offset in range(3):
            receptive_span = lax.dynamic_slice_in_dim(
                extended, reach + (kernel_offset - 1) * spread, bins, 0
            )
            running_total = running_total + jnp.dot(
                receptive_span, dilation_weight[kernel_offset], preferred_element_type=jnp.float32
            )
        return running_total

    def put(store, slot, valid, item):
        current = lax.dynamic_index_in_dim(store, slot, 0, keepdims=False)
        return lax.dynamic_update_index_in_dim(store, jnp.where(valid, item, current), slot, 0)

    kept_x = jnp.zeros(inputs.shape, jnp.bfloat16)
    kept_ext = jnp.zeros((seq_count, bins + 2 * reach, chans), jnp.bfloat16)
    kept_pre = jnp.zeros((seq_count, bins, inner_channel_count), jnp.float32)

    def fore_tick(carry, tick):
        received, store_x, store_ext, store_pre = carry
        micro = tick - section
        valid = (micro >= 0) & (micro < seq_count)
        slot = jnp.clip(micro, 0, seq_count - 1)
        first = lax.dynamic_index_in_dim(inputs, slot, 0, keepdims=False)
        trunk_in = jnp.where(section == 0, first, received)
        act = gelu(trunk_in.astype(jnp.float32)).astype(jnp.bfloat16)
        extended = padded(act, (("ctx", 0),), reach)
        pre = conv_fore(extended)
        inner = gelu(pre).astype(jnp.bfloat16)
        out = (
            trunk_in.astype(jnp.float32)
            + jnp.dot(inner, w_point, preferred_element_type=jnp.float32)
        ).astype(jnp.bfloat16)
        sent = shifted(out, "pipe", 1)
        store_x = put(store_x, slot, valid, trunk_in)
        store_ext = put(store_ext, slot, valid, extended)
        store_pre = put(store_pre, slot, valid, pre)
        return ((sent, store_x, store_ext, store_pre), None)

    start_recv = jnp.zeros((bins, chans), jnp.bfloat16)
    (unused, kept_x, kept_ext, kept_pre), unused_out = lax.scan(
        fore_tick, (start_recv, kept_x, kept_ext, kept_pre), ticks
    )

    def back_tick(carry, tick):
        received, grad = carry
        micro = tick - (sections - 1 - section)
        valid = (micro >= 0) & (micro < seq_count)
        slot = jnp.clip(micro, 0, seq_count - 1)
        last = (
            lax.dynamic_index_in_dim(cotangent, slot, 0, keepdims=False).astype(jnp.float32) * scale
        ).astype(jnp.bfloat16)
        upstream = jnp.where(section == sections - 1, last, received)
        trunk_in = lax.dynamic_index_in_dim(kept_x, slot, 0, keepdims=False)
        extended = lax.dynamic_index_in_dim(kept_ext, slot, 0, keepdims=False)
        pre = lax.dynamic_index_in_dim(kept_pre, slot, 0, keepdims=False)
        inner_grad = lax.dot_general(
            upstream, w_point, contract_last, preferred_element_type=jnp.float32
        )
        dpre = (inner_grad * gelu_slope(pre) * valid.astype(jnp.float32)).astype(jnp.bfloat16)
        dpre_ext = padded(dpre, (("ctx", 0),), reach)
        dact = jnp.zeros((bins, chans), jnp.float32)
        taps = []
        for kernel_offset in range(3):
            receptive_span = lax.dynamic_slice_in_dim(
                dpre_ext, reach - (kernel_offset - 1) * spread, bins, 0
            )
            dact = dact + lax.dot_general(
                receptive_span,
                dilation_weight[kernel_offset],
                contract_last,
                preferred_element_type=jnp.float32,
            )
            source = lax.dynamic_slice_in_dim(
                extended, reach + (kernel_offset - 1) * spread, bins, 0
            )
            taps.append(
                lax.dot_general(source, dpre, contract_first, preferred_element_type=jnp.float32)
            )
        grad = grad + jnp.stack(taps)
        back = (
            upstream.astype(jnp.float32) + dact * gelu_slope(trunk_in.astype(jnp.float32))
        ).astype(jnp.bfloat16)
        sent = shifted(back, "pipe", -1)
        return ((sent, grad), None)

    start_grad = jnp.zeros((3, chans, inner_channel_count), jnp.float32)
    (unused_back, grad), unused_seq = lax.scan(back_tick, (start_recv, start_grad), ticks)
    term = grad[None]
    return lax.psum_scatter(term, ("dp", "ctx"), scatter_dimension=2, tiled=True)


def moved(value, by, bins):
    pieces = []
    for start in range(0, value.shape[0], bins):
        piece = value[start : start + bins]
        place = lax.broadcasted_iota(jnp.int32, piece.shape, 0)
        if by > 0:
            keep = place >= by
        else:
            keep = place < bins + by
        pieces.append(jnp.where(keep, pltpu.roll(piece, by % bins, 0), 0.0))
    return jnp.concatenate(pieces, axis=0)


def fore(x, weight_ref, spread, bins):
    act = gelu(x.astype(jnp.float32)).astype(jnp.bfloat16)
    terms = [
        jnp.dot(act, weight_ref[0, tap], preferred_element_type=jnp.float32) for tap in range(3)
    ]
    return terms[1] + moved(terms[0], spread, bins) + moved(terms[2], -spread, bins)


def back_pre(dy, pre_slope, point_ref):
    inner_grad = jnp.dot(dy, point_ref[0], preferred_element_type=jnp.float32)
    return (inner_grad * pre_slope).astype(jnp.bfloat16)


def back_trunk(dy, dpre, x_slope, weight_ref, spread, bins):
    wide = dpre.astype(jnp.float32)
    spans = (
        moved(wide, -spread, bins).astype(jnp.bfloat16),
        dpre,
        moved(wide, spread, bins).astype(jnp.bfloat16),
    )
    dact = jnp.zeros(dy.shape, jnp.float32)
    for tap in range(3):
        dact = dact + jnp.dot(
            spans[tap], weight_ref[0, tap], preferred_element_type=jnp.float32
        )
    return (dy.astype(jnp.float32) + dact * x_slope).astype(jnp.bfloat16)


def of_seq(ref, seq, bins):
    if ref.shape[0] == bins:
        return ref[...]
    return ref[seq * bins : (seq + 1) * bins, :]


def split_kernel(last, payload_ref, *out_refs):
    count = len(out_refs)
    seq_count, bins, chans = payload_ref.shape
    part = bins // count
    section = lax.axis_index("pipe")
    place = lax.axis_index("ctx")

    @pl.when((section == 0) | (section == last))
    def send():
        source = payload_ref[...].reshape(seq_count * bins, chans)
        row = lax.broadcasted_iota(jnp.int32, (part, seq_count * bins), 0)
        col = lax.broadcasted_iota(jnp.int32, (part, seq_count * bins), 1)
        for hop in range(count):
            residue = lax.rem(place + hop, count)
            rows = [
                (col == seq * bins + count * row + residue).astype(jnp.float32)
                for seq in range(seq_count)
            ]
            pick = jnp.concatenate(rows, axis=0).astype(jnp.bfloat16)
            out_refs[hop][...] = jnp.dot(
                pick, source, preferred_element_type=jnp.float32
            ).astype(jnp.bfloat16)


def hold_kernel(weight_ref, point_ref, weight_out, point_out, sems):
    loads = [
        pltpu.make_async_copy(weight_ref, weight_out, sems.at[0]),
        pltpu.make_async_copy(point_ref, point_out, sems.at[1]),
    ]
    for load in loads:
        load.start()
    for load in loads:
        load.wait()


def first_kernel(last, bins, steps, *refs):
    parts, (weight_ref, point_ref, whole_ref, out_ref, pre_ref) = refs[:-5], refs[-5:]
    count = len(parts)
    section = lax.axis_index("pipe")
    place = lax.axis_index("ctx")
    part = bins // count
    seq_count = whole_ref.shape[0] // bins

    @pl.when((section == 0) | (section == last))
    def gather():
        for step, part_ref in zip(steps, parts):
            source = lax.rem(place + count - step, count)
            for seq in range(seq_count):
                at = pl.multiple_of(seq * bins + source * part, part)
                whole_ref[pl.ds(at, part), :] = part_ref[seq * part : (seq + 1) * part, :]

    @pl.when(section == 0)
    def layer():
        x = whole_ref[:bins, :]
        finish(x, fore(x, weight_ref, 1, bins), point_ref, out_ref, pre_ref)


def finish(x, pre, point_ref, out_ref, pre_ref):
    pre_ref[...] = pre
    branch = jnp.dot(
        gelu(pre).astype(jnp.bfloat16), point_ref[0], preferred_element_type=jnp.float32
    )
    out_ref[...] = (x.astype(jnp.float32) + branch).astype(jnp.bfloat16)


def fore_kernel(level, seq, bins, x_ref, weight_ref, point_ref, out_ref, pre_ref):
    @pl.when(lax.axis_index("pipe") == level)
    def layer():
        x = of_seq(x_ref, seq, bins)
        finish(x, fore(x, weight_ref, 2**level, bins), point_ref, out_ref, pre_ref)


def transpose_kernel(weight_ref, point_ref, weight_out, point_out):
    for tap in range(weight_ref.shape[1]):
        weight_out[0, tap] = weight_ref[0, tap].T
    point_out[0] = point_ref[0].T


def turn_kernel(level, seq, bins, scale, x_ref, cot_ref, weight_ref, weight_t_ref, point_t_ref, dy_ref, dpre_ref):
    @pl.when(lax.axis_index("pipe") == level)
    def layer():
        x = of_seq(x_ref, seq, bins)
        pre = fore(x, weight_ref, 2**level, bins)
        cot = of_seq(cot_ref, seq, bins)
        dy = (cot.astype(jnp.float32) * scale).astype(jnp.bfloat16)
        dpre = back_pre(dy, gelu_slope(pre), point_t_ref)
        dpre_ref[...] = dpre
        x_slope = gelu_slope(x.astype(jnp.float32))
        dy_ref[...] = back_trunk(dy, dpre, x_slope, weight_t_ref, 2**level, bins)


def slope_kernel(levels, seq_count, bins, *refs):
    xs, pres = refs[: levels * seq_count], refs[levels * seq_count : 2 * levels * seq_count]
    outs = refs[2 * levels * seq_count :]
    for level in range(levels):

        @pl.when(lax.axis_index("pipe") == level)
        def layer(level=level):
            for seq in range(seq_count):
                x = of_seq(xs[level * seq_count + seq], seq, bins)
                outs[2 * seq][...] = gelu_slope(x.astype(jnp.float32))
                outs[2 * seq + 1][...] = gelu_slope(pres[level * seq_count + seq][...])


def back_kernel(level, bins, dy_in_ref, x_slope_ref, pre_slope_ref, weight_ref, point_ref, dy_ref, dpre_ref):
    @pl.when(lax.axis_index("pipe") == level)
    def layer():
        dy = dy_in_ref[...]
        dpre = back_pre(dy, pre_slope_ref[...], point_ref)
        dpre_ref[...] = dpre
        dy_ref[...] = back_trunk(dy, dpre, x_slope_ref[...], weight_ref, 2**level, bins)


def message_kernel(places, *refs):
    blocks, message_ref = refs[:-1], refs[-1]
    size = message_ref.shape[0] // len(places)
    for to, (ref, at) in enumerate(zip(blocks, places)):
        message_ref[to * size : (to + 1) * size, :] = ref[at * size : (at + 1) * size, :]


def head_kernel(sections, earlier, dy_in_ref, slope_ref, point_ref, *refs):
    others, before, out_ref = refs[: sections - 1], refs[sections - 1 : -1], refs[-1]
    section = lax.axis_index("pipe")
    bins = dy_in_ref.shape[0]
    for ref in before:
        out_ref[:earlier, :] = ref[...]

    @pl.when(section == 0)
    def layer():
        out_ref[earlier : earlier + bins, :] = back_pre(dy_in_ref[...], slope_ref[...], point_ref)

    for level in range(1, sections):

        @pl.when(section == level)
        def keep(level=level):
            out_ref[earlier : earlier + bins, :] = others[level - 1][...]


def columns_kernel(groups, runs, kept, *refs):
    refs, (sent_ref,) = refs[:-1], refs[-1:]
    kept_refs = refs[sum(runs) :]
    count = 2 * len(kept)
    section = lax.axis_index("pipe")
    core = lax.axis_index("dp")
    place = lax.axis_index("ctx")
    x, start = None, 0
    for level, run in enumerate(runs):
        pieces = [ref[...] for ref in refs[start : start + run]]
        start += run
        whole = jnp.concatenate(pieces, axis=0).astype(jnp.float32)
        x = whole if x is None else jnp.where(section == level, whole, x)
    act = gelu(x).T.astype(jnp.bfloat16)
    chans = act.shape[0]
    width = chans // (groups * count)
    row = lax.broadcasted_iota(jnp.int32, (width, chans), 0)
    col = lax.broadcasted_iota(jnp.int32, (width, chans), 1)

    def block(offset):
        owner = lax.bitwise_xor(place, offset)
        rows = []
        for step in range(groups):
            first = (lax.rem(core + step, groups) * count + owner) * width
            rows.append((col == first + row).astype(jnp.float32))
        pick = jnp.concatenate(rows, axis=0).astype(jnp.bfloat16)
        return jnp.dot(pick, act, preferred_element_type=jnp.float32).astype(jnp.bfloat16)

    size = groups * width
    for at, offset in enumerate(kept):
        kept_refs[at][...] = block(offset)
        sent_ref[at * size : (at + 1) * size, :] = block(offset ^ 1)


def grad_kernel(sections, bins, places, *refs):
    columns, refs = refs[: len(places)], refs[len(places) :]
    grads, out_ref = refs[:-1], refs[-1]
    section = lax.axis_index("pipe")
    width = out_ref.shape[1]

    def taps(spread):
        act = jnp.concatenate(
            [ref[at : at + width, :] for ref, at in zip(columns, places)], axis=1
        )
        dpre = jnp.concatenate([ref[...] for ref in grads], axis=0)
        wide = dpre.astype(jnp.float32)
        spans = (
            moved(wide, -spread, bins).astype(jnp.bfloat16),
            dpre,
            moved(wide, spread, bins).astype(jnp.bfloat16),
        )
        for tap in range(3):
            out_ref[tap] = jnp.dot(
                act, spans[tap], preferred_element_type=jnp.float32
            ).astype(out_ref.dtype)

    for level in range(sections):

        @pl.when(section == level)
        def run(level=level):
            taps(2**level)


def kernel_call(body, outs, flops, name, waits=(), carries=(), in_spec=in_vmem, scratch=()):
    def call(*args):
        used, taken = len(args), len(args) + len(waits) + len(carries)

        def run(*refs):
            made = refs[taken : taken + len(outs)]
            body(*refs[:used], *made, *refs[taken + len(outs) + len(carries) :])

        moved_bytes = sum(math.prod(a.shape) * a.dtype.itemsize for a in (*args, *outs))
        return pl.pallas_call(
            run,
            out_shape=[*outs, *(jax.ShapeDtypeStruct(a.shape, a.dtype) for a in carries)],
            in_specs=[in_spec] * used + [anywhere] * (taken - used),
            out_specs=[in_vmem] * len(outs) + [anywhere] * len(carries),
            input_output_aliases={
                used + len(waits) + at: len(outs) + at for at in range(len(carries))
            },
            scratch_shapes=list(scratch),
            compiler_params=pltpu.CompilerParams(vmem_limit_bytes=24 * 2**20),
            cost_estimate=pl.CostEstimate(
                flops=flops, bytes_accessed=moved_bytes, transcendentals=0
            ),
            name=name,
        )(*args, *waits, *carries)

    return call


def residue_shards(inputs, cotangent, weight, point):
    sections = lax.axis_size("pipe")
    section = lax.axis_index("pipe")
    count = lax.axis_size("ctx")
    groups = lax.axis_size("dp")
    seq_count, bins, chans = inputs.shape
    inner = weight.shape[3]
    rows = seq_count * bins
    scale = 1.0 / math.sqrt(seq_count * groups * bins * count)
    last = sections - 1
    seqs = range(seq_count)
    layer_flops = 2 * bins * chans * inner * 4

    def shape(*dims, dtype=jnp.bfloat16):
        return jax.ShapeDtypeStruct(dims, dtype)

    def hop(value, source, target, third=None):
        sends = {source: target, target: source}
        if third is not None and third not in sends:
            sends.update({target: third, third: source})
        route = []
        for core in range(groups):
            for stage in range(sections):
                taker = core if stage in sends else (core + 1) % groups
                for i in range(count):
                    giver = (core * sections + stage) * count + i
                    route.append((giver, (taker * sections + sends.get(stage, stage)) * count + i))
        return lax.ppermute(value, ("dp", "pipe", "ctx"), route)

    def onward(value, step):
        return lax.ppermute(value, "ctx", [(i, (i + step) % count) for i in range(count)])

    def exchange(value, offset):
        return lax.ppermute(value, "ctx", [(i, i ^ offset) for i in range(count)])

    payload = jnp.where(section == last, cotangent, inputs)
    parts = kernel_call(
        functools.partial(split_kernel, last),
        [shape(rows // count, chans)] * count,
        10 * seq_count * layer_flops,
        "split",
    )(payload)
    weight, point = kernel_call(
        hold_kernel,
        [shape(*weight.shape), shape(*point.shape)],
        0,
        "hold",
        waits=[parts[0]],
        in_spec=anywhere,
        scratch=[pltpu.SemaphoreType.DMA((2,))],
    )(weight, point)
    steps = [1, *range(count - 1, 1, -1)]
    parts = [*(onward(parts[step], step) for step in steps), parts[0]]

    trunk, inside = shape(bins, chans), shape(bins, inner)
    inside_wide = shape(bins, inner, dtype=jnp.float32)
    whole, out, pre = kernel_call(
        functools.partial(first_kernel, last, bins, [*steps, 0]),
        [shape(rows, chans), trunk, inside_wide],
        layer_flops,
        "first",
    )(*parts, weight, point)
    outs, pres, xs, sent = [out], [[pre]], [[whole]], ()
    for level in range(last):
        if level > 0:
            third = last if level > 1 else None
            xs.append([hop(out, level - 1, level, third) for out in outs])
            outs = []
            pres.append([])
        for seq in range(len(outs), seq_count):
            out, pre = kernel_call(
                functools.partial(fore_kernel, level, seq, bins),
                [trunk, inside_wide],
                layer_flops,
                "fore",
                waits=outs[-1:] or sent,
            )(xs[level][seq if level else 0], weight, point)
            outs.append(out)
            pres[level].append(pre)
        sent = outs
        if level == 1:
            back_weights = kernel_call(
                transpose_kernel,
                [shape(1, weight.shape[1], inner, chans), shape(1, chans, inner)],
                0,
                "transpose",
                waits=outs,
            )(weight, point)
            sent = [*outs, *back_weights]
    slopes = kernel_call(
        functools.partial(slope_kernel, last, seq_count, bins),
        [shape(bins, chans, dtype=jnp.float32), inside_wide] * seq_count,
        0,
        "slopes",
        waits=outs,
    )(
        *[xs[level][seq if level else 0] for level in range(last) for seq in seqs],
        *[pre for some in pres for pre in some],
    )
    sent = [*sent, *slopes]
    xs.append([hop(out, last - 1, last, 0) for out in outs])

    dys, dpres = [], [[] for level in range(sections)]
    for seq in seqs:
        dy, dpre = kernel_call(
            functools.partial(turn_kernel, last, seq, bins, scale),
            [trunk, inside],
            2 * layer_flops,
            "turn",
            waits=dys[-1:] or sent,
        )(xs[last][seq], whole, weight, *back_weights)
        dys.append(dy)
        dpres[last].append(dpre)
    kept = list(range(0, count, 2))
    moving = [(offset, 0) for offset in range(1, count, 2)]
    size = chans // count
    *owned, message = kernel_call(
        functools.partial(columns_kernel, groups, [len(x) for x in xs], kept),
        [shape(size, rows)] * len(kept) + [shape(size * len(kept), rows)],
        2 * rows * chans * chans,
        "columns",
        waits=dys,
    )(*[x for some in xs for x in some])
    blocks = {(offset, 0): (array, 0) for offset, array in zip(kept, owned)}
    sent = [owned[0]]
    dys = [hop(dy, last, last - 1) for dy in dys]
    message, bit = exchange(message, 1), 1
    blocks.update({(to ^ 1, start ^ 1): (message, at) for at, (to, start) in enumerate(moving)})

    for level in range(last - 1, 0, -1):
        outs = []
        for seq in seqs:
            dy, dpre = kernel_call(
                functools.partial(back_kernel, level, bins),
                [trunk, inside],
                layer_flops,
                "back",
                waits=outs[-1:] or sent,
            )(dys[seq], *slopes[2 * seq : 2 * seq + 2], *back_weights)
            outs.append(dy)
            dpres[level].append(dpre)
        sent = outs
        dys = [hop(dy, level, level - 1, None if level > 1 else last) for dy in outs]
        bit *= 2
        moving = sorted(key for key in blocks if key[0] & bit)
        if moving:
            (message,) = kernel_call(
                functools.partial(message_kernel, [blocks[key][1] for key in moving]),
                [shape(size * len(moving), rows)],
                0,
                "message",
                waits=outs,
            )(*[blocks[key][0] for key in moving])
            sent = [*outs, message]
            message = exchange(message, bit)
            for at, (to, start) in enumerate(moving):
                blocks[to ^ bit, start ^ bit] = (message, at)

    sent = [*sent, message]
    dpre = []
    for seq in seqs:
        dpre = kernel_call(
            functools.partial(head_kernel, sections, seq * bins),
            [shape((seq + 1) * bins, inner)],
            layer_flops // 4,
            "head",
            waits=dpre or sent,
        )(dys[seq], slopes[2 * seq + 1], back_weights[1], *[dpres[level][seq] for level in range(1, sections)], *dpre)
    (dpre,) = dpre
    offsets = range(1, count)
    gathered = [*(exchange(dpre, offset) for offset in offsets), dpre]
    columns = [blocks[0, offset] for offset in [*offsets, 0]]
    width = size // groups

    def gradient(step, dtype, waits=()):
        places = [at * size + step * width for array, at in columns]
        (part,) = kernel_call(
            functools.partial(grad_kernel, sections, bins, places),
            [shape(3, width, inner, dtype=dtype)],
            2 * 3 * rows * count * width * inner,
            "grad",
            waits=waits,
        )(*[array for array, at in columns], *gathered)
        return part

    others = [gradient(step, jnp.bfloat16) for step in range(1, groups)]
    mine = gradient(0, jnp.float32, waits=others)
    for step, other in enumerate(others, 1):
        route = [(i, (i + step) % groups) for i in range(groups)]
        mine = mine + lax.ppermute(other, "dp", route).astype(jnp.float32)
    return mine[None]


def solution(mesh):
    def shards(inputs, cotangent, dilated_kernel_weight, point_weight):
        bins = inputs.shape[1]
        first_spread = bins // 2 // 2 ** (mesh.shape["pipe"] - 1)
        count = mesh.shape["ctx"]
        residues = (
            first_spread == count
            and mesh.shape["pipe"] > 2
            and bins % (16 * count) == 0
            and 1 < count == 1 << (count.bit_length() - 1) <= 1 << (mesh.shape["pipe"] - 2)
            and inputs.shape[2] % (count * mesh.shape["dp"]) == 0
        )
        plan = residue_shards if residues else edge_shards
        return plan(inputs, cotangent, dilated_kernel_weight, point_weight)

    return jax.shard_map(
        shards,
        mesh=mesh,
        in_specs=(
            P("dp", "ctx", None),
            P("dp", "ctx", None),
            P("pipe", None, None, None),
            P("pipe", None, None),
        ),
        out_specs=P("pipe", None, ("dp", "ctx"), None),
        check_vma=False,
    )
```

```python
import functools
import math

import jax
import jax.numpy as jnp
from jax import lax
from jax.experimental import pallas as pl
from jax.experimental.pallas import tpu as pltpu
from jax.sharding import PartitionSpec as P

root_half = 0.7071067811865476
inv_root_two_pi = 0.3989422804014327

in_vmem = pl.BlockSpec(memory_space=pltpu.VMEM)
anywhere = pl.BlockSpec(memory_space=pl.ANY)
contract_last = (((1,), (1,)), ((), ()))
contract_first = (((0,), (0,)), ((), ()))


def gelu(value):
    return 0.5 * value * (1.0 + lax.erf(value * root_half))


def gelu_slope(value):
    return (
        0.5 * (1.0 + lax.erf(value * root_half))
        + value * jnp.exp(-0.5 * value * value) * inv_root_two_pi
    )


def padded(cells, sides, width):
    for axis, dim in sides:
        count = lax.axis_size(axis)
        ends = count - 1
        head = lax.slice_in_dim(cells, 0, width, axis=dim)
        tail = lax.slice_in_dim(cells, cells.shape[dim] - width, cells.shape[dim], axis=dim)
        cells = jnp.concatenate(
            [
                lax.ppermute(tail, axis, [(i, (i + 1) % count) for i in range(ends)]),
                cells,
                lax.ppermute(head, axis, [((i + 1) % count, i) for i in range(ends)]),
            ],
            axis=dim,
        )
    return cells


def shifted(block, axis, distance):
    devices = range(lax.axis_size(axis))
    route = [(i - distance, i) for i in devices if i - distance in devices]
    return lax.ppermute(block, axis, route)


def edge_shards(inputs, cotangent, dilated_kernel_weight, point_weight):
    sections = lax.axis_size("pipe")
    section = lax.axis_index("pipe")
    seq_count, bins, chans = inputs.shape
    reach = bins // 2
    table = jnp.array(
        [reach // 2 ** (sections - 1 - level) for level in range(sections)], jnp.int32
    )
    spread = table[section]
    dilation_weight = dilated_kernel_weight[0]
    w_point = point_weight[0]
    inner_channel_count = dilation_weight.shape[2]
    scale = 1.0 / math.sqrt(seq_count * lax.axis_size("dp") * bins * lax.axis_size("ctx"))
    ticks = jnp.arange(seq_count + sections - 1, dtype=jnp.int32)

    def conv_fore(extended):
        running_total = jnp.zeros((bins, inner_channel_count), jnp.float32)
        for kernel_offset in range(3):
            receptive_span = lax.dynamic_slice_in_dim(
                extended, reach + (kernel_offset - 1) * spread, bins, 0
            )
            running_total = running_total + jnp.dot(
                receptive_span, dilation_weight[kernel_offset], preferred_element_type=jnp.float32
            )
        return running_total

    def put(store, slot, valid, item):
        current = lax.dynamic_index_in_dim(store, slot, 0, keepdims=False)
        return lax.dynamic_update_index_in_dim(store, jnp.where(valid, item, current), slot, 0)

    kept_x = jnp.zeros(inputs.shape, jnp.bfloat16)
    kept_ext = jnp.zeros((seq_count, bins + 2 * reach, chans), jnp.bfloat16)
    kept_pre = jnp.zeros((seq_count, bins, inner_channel_count), jnp.float32)

    def fore_tick(carry, tick):
        received, store_x, store_ext, store_pre = carry
        micro = tick - section
        valid = (micro >= 0) & (micro < seq_count)
        slot = jnp.clip(micro, 0, seq_count - 1)
        first = lax.dynamic_index_in_dim(inputs, slot, 0, keepdims=False)
        trunk_in = jnp.where(section == 0, first, received)
        act = gelu(trunk_in.astype(jnp.float32)).astype(jnp.bfloat16)
        extended = padded(act, (("ctx", 0),), reach)
        pre = conv_fore(extended)
        inner = gelu(pre).astype(jnp.bfloat16)
        out = (
            trunk_in.astype(jnp.float32)
            + jnp.dot(inner, w_point, preferred_element_type=jnp.float32)
        ).astype(jnp.bfloat16)
        sent = shifted(out, "pipe", 1)
        store_x = put(store_x, slot, valid, trunk_in)
        store_ext = put(store_ext, slot, valid, extended)
        store_pre = put(store_pre, slot, valid, pre)
        return ((sent, store_x, store_ext, store_pre), None)

    start_recv = jnp.zeros((bins, chans), jnp.bfloat16)
    (unused, kept_x, kept_ext, kept_pre), unused_out = lax.scan(
        fore_tick, (start_recv, kept_x, kept_ext, kept_pre), ticks
    )

    def back_tick(carry, tick):
        received, grad = carry
        micro = tick - (sections - 1 - section)
        valid = (micro >= 0) & (micro < seq_count)
        slot = jnp.clip(micro, 0, seq_count - 1)
        last = (
            lax.dynamic_index_in_dim(cotangent, slot, 0, keepdims=False).astype(jnp.float32) * scale
        ).astype(jnp.bfloat16)
        upstream = jnp.where(section == sections - 1, last, received)
        trunk_in = lax.dynamic_index_in_dim(kept_x, slot, 0, keepdims=False)
        extended = lax.dynamic_index_in_dim(kept_ext, slot, 0, keepdims=False)
        pre = lax.dynamic_index_in_dim(kept_pre, slot, 0, keepdims=False)
        inner_grad = lax.dot_general(
            upstream, w_point, contract_last, preferred_element_type=jnp.float32
        )
        dpre = (inner_grad * gelu_slope(pre) * valid.astype(jnp.float32)).astype(jnp.bfloat16)
        dpre_ext = padded(dpre, (("ctx", 0),), reach)
        dact = jnp.zeros((bins, chans), jnp.float32)
        taps = []
        for kernel_offset in range(3):
            receptive_span = lax.dynamic_slice_in_dim(
                dpre_ext, reach - (kernel_offset - 1) * spread, bins, 0
            )
            dact = dact + lax.dot_general(
                receptive_span,
                dilation_weight[kernel_offset],
                contract_last,
                preferred_element_type=jnp.float32,
            )
            source = lax.dynamic_slice_in_dim(
                extended, reach + (kernel_offset - 1) * spread, bins, 0
            )
            taps.append(
                lax.dot_general(source, dpre, contract_first, preferred_element_type=jnp.float32)
            )
        grad = grad + jnp.stack(taps)
        back = (
            upstream.astype(jnp.float32) + dact * gelu_slope(trunk_in.astype(jnp.float32))
        ).astype(jnp.bfloat16)
        sent = shifted(back, "pipe", -1)
        return ((sent, grad), None)

    start_grad = jnp.zeros((3, chans, inner_channel_count), jnp.float32)
    (unused_back, grad), unused_seq = lax.scan(back_tick, (start_recv, start_grad), ticks)
    term = grad[None]
    return lax.psum_scatter(term, ("dp", "ctx"), scatter_dimension=2, tiled=True)


def moved(value, by, bins):
    pieces = []
    for start in range(0, value.shape[0], bins):
        piece = value[start : start + bins]
        place = lax.broadcasted_iota(jnp.int32, piece.shape, 0)
        if by > 0:
            keep = place >= by
        else:
            keep = place < bins + by
        pieces.append(jnp.where(keep, pltpu.roll(piece, by % bins, 0), 0.0))
    return jnp.concatenate(pieces, axis=0)


def fore(x, weight_ref, spread, bins):
    act = gelu(x.astype(jnp.float32)).astype(jnp.bfloat16)
    terms = [
        jnp.dot(act, weight_ref[0, tap], preferred_element_type=jnp.float32) for tap in range(3)
    ]
    return terms[1] + moved(terms[0], spread, bins) + moved(terms[2], -spread, bins)


def back_pre(dy, pre_slope, point_ref):
    inner_grad = jnp.dot(dy, point_ref[0], preferred_element_type=jnp.float32)
    return (inner_grad * pre_slope).astype(jnp.bfloat16)


def back_trunk(dy, dpre, x_slope, weight_ref, spread, bins):
    wide = dpre.astype(jnp.float32)
    spans = (
        moved(wide, -spread, bins).astype(jnp.bfloat16),
        dpre,
        moved(wide, spread, bins).astype(jnp.bfloat16),
    )
    dact = jnp.zeros(dy.shape, jnp.float32)
    for tap in range(3):
        dact = dact + jnp.dot(
            spans[tap], weight_ref[0, tap], preferred_element_type=jnp.float32
        )
    return (dy.astype(jnp.float32) + dact * x_slope).astype(jnp.bfloat16)


def of_seq(ref, seq, bins):
    if ref.shape[0] == bins:
        return ref[...]
    return ref[seq * bins : (seq + 1) * bins, :]


def split_kernel(last, payload_ref, *out_refs):
    count = len(out_refs)
    seq_count, bins, chans = payload_ref.shape
    part = bins // count
    section = lax.axis_index("pipe")
    place = lax.axis_index("ctx")

    @pl.when((section == 0) | (section == last))
    def send():
        source = payload_ref[...].reshape(seq_count * bins, chans)
        row = lax.broadcasted_iota(jnp.int32, (part, seq_count * bins), 0)
        col = lax.broadcasted_iota(jnp.int32, (part, seq_count * bins), 1)
        for hop in range(count):
            residue = lax.rem(place + hop, count)
            rows = [
                (col == seq * bins + count * row + residue).astype(jnp.float32)
                for seq in range(seq_count)
            ]
            pick = jnp.concatenate(rows, axis=0).astype(jnp.bfloat16)
            out_refs[hop][...] = jnp.dot(
                pick, source, preferred_element_type=jnp.float32
            ).astype(jnp.bfloat16)


def hold_kernel(weight_ref, point_ref, weight_out, point_out, sems):
    loads = [
        pltpu.make_async_copy(weight_ref, weight_out, sems.at[0]),
        pltpu.make_async_copy(point_ref, point_out, sems.at[1]),
    ]
    for load in loads:
        load.start()
    for load in loads:
        load.wait()


def first_kernel(last, bins, steps, *refs):
    parts, (weight_ref, point_ref, whole_ref, out_ref, pre_ref) = refs[:-5], refs[-5:]
    count = len(parts)
    section = lax.axis_index("pipe")
    place = lax.axis_index("ctx")
    part = bins // count
    seq_count = whole_ref.shape[0] // bins

    @pl.when((section == 0) | (section == last))
    def gather():
        for step, part_ref in zip(steps, parts):
            source = lax.rem(place + count - step, count)
            for seq in range(seq_count):
                at = pl.multiple_of(seq * bins + source * part, part)
                whole_ref[pl.ds(at, part), :] = part_ref[seq * part : (seq + 1) * part, :]

    @pl.when(section == 0)
    def layer():
        x = whole_ref[:bins, :]
        finish(x, fore(x, weight_ref, 1, bins), point_ref, out_ref, pre_ref)


def finish(x, pre, point_ref, out_ref, pre_ref):
    pre_ref[...] = pre
    branch = jnp.dot(
        gelu(pre).astype(jnp.bfloat16), point_ref[0], preferred_element_type=jnp.float32
    )
    out_ref[...] = (x.astype(jnp.float32) + branch).astype(jnp.bfloat16)


def fore_kernel(level, seq, bins, x_ref, weight_ref, point_ref, out_ref, pre_ref):
    @pl.when(lax.axis_index("pipe") == level)
    def layer():
        x = of_seq(x_ref, seq, bins)
        finish(x, fore(x, weight_ref, 2**level, bins), point_ref, out_ref, pre_ref)


def transpose_kernel(weight_ref, point_ref, weight_out, point_out):
    for tap in range(weight_ref.shape[1]):
        weight_out[0, tap] = weight_ref[0, tap].T
    point_out[0] = point_ref[0].T


def turn_kernel(level, seq, bins, scale, x_ref, cot_ref, weight_ref, weight_t_ref, point_t_ref, dy_ref, dpre_ref):
    @pl.when(lax.axis_index("pipe") == level)
    def layer():
        x = of_seq(x_ref, seq, bins)
        pre = fore(x, weight_ref, 2**level, bins)
        cot = of_seq(cot_ref, seq, bins)
        dy = (cot.astype(jnp.float32) * scale).astype(jnp.bfloat16)
        dpre = back_pre(dy, gelu_slope(pre), point_t_ref)
        dpre_ref[...] = dpre
        x_slope = gelu_slope(x.astype(jnp.float32))
        dy_ref[...] = back_trunk(dy, dpre, x_slope, weight_t_ref, 2**level, bins)


def slope_kernel(levels, seq_count, bins, *refs):
    xs, pres = refs[: levels * seq_count], refs[levels * seq_count : 2 * levels * seq_count]
    outs = refs[2 * levels * seq_count :]
    for level in range(levels):

        @pl.when(lax.axis_index("pipe") == level)
        def layer(level=level):
            for seq in range(seq_count):
                x = of_seq(xs[level * seq_count + seq], seq, bins)
                outs[2 * seq][...] = gelu_slope(x.astype(jnp.float32))
                outs[2 * seq + 1][...] = gelu_slope(pres[level * seq_count + seq][...])


def back_kernel(level, bins, dy_in_ref, x_slope_ref, pre_slope_ref, weight_ref, point_ref, dy_ref, dpre_ref):
    @pl.when(lax.axis_index("pipe") == level)
    def layer():
        dy = dy_in_ref[...]
        dpre = back_pre(dy, pre_slope_ref[...], point_ref)
        dpre_ref[...] = dpre
        dy_ref[...] = back_trunk(dy, dpre, x_slope_ref[...], weight_ref, 2**level, bins)


def message_kernel(places, *refs):
    blocks, message_ref = refs[:-1], refs[-1]
    size = message_ref.shape[0] // len(places)
    for to, (ref, at) in enumerate(zip(blocks, places)):
        message_ref[to * size : (to + 1) * size, :] = ref[at * size : (at + 1) * size, :]


def head_kernel(sections, earlier, dy_in_ref, slope_ref, point_ref, *refs):
    others, before, out_ref = refs[: sections - 1], refs[sections - 1 : -1], refs[-1]
    section = lax.axis_index("pipe")
    bins = dy_in_ref.shape[0]
    for ref in before:
        out_ref[:earlier, :] = ref[...]

    @pl.when(section == 0)
    def layer():
        out_ref[earlier : earlier + bins, :] = back_pre(dy_in_ref[...], slope_ref[...], point_ref)

    for level in range(1, sections):

        @pl.when(section == level)
        def keep(level=level):
            out_ref[earlier : earlier + bins, :] = others[level - 1][...]


def columns_kernel(groups, runs, kept, *refs):
    refs, (sent_ref,) = refs[:-1], refs[-1:]
    kept_refs = refs[sum(runs) :]
    count = 2 * len(kept)
    section = lax.axis_index("pipe")
    core = lax.axis_index("dp")
    place = lax.axis_index("ctx")
    x, start = None, 0
    for level, run in enumerate(runs):
        pieces = [ref[...] for ref in refs[start : start + run]]
        start += run
        whole = jnp.concatenate(pieces, axis=0).astype(jnp.float32)
        x = whole if x is None else jnp.where(section == level, whole, x)
    act = gelu(x).T.astype(jnp.bfloat16)
    chans = act.shape[0]
    width = chans // (groups * count)
    row = lax.broadcasted_iota(jnp.int32, (width, chans), 0)
    col = lax.broadcasted_iota(jnp.int32, (width, chans), 1)

    def block(offset):
        owner = lax.bitwise_xor(place, offset)
        rows = []
        for step in range(groups):
            first = (lax.rem(core + step, groups) * count + owner) * width
            rows.append((col == first + row).astype(jnp.float32))
        pick = jnp.concatenate(rows, axis=0).astype(jnp.bfloat16)
        return jnp.dot(pick, act, preferred_element_type=jnp.float32).astype(jnp.bfloat16)

    size = groups * width
    for at, offset in enumerate(kept):
        kept_refs[at][...] = block(offset)
        sent_ref[at * size : (at + 1) * size, :] = block(offset ^ 1)


def grad_kernel(sections, bins, places, *refs):
    columns, refs = refs[: len(places)], refs[len(places) :]
    grads, out_ref = refs[:-1], refs[-1]
    section = lax.axis_index("pipe")
    width = out_ref.shape[1]

    def taps(spread):
        act = jnp.concatenate(
            [ref[at : at + width, :] for ref, at in zip(columns, places)], axis=1
        )
        dpre = jnp.concatenate([ref[...] for ref in grads], axis=0)
        wide = dpre.astype(jnp.float32)
        spans = (
            moved(wide, -spread, bins).astype(jnp.bfloat16),
            dpre,
            moved(wide, spread, bins).astype(jnp.bfloat16),
        )
        for tap in range(3):
            out_ref[tap] = jnp.dot(
                act, spans[tap], preferred_element_type=jnp.float32
            ).astype(out_ref.dtype)

    for level in range(sections):

        @pl.when(section == level)
        def run(level=level):
            taps(2**level)


def kernel_call(body, outs, flops, name, waits=(), carries=(), in_spec=in_vmem, scratch=()):
    def call(*args):
        used, taken = len(args), len(args) + len(waits) + len(carries)

        def run(*refs):
            made = refs[taken : taken + len(outs)]
            body(*refs[:used], *made, *refs[taken + len(outs) + len(carries) :])

        moved_bytes = sum(math.prod(a.shape) * a.dtype.itemsize for a in (*args, *outs))
        return pl.pallas_call(
            run,
            out_shape=[*outs, *(jax.ShapeDtypeStruct(a.shape, a.dtype) for a in carries)],
            in_specs=[in_spec] * used + [anywhere] * (taken - used),
            out_specs=[in_vmem] * len(outs) + [anywhere] * len(carries),
            input_output_aliases={
                used + len(waits) + at: len(outs) + at for at in range(len(carries))
            },
            scratch_shapes=list(scratch),
            compiler_params=pltpu.CompilerParams(vmem_limit_bytes=24 * 2**20),
            cost_estimate=pl.CostEstimate(
                flops=flops, bytes_accessed=moved_bytes, transcendentals=0
            ),
            name=name,
        )(*args, *waits, *carries)

    return call


def residue_shards(inputs, cotangent, weight, point):
    sections = lax.axis_size("pipe")
    section = lax.axis_index("pipe")
    count = lax.axis_size("ctx")
    groups = lax.axis_size("dp")
    seq_count, bins, chans = inputs.shape
    inner = weight.shape[3]
    rows = seq_count * bins
    scale = 1.0 / math.sqrt(seq_count * groups * bins * count)
    last = sections - 1
    seqs = range(seq_count)
    layer_flops = 2 * bins * chans * inner * 4

    def shape(*dims, dtype=jnp.bfloat16):
        return jax.ShapeDtypeStruct(dims, dtype)

    def hop(value, source, target, third=None):
        sends = {source: target, target: source}
        if third is not None and third not in sends:
            sends.update({target: third, third: source})
        route = []
        for core in range(groups):
            for stage in range(sections):
                taker = core if stage in sends else (core + 1) % groups
                for i in range(count):
                    giver = (core * sections + stage) * count + i
                    route.append((giver, (taker * sections + sends.get(stage, stage)) * count + i))
        return lax.ppermute(value, ("dp", "pipe", "ctx"), route)

    def onward(value, step):
        return lax.ppermute(value, "ctx", [(i, (i + step) % count) for i in range(count)])

    def exchange(value, offset):
        return lax.ppermute(value, "ctx", [(i, i ^ offset) for i in range(count)])

    payload = jnp.where(section == last, cotangent, inputs)
    parts = kernel_call(
        functools.partial(split_kernel, last),
        [shape(rows // count, chans)] * count,
        10 * seq_count * layer_flops,
        "split",
    )(payload)
    weight, point = kernel_call(
        hold_kernel,
        [shape(*weight.shape), shape(*point.shape)],
        0,
        "hold",
        waits=[parts[0]],
        in_spec=anywhere,
        scratch=[pltpu.SemaphoreType.DMA((2,))],
    )(weight, point)
    steps = [1, *range(count - 1, 1, -1)]
    parts = [*(onward(parts[step], step) for step in steps), parts[0]]

    trunk, inside = shape(bins, chans), shape(bins, inner)
    inside_wide = shape(bins, inner, dtype=jnp.float32)
    whole, out, pre = kernel_call(
        functools.partial(first_kernel, last, bins, [*steps, 0]),
        [shape(rows, chans), trunk, inside_wide],
        layer_flops,
        "first",
    )(*parts, weight, point)
    outs, pres, xs, sent = [out], [[pre]], [[whole]], ()
    for level in range(last):
        if level > 0:
            third = last if level > 1 else None
            xs.append([hop(out, level - 1, level, third) for out in outs])
            outs = []
            pres.append([])
        for seq in range(len(outs), seq_count):
            out, pre = kernel_call(
                functools.partial(fore_kernel, level, seq, bins),
                [trunk, inside_wide],
                layer_flops,
                "fore",
                waits=outs[-1:] or sent,
            )(xs[level][seq if level else 0], weight, point)
            outs.append(out)
            pres[level].append(pre)
        sent = outs
        if level == 1:
            back_weights = kernel_call(
                transpose_kernel,
                [shape(1, weight.shape[1], inner, chans), shape(1, chans, inner)],
                0,
                "transpose",
                waits=outs,
            )(weight, point)
            sent = [*outs, *back_weights]
    slopes = kernel_call(
        functools.partial(slope_kernel, last, seq_count, bins),
        [shape(bins, chans, dtype=jnp.float32), inside_wide] * seq_count,
        0,
        "slopes",
        waits=outs,
    )(
        *[xs[level][seq if level else 0] for level in range(last) for seq in seqs],
        *[pre for some in pres for pre in some],
    )
    sent = [*sent, *slopes]
    xs.append([hop(out, last - 1, last, 0) for out in outs])

    dys, dpres = [], [[] for level in range(sections)]
    for seq in seqs:
        dy, dpre = kernel_call(
            functools.partial(turn_kernel, last, seq, bins, scale),
            [trunk, inside],
            2 * layer_flops,
            "turn",
            waits=dys[-1:] or sent,
        )(xs[last][seq], whole, weight, *back_weights)
        dys.append(dy)
        dpres[last].append(dpre)
    kept = list(range(0, count, 2))
    moving = [(offset, 0) for offset in range(1, count, 2)]
    size = chans // count
    *owned, message = kernel_call(
        functools.partial(columns_kernel, groups, [len(x) for x in xs], kept),
        [shape(size, rows)] * len(kept) + [shape(size * len(kept), rows)],
        2 * rows * chans * chans,
        "columns",
        waits=dys,
    )(*[x for some in xs for x in some])
    blocks = {(offset, 0): (array, 0) for offset, array in zip(kept, owned)}
    sent = [owned[0]]
    dys = [hop(dy, last, last - 1) for dy in dys]
    message, bit = exchange(message, 1), 1
    blocks.update({(to ^ 1, start ^ 1): (message, at) for at, (to, start) in enumerate(moving)})

    for level in range(last - 1, 0, -1):
        outs = []
        for seq in seqs:
            dy, dpre = kernel_call(
                functools.partial(back_kernel, level, bins),
                [trunk, inside],
                layer_flops,
                "back",
                waits=outs[-1:] or sent,
            )(dys[seq], *slopes[2 * seq : 2 * seq + 2], *back_weights)
            outs.append(dy)
            dpres[level].append(dpre)
        sent = outs
        dys = [hop(dy, level, level - 1, None if level > 1 else last) for dy in outs]
        bit *= 2
        moving = sorted(key for key in blocks if key[0] & bit)
        if moving:
            (message,) = kernel_call(
                functools.partial(message_kernel, [blocks[key][1] for key in moving]),
                [shape(size * len(moving), rows)],
                0,
                "message",
                waits=outs,
            )(*[blocks[key][0] for key in moving])
            sent = [*outs, message]
            message = exchange(message, bit)
            for at, (to, start) in enumerate(moving):
                blocks[to ^ bit, start ^ bit] = (message, at)

    sent = [*sent, message]
    dpre = []
    for seq in seqs:
        dpre = kernel_call(
            functools.partial(head_kernel, sections, seq * bins),
            [shape((seq + 1) * bins, inner)],
            layer_flops // 4,
            "head",
            waits=dpre or sent,
        )(dys[seq], slopes[2 * seq + 1], back_weights[1], *[dpres[level][seq] for level in range(1, sections)], *dpre)
    (dpre,) = dpre
    received, bit = {0: dpre}, count // 2
    while bit:
        received.update({offset ^ bit: exchange(block, bit) for offset, block in received.items()})
        bit //= 2
    offsets = [*received]
    gathered = [received[offset] for offset in offsets]
    columns = [blocks[0, offset] for offset in offsets]
    width = size // groups

    def gradient(step, dtype, waits=()):
        places = [at * size + step * width for array, at in columns]
        (part,) = kernel_call(
            functools.partial(grad_kernel, sections, bins, places),
            [shape(3, width, inner, dtype=dtype)],
            2 * 3 * rows * count * width * inner,
            "grad",
            waits=waits,
        )(*[array for array, at in columns], *gathered)
        return part

    others = [gradient(step, jnp.bfloat16) for step in range(1, groups)]
    mine = gradient(0, jnp.float32, waits=others)
    for step, other in enumerate(others, 1):
        route = [(i, (i + step) % groups) for i in range(groups)]
        mine = mine + lax.ppermute(other, "dp", route).astype(jnp.float32)
    return mine[None]


def solution(mesh):
    def shards(inputs, cotangent, dilated_kernel_weight, point_weight):
        bins = inputs.shape[1]
        first_spread = bins // 2 // 2 ** (mesh.shape["pipe"] - 1)
        count = mesh.shape["ctx"]
        residues = (
            first_spread == count
            and mesh.shape["pipe"] > 2
            and bins % (16 * count) == 0
            and 1 < count == 1 << (count.bit_length() - 1) <= 1 << (mesh.shape["pipe"] - 2)
            and inputs.shape[2] % (count * mesh.shape["dp"]) == 0
        )
        plan = residue_shards if residues else edge_shards
        return plan(inputs, cotangent, dilated_kernel_weight, point_weight)

    return jax.shard_map(
        shards,
        mesh=mesh,
        in_specs=(
            P("dp", "ctx", None),
            P("dp", "ctx", None),
            P("pipe", None, None, None),
            P("pipe", None, None),
        ),
        out_specs=P("pipe", None, ("dp", "ctx"), None),
        check_vma=False,
    )
```

```python
import functools
import math

import jax
import jax.numpy as jnp
from jax import lax
from jax.experimental import pallas as pl
from jax.experimental.pallas import tpu as pltpu
from jax.sharding import PartitionSpec as P

root_half = 0.7071067811865476
inv_root_two_pi = 0.3989422804014327

in_vmem = pl.BlockSpec(memory_space=pltpu.VMEM)
anywhere = pl.BlockSpec(memory_space=pl.ANY)
contract_last = (((1,), (1,)), ((), ()))
contract_first = (((0,), (0,)), ((), ()))


def gelu(value):
    return 0.5 * value * (1.0 + lax.erf(value * root_half))


def gelu_slope(value):
    return (
        0.5 * (1.0 + lax.erf(value * root_half))
        + value * jnp.exp(-0.5 * value * value) * inv_root_two_pi
    )


def padded(cells, sides, width):
    for axis, dim in sides:
        count = lax.axis_size(axis)
        ends = count - 1
        head = lax.slice_in_dim(cells, 0, width, axis=dim)
        tail = lax.slice_in_dim(cells, cells.shape[dim] - width, cells.shape[dim], axis=dim)
        cells = jnp.concatenate(
            [
                lax.ppermute(tail, axis, [(i, (i + 1) % count) for i in range(ends)]),
                cells,
                lax.ppermute(head, axis, [((i + 1) % count, i) for i in range(ends)]),
            ],
            axis=dim,
        )
    return cells


def shifted(block, axis, distance):
    devices = range(lax.axis_size(axis))
    route = [(i - distance, i) for i in devices if i - distance in devices]
    return lax.ppermute(block, axis, route)


def edge_shards(inputs, cotangent, dilated_kernel_weight, point_weight):
    sections = lax.axis_size("pipe")
    section = lax.axis_index("pipe")
    seq_count, bins, chans = inputs.shape
    reach = bins // 2
    table = jnp.array(
        [reach // 2 ** (sections - 1 - level) for level in range(sections)], jnp.int32
    )
    spread = table[section]
    dilation_weight = dilated_kernel_weight[0]
    w_point = point_weight[0]
    inner_channel_count = dilation_weight.shape[2]
    scale = 1.0 / math.sqrt(seq_count * lax.axis_size("dp") * bins * lax.axis_size("ctx"))
    ticks = jnp.arange(seq_count + sections - 1, dtype=jnp.int32)

    def conv_fore(extended):
        running_total = jnp.zeros((bins, inner_channel_count), jnp.float32)
        for kernel_offset in range(3):
            receptive_span = lax.dynamic_slice_in_dim(
                extended, reach + (kernel_offset - 1) * spread, bins, 0
            )
            running_total = running_total + jnp.dot(
                receptive_span, dilation_weight[kernel_offset], preferred_element_type=jnp.float32
            )
        return running_total

    def put(store, slot, valid, item):
        current = lax.dynamic_index_in_dim(store, slot, 0, keepdims=False)
        return lax.dynamic_update_index_in_dim(store, jnp.where(valid, item, current), slot, 0)

    kept_x = jnp.zeros(inputs.shape, jnp.bfloat16)
    kept_ext = jnp.zeros((seq_count, bins + 2 * reach, chans), jnp.bfloat16)
    kept_pre = jnp.zeros((seq_count, bins, inner_channel_count), jnp.float32)

    def fore_tick(carry, tick):
        received, store_x, store_ext, store_pre = carry
        micro = tick - section
        valid = (micro >= 0) & (micro < seq_count)
        slot = jnp.clip(micro, 0, seq_count - 1)
        first = lax.dynamic_index_in_dim(inputs, slot, 0, keepdims=False)
        trunk_in = jnp.where(section == 0, first, received)
        act = gelu(trunk_in.astype(jnp.float32)).astype(jnp.bfloat16)
        extended = padded(act, (("ctx", 0),), reach)
        pre = conv_fore(extended)
        inner = gelu(pre).astype(jnp.bfloat16)
        out = (
            trunk_in.astype(jnp.float32)
            + jnp.dot(inner, w_point, preferred_element_type=jnp.float32)
        ).astype(jnp.bfloat16)
        sent = shifted(out, "pipe", 1)
        store_x = put(store_x, slot, valid, trunk_in)
        store_ext = put(store_ext, slot, valid, extended)
        store_pre = put(store_pre, slot, valid, pre)
        return ((sent, store_x, store_ext, store_pre), None)

    start_recv = jnp.zeros((bins, chans), jnp.bfloat16)
    (unused, kept_x, kept_ext, kept_pre), unused_out = lax.scan(
        fore_tick, (start_recv, kept_x, kept_ext, kept_pre), ticks
    )

    def back_tick(carry, tick):
        received, grad = carry
        micro = tick - (sections - 1 - section)
        valid = (micro >= 0) & (micro < seq_count)
        slot = jnp.clip(micro, 0, seq_count - 1)
        last = (
            lax.dynamic_index_in_dim(cotangent, slot, 0, keepdims=False).astype(jnp.float32) * scale
        ).astype(jnp.bfloat16)
        upstream = jnp.where(section == sections - 1, last, received)
        trunk_in = lax.dynamic_index_in_dim(kept_x, slot, 0, keepdims=False)
        extended = lax.dynamic_index_in_dim(kept_ext, slot, 0, keepdims=False)
        pre = lax.dynamic_index_in_dim(kept_pre, slot, 0, keepdims=False)
        inner_grad = lax.dot_general(
            upstream, w_point, contract_last, preferred_element_type=jnp.float32
        )
        dpre = (inner_grad * gelu_slope(pre) * valid.astype(jnp.float32)).astype(jnp.bfloat16)
        dpre_ext = padded(dpre, (("ctx", 0),), reach)
        dact = jnp.zeros((bins, chans), jnp.float32)
        taps = []
        for kernel_offset in range(3):
            receptive_span = lax.dynamic_slice_in_dim(
                dpre_ext, reach - (kernel_offset - 1) * spread, bins, 0
            )
            dact = dact + lax.dot_general(
                receptive_span,
                dilation_weight[kernel_offset],
                contract_last,
                preferred_element_type=jnp.float32,
            )
            source = lax.dynamic_slice_in_dim(
                extended, reach + (kernel_offset - 1) * spread, bins, 0
            )
            taps.append(
                lax.dot_general(source, dpre, contract_first, preferred_element_type=jnp.float32)
            )
        grad = grad + jnp.stack(taps)
        back = (
            upstream.astype(jnp.float32) + dact * gelu_slope(trunk_in.astype(jnp.float32))
        ).astype(jnp.bfloat16)
        sent = shifted(back, "pipe", -1)
        return ((sent, grad), None)

    start_grad = jnp.zeros((3, chans, inner_channel_count), jnp.float32)
    (unused_back, grad), unused_seq = lax.scan(back_tick, (start_recv, start_grad), ticks)
    term = grad[None]
    return lax.psum_scatter(term, ("dp", "ctx"), scatter_dimension=2, tiled=True)


def moved(value, by, bins):
    pieces = []
    for start in range(0, value.shape[0], bins):
        piece = value[start : start + bins]
        place = lax.broadcasted_iota(jnp.int32, piece.shape, 0)
        if by > 0:
            keep = place >= by
        else:
            keep = place < bins + by
        pieces.append(jnp.where(keep, pltpu.roll(piece, by % bins, 0), 0.0))
    return jnp.concatenate(pieces, axis=0)


def fore(x, weight_ref, spread, bins):
    act = gelu(x.astype(jnp.float32)).astype(jnp.bfloat16)
    terms = [
        jnp.dot(act, weight_ref[0, tap], preferred_element_type=jnp.float32) for tap in range(3)
    ]
    return terms[1] + moved(terms[0], spread, bins) + moved(terms[2], -spread, bins)


def back_pre(dy, pre_slope, point_ref):
    inner_grad = jnp.dot(dy, point_ref[0], preferred_element_type=jnp.float32)
    return (inner_grad * pre_slope).astype(jnp.bfloat16)


def back_trunk(dy, dpre, x_slope, weight_ref, spread, bins):
    wide = dpre.astype(jnp.float32)
    spans = (
        moved(wide, -spread, bins).astype(jnp.bfloat16),
        dpre,
        moved(wide, spread, bins).astype(jnp.bfloat16),
    )
    dact = jnp.zeros(dy.shape, jnp.float32)
    for tap in range(3):
        dact = dact + jnp.dot(
            spans[tap], weight_ref[0, tap], preferred_element_type=jnp.float32
        )
    return (dy.astype(jnp.float32) + dact * x_slope).astype(jnp.bfloat16)


def of_seq(ref, seq, bins):
    if ref.shape[0] == bins:
        return ref[...]
    return ref[seq * bins : (seq + 1) * bins, :]


def split_kernel(last, payload_ref, *out_refs):
    count = len(out_refs)
    seq_count, bins, chans = payload_ref.shape
    part = bins // count
    section = lax.axis_index("pipe")
    place = lax.axis_index("ctx")

    @pl.when((section == 0) | (section == last))
    def send():
        source = payload_ref[...].reshape(seq_count * bins, chans)
        row = lax.broadcasted_iota(jnp.int32, (part, seq_count * bins), 0)
        col = lax.broadcasted_iota(jnp.int32, (part, seq_count * bins), 1)
        for hop in range(count):
            residue = lax.rem(place + hop, count)
            rows = [
                (col == seq * bins + count * row + residue).astype(jnp.float32)
                for seq in range(seq_count)
            ]
            pick = jnp.concatenate(rows, axis=0).astype(jnp.bfloat16)
            out_refs[hop][...] = jnp.dot(
                pick, source, preferred_element_type=jnp.float32
            ).astype(jnp.bfloat16)


def hold_kernel(weight_ref, point_ref, weight_out, point_out, sems):
    loads = [
        pltpu.make_async_copy(weight_ref, weight_out, sems.at[0]),
        pltpu.make_async_copy(point_ref, point_out, sems.at[1]),
    ]
    for load in loads:
        load.start()
    for load in loads:
        load.wait()


def first_kernel(last, bins, steps, *refs):
    parts, (weight_ref, point_ref, whole_ref, out_ref, pre_ref) = refs[:-5], refs[-5:]
    count = len(parts)
    section = lax.axis_index("pipe")
    place = lax.axis_index("ctx")
    part = bins // count
    seq_count = whole_ref.shape[0] // bins

    @pl.when((section == 0) | (section == last))
    def gather():
        for step, part_ref in zip(steps, parts):
            source = lax.rem(place + count - step, count)
            for seq in range(seq_count):
                at = pl.multiple_of(seq * bins + source * part, part)
                whole_ref[pl.ds(at, part), :] = part_ref[seq * part : (seq + 1) * part, :]

    @pl.when(section == 0)
    def layer():
        x = whole_ref[:bins, :]
        finish(x, fore(x, weight_ref, 1, bins), point_ref, out_ref, pre_ref)


def finish(x, pre, point_ref, out_ref, pre_ref):
    pre_ref[...] = pre
    branch = jnp.dot(
        gelu(pre).astype(jnp.bfloat16), point_ref[0], preferred_element_type=jnp.float32
    )
    out_ref[...] = (x.astype(jnp.float32) + branch).astype(jnp.bfloat16)


def fore_kernel(level, seq, bins, x_ref, weight_ref, point_ref, out_ref, pre_ref):
    @pl.when(lax.axis_index("pipe") == level)
    def layer():
        x = of_seq(x_ref, seq, bins)
        finish(x, fore(x, weight_ref, 2**level, bins), point_ref, out_ref, pre_ref)


def transpose_kernel(weight_ref, point_ref, weight_out, point_out):
    for tap in range(weight_ref.shape[1]):
        weight_out[0, tap] = weight_ref[0, tap].T
    point_out[0] = point_ref[0].T


def turn_kernel(level, seq, bins, scale, x_ref, cot_ref, weight_ref, weight_t_ref, point_t_ref, dy_ref, dpre_ref):
    @pl.when(lax.axis_index("pipe") == level)
    def layer():
        x = of_seq(x_ref, seq, bins)
        pre = fore(x, weight_ref, 2**level, bins)
        cot = of_seq(cot_ref, seq, bins)
        dy = (cot.astype(jnp.float32) * scale).astype(jnp.bfloat16)
        dpre = back_pre(dy, gelu_slope(pre), point_t_ref)
        dpre_ref[...] = dpre
        x_slope = gelu_slope(x.astype(jnp.float32))
        dy_ref[...] = back_trunk(dy, dpre, x_slope, weight_t_ref, 2**level, bins)


def slope_kernel(levels, seq_count, bins, *refs):
    xs, pres = refs[: levels * seq_count], refs[levels * seq_count : 2 * levels * seq_count]
    outs = refs[2 * levels * seq_count :]
    for level in range(levels):

        @pl.when(lax.axis_index("pipe") == level)
        def layer(level=level):
            for seq in range(seq_count):
                x = of_seq(xs[level * seq_count + seq], seq, bins)
                outs[2 * seq][...] = gelu_slope(x.astype(jnp.float32))
                outs[2 * seq + 1][...] = gelu_slope(pres[level * seq_count + seq][...])


def back_kernel(level, bins, dy_in_ref, x_slope_ref, pre_slope_ref, weight_ref, point_ref, dy_ref, dpre_ref):
    @pl.when(lax.axis_index("pipe") == level)
    def layer():
        dy = dy_in_ref[...]
        dpre = back_pre(dy, pre_slope_ref[...], point_ref)
        dpre_ref[...] = dpre
        dy_ref[...] = back_trunk(dy, dpre, x_slope_ref[...], weight_ref, 2**level, bins)


def message_kernel(early, places, late_places, *refs):
    blocks, late_blocks = refs[: len(places)], refs[len(places) : -1]
    message_ref = refs[-1]
    section = lax.axis_index("pipe")
    is_early = functools.reduce(jnp.logical_or, [section == stage for stage in early])

    def fill(blocks, places):
        size = message_ref.shape[0] // max(len(places), 1)
        for to, (ref, at) in enumerate(zip(blocks, places)):
            message_ref[to * size : (to + 1) * size, :] = ref[at * size : (at + 1) * size, :]

    @pl.when(is_early)
    def on_early():
        fill(blocks, places)

    @pl.when(jnp.logical_not(is_early))
    def on_late():
        fill(late_blocks, late_places)


def head_kernel(sections, earlier, dy_in_ref, slope_ref, point_ref, *refs):
    others, before, out_ref = refs[: sections - 1], refs[sections - 1 : -1], refs[-1]
    section = lax.axis_index("pipe")
    bins = dy_in_ref.shape[0]
    for ref in before:
        out_ref[:earlier, :] = ref[...]

    @pl.when(section == 0)
    def layer():
        out_ref[earlier : earlier + bins, :] = back_pre(dy_in_ref[...], slope_ref[...], point_ref)

    for level in range(1, sections):

        @pl.when(section == level)
        def keep(level=level):
            out_ref[earlier : earlier + bins, :] = others[level - 1][...]


def columns_kernel(groups, runs, kept, *refs):
    refs, (sent_ref,) = refs[:-1], refs[-1:]
    kept_refs = refs[sum(runs) :]
    count = 2 * len(kept)
    section = lax.axis_index("pipe")
    core = lax.axis_index("dp")
    place = lax.axis_index("ctx")
    x, start = None, 0
    for level, run in enumerate(runs):
        pieces = [ref[...] for ref in refs[start : start + run]]
        start += run
        whole = jnp.concatenate(pieces, axis=0).astype(jnp.float32)
        x = whole if x is None else jnp.where(section == level, whole, x)
    act = gelu(x).T.astype(jnp.bfloat16)
    chans = act.shape[0]
    width = chans // (groups * count)
    row = lax.broadcasted_iota(jnp.int32, (width, chans), 0)
    col = lax.broadcasted_iota(jnp.int32, (width, chans), 1)

    def block(offset):
        owner = lax.bitwise_xor(place, offset)
        rows = []
        for step in range(groups):
            first = (lax.rem(core + step, groups) * count + owner) * width
            rows.append((col == first + row).astype(jnp.float32))
        pick = jnp.concatenate(rows, axis=0).astype(jnp.bfloat16)
        return jnp.dot(pick, act, preferred_element_type=jnp.float32).astype(jnp.bfloat16)

    size = groups * width
    for at, offset in enumerate(kept):
        kept_refs[at][...] = block(offset)
        sent_ref[at * size : (at + 1) * size, :] = block(offset ^ 1)


def grad_kernel(sections, early, bins, places, late_places, *refs):
    columns, refs = refs[: len(places)], refs[len(places) :]
    late_columns, refs = refs[: len(places)], refs[len(places) :]
    grads, out_ref = refs[:-1], refs[-1]
    section = lax.axis_index("pipe")
    width = out_ref.shape[1]

    def taps(spread, columns, places):
        act = jnp.concatenate(
            [ref[at : at + width, :] for ref, at in zip(columns, places)], axis=1
        )
        dpre = jnp.concatenate([ref[...] for ref in grads], axis=0)
        wide = dpre.astype(jnp.float32)
        spans = (
            moved(wide, -spread, bins).astype(jnp.bfloat16),
            dpre,
            moved(wide, spread, bins).astype(jnp.bfloat16),
        )
        for tap in range(3):
            out_ref[tap] = jnp.dot(
                act, spans[tap], preferred_element_type=jnp.float32
            ).astype(out_ref.dtype)

    for level in range(sections):

        @pl.when(section == level)
        def run(level=level):
            if level in early:
                taps(2**level, columns, places)
            else:
                taps(2**level, late_columns, late_places)


def kernel_call(body, outs, flops, name, waits=(), carries=(), in_spec=in_vmem, scratch=()):
    def call(*args):
        used, taken = len(args), len(args) + len(waits) + len(carries)

        def run(*refs):
            made = refs[taken : taken + len(outs)]
            body(*refs[:used], *made, *refs[taken + len(outs) + len(carries) :])

        moved_bytes = sum(math.prod(a.shape) * a.dtype.itemsize for a in (*args, *outs))
        return pl.pallas_call(
            run,
            out_shape=[*outs, *(jax.ShapeDtypeStruct(a.shape, a.dtype) for a in carries)],
            in_specs=[in_spec] * used + [anywhere] * (taken - used),
            out_specs=[in_vmem] * len(outs) + [anywhere] * len(carries),
            input_output_aliases={
                used + len(waits) + at: len(outs) + at for at in range(len(carries))
            },
            scratch_shapes=list(scratch),
            compiler_params=pltpu.CompilerParams(vmem_limit_bytes=24 * 2**20),
            cost_estimate=pl.CostEstimate(
                flops=flops, bytes_accessed=moved_bytes, transcendentals=0
            ),
            name=name,
        )(*args, *waits, *carries)

    return call


def residue_shards(inputs, cotangent, weight, point):
    sections = lax.axis_size("pipe")
    section = lax.axis_index("pipe")
    count = lax.axis_size("ctx")
    groups = lax.axis_size("dp")
    seq_count, bins, chans = inputs.shape
    inner = weight.shape[3]
    rows = seq_count * bins
    scale = 1.0 / math.sqrt(seq_count * groups * bins * count)
    last = sections - 1
    seqs = range(seq_count)
    layer_flops = 2 * bins * chans * inner * 4

    def shape(*dims, dtype=jnp.bfloat16):
        return jax.ShapeDtypeStruct(dims, dtype)

    def hop(value, source, target, third=None):
        sends = {source: target, target: source}
        if third is not None and third not in sends:
            sends.update({target: third, third: source})
        route = []
        for core in range(groups):
            for stage in range(sections):
                taker = core if stage in sends else (core + 1) % groups
                for i in range(count):
                    giver = (core * sections + stage) * count + i
                    route.append((giver, (taker * sections + sends.get(stage, stage)) * count + i))
        return lax.ppermute(value, ("dp", "pipe", "ctx"), route)

    def onward(value, step):
        return lax.ppermute(value, "ctx", [(i, (i + step) % count) for i in range(count)])

    def exchange(value, offset):
        return lax.ppermute(value, "ctx", [(i, i ^ offset) for i in range(count)])

    payload = jnp.where(section == last, cotangent, inputs)
    parts = kernel_call(
        functools.partial(split_kernel, last),
        [shape(rows // count, chans)] * count,
        10 * seq_count * layer_flops,
        "split",
    )(payload)
    weight, point = kernel_call(
        hold_kernel,
        [shape(*weight.shape), shape(*point.shape)],
        0,
        "hold",
        waits=[parts[0]],
        in_spec=anywhere,
        scratch=[pltpu.SemaphoreType.DMA((2,))],
    )(weight, point)
    steps = [1, *range(count - 1, 1, -1)]
    parts = [*(onward(parts[step], step) for step in steps), parts[0]]

    trunk, inside = shape(bins, chans), shape(bins, inner)
    inside_wide = shape(bins, inner, dtype=jnp.float32)
    whole, out, pre = kernel_call(
        functools.partial(first_kernel, last, bins, [*steps, 0]),
        [shape(rows, chans), trunk, inside_wide],
        layer_flops,
        "first",
    )(*parts, weight, point)
    outs, pres, xs, sent = [out], [[pre]], [[whole]], ()
    for level in range(last):
        if level > 0:
            third = last if level > 1 else None
            xs.append([hop(out, level - 1, level, third) for out in outs])
            outs = []
            pres.append([])
        for seq in range(len(outs), seq_count):
            out, pre = kernel_call(
                functools.partial(fore_kernel, level, seq, bins),
                [trunk, inside_wide],
                layer_flops,
                "fore",
                waits=outs[-1:] or sent,
            )(xs[level][seq if level else 0], weight, point)
            outs.append(out)
            pres[level].append(pre)
        sent = outs
        if level == 1:
            back_weights = kernel_call(
                transpose_kernel,
                [shape(1, weight.shape[1], inner, chans), shape(1, chans, inner)],
                0,
                "transpose",
                waits=outs,
            )(weight, point)
            sent = [*outs, *back_weights]
    slopes = kernel_call(
        functools.partial(slope_kernel, last, seq_count, bins),
        [shape(bins, chans, dtype=jnp.float32), inside_wide] * seq_count,
        0,
        "slopes",
        waits=outs,
    )(
        *[xs[level][seq if level else 0] for level in range(last) for seq in seqs],
        *[pre for some in pres for pre in some],
    )
    sent = [*sent, *slopes]
    xs.append([hop(out, last - 1, last, 0) for out in outs])

    dys, dpres = [], [[] for level in range(sections)]
    for seq in seqs:
        dy, dpre = kernel_call(
            functools.partial(turn_kernel, last, seq, bins, scale),
            [trunk, inside],
            2 * layer_flops,
            "turn",
            waits=dys[-1:] or sent,
        )(xs[last][seq], whole, weight, *back_weights)
        dys.append(dy)
        dpres[last].append(dpre)
    early = (0, last)
    kept = list(range(0, count, 2))
    size = chans // count
    *owned, message = kernel_call(
        functools.partial(columns_kernel, groups, [len(x) for x in xs], kept),
        [shape(size, rows)] * len(kept) + [shape(size * len(kept), rows)],
        2 * rows * chans * chans,
        "columns",
        waits=dys,
    )(*[x for some in xs for x in some])
    table = {(offset, 0): (array, 0) for offset, array in zip(kept, owned)}
    table.update({(offset ^ 1, 0): (message, at) for at, offset in enumerate(kept)})
    late_table = dict(table)
    phases = count.bit_length() - 1

    def moving(table, phase):
        if not 0 <= phase < phases:
            return []
        return sorted(key for key in table if key[0] >> phase & 1)

    def columns_slot(slot, message):
        others = [stage for stage in range(sections) if stage not in early]
        route = []
        for kind, phase in ((list(early), slot), (others, slot - 1)):
            for at, stage in enumerate(kind):
                for i in range(count):
                    taker, j = kind[(at + 1) % len(kind)], i
                    if 0 <= phase < phases:
                        taker, j = stage, i ^ 1 << phase
                    route.append((stage * count + i, taker * count + j))
        arrived = lax.ppermute(message, ("pipe", "ctx"), route)
        for table_of, phase in ((table, slot), (late_table, slot - 1)):
            for at, (to, start) in enumerate(moving(table_of, phase)):
                del table_of[to, start]
                table_of[to ^ 1 << phase, start ^ 1 << phase] = (arrived, at)
        return arrived

    sent = [owned[0]]
    dys = [hop(dy, last, last - 1) for dy in dys]
    columns_slot(0, message)
    slot = 0

    for level in range(last - 1, 0, -1):
        outs = []
        for seq in seqs:
            dy, dpre = kernel_call(
                functools.partial(back_kernel, level, bins),
                [trunk, inside],
                layer_flops,
                "back",
                waits=outs[-1:] or sent,
            )(dys[seq], *slopes[2 * seq : 2 * seq + 2], *back_weights)
            outs.append(dy)
            dpres[level].append(dpre)
        sent = outs
        dys = [hop(dy, level, level - 1, None if level > 1 else last) for dy in outs]
        slot += 1
        if slot <= phases:
            chosen = [table[key] for key in moving(table, slot)]
            late_chosen = [late_table[key] for key in moving(late_table, slot - 1)]
            (message,) = kernel_call(
                functools.partial(
                    message_kernel,
                    early,
                    [at for array, at in chosen],
                    [at for array, at in late_chosen],
                ),
                [shape(size * len(kept), rows)],
                0,
                "message",
                waits=outs,
            )(*[array for array, at in (*chosen, *late_chosen)])
            sent = [*outs, message]
            columns_slot(slot, message)

    dpre = []
    for seq in seqs:
        dpre = kernel_call(
            functools.partial(head_kernel, sections, seq * bins),
            [shape((seq + 1) * bins, inner)],
            layer_flops // 4,
            "head",
            waits=dpre or sent,
        )(dys[seq], slopes[2 * seq + 1], back_weights[1], *[dpres[level][seq] for level in range(1, sections)], *dpre)
    (dpre,) = dpre
    received, bit = {0: dpre}, count // 2
    while bit:
        received.update({offset ^ bit: exchange(block, bit) for offset, block in received.items()})
        bit //= 2
    offsets = [*received]
    gathered = [received[offset] for offset in offsets]
    columns = [table[0, offset] for offset in offsets]
    late_columns = [late_table[0, offset] for offset in offsets]
    width = size // groups

    def gradient(step, dtype, waits=()):
        places, late_places = (
            [at * size + step * width for array, at in kind] for kind in (columns, late_columns)
        )
        (part,) = kernel_call(
            functools.partial(grad_kernel, sections, early, bins, places, late_places),
            [shape(3, width, inner, dtype=dtype)],
            2 * 3 * rows * count * width * inner,
            "grad",
            waits=waits,
        )(*[array for array, at in (*columns, *late_columns)], *gathered)
        return part

    others = [gradient(step, jnp.bfloat16) for step in range(1, groups)]
    mine = gradient(0, jnp.float32, waits=others)
    for step, other in enumerate(others, 1):
        route = [(i, (i + step) % groups) for i in range(groups)]
        mine = mine + lax.ppermute(other, "dp", route).astype(jnp.float32)
    return mine[None]


def solution(mesh):
    def shards(inputs, cotangent, dilated_kernel_weight, point_weight):
        bins = inputs.shape[1]
        first_spread = bins // 2 // 2 ** (mesh.shape["pipe"] - 1)
        count = mesh.shape["ctx"]
        residues = (
            first_spread == count
            and mesh.shape["pipe"] > 3
            and bins % (16 * count) == 0
            and 1 < count == 1 << (count.bit_length() - 1) <= 1 << (mesh.shape["pipe"] - 2)
            and inputs.shape[2] % (count * mesh.shape["dp"]) == 0
        )
        plan = residue_shards if residues else edge_shards
        return plan(inputs, cotangent, dilated_kernel_weight, point_weight)

    return jax.shard_map(
        shards,
        mesh=mesh,
        in_specs=(
            P("dp", "ctx", None),
            P("dp", "ctx", None),
            P("pipe", None, None, None),
            P("pipe", None, None),
        ),
        out_specs=P("pipe", None, ("dp", "ctx"), None),
        check_vma=False,
    )
```

```python
import functools
import math

import jax
import jax.numpy as jnp
from jax import lax
from jax.experimental import pallas as pl
from jax.experimental.pallas import tpu as pltpu
from jax.sharding import PartitionSpec as P

root_half = 0.7071067811865476
inv_root_two_pi = 0.3989422804014327

in_vmem = pl.BlockSpec(memory_space=pltpu.VMEM)
anywhere = pl.BlockSpec(memory_space=pl.ANY)
contract_last = (((1,), (1,)), ((), ()))
contract_first = (((0,), (0,)), ((), ()))


def gelu(value):
    return 0.5 * value * (1.0 + lax.erf(value * root_half))


def gelu_slope(value):
    return (
        0.5 * (1.0 + lax.erf(value * root_half))
        + value * jnp.exp(-0.5 * value * value) * inv_root_two_pi
    )


def padded(cells, sides, width):
    for axis, dim in sides:
        count = lax.axis_size(axis)
        ends = count - 1
        head = lax.slice_in_dim(cells, 0, width, axis=dim)
        tail = lax.slice_in_dim(cells, cells.shape[dim] - width, cells.shape[dim], axis=dim)
        cells = jnp.concatenate(
            [
                lax.ppermute(tail, axis, [(i, (i + 1) % count) for i in range(ends)]),
                cells,
                lax.ppermute(head, axis, [((i + 1) % count, i) for i in range(ends)]),
            ],
            axis=dim,
        )
    return cells


def shifted(block, axis, distance):
    devices = range(lax.axis_size(axis))
    route = [(i - distance, i) for i in devices if i - distance in devices]
    return lax.ppermute(block, axis, route)


def edge_shards(inputs, cotangent, dilated_kernel_weight, point_weight):
    sections = lax.axis_size("pipe")
    section = lax.axis_index("pipe")
    seq_count, bins, chans = inputs.shape
    reach = bins // 2
    table = jnp.array(
        [reach // 2 ** (sections - 1 - level) for level in range(sections)], jnp.int32
    )
    spread = table[section]
    dilation_weight = dilated_kernel_weight[0]
    w_point = point_weight[0]
    inner_channel_count = dilation_weight.shape[2]
    scale = 1.0 / math.sqrt(seq_count * lax.axis_size("dp") * bins * lax.axis_size("ctx"))
    ticks = jnp.arange(seq_count + sections - 1, dtype=jnp.int32)

    def conv_fore(extended):
        running_total = jnp.zeros((bins, inner_channel_count), jnp.float32)
        for kernel_offset in range(3):
            receptive_span = lax.dynamic_slice_in_dim(
                extended, reach + (kernel_offset - 1) * spread, bins, 0
            )
            running_total = running_total + jnp.dot(
                receptive_span, dilation_weight[kernel_offset], preferred_element_type=jnp.float32
            )
        return running_total

    def put(store, slot, valid, item):
        current = lax.dynamic_index_in_dim(store, slot, 0, keepdims=False)
        return lax.dynamic_update_index_in_dim(store, jnp.where(valid, item, current), slot, 0)

    kept_x = jnp.zeros(inputs.shape, jnp.bfloat16)
    kept_ext = jnp.zeros((seq_count, bins + 2 * reach, chans), jnp.bfloat16)
    kept_pre = jnp.zeros((seq_count, bins, inner_channel_count), jnp.float32)

    def fore_tick(carry, tick):
        received, store_x, store_ext, store_pre = carry
        micro = tick - section
        valid = (micro >= 0) & (micro < seq_count)
        slot = jnp.clip(micro, 0, seq_count - 1)
        first = lax.dynamic_index_in_dim(inputs, slot, 0, keepdims=False)
        trunk_in = jnp.where(section == 0, first, received)
        act = gelu(trunk_in.astype(jnp.float32)).astype(jnp.bfloat16)
        extended = padded(act, (("ctx", 0),), reach)
        pre = conv_fore(extended)
        inner = gelu(pre).astype(jnp.bfloat16)
        out = (
            trunk_in.astype(jnp.float32)
            + jnp.dot(inner, w_point, preferred_element_type=jnp.float32)
        ).astype(jnp.bfloat16)
        sent = shifted(out, "pipe", 1)
        store_x = put(store_x, slot, valid, trunk_in)
        store_ext = put(store_ext, slot, valid, extended)
        store_pre = put(store_pre, slot, valid, pre)
        return ((sent, store_x, store_ext, store_pre), None)

    start_recv = jnp.zeros((bins, chans), jnp.bfloat16)
    (unused, kept_x, kept_ext, kept_pre), unused_out = lax.scan(
        fore_tick, (start_recv, kept_x, kept_ext, kept_pre), ticks
    )

    def back_tick(carry, tick):
        received, grad = carry
        micro = tick - (sections - 1 - section)
        valid = (micro >= 0) & (micro < seq_count)
        slot = jnp.clip(micro, 0, seq_count - 1)
        last = (
            lax.dynamic_index_in_dim(cotangent, slot, 0, keepdims=False).astype(jnp.float32) * scale
        ).astype(jnp.bfloat16)
        upstream = jnp.where(section == sections - 1, last, received)
        trunk_in = lax.dynamic_index_in_dim(kept_x, slot, 0, keepdims=False)
        extended = lax.dynamic_index_in_dim(kept_ext, slot, 0, keepdims=False)
        pre = lax.dynamic_index_in_dim(kept_pre, slot, 0, keepdims=False)
        inner_grad = lax.dot_general(
            upstream, w_point, contract_last, preferred_element_type=jnp.float32
        )
        dpre = (inner_grad * gelu_slope(pre) * valid.astype(jnp.float32)).astype(jnp.bfloat16)
        dpre_ext = padded(dpre, (("ctx", 0),), reach)
        dact = jnp.zeros((bins, chans), jnp.float32)
        taps = []
        for kernel_offset in range(3):
            receptive_span = lax.dynamic_slice_in_dim(
                dpre_ext, reach - (kernel_offset - 1) * spread, bins, 0
            )
            dact = dact + lax.dot_general(
                receptive_span,
                dilation_weight[kernel_offset],
                contract_last,
                preferred_element_type=jnp.float32,
            )
            source = lax.dynamic_slice_in_dim(
                extended, reach + (kernel_offset - 1) * spread, bins, 0
            )
            taps.append(
                lax.dot_general(source, dpre, contract_first, preferred_element_type=jnp.float32)
            )
        grad = grad + jnp.stack(taps)
        back = (
            upstream.astype(jnp.float32) + dact * gelu_slope(trunk_in.astype(jnp.float32))
        ).astype(jnp.bfloat16)
        sent = shifted(back, "pipe", -1)
        return ((sent, grad), None)

    start_grad = jnp.zeros((3, chans, inner_channel_count), jnp.float32)
    (unused_back, grad), unused_seq = lax.scan(back_tick, (start_recv, start_grad), ticks)
    term = grad[None]
    return lax.psum_scatter(term, ("dp", "ctx"), scatter_dimension=2, tiled=True)


def moved(value, by, bins):
    pieces = []
    for start in range(0, value.shape[0], bins):
        piece = value[start : start + bins]
        place = lax.broadcasted_iota(jnp.int32, piece.shape, 0)
        if by > 0:
            keep = place >= by
        else:
            keep = place < bins + by
        pieces.append(jnp.where(keep, pltpu.roll(piece, by % bins, 0), 0.0))
    return jnp.concatenate(pieces, axis=0)


def fore(x, weight_ref, spread, bins):
    act = gelu(x.astype(jnp.float32)).astype(jnp.bfloat16)
    terms = [
        jnp.dot(act, weight_ref[0, tap], preferred_element_type=jnp.float32) for tap in range(3)
    ]
    return terms[1] + moved(terms[0], spread, bins) + moved(terms[2], -spread, bins)


def back_pre(dy, pre_slope, point_ref):
    inner_grad = jnp.dot(dy, point_ref[0], preferred_element_type=jnp.float32)
    return (inner_grad * pre_slope).astype(jnp.bfloat16)


def back_trunk(dy, dpre, x_slope, weight_ref, spread, bins):
    wide = dpre.astype(jnp.float32)
    spans = (
        moved(wide, -spread, bins).astype(jnp.bfloat16),
        dpre,
        moved(wide, spread, bins).astype(jnp.bfloat16),
    )
    dact = jnp.zeros(dy.shape, jnp.float32)
    for tap in range(3):
        dact = dact + jnp.dot(
            spans[tap], weight_ref[0, tap], preferred_element_type=jnp.float32
        )
    return (dy.astype(jnp.float32) + dact * x_slope).astype(jnp.bfloat16)


def of_seq(ref, seq, bins):
    if ref.shape[0] == bins:
        return ref[...]
    return ref[seq * bins : (seq + 1) * bins, :]


def split_kernel(last, payload_ref, *out_refs):
    count = len(out_refs)
    seq_count, bins, chans = payload_ref.shape
    part = bins // count
    section = lax.axis_index("pipe")
    place = lax.axis_index("ctx")

    @pl.when((section == 0) | (section == last))
    def send():
        source = payload_ref[...].reshape(seq_count * bins, chans)
        row = lax.broadcasted_iota(jnp.int32, (part, seq_count * bins), 0)
        col = lax.broadcasted_iota(jnp.int32, (part, seq_count * bins), 1)
        for hop in range(count):
            residue = lax.rem(place + hop, count)
            rows = [
                (col == seq * bins + count * row + residue).astype(jnp.float32)
                for seq in range(seq_count)
            ]
            pick = jnp.concatenate(rows, axis=0).astype(jnp.bfloat16)
            out_refs[hop][...] = jnp.dot(
                pick, source, preferred_element_type=jnp.float32
            ).astype(jnp.bfloat16)


def hold_kernel(weight_ref, point_ref, weight_out, point_out, sems):
    loads = [
        pltpu.make_async_copy(weight_ref, weight_out, sems.at[0]),
        pltpu.make_async_copy(point_ref, point_out, sems.at[1]),
    ]
    for load in loads:
        load.start()
    for load in loads:
        load.wait()


def first_kernel(last, bins, steps, *refs):
    parts, (weight_ref, point_ref, whole_ref, out_ref, pre_ref) = refs[:-5], refs[-5:]
    count = len(parts)
    section = lax.axis_index("pipe")
    place = lax.axis_index("ctx")
    part = bins // count
    seq_count = whole_ref.shape[0] // bins

    @pl.when((section == 0) | (section == last))
    def gather():
        for step, part_ref in zip(steps, parts):
            source = lax.rem(place + count - step, count)
            for seq in range(seq_count):
                at = pl.multiple_of(seq * bins + source * part, part)
                whole_ref[pl.ds(at, part), :] = part_ref[seq * part : (seq + 1) * part, :]

    @pl.when(section == 0)
    def layer():
        x = whole_ref[:bins, :]
        finish(x, fore(x, weight_ref, 1, bins), point_ref, out_ref, pre_ref)


def finish(x, pre, point_ref, out_ref, pre_ref):
    pre_ref[...] = pre
    branch = jnp.dot(
        gelu(pre).astype(jnp.bfloat16), point_ref[0], preferred_element_type=jnp.float32
    )
    out_ref[...] = (x.astype(jnp.float32) + branch).astype(jnp.bfloat16)


def fore_kernel(level, seq, bins, x_ref, weight_ref, point_ref, out_ref, pre_ref):
    @pl.when(lax.axis_index("pipe") == level)
    def layer():
        x = of_seq(x_ref, seq, bins)
        finish(x, fore(x, weight_ref, 2**level, bins), point_ref, out_ref, pre_ref)


def transpose_kernel(weight_ref, point_ref, weight_out, point_out):
    for tap in range(weight_ref.shape[1]):
        weight_out[0, tap] = weight_ref[0, tap].T
    point_out[0] = point_ref[0].T


def turn_kernel(level, seq, bins, scale, x_ref, cot_ref, weight_ref, weight_t_ref, point_t_ref, dy_ref, dpre_ref):
    @pl.when(lax.axis_index("pipe") == level)
    def layer():
        x = of_seq(x_ref, seq, bins)
        pre = fore(x, weight_ref, 2**level, bins)
        cot = of_seq(cot_ref, seq, bins)
        dy = (cot.astype(jnp.float32) * scale).astype(jnp.bfloat16)
        dpre = back_pre(dy, gelu_slope(pre), point_t_ref)
        dpre_ref[...] = dpre
        x_slope = gelu_slope(x.astype(jnp.float32))
        dy_ref[...] = back_trunk(dy, dpre, x_slope, weight_t_ref, 2**level, bins)


def slope_kernel(levels, seq_count, bins, *refs):
    xs, pres = refs[: levels * seq_count], refs[levels * seq_count : 2 * levels * seq_count]
    outs = refs[2 * levels * seq_count :]
    for level in range(levels):

        @pl.when(lax.axis_index("pipe") == level)
        def layer(level=level):
            for seq in range(seq_count):
                x = of_seq(xs[level * seq_count + seq], seq, bins)
                outs[2 * seq][...] = gelu_slope(x.astype(jnp.float32))
                outs[2 * seq + 1][...] = gelu_slope(pres[level * seq_count + seq][...])


def back_kernel(level, bins, dy_in_ref, x_slope_ref, pre_slope_ref, weight_ref, point_ref, dy_ref, dpre_ref):
    @pl.when(lax.axis_index("pipe") == level)
    def layer():
        dy = dy_in_ref[...]
        dpre = back_pre(dy, pre_slope_ref[...], point_ref)
        dpre_ref[...] = dpre
        dy_ref[...] = back_trunk(dy, dpre, x_slope_ref[...], weight_ref, 2**level, bins)


def message_kernel(early, places, late_places, *refs):
    blocks, late_blocks = refs[: len(places)], refs[len(places) : -1]
    message_ref = refs[-1]
    section = lax.axis_index("pipe")
    is_early = functools.reduce(jnp.logical_or, [section == stage for stage in early])

    def fill(blocks, places):
        size = message_ref.shape[0] // max(len(places), 1)
        for to, (ref, at) in enumerate(zip(blocks, places)):
            message_ref[to * size : (to + 1) * size, :] = ref[at * size : (at + 1) * size, :]

    @pl.when(is_early)
    def on_early():
        fill(blocks, places)

    @pl.when(jnp.logical_not(is_early))
    def on_late():
        fill(late_blocks, late_places)


def head_kernel(sections, earlier, dy_in_ref, slope_ref, point_ref, *refs):
    others, before, out_ref = refs[: sections - 1], refs[sections - 1 : -1], refs[-1]
    section = lax.axis_index("pipe")
    bins = dy_in_ref.shape[0]
    for ref in before:
        out_ref[:earlier, :] = ref[...]

    @pl.when(section == 0)
    def layer():
        out_ref[earlier : earlier + bins, :] = back_pre(dy_in_ref[...], slope_ref[...], point_ref)

    for level in range(1, sections):

        @pl.when(section == level)
        def keep(level=level):
            out_ref[earlier : earlier + bins, :] = others[level - 1][...]


def columns_kernel(groups, runs, kept, *refs):
    refs, (sent_ref,) = refs[:-1], refs[-1:]
    kept_refs = refs[sum(runs) :]
    count = 2 * len(kept)
    section = lax.axis_index("pipe")
    core = lax.axis_index("dp")
    place = lax.axis_index("ctx")
    x, start = None, 0
    for level, run in enumerate(runs):
        pieces = [ref[...] for ref in refs[start : start + run]]
        start += run
        whole = jnp.concatenate(pieces, axis=0).astype(jnp.float32)
        x = whole if x is None else jnp.where(section == level, whole, x)
    act = gelu(x).T.astype(jnp.bfloat16)
    chans = act.shape[0]
    width = chans // (groups * count)
    row = lax.broadcasted_iota(jnp.int32, (width, chans), 0)
    col = lax.broadcasted_iota(jnp.int32, (width, chans), 1)

    def block(offset):
        owner = lax.bitwise_xor(place, offset)
        rows = []
        for step in range(groups):
            first = (lax.rem(core + step, groups) * count + owner) * width
            rows.append((col == first + row).astype(jnp.float32))
        pick = jnp.concatenate(rows, axis=0).astype(jnp.bfloat16)
        return jnp.dot(pick, act, preferred_element_type=jnp.float32).astype(jnp.bfloat16)

    size = groups * width
    for at, offset in enumerate(kept):
        kept_refs[at][...] = block(offset)
        sent_ref[at * size : (at + 1) * size, :] = block(offset ^ 1)


def grad_kernel(sections, early, bins, places, late_places, *refs):
    columns, refs = refs[: len(places)], refs[len(places) :]
    late_columns, refs = refs[: len(places)], refs[len(places) :]
    grads, out_ref = refs[:-1], refs[-1]
    section = lax.axis_index("pipe")
    width = out_ref.shape[1]

    def taps(spread, columns, places):
        act = jnp.concatenate(
            [ref[at : at + width, :] for ref, at in zip(columns, places)], axis=1
        )
        dpre = jnp.concatenate([ref[...] for ref in grads], axis=0)
        wide = dpre.astype(jnp.float32)
        spans = (
            moved(wide, -spread, bins).astype(jnp.bfloat16),
            dpre,
            moved(wide, spread, bins).astype(jnp.bfloat16),
        )
        for tap in range(3):
            out_ref[tap] = jnp.dot(
                act, spans[tap], preferred_element_type=jnp.float32
            ).astype(out_ref.dtype)

    for level in range(sections):

        @pl.when(section == level)
        def run(level=level):
            if level in early:
                taps(2**level, columns, places)
            else:
                taps(2**level, late_columns, late_places)


def kernel_call(body, outs, flops, name, waits=(), carries=(), in_spec=in_vmem, scratch=()):
    def call(*args):
        used, taken = len(args), len(args) + len(waits) + len(carries)

        def run(*refs):
            made = refs[taken : taken + len(outs)]
            body(*refs[:used], *made, *refs[taken + len(outs) + len(carries) :])

        moved_bytes = sum(math.prod(a.shape) * a.dtype.itemsize for a in (*args, *outs))
        return pl.pallas_call(
            run,
            out_shape=[*outs, *(jax.ShapeDtypeStruct(a.shape, a.dtype) for a in carries)],
            in_specs=[in_spec] * used + [anywhere] * (taken - used),
            out_specs=[in_vmem] * len(outs) + [anywhere] * len(carries),
            input_output_aliases={
                used + len(waits) + at: len(outs) + at for at in range(len(carries))
            },
            scratch_shapes=list(scratch),
            compiler_params=pltpu.CompilerParams(vmem_limit_bytes=24 * 2**20),
            cost_estimate=pl.CostEstimate(
                flops=flops, bytes_accessed=moved_bytes, transcendentals=0
            ),
            name=name,
        )(*args, *waits, *carries)

    return call


def residue_shards(inputs, cotangent, weight, point):
    sections = lax.axis_size("pipe")
    section = lax.axis_index("pipe")
    count = lax.axis_size("ctx")
    groups = lax.axis_size("dp")
    seq_count, bins, chans = inputs.shape
    inner = weight.shape[3]
    rows = seq_count * bins
    scale = 1.0 / math.sqrt(seq_count * groups * bins * count)
    last = sections - 1
    seqs = range(seq_count)
    layer_flops = 2 * bins * chans * inner * 4

    def shape(*dims, dtype=jnp.bfloat16):
        return jax.ShapeDtypeStruct(dims, dtype)

    def hop(value, source, target, third=None):
        sends = {source: target, target: source}
        if third is not None and third not in sends:
            sends.update({target: third, third: source})
        route = []
        for core in range(groups):
            for stage in range(sections):
                taker = core if stage in sends else (core + 1) % groups
                for i in range(count):
                    giver = (core * sections + stage) * count + i
                    route.append((giver, (taker * sections + sends.get(stage, stage)) * count + i))
        return lax.ppermute(value, ("dp", "pipe", "ctx"), route)

    def onward(value, step):
        return lax.ppermute(value, "ctx", [(i, (i + step) % count) for i in range(count)])

    def exchange(value, offset):
        return lax.ppermute(value, "ctx", [(i, i ^ offset) for i in range(count)])

    payload = jnp.where(section == last, cotangent, inputs)
    parts = kernel_call(
        functools.partial(split_kernel, last),
        [shape(rows // count, chans)] * count,
        10 * seq_count * layer_flops,
        "split",
    )(payload)
    weight, point = kernel_call(
        hold_kernel,
        [shape(*weight.shape), shape(*point.shape)],
        0,
        "hold",
        waits=[parts[0]],
        in_spec=anywhere,
        scratch=[pltpu.SemaphoreType.DMA((2,))],
    )(weight, point)
    steps = [1, *range(count - 1, 1, -1)]
    parts = [*(onward(parts[step], step) for step in steps), parts[0]]

    trunk, inside = shape(bins, chans), shape(bins, inner)
    inside_wide = shape(bins, inner, dtype=jnp.float32)
    whole, out, pre = kernel_call(
        functools.partial(first_kernel, last, bins, [*steps, 0]),
        [shape(rows, chans), trunk, inside_wide],
        layer_flops,
        "first",
    )(*parts, weight, point)
    outs, pres, xs, sent = [out], [[pre]], [[whole]], ()
    for level in range(last):
        if level > 0:
            third = last if level > 1 else None
            xs.append([hop(out, level - 1, level, third) for out in outs])
            outs = []
            pres.append([])
        for seq in range(len(outs), seq_count):
            out, pre = kernel_call(
                functools.partial(fore_kernel, level, seq, bins),
                [trunk, inside_wide],
                layer_flops,
                "fore",
                waits=outs[-1:] or sent,
            )(xs[level][seq if level else 0], weight, point)
            outs.append(out)
            pres[level].append(pre)
        sent = outs
        if level == 1:
            back_weights = kernel_call(
                transpose_kernel,
                [shape(1, weight.shape[1], inner, chans), shape(1, chans, inner)],
                0,
                "transpose",
                waits=outs,
            )(weight, point)
            sent = [*outs, *back_weights]
    slopes = kernel_call(
        functools.partial(slope_kernel, last, seq_count, bins),
        [shape(bins, chans, dtype=jnp.float32), inside_wide] * seq_count,
        0,
        "slopes",
        waits=outs,
    )(
        *[xs[level][seq if level else 0] for level in range(last) for seq in seqs],
        *[pre for some in pres for pre in some],
    )
    sent = [*sent, *slopes]
    xs.append([hop(out, last - 1, last, 0) for out in outs])

    dys, dpres = [], [[] for level in range(sections)]
    for seq in seqs:
        dy, dpre = kernel_call(
            functools.partial(turn_kernel, last, seq, bins, scale),
            [trunk, inside],
            2 * layer_flops,
            "turn",
            waits=dys[-1:] or sent,
        )(xs[last][seq], whole, weight, *back_weights)
        dys.append(dy)
        dpres[last].append(dpre)
    early = (0, last)
    kept = list(range(0, count, 2))
    size = chans // count
    *owned, message = kernel_call(
        functools.partial(columns_kernel, groups, [len(x) for x in xs], kept),
        [shape(size, rows)] * len(kept) + [shape(size * len(kept), rows)],
        2 * rows * chans * chans,
        "columns",
        waits=dys,
    )(*[x for some in xs for x in some])
    table = {(offset, 0): (array, 0) for offset, array in zip(kept, owned)}
    table.update({(offset ^ 1, 0): (message, at) for at, offset in enumerate(kept)})
    late_table = dict(table)
    phases = count.bit_length() - 1

    def moving(table, phase):
        if not 0 <= phase < phases:
            return []
        return sorted(key for key in table if key[0] >> phase & 1)

    def columns_slot(slot, message):
        others = [stage for stage in range(sections) if stage not in early]
        route = []
        for core in range(groups):
            for kind, phase in ((list(early), slot), (others, slot - 1)):
                for at, stage in enumerate(kind):
                    for i in range(count):
                        taker, to_stage, j = core, stage, i
                        if 0 <= phase < phases:
                            j = i ^ 1 << phase
                        elif phase < 0:
                            to_stage = kind[(at + 1) % len(kind)]
                        else:
                            taker = (core + 1) % groups
                        giver = (core * sections + stage) * count + i
                        route.append((giver, (taker * sections + to_stage) * count + j))
        arrived = lax.ppermute(message, ("dp", "pipe", "ctx"), route)
        for table_of, phase in ((table, slot), (late_table, slot - 1)):
            for at, (to, start) in enumerate(moving(table_of, phase)):
                del table_of[to, start]
                table_of[to ^ 1 << phase, start ^ 1 << phase] = (arrived, at)
        return arrived

    sent = [owned[0]]
    dys = [hop(dy, last, last - 1) for dy in dys]
    columns_slot(0, message)
    slot = 0

    for level in range(last - 1, 0, -1):
        outs = []
        for seq in seqs:
            dy, dpre = kernel_call(
                functools.partial(back_kernel, level, bins),
                [trunk, inside],
                layer_flops,
                "back",
                waits=outs[-1:] or sent,
            )(dys[seq], *slopes[2 * seq : 2 * seq + 2], *back_weights)
            outs.append(dy)
            dpres[level].append(dpre)
        sent = outs
        dys = [hop(dy, level, level - 1, None if level > 1 else last) for dy in outs]
        slot += 1
        if slot <= phases:
            chosen = [table[key] for key in moving(table, slot)]
            late_chosen = [late_table[key] for key in moving(late_table, slot - 1)]
            (message,) = kernel_call(
                functools.partial(
                    message_kernel,
                    early,
                    [at for array, at in chosen],
                    [at for array, at in late_chosen],
                ),
                [shape(size * len(kept), rows)],
                0,
                "message",
                waits=outs if level > 1 else [*outs, dys[0]],
            )(*[array for array, at in (*chosen, *late_chosen)])
            sent = [*outs, message]
            late = columns_slot(slot, message)

    dpre = []
    for seq in seqs:
        dpre = kernel_call(
            functools.partial(head_kernel, sections, seq * bins),
            [shape((seq + 1) * bins, inner)],
            layer_flops // 4,
            "head",
            waits=[*dpre, late] if seq == seq_count - 1 else sent,
        )(dys[seq], slopes[2 * seq + 1], back_weights[1], *[dpres[level][seq] for level in range(1, sections)], *dpre)
    (dpre,) = dpre
    received, bit = {0: dpre}, count // 2
    while bit:
        received.update({offset ^ bit: exchange(block, bit) for offset, block in received.items()})
        bit //= 2
    offsets = [*received]
    gathered = [received[offset] for offset in offsets]
    columns = [table[0, offset] for offset in offsets]
    late_columns = [late_table[0, offset] for offset in offsets]
    width = size // groups

    def gradient(step, dtype, waits=()):
        places, late_places = (
            [at * size + step * width for array, at in kind] for kind in (columns, late_columns)
        )
        (part,) = kernel_call(
            functools.partial(grad_kernel, sections, early, bins, places, late_places),
            [shape(3, width, inner, dtype=dtype)],
            2 * 3 * rows * count * width * inner,
            "grad",
            waits=waits,
        )(*[array for array, at in (*columns, *late_columns)], *gathered)
        return part

    others = [gradient(step, jnp.bfloat16) for step in range(1, groups)]
    mine = gradient(0, jnp.float32, waits=others)
    for step, other in enumerate(others, 1):
        route = [(i, (i + step) % groups) for i in range(groups)]
        mine = mine + lax.ppermute(other, "dp", route).astype(jnp.float32)
    return mine[None]


def solution(mesh):
    def shards(inputs, cotangent, dilated_kernel_weight, point_weight):
        bins = inputs.shape[1]
        first_spread = bins // 2 // 2 ** (mesh.shape["pipe"] - 1)
        count = mesh.shape["ctx"]
        residues = (
            first_spread == count
            and mesh.shape["pipe"] > 3
            and bins % (16 * count) == 0
            and 1 < count == 1 << (count.bit_length() - 1) <= 1 << (mesh.shape["pipe"] - 2)
            and inputs.shape[2] % (count * mesh.shape["dp"]) == 0
        )
        plan = residue_shards if residues else edge_shards
        return plan(inputs, cotangent, dilated_kernel_weight, point_weight)

    return jax.shard_map(
        shards,
        mesh=mesh,
        in_specs=(
            P("dp", "ctx", None),
            P("dp", "ctx", None),
            P("pipe", None, None, None),
            P("pipe", None, None),
        ),
        out_specs=P("pipe", None, ("dp", "ctx"), None),
        check_vma=False,
    )
```

```python
import functools
import math

import jax
import jax.numpy as jnp
from jax import lax
from jax.experimental import pallas as pl
from jax.experimental.pallas import tpu as pltpu
from jax.sharding import PartitionSpec as P

root_half = 0.7071067811865476
inv_root_two_pi = 0.3989422804014327

in_vmem = pl.BlockSpec(memory_space=pltpu.VMEM)
anywhere = pl.BlockSpec(memory_space=pl.ANY)
contract_last = (((1,), (1,)), ((), ()))
contract_first = (((0,), (0,)), ((), ()))


def gelu(value):
    return 0.5 * value * (1.0 + lax.erf(value * root_half))


def gelu_slope(value):
    return (
        0.5 * (1.0 + lax.erf(value * root_half))
        + value * jnp.exp(-0.5 * value * value) * inv_root_two_pi
    )


def padded(cells, sides, width):
    for axis, dim in sides:
        count = lax.axis_size(axis)
        ends = count - 1
        head = lax.slice_in_dim(cells, 0, width, axis=dim)
        tail = lax.slice_in_dim(cells, cells.shape[dim] - width, cells.shape[dim], axis=dim)
        cells = jnp.concatenate(
            [
                lax.ppermute(tail, axis, [(i, (i + 1) % count) for i in range(ends)]),
                cells,
                lax.ppermute(head, axis, [((i + 1) % count, i) for i in range(ends)]),
            ],
            axis=dim,
        )
    return cells


def shifted(block, axis, distance):
    devices = range(lax.axis_size(axis))
    route = [(i - distance, i) for i in devices if i - distance in devices]
    return lax.ppermute(block, axis, route)


def edge_shards(inputs, cotangent, dilated_kernel_weight, point_weight):
    sections = lax.axis_size("pipe")
    section = lax.axis_index("pipe")
    seq_count, bins, chans = inputs.shape
    reach = bins // 2
    table = jnp.array(
        [reach // 2 ** (sections - 1 - level) for level in range(sections)], jnp.int32
    )
    spread = table[section]
    dilation_weight = dilated_kernel_weight[0]
    w_point = point_weight[0]
    inner_channel_count = dilation_weight.shape[2]
    scale = 1.0 / math.sqrt(seq_count * lax.axis_size("dp") * bins * lax.axis_size("ctx"))
    ticks = jnp.arange(seq_count + sections - 1, dtype=jnp.int32)

    def conv_fore(extended):
        running_total = jnp.zeros((bins, inner_channel_count), jnp.float32)
        for kernel_offset in range(3):
            receptive_span = lax.dynamic_slice_in_dim(
                extended, reach + (kernel_offset - 1) * spread, bins, 0
            )
            running_total = running_total + jnp.dot(
                receptive_span, dilation_weight[kernel_offset], preferred_element_type=jnp.float32
            )
        return running_total

    def put(store, slot, valid, item):
        current = lax.dynamic_index_in_dim(store, slot, 0, keepdims=False)
        return lax.dynamic_update_index_in_dim(store, jnp.where(valid, item, current), slot, 0)

    kept_x = jnp.zeros(inputs.shape, jnp.bfloat16)
    kept_ext = jnp.zeros((seq_count, bins + 2 * reach, chans), jnp.bfloat16)
    kept_pre = jnp.zeros((seq_count, bins, inner_channel_count), jnp.float32)

    def fore_tick(carry, tick):
        received, store_x, store_ext, store_pre = carry
        micro = tick - section
        valid = (micro >= 0) & (micro < seq_count)
        slot = jnp.clip(micro, 0, seq_count - 1)
        first = lax.dynamic_index_in_dim(inputs, slot, 0, keepdims=False)
        trunk_in = jnp.where(section == 0, first, received)
        act = gelu(trunk_in.astype(jnp.float32)).astype(jnp.bfloat16)
        extended = padded(act, (("ctx", 0),), reach)
        pre = conv_fore(extended)
        inner = gelu(pre).astype(jnp.bfloat16)
        out = (
            trunk_in.astype(jnp.float32)
            + jnp.dot(inner, w_point, preferred_element_type=jnp.float32)
        ).astype(jnp.bfloat16)
        sent = shifted(out, "pipe", 1)
        store_x = put(store_x, slot, valid, trunk_in)
        store_ext = put(store_ext, slot, valid, extended)
        store_pre = put(store_pre, slot, valid, pre)
        return ((sent, store_x, store_ext, store_pre), None)

    start_recv = jnp.zeros((bins, chans), jnp.bfloat16)
    (unused, kept_x, kept_ext, kept_pre), unused_out = lax.scan(
        fore_tick, (start_recv, kept_x, kept_ext, kept_pre), ticks
    )

    def back_tick(carry, tick):
        received, grad = carry
        micro = tick - (sections - 1 - section)
        valid = (micro >= 0) & (micro < seq_count)
        slot = jnp.clip(micro, 0, seq_count - 1)
        last = (
            lax.dynamic_index_in_dim(cotangent, slot, 0, keepdims=False).astype(jnp.float32) * scale
        ).astype(jnp.bfloat16)
        upstream = jnp.where(section == sections - 1, last, received)
        trunk_in = lax.dynamic_index_in_dim(kept_x, slot, 0, keepdims=False)
        extended = lax.dynamic_index_in_dim(kept_ext, slot, 0, keepdims=False)
        pre = lax.dynamic_index_in_dim(kept_pre, slot, 0, keepdims=False)
        inner_grad = lax.dot_general(
            upstream, w_point, contract_last, preferred_element_type=jnp.float32
        )
        dpre = (inner_grad * gelu_slope(pre) * valid.astype(jnp.float32)).astype(jnp.bfloat16)
        dpre_ext = padded(dpre, (("ctx", 0),), reach)
        dact = jnp.zeros((bins, chans), jnp.float32)
        taps = []
        for kernel_offset in range(3):
            receptive_span = lax.dynamic_slice_in_dim(
                dpre_ext, reach - (kernel_offset - 1) * spread, bins, 0
            )
            dact = dact + lax.dot_general(
                receptive_span,
                dilation_weight[kernel_offset],
                contract_last,
                preferred_element_type=jnp.float32,
            )
            source = lax.dynamic_slice_in_dim(
                extended, reach + (kernel_offset - 1) * spread, bins, 0
            )
            taps.append(
                lax.dot_general(source, dpre, contract_first, preferred_element_type=jnp.float32)
            )
        grad = grad + jnp.stack(taps)
        back = (
            upstream.astype(jnp.float32) + dact * gelu_slope(trunk_in.astype(jnp.float32))
        ).astype(jnp.bfloat16)
        sent = shifted(back, "pipe", -1)
        return ((sent, grad), None)

    start_grad = jnp.zeros((3, chans, inner_channel_count), jnp.float32)
    (unused_back, grad), unused_seq = lax.scan(back_tick, (start_recv, start_grad), ticks)
    term = grad[None]
    return lax.psum_scatter(term, ("dp", "ctx"), scatter_dimension=2, tiled=True)


def moved(value, by, bins):
    pieces = []
    for start in range(0, value.shape[0], bins):
        piece = value[start : start + bins]
        place = lax.broadcasted_iota(jnp.int32, piece.shape, 0)
        if by > 0:
            keep = place >= by
        else:
            keep = place < bins + by
        pieces.append(jnp.where(keep, pltpu.roll(piece, by % bins, 0), 0.0))
    return jnp.concatenate(pieces, axis=0)


def fore(x, weight_ref, spread, bins):
    act = gelu(x.astype(jnp.float32)).astype(jnp.bfloat16)
    terms = [
        jnp.dot(act, weight_ref[0, tap], preferred_element_type=jnp.float32) for tap in range(3)
    ]
    return terms[1] + moved(terms[0], spread, bins) + moved(terms[2], -spread, bins)


def back_pre(dy, pre_slope, point_ref):
    inner_grad = jnp.dot(dy, point_ref[0], preferred_element_type=jnp.float32)
    return (inner_grad * pre_slope).astype(jnp.bfloat16)


def back_trunk(dy, dpre, x_slope, weight_ref, spread, bins):
    wide = dpre.astype(jnp.float32)
    spans = (
        moved(wide, -spread, bins).astype(jnp.bfloat16),
        dpre,
        moved(wide, spread, bins).astype(jnp.bfloat16),
    )
    dact = jnp.zeros(dy.shape, jnp.float32)
    for tap in range(3):
        dact = dact + jnp.dot(
            spans[tap], weight_ref[0, tap], preferred_element_type=jnp.float32
        )
    return (dy.astype(jnp.float32) + dact * x_slope).astype(jnp.bfloat16)


def of_seq(ref, seq, bins):
    if ref.shape[0] == bins:
        return ref[...]
    return ref[seq * bins : (seq + 1) * bins, :]


def split_kernel(last, payload_ref, *out_refs):
    count = len(out_refs)
    seq_count, bins, chans = payload_ref.shape
    part = bins // count
    section = lax.axis_index("pipe")
    place = lax.axis_index("ctx")

    @pl.when((section == 0) | (section == last))
    def send():
        source = payload_ref[...].reshape(seq_count * bins, chans)
        row = lax.broadcasted_iota(jnp.int32, (part, seq_count * bins), 0)
        col = lax.broadcasted_iota(jnp.int32, (part, seq_count * bins), 1)
        for hop in range(count):
            residue = lax.rem(place + hop, count)
            rows = [
                (col == seq * bins + count * row + residue).astype(jnp.float32)
                for seq in range(seq_count)
            ]
            pick = jnp.concatenate(rows, axis=0).astype(jnp.bfloat16)
            out_refs[hop][...] = jnp.dot(
                pick, source, preferred_element_type=jnp.float32
            ).astype(jnp.bfloat16)


def hold_kernel(weight_ref, point_ref, weight_out, point_out, sems):
    loads = [
        pltpu.make_async_copy(weight_ref, weight_out, sems.at[0]),
        pltpu.make_async_copy(point_ref, point_out, sems.at[1]),
    ]
    for load in loads:
        load.start()
    for load in loads:
        load.wait()


def first_kernel(last, bins, steps, *refs):
    parts, (weight_ref, point_ref, whole_ref, out_ref, pre_ref) = refs[:-5], refs[-5:]
    count = len(parts)
    section = lax.axis_index("pipe")
    place = lax.axis_index("ctx")
    part = bins // count
    seq_count = whole_ref.shape[0] // bins

    @pl.when((section == 0) | (section == last))
    def gather():
        for step, part_ref in zip(steps, parts):
            source = lax.rem(place + count - step, count)
            for seq in range(seq_count):
                at = pl.multiple_of(seq * bins + source * part, part)
                whole_ref[pl.ds(at, part), :] = part_ref[seq * part : (seq + 1) * part, :]

    @pl.when(section == 0)
    def layer():
        x = whole_ref[:bins, :]
        finish(x, fore(x, weight_ref, 1, bins), point_ref, out_ref, pre_ref)


def finish(x, pre, point_ref, out_ref, pre_ref):
    pre_ref[...] = pre
    branch = jnp.dot(
        gelu(pre).astype(jnp.bfloat16), point_ref[0], preferred_element_type=jnp.float32
    )
    out_ref[...] = (x.astype(jnp.float32) + branch).astype(jnp.bfloat16)


def fore_kernel(level, seq, bins, x_ref, weight_ref, point_ref, out_ref, pre_ref):
    @pl.when(lax.axis_index("pipe") == level)
    def layer():
        x = of_seq(x_ref, seq, bins)
        finish(x, fore(x, weight_ref, 2**level, bins), point_ref, out_ref, pre_ref)


def transpose_kernel(weight_ref, point_ref, weight_out, point_out):
    for tap in range(weight_ref.shape[1]):
        weight_out[0, tap] = weight_ref[0, tap].T
    point_out[0] = point_ref[0].T


def turn_kernel(level, seq, bins, scale, x_ref, cot_ref, weight_ref, weight_t_ref, point_t_ref, dy_ref, dpre_ref):
    @pl.when(lax.axis_index("pipe") == level)
    def layer():
        x = of_seq(x_ref, seq, bins)
        pre = fore(x, weight_ref, 2**level, bins)
        cot = of_seq(cot_ref, seq, bins)
        dy = (cot.astype(jnp.float32) * scale).astype(jnp.bfloat16)
        dpre = back_pre(dy, gelu_slope(pre), point_t_ref)
        dpre_ref[...] = dpre
        x_slope = gelu_slope(x.astype(jnp.float32))
        dy_ref[...] = back_trunk(dy, dpre, x_slope, weight_t_ref, 2**level, bins)


def slope_kernel(levels, seq_count, bins, *refs):
    xs, pres = refs[: levels * seq_count], refs[levels * seq_count : 2 * levels * seq_count]
    outs = refs[2 * levels * seq_count :]
    for level in range(levels):

        @pl.when(lax.axis_index("pipe") == level)
        def layer(level=level):
            for seq in range(seq_count):
                x = of_seq(xs[level * seq_count + seq], seq, bins)
                outs[2 * seq][...] = gelu_slope(x.astype(jnp.float32))
                outs[2 * seq + 1][...] = gelu_slope(pres[level * seq_count + seq][...])


def back_kernel(level, bins, dy_in_ref, x_slope_ref, pre_slope_ref, weight_ref, point_ref, dy_ref, dpre_ref):
    @pl.when(lax.axis_index("pipe") == level)
    def layer():
        dy = dy_in_ref[...]
        dpre = back_pre(dy, pre_slope_ref[...], point_ref)
        dpre_ref[...] = dpre
        dy_ref[...] = back_trunk(dy, dpre, x_slope_ref[...], weight_ref, 2**level, bins)


def message_kernel(places, *refs):
    blocks, message_ref = refs[:-1], refs[-1]
    size = message_ref.shape[0] // len(places)
    for to, (ref, at) in enumerate(zip(blocks, places)):
        message_ref[to * size : (to + 1) * size, :] = ref[at * size : (at + 1) * size, :]


def head_kernel(sections, earlier, dy_in_ref, slope_ref, point_ref, *refs):
    others, before, out_ref = refs[: sections - 1], refs[sections - 1 : -1], refs[-1]
    section = lax.axis_index("pipe")
    bins = dy_in_ref.shape[0]
    for ref in before:
        out_ref[:earlier, :] = ref[...]

    @pl.when(section == 0)
    def layer():
        out_ref[earlier : earlier + bins, :] = back_pre(dy_in_ref[...], slope_ref[...], point_ref)

    for level in range(1, sections):

        @pl.when(section == level)
        def keep(level=level):
            out_ref[earlier : earlier + bins, :] = others[level - 1][...]


def columns_kernel(groups, runs, kept, *refs):
    refs, (sent_ref,) = refs[:-1], refs[-1:]
    kept_refs = refs[sum(runs) :]
    count = 2 * len(kept)
    section = lax.axis_index("pipe")
    core = lax.axis_index("dp")
    place = lax.axis_index("ctx")
    x, start = None, 0
    for level, run in enumerate(runs):
        pieces = [ref[...] for ref in refs[start : start + run]]
        start += run
        whole = jnp.concatenate(pieces, axis=0).astype(jnp.float32)
        x = whole if x is None else jnp.where(section == level, whole, x)
    act = gelu(x).astype(jnp.bfloat16)
    chans = act.shape[1]
    width = chans // (groups * count)
    row = lax.broadcasted_iota(jnp.int32, (width, chans), 0)
    col = lax.broadcasted_iota(jnp.int32, (width, chans), 1)

    def block(offset):
        owner = lax.bitwise_xor(place, offset)
        rows = []
        for step in range(groups):
            first = (lax.rem(core + step, groups) * count + owner) * width
            rows.append((col == first + row).astype(jnp.float32))
        pick = jnp.concatenate(rows, axis=0).astype(jnp.bfloat16)
        return lax.dot_general(
            pick, act, contract_last, preferred_element_type=jnp.float32
        ).astype(jnp.bfloat16)

    size = groups * width
    for at, offset in enumerate(kept):
        kept_refs[at][...] = block(offset)
        sent_ref[at * size : (at + 1) * size, :] = block(offset ^ count // 2)


def grad_kernel(sections, bins, places, *refs):
    columns, refs = refs[: len(places)], refs[len(places) :]
    grads, out_ref = refs[:-1], refs[-1]
    section = lax.axis_index("pipe")
    width = out_ref.shape[1]

    def taps(spread):
        act = jnp.concatenate(
            [ref[at : at + width, :] for ref, at in zip(columns, places)], axis=1
        )
        dpre = jnp.concatenate([ref[...] for ref in grads], axis=0)
        wide = dpre.astype(jnp.float32)
        spans = (
            moved(wide, -spread, bins).astype(jnp.bfloat16),
            dpre,
            moved(wide, spread, bins).astype(jnp.bfloat16),
        )
        for tap in range(3):
            out_ref[tap] = jnp.dot(
                act, spans[tap], preferred_element_type=jnp.float32
            ).astype(out_ref.dtype)

    for level in range(sections):

        @pl.when(section == level)
        def run(level=level):
            taps(2**level)


def kernel_call(body, outs, flops, name, waits=(), carries=(), in_spec=in_vmem, scratch=()):
    def call(*args):
        used, taken = len(args), len(args) + len(waits) + len(carries)

        def run(*refs):
            made = refs[taken : taken + len(outs)]
            body(*refs[:used], *made, *refs[taken + len(outs) + len(carries) :])

        moved_bytes = sum(math.prod(a.shape) * a.dtype.itemsize for a in (*args, *outs))
        return pl.pallas_call(
            run,
            out_shape=[*outs, *(jax.ShapeDtypeStruct(a.shape, a.dtype) for a in carries)],
            in_specs=[in_spec] * used + [anywhere] * (taken - used),
            out_specs=[in_vmem] * len(outs) + [anywhere] * len(carries),
            input_output_aliases={
                used + len(waits) + at: len(outs) + at for at in range(len(carries))
            },
            scratch_shapes=list(scratch),
            compiler_params=pltpu.CompilerParams(vmem_limit_bytes=24 * 2**20),
            cost_estimate=pl.CostEstimate(
                flops=flops, bytes_accessed=moved_bytes, transcendentals=0
            ),
            name=name,
        )(*args, *waits, *carries)

    return call


def residue_shards(inputs, cotangent, weight, point):
    sections = lax.axis_size("pipe")
    section = lax.axis_index("pipe")
    count = lax.axis_size("ctx")
    groups = lax.axis_size("dp")
    seq_count, bins, chans = inputs.shape
    inner = weight.shape[3]
    rows = seq_count * bins
    scale = 1.0 / math.sqrt(seq_count * groups * bins * count)
    last = sections - 1
    seqs = range(seq_count)
    layer_flops = 2 * bins * chans * inner * 4

    def shape(*dims, dtype=jnp.bfloat16):
        return jax.ShapeDtypeStruct(dims, dtype)

    def hop(value, source, target, third=None):
        sends = {source: target, target: source}
        if third is not None and third not in sends:
            sends.update({target: third, third: source})
        route = []
        for core in range(groups):
            for stage in range(sections):
                taker = core if stage in sends else (core + 1) % groups
                for i in range(count):
                    giver = (core * sections + stage) * count + i
                    route.append((giver, (taker * sections + sends.get(stage, stage)) * count + i))
        return lax.ppermute(value, ("dp", "pipe", "ctx"), route)

    def onward(value, step):
        return lax.ppermute(value, "ctx", [(i, (i + step) % count) for i in range(count)])

    def exchange(value, offset):
        return lax.ppermute(value, "ctx", [(i, i ^ offset) for i in range(count)])

    payload = jnp.where(section == last, cotangent, inputs)
    parts = kernel_call(
        functools.partial(split_kernel, last),
        [shape(rows // count, chans)] * count,
        10 * seq_count * layer_flops,
        "split",
    )(payload)
    weight, point = kernel_call(
        hold_kernel,
        [shape(*weight.shape), shape(*point.shape)],
        0,
        "hold",
        waits=[parts[0]],
        in_spec=anywhere,
        scratch=[pltpu.SemaphoreType.DMA((2,))],
    )(weight, point)
    steps = [1, *range(count - 1, 1, -1)]
    parts = [*(onward(parts[step], step) for step in steps), parts[0]]

    trunk, inside = shape(bins, chans), shape(bins, inner)
    inside_wide = shape(bins, inner, dtype=jnp.float32)
    whole, out, pre = kernel_call(
        functools.partial(first_kernel, last, bins, [*steps, 0]),
        [shape(rows, chans), trunk, inside_wide],
        layer_flops,
        "first",
    )(*parts, weight, point)
    outs, pres, xs, sent = [out], [[pre]], [[whole]], ()
    for level in range(last):
        if level > 0:
            third = last if level > 1 else None
            xs.append([hop(out, level - 1, level, third) for out in outs])
            outs = []
            pres.append([])
        for seq in range(len(outs), seq_count):
            out, pre = kernel_call(
                functools.partial(fore_kernel, level, seq, bins),
                [trunk, inside_wide],
                layer_flops,
                "fore",
                waits=outs[-1:] or sent,
            )(xs[level][seq if level else 0], weight, point)
            outs.append(out)
            pres[level].append(pre)
        sent = outs
        if level == 1:
            back_weights = kernel_call(
                transpose_kernel,
                [shape(1, weight.shape[1], inner, chans), shape(1, chans, inner)],
                0,
                "transpose",
                waits=outs,
            )(weight, point)
            sent = [*outs, *back_weights]
    slopes = kernel_call(
        functools.partial(slope_kernel, last, seq_count, bins),
        [shape(bins, chans, dtype=jnp.float32), inside_wide] * seq_count,
        0,
        "slopes",
        waits=outs,
    )(
        *[xs[level][seq if level else 0] for level in range(last) for seq in seqs],
        *[pre for some in pres for pre in some],
    )
    sent = [*sent, *slopes]
    xs.append([hop(out, last - 1, last, 0) for out in outs])

    dys, dpres = [], [[] for level in range(sections)]
    for seq in seqs:
        dy, dpre = kernel_call(
            functools.partial(turn_kernel, last, seq, bins, scale),
            [trunk, inside],
            2 * layer_flops,
            "turn",
            waits=dys[-1:] or sent,
        )(xs[last][seq], whole, weight, *back_weights)
        dys.append(dy)
        dpres[last].append(dpre)
    bit = count // 2
    kept = list(range(bit))
    moving = [(offset, 0) for offset in range(bit, count)]
    size = chans // count
    *owned, message = kernel_call(
        functools.partial(columns_kernel, groups, [len(x) for x in xs], kept),
        [shape(size, rows)] * len(kept) + [shape(size * len(kept), rows)],
        2 * rows * chans * chans,
        "columns",
        waits=dys,
    )(*[x for some in xs for x in some])
    blocks = {(offset, 0): (array, 0) for offset, array in zip(kept, owned)}
    sent = [owned[0]]
    dys = [hop(dy, last, last - 1) for dy in dys]
    message = exchange(message, bit)
    blocks.update({(to ^ bit, start ^ bit): (message, at) for at, (to, start) in enumerate(moving)})

    for level in range(last - 1, 0, -1):
        outs = []
        for seq in seqs:
            dy, dpre = kernel_call(
                functools.partial(back_kernel, level, bins),
                [trunk, inside],
                layer_flops,
                "back",
                waits=outs[-1:] or sent,
            )(dys[seq], *slopes[2 * seq : 2 * seq + 2], *back_weights)
            outs.append(dy)
            dpres[level].append(dpre)
        sent = outs
        dys = [hop(dy, level, level - 1, None if level > 1 else last) for dy in outs]
        bit //= 2
        moving = sorted(key for key in blocks if key[0] & bit)
        if moving:
            (message,) = kernel_call(
                functools.partial(message_kernel, [blocks[key][1] for key in moving]),
                [shape(size * len(moving), rows)],
                0,
                "message",
                waits=outs,
            )(*[blocks[key][0] for key in moving])
            sent = [*outs, message]
            message = exchange(message, bit)
            for at, (to, start) in enumerate(moving):
                blocks[to ^ bit, start ^ bit] = (message, at)

    sent = [*sent, message]
    dpre = []
    for seq in seqs:
        dpre = kernel_call(
            functools.partial(head_kernel, sections, seq * bins),
            [shape((seq + 1) * bins, inner)],
            layer_flops // 4,
            "head",
            waits=dpre or sent,
        )(dys[seq], slopes[2 * seq + 1], back_weights[1], *[dpres[level][seq] for level in range(1, sections)], *dpre)
    (dpre,) = dpre
    received, bit = {0: dpre}, count // 2
    while bit:
        received.update({offset ^ bit: exchange(block, bit) for offset, block in received.items()})
        bit //= 2
    offsets = [*received]
    gathered = [received[offset] for offset in offsets]
    columns = [blocks[0, offset] for offset in offsets]
    width = size // groups

    def gradient(step, dtype, waits=()):
        places = [at * size + step * width for array, at in columns]
        (part,) = kernel_call(
            functools.partial(grad_kernel, sections, bins, places),
            [shape(3, width, inner, dtype=dtype)],
            2 * 3 * rows * count * width * inner,
            "grad",
            waits=waits,
        )(*[array for array, at in columns], *gathered)
        return part

    others = [gradient(step, jnp.bfloat16) for step in range(1, groups)]
    mine = gradient(0, jnp.float32, waits=others)
    for step, other in enumerate(others, 1):
        route = [(i, (i + step) % groups) for i in range(groups)]
        mine = mine + lax.ppermute(other, "dp", route).astype(jnp.float32)
    return mine[None]


def solution(mesh):
    def shards(inputs, cotangent, dilated_kernel_weight, point_weight):
        bins = inputs.shape[1]
        first_spread = bins // 2 // 2 ** (mesh.shape["pipe"] - 1)
        count = mesh.shape["ctx"]
        residues = (
            first_spread == count
            and mesh.shape["pipe"] > 2
            and bins % (16 * count) == 0
            and 1 < count == 1 << (count.bit_length() - 1) <= 1 << (mesh.shape["pipe"] - 2)
            and inputs.shape[2] % (count * mesh.shape["dp"]) == 0
        )
        plan = residue_shards if residues else edge_shards
        return plan(inputs, cotangent, dilated_kernel_weight, point_weight)

    return jax.shard_map(
        shards,
        mesh=mesh,
        in_specs=(
            P("dp", "ctx", None),
            P("dp", "ctx", None),
            P("pipe", None, None, None),
            P("pipe", None, None),
        ),
        out_specs=P("pipe", None, ("dp", "ctx"), None),
        check_vma=False,
    )
```

```python
import functools
import math

import jax
import jax.numpy as jnp
from jax import lax
from jax.experimental import pallas as pl
from jax.experimental.pallas import tpu as pltpu
from jax.sharding import PartitionSpec as P

root_half = 0.7071067811865476
inv_root_two_pi = 0.3989422804014327

in_vmem = pl.BlockSpec(memory_space=pltpu.VMEM)
anywhere = pl.BlockSpec(memory_space=pl.ANY)
contract_last = (((1,), (1,)), ((), ()))
contract_first = (((0,), (0,)), ((), ()))


def gelu(value):
    return 0.5 * value * (1.0 + lax.erf(value * root_half))


def gelu_slope(value):
    return (
        0.5 * (1.0 + lax.erf(value * root_half))
        + value * jnp.exp(-0.5 * value * value) * inv_root_two_pi
    )


def padded(cells, sides, width):
    for axis, dim in sides:
        count = lax.axis_size(axis)
        ends = count - 1
        head = lax.slice_in_dim(cells, 0, width, axis=dim)
        tail = lax.slice_in_dim(cells, cells.shape[dim] - width, cells.shape[dim], axis=dim)
        cells = jnp.concatenate(
            [
                lax.ppermute(tail, axis, [(i, (i + 1) % count) for i in range(ends)]),
                cells,
                lax.ppermute(head, axis, [((i + 1) % count, i) for i in range(ends)]),
            ],
            axis=dim,
        )
    return cells


def shifted(block, axis, distance):
    devices = range(lax.axis_size(axis))
    route = [(i - distance, i) for i in devices if i - distance in devices]
    return lax.ppermute(block, axis, route)


def edge_shards(inputs, cotangent, dilated_kernel_weight, point_weight):
    sections = lax.axis_size("pipe")
    section = lax.axis_index("pipe")
    seq_count, bins, chans = inputs.shape
    reach = bins // 2
    table = jnp.array(
        [reach // 2 ** (sections - 1 - level) for level in range(sections)], jnp.int32
    )
    spread = table[section]
    dilation_weight = dilated_kernel_weight[0]
    w_point = point_weight[0]
    inner_channel_count = dilation_weight.shape[2]
    scale = 1.0 / math.sqrt(seq_count * lax.axis_size("dp") * bins * lax.axis_size("ctx"))
    ticks = jnp.arange(seq_count + sections - 1, dtype=jnp.int32)

    def conv_fore(extended):
        running_total = jnp.zeros((bins, inner_channel_count), jnp.float32)
        for kernel_offset in range(3):
            receptive_span = lax.dynamic_slice_in_dim(
                extended, reach + (kernel_offset - 1) * spread, bins, 0
            )
            running_total = running_total + jnp.dot(
                receptive_span, dilation_weight[kernel_offset], preferred_element_type=jnp.float32
            )
        return running_total

    def put(store, slot, valid, item):
        current = lax.dynamic_index_in_dim(store, slot, 0, keepdims=False)
        return lax.dynamic_update_index_in_dim(store, jnp.where(valid, item, current), slot, 0)

    kept_x = jnp.zeros(inputs.shape, jnp.bfloat16)
    kept_ext = jnp.zeros((seq_count, bins + 2 * reach, chans), jnp.bfloat16)
    kept_pre = jnp.zeros((seq_count, bins, inner_channel_count), jnp.float32)

    def fore_tick(carry, tick):
        received, store_x, store_ext, store_pre = carry
        micro = tick - section
        valid = (micro >= 0) & (micro < seq_count)
        slot = jnp.clip(micro, 0, seq_count - 1)
        first = lax.dynamic_index_in_dim(inputs, slot, 0, keepdims=False)
        trunk_in = jnp.where(section == 0, first, received)
        act = gelu(trunk_in.astype(jnp.float32)).astype(jnp.bfloat16)
        extended = padded(act, (("ctx", 0),), reach)
        pre = conv_fore(extended)
        inner = gelu(pre).astype(jnp.bfloat16)
        out = (
            trunk_in.astype(jnp.float32)
            + jnp.dot(inner, w_point, preferred_element_type=jnp.float32)
        ).astype(jnp.bfloat16)
        sent = shifted(out, "pipe", 1)
        store_x = put(store_x, slot, valid, trunk_in)
        store_ext = put(store_ext, slot, valid, extended)
        store_pre = put(store_pre, slot, valid, pre)
        return ((sent, store_x, store_ext, store_pre), None)

    start_recv = jnp.zeros((bins, chans), jnp.bfloat16)
    (unused, kept_x, kept_ext, kept_pre), unused_out = lax.scan(
        fore_tick, (start_recv, kept_x, kept_ext, kept_pre), ticks
    )

    def back_tick(carry, tick):
        received, grad = carry
        micro = tick - (sections - 1 - section)
        valid = (micro >= 0) & (micro < seq_count)
        slot = jnp.clip(micro, 0, seq_count - 1)
        last = (
            lax.dynamic_index_in_dim(cotangent, slot, 0, keepdims=False).astype(jnp.float32) * scale
        ).astype(jnp.bfloat16)
        upstream = jnp.where(section == sections - 1, last, received)
        trunk_in = lax.dynamic_index_in_dim(kept_x, slot, 0, keepdims=False)
        extended = lax.dynamic_index_in_dim(kept_ext, slot, 0, keepdims=False)
        pre = lax.dynamic_index_in_dim(kept_pre, slot, 0, keepdims=False)
        inner_grad = lax.dot_general(
            upstream, w_point, contract_last, preferred_element_type=jnp.float32
        )
        dpre = (inner_grad * gelu_slope(pre) * valid.astype(jnp.float32)).astype(jnp.bfloat16)
        dpre_ext = padded(dpre, (("ctx", 0),), reach)
        dact = jnp.zeros((bins, chans), jnp.float32)
        taps = []
        for kernel_offset in range(3):
            receptive_span = lax.dynamic_slice_in_dim(
                dpre_ext, reach - (kernel_offset - 1) * spread, bins, 0
            )
            dact = dact + lax.dot_general(
                receptive_span,
                dilation_weight[kernel_offset],
                contract_last,
                preferred_element_type=jnp.float32,
            )
            source = lax.dynamic_slice_in_dim(
                extended, reach + (kernel_offset - 1) * spread, bins, 0
            )
            taps.append(
                lax.dot_general(source, dpre, contract_first, preferred_element_type=jnp.float32)
            )
        grad = grad + jnp.stack(taps)
        back = (
            upstream.astype(jnp.float32) + dact * gelu_slope(trunk_in.astype(jnp.float32))
        ).astype(jnp.bfloat16)
        sent = shifted(back, "pipe", -1)
        return ((sent, grad), None)

    start_grad = jnp.zeros((3, chans, inner_channel_count), jnp.float32)
    (unused_back, grad), unused_seq = lax.scan(back_tick, (start_recv, start_grad), ticks)
    term = grad[None]
    return lax.psum_scatter(term, ("dp", "ctx"), scatter_dimension=2, tiled=True)


def moved(value, by, bins):
    pieces = []
    for start in range(0, value.shape[0], bins):
        piece = value[start : start + bins]
        place = lax.broadcasted_iota(jnp.int32, piece.shape, 0)
        if by > 0:
            keep = place >= by
        else:
            keep = place < bins + by
        pieces.append(jnp.where(keep, pltpu.roll(piece, by % bins, 0), 0.0))
    return jnp.concatenate(pieces, axis=0)


def fore(x, weight_ref, spread, bins):
    act = gelu(x.astype(jnp.float32)).astype(jnp.bfloat16)
    terms = [
        jnp.dot(act, weight_ref[0, tap], preferred_element_type=jnp.float32) for tap in range(3)
    ]
    return terms[1] + moved(terms[0], spread, bins) + moved(terms[2], -spread, bins)


def back_pre(dy, pre_slope, point_ref):
    inner_grad = jnp.dot(dy, point_ref[0], preferred_element_type=jnp.float32)
    return (inner_grad * pre_slope).astype(jnp.bfloat16)


def back_trunk(dy, dpre, x_slope, weight_ref, spread, bins):
    wide = dpre.astype(jnp.float32)
    spans = (
        moved(wide, -spread, bins).astype(jnp.bfloat16),
        dpre,
        moved(wide, spread, bins).astype(jnp.bfloat16),
    )
    dact = jnp.zeros(dy.shape, jnp.float32)
    for tap in range(3):
        dact = dact + jnp.dot(
            spans[tap], weight_ref[0, tap], preferred_element_type=jnp.float32
        )
    return (dy.astype(jnp.float32) + dact * x_slope).astype(jnp.bfloat16)


def of_seq(ref, seq, bins):
    if ref.shape[0] == bins:
        return ref[...]
    return ref[seq * bins : (seq + 1) * bins, :]


def split_kernel(last, payload_ref, *out_refs):
    count = len(out_refs)
    seq_count, bins, chans = payload_ref.shape
    part = bins // count
    section = lax.axis_index("pipe")
    place = lax.axis_index("ctx")

    @pl.when((section == 0) | (section == last))
    def send():
        source = payload_ref[...].reshape(seq_count * bins, chans)
        row = lax.broadcasted_iota(jnp.int32, (part, seq_count * bins), 0)
        col = lax.broadcasted_iota(jnp.int32, (part, seq_count * bins), 1)
        for hop in range(count):
            residue = lax.rem(place + hop, count)
            rows = [
                (col == seq * bins + count * row + residue).astype(jnp.float32)
                for seq in range(seq_count)
            ]
            pick = jnp.concatenate(rows, axis=0).astype(jnp.bfloat16)
            out_refs[hop][...] = jnp.dot(
                pick, source, preferred_element_type=jnp.float32
            ).astype(jnp.bfloat16)


def hold_kernel(weight_ref, point_ref, weight_out, point_out, sems):
    loads = [
        pltpu.make_async_copy(weight_ref, weight_out, sems.at[0]),
        pltpu.make_async_copy(point_ref, point_out, sems.at[1]),
    ]
    for load in loads:
        load.start()
    for load in loads:
        load.wait()


def first_kernel(last, bins, steps, *refs):
    parts, (weight_ref, point_ref, whole_ref, out_ref, pre_ref) = refs[:-5], refs[-5:]
    count = len(parts)
    section = lax.axis_index("pipe")
    place = lax.axis_index("ctx")
    part = bins // count
    seq_count = whole_ref.shape[0] // bins

    @pl.when((section == 0) | (section == last))
    def gather():
        for step, part_ref in zip(steps, parts):
            source = lax.rem(place + count - step, count)
            for seq in range(seq_count):
                at = pl.multiple_of(seq * bins + source * part, part)
                whole_ref[pl.ds(at, part), :] = part_ref[seq * part : (seq + 1) * part, :]

    @pl.when(section == 0)
    def layer():
        x = whole_ref[:bins, :]
        finish(x, fore(x, weight_ref, 1, bins), point_ref, out_ref, pre_ref)


def finish(x, pre, point_ref, out_ref, pre_ref):
    pre_ref[...] = pre
    branch = jnp.dot(
        gelu(pre).astype(jnp.bfloat16), point_ref[0], preferred_element_type=jnp.float32
    )
    out_ref[...] = (x.astype(jnp.float32) + branch).astype(jnp.bfloat16)


def fore_kernel(level, seq, bins, x_ref, weight_ref, point_ref, out_ref, pre_ref):
    @pl.when(lax.axis_index("pipe") == level)
    def layer():
        x = of_seq(x_ref, seq, bins)
        finish(x, fore(x, weight_ref, 2**level, bins), point_ref, out_ref, pre_ref)


def transpose_kernel(weight_ref, point_ref, weight_out, point_out):
    for tap in range(weight_ref.shape[1]):
        weight_out[0, tap] = weight_ref[0, tap].T
    point_out[0] = point_ref[0].T


def turn_kernel(level, seq, bins, scale, x_ref, cot_ref, weight_ref, weight_t_ref, point_t_ref, dy_ref, dpre_ref):
    @pl.when(lax.axis_index("pipe") == level)
    def layer():
        x = of_seq(x_ref, seq, bins)
        pre = fore(x, weight_ref, 2**level, bins)
        cot = of_seq(cot_ref, seq, bins)
        dy = (cot.astype(jnp.float32) * scale).astype(jnp.bfloat16)
        dpre = back_pre(dy, gelu_slope(pre), point_t_ref)
        dpre_ref[...] = dpre
        x_slope = gelu_slope(x.astype(jnp.float32))
        dy_ref[...] = back_trunk(dy, dpre, x_slope, weight_t_ref, 2**level, bins)


def slope_kernel(levels, seq_count, bins, *refs):
    xs, pres = refs[: levels * seq_count], refs[levels * seq_count : 2 * levels * seq_count]
    outs = refs[2 * levels * seq_count :]
    for level in range(levels):

        @pl.when(lax.axis_index("pipe") == level)
        def layer(level=level):
            for seq in range(seq_count):
                x = of_seq(xs[level * seq_count + seq], seq, bins)
                outs[2 * seq][...] = gelu_slope(x.astype(jnp.float32))
                outs[2 * seq + 1][...] = gelu_slope(pres[level * seq_count + seq][...])


def back_kernel(level, bins, dy_in_ref, x_slope_ref, pre_slope_ref, weight_ref, point_ref, dy_ref, dpre_ref):
    @pl.when(lax.axis_index("pipe") == level)
    def layer():
        dy = dy_in_ref[...]
        dpre = back_pre(dy, pre_slope_ref[...], point_ref)
        dpre_ref[...] = dpre
        dy_ref[...] = back_trunk(dy, dpre, x_slope_ref[...], weight_ref, 2**level, bins)


def message_kernel(places, *refs):
    blocks, message_ref = refs[:-1], refs[-1]
    size = message_ref.shape[0] // len(places)
    for to, (ref, at) in enumerate(zip(blocks, places)):
        message_ref[to * size : (to + 1) * size, :] = ref[at * size : (at + 1) * size, :]


def head_kernel(sections, earlier, dy_in_ref, slope_ref, point_ref, *refs):
    others, before, out_ref = refs[: sections - 1], refs[sections - 1 : -1], refs[-1]
    section = lax.axis_index("pipe")
    bins = dy_in_ref.shape[0]
    for ref in before:
        out_ref[:earlier, :] = ref[...]

    @pl.when(section == 0)
    def layer():
        out_ref[earlier : earlier + bins, :] = back_pre(dy_in_ref[...], slope_ref[...], point_ref)

    for level in range(1, sections):

        @pl.when(section == level)
        def keep(level=level):
            out_ref[earlier : earlier + bins, :] = others[level - 1][...]


def columns_kernel(groups, runs, kept, *refs):
    refs, (sent_ref,) = refs[:-1], refs[-1:]
    kept_refs = refs[sum(runs) :]
    count = 2 * len(kept)
    section = lax.axis_index("pipe")
    core = lax.axis_index("dp")
    place = lax.axis_index("ctx")
    x, start = None, 0
    for level, run in enumerate(runs):
        pieces = [ref[...] for ref in refs[start : start + run]]
        start += run
        whole = jnp.concatenate(pieces, axis=0).astype(jnp.float32)
        x = whole if x is None else jnp.where(section == level, whole, x)
    act = gelu(x).astype(jnp.bfloat16)
    chans = act.shape[1]
    width = chans // (groups * count)
    row = lax.broadcasted_iota(jnp.int32, (width, chans), 0)
    col = lax.broadcasted_iota(jnp.int32, (width, chans), 1)

    def block(offset):
        owner = lax.bitwise_xor(place, offset)
        rows = []
        for step in range(groups):
            first = (lax.rem(core + step, groups) * count + owner) * width
            rows.append((col == first + row).astype(jnp.float32))
        pick = jnp.concatenate(rows, axis=0).astype(jnp.bfloat16)
        return lax.dot_general(
            pick, act, contract_last, preferred_element_type=jnp.float32
        ).astype(jnp.bfloat16)

    size = groups * width
    for at, offset in enumerate(kept):
        kept_refs[at][...] = block(offset)
        sent_ref[at * size : (at + 1) * size, :] = block(offset ^ count // 2)


def grad_kernel(sections, bins, places, *refs):
    columns, refs = refs[: len(places)], refs[len(places) :]
    grads, out_ref = refs[:-1], refs[-1]
    section = lax.axis_index("pipe")
    width = out_ref.shape[1]

    def taps(spread):
        act = jnp.concatenate(
            [ref[at : at + width, :] for ref, at in zip(columns, places)], axis=1
        )
        dpre = jnp.concatenate([ref[...] for ref in grads], axis=0)
        wide = dpre.astype(jnp.float32)
        spans = (
            moved(wide, -spread, bins).astype(jnp.bfloat16),
            dpre,
            moved(wide, spread, bins).astype(jnp.bfloat16),
        )
        for tap in range(3):
            out_ref[tap] = jnp.dot(
                act, spans[tap], preferred_element_type=jnp.float32
            ).astype(out_ref.dtype)

    for level in range(sections):

        @pl.when(section == level)
        def run(level=level):
            taps(2**level)


def kernel_call(body, outs, flops, name, waits=(), carries=(), in_spec=in_vmem, scratch=()):
    def call(*args):
        used, taken = len(args), len(args) + len(waits) + len(carries)

        def run(*refs):
            made = refs[taken : taken + len(outs)]
            body(*refs[:used], *made, *refs[taken + len(outs) + len(carries) :])

        moved_bytes = sum(math.prod(a.shape) * a.dtype.itemsize for a in (*args, *outs))
        return pl.pallas_call(
            run,
            out_shape=[*outs, *(jax.ShapeDtypeStruct(a.shape, a.dtype) for a in carries)],
            in_specs=[in_spec] * used + [anywhere] * (taken - used),
            out_specs=[in_vmem] * len(outs) + [anywhere] * len(carries),
            input_output_aliases={
                used + len(waits) + at: len(outs) + at for at in range(len(carries))
            },
            scratch_shapes=list(scratch),
            compiler_params=pltpu.CompilerParams(vmem_limit_bytes=24 * 2**20),
            cost_estimate=pl.CostEstimate(
                flops=flops, bytes_accessed=moved_bytes, transcendentals=0
            ),
            name=name,
        )(*args, *waits, *carries)

    return call


def residue_shards(inputs, cotangent, weight, point):
    sections = lax.axis_size("pipe")
    section = lax.axis_index("pipe")
    count = lax.axis_size("ctx")
    groups = lax.axis_size("dp")
    seq_count, bins, chans = inputs.shape
    inner = weight.shape[3]
    rows = seq_count * bins
    scale = 1.0 / math.sqrt(seq_count * groups * bins * count)
    last = sections - 1
    seqs = range(seq_count)
    layer_flops = 2 * bins * chans * inner * 4

    def shape(*dims, dtype=jnp.bfloat16):
        return jax.ShapeDtypeStruct(dims, dtype)

    def hop(value, source, target, third=None):
        sends = {source: target, target: source}
        if third is not None and third not in sends:
            sends.update({target: third, third: source})
        route = []
        for core in range(groups):
            for stage in range(sections):
                taker = core if stage in sends else (core + 1) % groups
                for i in range(count):
                    giver = (core * sections + stage) * count + i
                    route.append((giver, (taker * sections + sends.get(stage, stage)) * count + i))
        return lax.ppermute(value, ("dp", "pipe", "ctx"), route)

    def onward(value, step):
        return lax.ppermute(value, "ctx", [(i, (i + step) % count) for i in range(count)])

    def exchange(value, offset):
        return lax.ppermute(value, "ctx", [(i, i ^ offset) for i in range(count)])

    payload = jnp.where(section == last, cotangent, inputs)
    parts = kernel_call(
        functools.partial(split_kernel, last),
        [shape(rows // count, chans)] * count,
        10 * seq_count * layer_flops,
        "split",
    )(payload)
    weight, point = kernel_call(
        hold_kernel,
        [shape(*weight.shape), shape(*point.shape)],
        0,
        "hold",
        waits=[parts[0]],
        in_spec=anywhere,
        scratch=[pltpu.SemaphoreType.DMA((2,))],
    )(weight, point)
    steps = [1, *range(count - 1, 1, -1)]
    parts = [*(onward(parts[step], step) for step in steps), parts[0]]

    trunk, inside = shape(bins, chans), shape(bins, inner)
    inside_wide = shape(bins, inner, dtype=jnp.float32)
    whole, out, pre = kernel_call(
        functools.partial(first_kernel, last, bins, [*steps, 0]),
        [shape(rows, chans), trunk, inside_wide],
        layer_flops,
        "first",
    )(*parts, weight, point)
    outs, pres, xs, sent = [out], [[pre]], [[whole]], ()
    for level in range(last):
        if level > 0:
            third = last if level > 1 else None
            xs.append([hop(out, level - 1, level, third) for out in outs])
            outs = []
            pres.append([])
        for seq in range(len(outs), seq_count):
            out, pre = kernel_call(
                functools.partial(fore_kernel, level, seq, bins),
                [trunk, inside_wide],
                layer_flops,
                "fore",
                waits=outs[-1:] or sent,
            )(xs[level][seq if level else 0], weight, point)
            outs.append(out)
            pres[level].append(pre)
        sent = outs
        if level == 1:
            back_weights = kernel_call(
                transpose_kernel,
                [shape(1, weight.shape[1], inner, chans), shape(1, chans, inner)],
                0,
                "transpose",
                waits=outs,
            )(weight, point)
            sent = [*outs, *back_weights]
    slopes = kernel_call(
        functools.partial(slope_kernel, last, seq_count, bins),
        [shape(bins, chans, dtype=jnp.float32), inside_wide] * seq_count,
        0,
        "slopes",
        waits=outs,
    )(
        *[xs[level][seq if level else 0] for level in range(last) for seq in seqs],
        *[pre for some in pres for pre in some],
    )
    sent = [*sent, *slopes]
    xs.append([hop(out, last - 1, last, 0) for out in outs])

    dys, dpres = [], [[] for level in range(sections)]
    for seq in seqs:
        dy, dpre = kernel_call(
            functools.partial(turn_kernel, last, seq, bins, scale),
            [trunk, inside],
            2 * layer_flops,
            "turn",
            waits=dys[-1:] or sent,
        )(xs[last][seq], whole, weight, *back_weights)
        dys.append(dy)
        dpres[last].append(dpre)
    bit = count // 2
    kept = list(range(bit))
    moving = [(offset, 0) for offset in range(bit, count)]
    size = chans // count
    *owned, message = kernel_call(
        functools.partial(columns_kernel, groups, [len(x) for x in xs], kept),
        [shape(size, rows)] * len(kept) + [shape(size * len(kept), rows)],
        2 * rows * chans * chans,
        "columns",
        waits=dys,
    )(*[x for some in xs for x in some])
    blocks = {(offset, 0): (array, 0) for offset, array in zip(kept, owned)}
    sent = [owned[0]]
    dys = [hop(dy, last, last - 1) for dy in dys]
    message = exchange(message, bit)
    blocks.update({(to ^ bit, start ^ bit): (message, at) for at, (to, start) in enumerate(moving)})

    for level in range(last - 1, 0, -1):
        outs = []
        for seq in seqs:
            dy, dpre = kernel_call(
                functools.partial(back_kernel, level, bins),
                [trunk, inside],
                layer_flops,
                "back",
                waits=outs[-1:] or sent,
            )(dys[seq], *slopes[2 * seq : 2 * seq + 2], *back_weights)
            outs.append(dy)
            dpres[level].append(dpre)
        sent = outs
        dys = [hop(dy, level, level - 1, None if level > 1 else last) for dy in outs]
        bit //= 2
        moving = sorted(key for key in blocks if key[0] & bit)
        if moving:
            (message,) = kernel_call(
                functools.partial(message_kernel, [blocks[key][1] for key in moving]),
                [shape(size * len(moving), rows)],
                0,
                "message",
                waits=outs,
            )(*[blocks[key][0] for key in moving])
            sent = [*outs, message]
            message = exchange(message, bit)
            for at, (to, start) in enumerate(moving):
                blocks[to ^ bit, start ^ bit] = (message, at)

    sent = [*sent, message]
    dpre = []
    for seq in seqs:
        dpre = kernel_call(
            functools.partial(head_kernel, sections, seq * bins),
            [shape((seq + 1) * bins, inner)],
            layer_flops // 4,
            "head",
            waits=dpre or sent,
        )(dys[seq], slopes[2 * seq + 1], back_weights[1], *[dpres[level][seq] for level in range(1, sections)], *dpre)
    (dpre,) = dpre
    offsets = range(1, count)
    gathered = [*(exchange(dpre, offset) for offset in offsets), dpre]
    columns = [blocks[0, offset] for offset in [*offsets, 0]]
    width = size // groups

    def gradient(step, dtype, waits=()):
        places = [at * size + step * width for array, at in columns]
        (part,) = kernel_call(
            functools.partial(grad_kernel, sections, bins, places),
            [shape(3, width, inner, dtype=dtype)],
            2 * 3 * rows * count * width * inner,
            "grad",
            waits=waits,
        )(*[array for array, at in columns], *gathered)
        return part

    others = [gradient(step, jnp.bfloat16) for step in range(1, groups)]
    mine = gradient(0, jnp.float32, waits=others)
    for step, other in enumerate(others, 1):
        route = [(i, (i + step) % groups) for i in range(groups)]
        mine = mine + lax.ppermute(other, "dp", route).astype(jnp.float32)
    return mine[None]


def solution(mesh):
    def shards(inputs, cotangent, dilated_kernel_weight, point_weight):
        bins = inputs.shape[1]
        first_spread = bins // 2 // 2 ** (mesh.shape["pipe"] - 1)
        count = mesh.shape["ctx"]
        residues = (
            first_spread == count
            and mesh.shape["pipe"] > 2
            and bins % (16 * count) == 0
            and 1 < count == 1 << (count.bit_length() - 1) <= 1 << (mesh.shape["pipe"] - 2)
            and inputs.shape[2] % (count * mesh.shape["dp"]) == 0
        )
        plan = residue_shards if residues else edge_shards
        return plan(inputs, cotangent, dilated_kernel_weight, point_weight)

    return jax.shard_map(
        shards,
        mesh=mesh,
        in_specs=(
            P("dp", "ctx", None),
            P("dp", "ctx", None),
            P("pipe", None, None, None),
            P("pipe", None, None),
        ),
        out_specs=P("pipe", None, ("dp", "ctx"), None),
        check_vma=False,
    )
```

```python
import functools
import math

import jax
import jax.numpy as jnp
from jax import lax
from jax.experimental import pallas as pl
from jax.experimental.pallas import tpu as pltpu
from jax.sharding import PartitionSpec as P

root_half = 0.7071067811865476
inv_root_two_pi = 0.3989422804014327

in_vmem = pl.BlockSpec(memory_space=pltpu.VMEM)
anywhere = pl.BlockSpec(memory_space=pl.ANY)
contract_last = (((1,), (1,)), ((), ()))
contract_first = (((0,), (0,)), ((), ()))


def gelu(value):
    return 0.5 * value * (1.0 + lax.erf(value * root_half))


def gelu_slope(value):
    return (
        0.5 * (1.0 + lax.erf(value * root_half))
        + value * jnp.exp(-0.5 * value * value) * inv_root_two_pi
    )


def padded(cells, sides, width):
    for axis, dim in sides:
        count = lax.axis_size(axis)
        ends = count - 1
        head = lax.slice_in_dim(cells, 0, width, axis=dim)
        tail = lax.slice_in_dim(cells, cells.shape[dim] - width, cells.shape[dim], axis=dim)
        cells = jnp.concatenate(
            [
                lax.ppermute(tail, axis, [(i, (i + 1) % count) for i in range(ends)]),
                cells,
                lax.ppermute(head, axis, [((i + 1) % count, i) for i in range(ends)]),
            ],
            axis=dim,
        )
    return cells


def shifted(block, axis, distance):
    devices = range(lax.axis_size(axis))
    route = [(i - distance, i) for i in devices if i - distance in devices]
    return lax.ppermute(block, axis, route)


def edge_shards(inputs, cotangent, dilated_kernel_weight, point_weight):
    sections = lax.axis_size("pipe")
    section = lax.axis_index("pipe")
    seq_count, bins, chans = inputs.shape
    reach = bins // 2
    table = jnp.array(
        [reach // 2 ** (sections - 1 - level) for level in range(sections)], jnp.int32
    )
    spread = table[section]
    dilation_weight = dilated_kernel_weight[0]
    w_point = point_weight[0]
    inner_channel_count = dilation_weight.shape[2]
    scale = 1.0 / math.sqrt(seq_count * lax.axis_size("dp") * bins * lax.axis_size("ctx"))
    ticks = jnp.arange(seq_count + sections - 1, dtype=jnp.int32)

    def conv_fore(extended):
        running_total = jnp.zeros((bins, inner_channel_count), jnp.float32)
        for kernel_offset in range(3):
            receptive_span = lax.dynamic_slice_in_dim(
                extended, reach + (kernel_offset - 1) * spread, bins, 0
            )
            running_total = running_total + jnp.dot(
                receptive_span, dilation_weight[kernel_offset], preferred_element_type=jnp.float32
            )
        return running_total

    def put(store, slot, valid, item):
        current = lax.dynamic_index_in_dim(store, slot, 0, keepdims=False)
        return lax.dynamic_update_index_in_dim(store, jnp.where(valid, item, current), slot, 0)

    kept_x = jnp.zeros(inputs.shape, jnp.bfloat16)
    kept_ext = jnp.zeros((seq_count, bins + 2 * reach, chans), jnp.bfloat16)
    kept_pre = jnp.zeros((seq_count, bins, inner_channel_count), jnp.float32)

    def fore_tick(carry, tick):
        received, store_x, store_ext, store_pre = carry
        micro = tick - section
        valid = (micro >= 0) & (micro < seq_count)
        slot = jnp.clip(micro, 0, seq_count - 1)
        first = lax.dynamic_index_in_dim(inputs, slot, 0, keepdims=False)
        trunk_in = jnp.where(section == 0, first, received)
        act = gelu(trunk_in.astype(jnp.float32)).astype(jnp.bfloat16)
        extended = padded(act, (("ctx", 0),), reach)
        pre = conv_fore(extended)
        inner = gelu(pre).astype(jnp.bfloat16)
        out = (
            trunk_in.astype(jnp.float32)
            + jnp.dot(inner, w_point, preferred_element_type=jnp.float32)
        ).astype(jnp.bfloat16)
        sent = shifted(out, "pipe", 1)
        store_x = put(store_x, slot, valid, trunk_in)
        store_ext = put(store_ext, slot, valid, extended)
        store_pre = put(store_pre, slot, valid, pre)
        return ((sent, store_x, store_ext, store_pre), None)

    start_recv = jnp.zeros((bins, chans), jnp.bfloat16)
    (unused, kept_x, kept_ext, kept_pre), unused_out = lax.scan(
        fore_tick, (start_recv, kept_x, kept_ext, kept_pre), ticks
    )

    def back_tick(carry, tick):
        received, grad = carry
        micro = tick - (sections - 1 - section)
        valid = (micro >= 0) & (micro < seq_count)
        slot = jnp.clip(micro, 0, seq_count - 1)
        last = (
            lax.dynamic_index_in_dim(cotangent, slot, 0, keepdims=False).astype(jnp.float32) * scale
        ).astype(jnp.bfloat16)
        upstream = jnp.where(section == sections - 1, last, received)
        trunk_in = lax.dynamic_index_in_dim(kept_x, slot, 0, keepdims=False)
        extended = lax.dynamic_index_in_dim(kept_ext, slot, 0, keepdims=False)
        pre = lax.dynamic_index_in_dim(kept_pre, slot, 0, keepdims=False)
        inner_grad = lax.dot_general(
            upstream, w_point, contract_last, preferred_element_type=jnp.float32
        )
        dpre = (inner_grad * gelu_slope(pre) * valid.astype(jnp.float32)).astype(jnp.bfloat16)
        dpre_ext = padded(dpre, (("ctx", 0),), reach)
        dact = jnp.zeros((bins, chans), jnp.float32)
        taps = []
        for kernel_offset in range(3):
            receptive_span = lax.dynamic_slice_in_dim(
                dpre_ext, reach - (kernel_offset - 1) * spread, bins, 0
            )
            dact = dact + lax.dot_general(
                receptive_span,
                dilation_weight[kernel_offset],
                contract_last,
                preferred_element_type=jnp.float32,
            )
            source = lax.dynamic_slice_in_dim(
                extended, reach + (kernel_offset - 1) * spread, bins, 0
            )
            taps.append(
                lax.dot_general(source, dpre, contract_first, preferred_element_type=jnp.float32)
            )
        grad = grad + jnp.stack(taps)
        back = (
            upstream.astype(jnp.float32) + dact * gelu_slope(trunk_in.astype(jnp.float32))
        ).astype(jnp.bfloat16)
        sent = shifted(back, "pipe", -1)
        return ((sent, grad), None)

    start_grad = jnp.zeros((3, chans, inner_channel_count), jnp.float32)
    (unused_back, grad), unused_seq = lax.scan(back_tick, (start_recv, start_grad), ticks)
    term = grad[None]
    return lax.psum_scatter(term, ("dp", "ctx"), scatter_dimension=2, tiled=True)


def moved(value, by, bins):
    pieces = []
    for start in range(0, value.shape[0], bins):
        piece = value[start : start + bins]
        place = lax.broadcasted_iota(jnp.int32, piece.shape, 0)
        if by > 0:
            keep = place >= by
        else:
            keep = place < bins + by
        pieces.append(jnp.where(keep, pltpu.roll(piece, by % bins, 0), 0.0))
    return jnp.concatenate(pieces, axis=0)


def fore(x, weight_ref, spread, bins):
    act = gelu(x.astype(jnp.float32)).astype(jnp.bfloat16)
    terms = [
        jnp.dot(act, weight_ref[0, tap], preferred_element_type=jnp.float32) for tap in range(3)
    ]
    return terms[1] + moved(terms[0], spread, bins) + moved(terms[2], -spread, bins)


def back_pre(dy, pre_slope, point_ref):
    inner_grad = jnp.dot(dy, point_ref[0], preferred_element_type=jnp.float32)
    return (inner_grad * pre_slope).astype(jnp.bfloat16)


def back_trunk(dy, dpre, x_slope, weight_ref, spread, bins):
    wide = dpre.astype(jnp.float32)
    spans = (
        moved(wide, -spread, bins).astype(jnp.bfloat16),
        dpre,
        moved(wide, spread, bins).astype(jnp.bfloat16),
    )
    dact = jnp.zeros(dy.shape, jnp.float32)
    for tap in range(3):
        dact = dact + jnp.dot(
            spans[tap], weight_ref[0, tap], preferred_element_type=jnp.float32
        )
    return (dy.astype(jnp.float32) + dact * x_slope).astype(jnp.bfloat16)


def of_seq(ref, seq, bins):
    if ref.shape[0] == bins:
        return ref[...]
    return ref[seq * bins : (seq + 1) * bins, :]


def split_kernel(last, payload_ref, *out_refs):
    count = len(out_refs)
    seq_count, bins, chans = payload_ref.shape
    part = bins // count
    section = lax.axis_index("pipe")
    place = lax.axis_index("ctx")

    @pl.when((section == 0) | (section == last))
    def send():
        source = payload_ref[...].reshape(seq_count * bins, chans)
        row = lax.broadcasted_iota(jnp.int32, (part, seq_count * bins), 0)
        col = lax.broadcasted_iota(jnp.int32, (part, seq_count * bins), 1)
        for hop in range(count):
            residue = lax.rem(place + hop, count)
            rows = [
                (col == seq * bins + count * row + residue).astype(jnp.float32)
                for seq in range(seq_count)
            ]
            pick = jnp.concatenate(rows, axis=0).astype(jnp.bfloat16)
            out_refs[hop][...] = jnp.dot(
                pick, source, preferred_element_type=jnp.float32
            ).astype(jnp.bfloat16)


def hold_kernel(weight_ref, point_ref, weight_out, point_out, sems):
    loads = [
        pltpu.make_async_copy(weight_ref, weight_out, sems.at[0]),
        pltpu.make_async_copy(point_ref, point_out, sems.at[1]),
    ]
    for load in loads:
        load.start()
    for load in loads:
        load.wait()


def first_kernel(last, bins, steps, *refs):
    parts, (weight_ref, point_ref, whole_ref, out_ref, pre_ref) = refs[:-5], refs[-5:]
    count = len(parts)
    section = lax.axis_index("pipe")
    place = lax.axis_index("ctx")
    part = bins // count
    seq_count = whole_ref.shape[0] // bins

    @pl.when((section == 0) | (section == last))
    def gather():
        for step, part_ref in zip(steps, parts):
            source = lax.rem(place + count - step, count)
            for seq in range(seq_count):
                at = pl.multiple_of(seq * bins + source * part, part)
                whole_ref[pl.ds(at, part), :] = part_ref[seq * part : (seq + 1) * part, :]

    @pl.when(section == 0)
    def layer():
        x = whole_ref[:bins, :]
        finish(x, fore(x, weight_ref, 1, bins), point_ref, out_ref, pre_ref)


def finish(x, pre, point_ref, out_ref, pre_ref):
    pre_ref[...] = pre
    branch = jnp.dot(
        gelu(pre).astype(jnp.bfloat16), point_ref[0], preferred_element_type=jnp.float32
    )
    out_ref[...] = (x.astype(jnp.float32) + branch).astype(jnp.bfloat16)


def fore_kernel(level, seq, bins, x_ref, weight_ref, point_ref, out_ref, pre_ref):
    @pl.when(lax.axis_index("pipe") == level)
    def layer():
        x = of_seq(x_ref, seq, bins)
        finish(x, fore(x, weight_ref, 2**level, bins), point_ref, out_ref, pre_ref)


def transpose_kernel(weight_ref, point_ref, weight_out, point_out):
    for tap in range(weight_ref.shape[1]):
        weight_out[0, tap] = weight_ref[0, tap].T
    point_out[0] = point_ref[0].T


def turn_kernel(level, seq, bins, scale, x_ref, cot_ref, weight_ref, weight_t_ref, point_t_ref, dy_ref, dpre_ref):
    @pl.when(lax.axis_index("pipe") == level)
    def layer():
        x = of_seq(x_ref, seq, bins)
        pre = fore(x, weight_ref, 2**level, bins)
        cot = of_seq(cot_ref, seq, bins)
        dy = (cot.astype(jnp.float32) * scale).astype(jnp.bfloat16)
        dpre = back_pre(dy, gelu_slope(pre), point_t_ref)
        dpre_ref[...] = dpre
        x_slope = gelu_slope(x.astype(jnp.float32))
        dy_ref[...] = back_trunk(dy, dpre, x_slope, weight_t_ref, 2**level, bins)


def slope_kernel(levels, seq_count, bins, *refs):
    xs, pres = refs[: levels * seq_count], refs[levels * seq_count : 2 * levels * seq_count]
    outs = refs[2 * levels * seq_count :]
    for level in range(levels):

        @pl.when(lax.axis_index("pipe") == level)
        def layer(level=level):
            for seq in range(seq_count):
                x = of_seq(xs[level * seq_count + seq], seq, bins)
                outs[2 * seq][...] = gelu_slope(x.astype(jnp.float32))
                outs[2 * seq + 1][...] = gelu_slope(pres[level * seq_count + seq][...])


def back_kernel(level, bins, dy_in_ref, x_slope_ref, pre_slope_ref, weight_ref, point_ref, dy_ref, dpre_ref):
    @pl.when(lax.axis_index("pipe") == level)
    def layer():
        dy = dy_in_ref[...]
        dpre = back_pre(dy, pre_slope_ref[...], point_ref)
        dpre_ref[...] = dpre
        dy_ref[...] = back_trunk(dy, dpre, x_slope_ref[...], weight_ref, 2**level, bins)


def message_kernel(places, *refs):
    blocks, message_ref = refs[:-1], refs[-1]
    size = message_ref.shape[0] // len(places)
    for to, (ref, at) in enumerate(zip(blocks, places)):
        message_ref[to * size : (to + 1) * size, :] = ref[at * size : (at + 1) * size, :]


def head_kernel(sections, dy_in_ref, slope_ref, point_ref, *refs):
    others, out_ref = refs[:-1], refs[-1]
    section = lax.axis_index("pipe")

    @pl.when(section == 0)
    def layer():
        out_ref[...] = back_pre(dy_in_ref[...], slope_ref[...], point_ref)

    for level in range(1, sections):

        @pl.when(section == level)
        def keep(level=level):
            out_ref[...] = others[level - 1][...]


def join_kernel(*refs):
    parts, whole_ref = refs[:-1], refs[-1]
    bins = parts[0].shape[0]
    for at, ref in enumerate(parts):
        whole_ref[at * bins : (at + 1) * bins, :] = ref[...]


def columns_kernel(groups, runs, kept, *refs):
    refs, (sent_ref,) = refs[:-1], refs[-1:]
    kept_refs = refs[sum(runs) :]
    count = 2 * len(kept)
    section = lax.axis_index("pipe")
    core = lax.axis_index("dp")
    place = lax.axis_index("ctx")
    x, start = None, 0
    for level, run in enumerate(runs):
        pieces = [ref[...] for ref in refs[start : start + run]]
        start += run
        whole = jnp.concatenate(pieces, axis=0).astype(jnp.float32)
        x = whole if x is None else jnp.where(section == level, whole, x)
    act = gelu(x).astype(jnp.bfloat16)
    chans = act.shape[1]
    width = chans // (groups * count)
    row = lax.broadcasted_iota(jnp.int32, (width, chans), 0)
    col = lax.broadcasted_iota(jnp.int32, (width, chans), 1)

    def block(offset):
        owner = lax.bitwise_xor(place, offset)
        rows = []
        for step in range(groups):
            first = (lax.rem(core + step, groups) * count + owner) * width
            rows.append((col == first + row).astype(jnp.float32))
        pick = jnp.concatenate(rows, axis=0).astype(jnp.bfloat16)
        return lax.dot_general(
            pick, act, contract_last, preferred_element_type=jnp.float32
        ).astype(jnp.bfloat16)

    size = groups * width
    for at, offset in enumerate(kept):
        kept_refs[at][...] = block(offset)
        sent_ref[at * size : (at + 1) * size, :] = block(offset ^ count // 2)


def grad_kernel(sections, bins, places, *refs):
    columns, refs = refs[: len(places)], refs[len(places) :]
    grads, out_ref = refs[:-1], refs[-1]
    section = lax.axis_index("pipe")
    width = out_ref.shape[1]

    def taps(spread):
        act = jnp.concatenate(
            [ref[at : at + width, :] for ref, at in zip(columns, places)], axis=1
        )
        dpre = jnp.concatenate([ref[...] for ref in grads], axis=0)
        wide = dpre.astype(jnp.float32)
        spans = (
            moved(wide, -spread, bins).astype(jnp.bfloat16),
            dpre,
            moved(wide, spread, bins).astype(jnp.bfloat16),
        )
        for tap in range(3):
            out_ref[tap] = jnp.dot(
                act, spans[tap], preferred_element_type=jnp.float32
            ).astype(out_ref.dtype)

    for level in range(sections):

        @pl.when(section == level)
        def run(level=level):
            taps(2**level)


def kernel_call(body, outs, flops, name, waits=(), carries=(), in_spec=in_vmem, scratch=()):
    def call(*args):
        used, taken = len(args), len(args) + len(waits) + len(carries)

        def run(*refs):
            made = refs[taken : taken + len(outs)]
            body(*refs[:used], *made, *refs[taken + len(outs) + len(carries) :])

        moved_bytes = sum(math.prod(a.shape) * a.dtype.itemsize for a in (*args, *outs))
        return pl.pallas_call(
            run,
            out_shape=[*outs, *(jax.ShapeDtypeStruct(a.shape, a.dtype) for a in carries)],
            in_specs=[in_spec] * used + [anywhere] * (taken - used),
            out_specs=[in_vmem] * len(outs) + [anywhere] * len(carries),
            input_output_aliases={
                used + len(waits) + at: len(outs) + at for at in range(len(carries))
            },
            scratch_shapes=list(scratch),
            compiler_params=pltpu.CompilerParams(vmem_limit_bytes=24 * 2**20),
            cost_estimate=pl.CostEstimate(
                flops=flops, bytes_accessed=moved_bytes, transcendentals=0
            ),
            name=name,
        )(*args, *waits, *carries)

    return call


def residue_shards(inputs, cotangent, weight, point):
    sections = lax.axis_size("pipe")
    section = lax.axis_index("pipe")
    count = lax.axis_size("ctx")
    groups = lax.axis_size("dp")
    seq_count, bins, chans = inputs.shape
    inner = weight.shape[3]
    rows = seq_count * bins
    scale = 1.0 / math.sqrt(seq_count * groups * bins * count)
    last = sections - 1
    seqs = range(seq_count)
    layer_flops = 2 * bins * chans * inner * 4

    def shape(*dims, dtype=jnp.bfloat16):
        return jax.ShapeDtypeStruct(dims, dtype)

    def hop(value, source, target, third=None):
        sends = {source: target, target: source}
        if third is not None and third not in sends:
            sends.update({target: third, third: source})
        route = []
        for core in range(groups):
            for stage in range(sections):
                taker = core if stage in sends else (core + 1) % groups
                for i in range(count):
                    giver = (core * sections + stage) * count + i
                    route.append((giver, (taker * sections + sends.get(stage, stage)) * count + i))
        return lax.ppermute(value, ("dp", "pipe", "ctx"), route)

    def onward(value, step):
        return lax.ppermute(value, "ctx", [(i, (i + step) % count) for i in range(count)])

    def exchange(value, offset):
        return lax.ppermute(value, "ctx", [(i, i ^ offset) for i in range(count)])

    payload = jnp.where(section == last, cotangent, inputs)
    parts = kernel_call(
        functools.partial(split_kernel, last),
        [shape(rows // count, chans)] * count,
        10 * seq_count * layer_flops,
        "split",
    )(payload)
    weight, point = kernel_call(
        hold_kernel,
        [shape(*weight.shape), shape(*point.shape)],
        0,
        "hold",
        waits=[parts[0]],
        in_spec=anywhere,
        scratch=[pltpu.SemaphoreType.DMA((2,))],
    )(weight, point)
    steps = [1, *range(count - 1, 1, -1)]
    parts = [*(onward(parts[step], step) for step in steps), parts[0]]

    trunk, inside = shape(bins, chans), shape(bins, inner)
    inside_wide = shape(bins, inner, dtype=jnp.float32)
    whole, out, pre = kernel_call(
        functools.partial(first_kernel, last, bins, [*steps, 0]),
        [shape(rows, chans), trunk, inside_wide],
        layer_flops,
        "first",
    )(*parts, weight, point)
    outs, pres, xs, sent = [out], [[pre]], [[whole]], ()
    for level in range(last):
        if level > 0:
            third = last if level > 1 else None
            xs.append([hop(out, level - 1, level, third) for out in outs])
            outs = []
            pres.append([])
        for seq in range(len(outs), seq_count):
            out, pre = kernel_call(
                functools.partial(fore_kernel, level, seq, bins),
                [trunk, inside_wide],
                layer_flops,
                "fore",
                waits=outs[-1:] or sent,
            )(xs[level][seq if level else 0], weight, point)
            outs.append(out)
            pres[level].append(pre)
        sent = outs
        if level == 1:
            back_weights = kernel_call(
                transpose_kernel,
                [shape(1, weight.shape[1], inner, chans), shape(1, chans, inner)],
                0,
                "transpose",
                waits=outs,
            )(weight, point)
            sent = [*outs, *back_weights]
    slopes = kernel_call(
        functools.partial(slope_kernel, last, seq_count, bins),
        [shape(bins, chans, dtype=jnp.float32), inside_wide] * seq_count,
        0,
        "slopes",
        waits=outs,
    )(
        *[xs[level][seq if level else 0] for level in range(last) for seq in seqs],
        *[pre for some in pres for pre in some],
    )
    sent = [*sent, *slopes]
    xs.append([hop(out, last - 1, last, 0) for out in outs])

    dys, dpres = [], [[] for level in range(sections)]
    for seq in seqs:
        dy, dpre = kernel_call(
            functools.partial(turn_kernel, last, seq, bins, scale),
            [trunk, inside],
            2 * layer_flops,
            "turn",
            waits=dys[-1:] or sent,
        )(xs[last][seq], whole, weight, *back_weights)
        dys.append(dy)
        dpres[last].append(dpre)
    bit = count // 2
    kept = list(range(bit))
    moving = [(offset, 0) for offset in range(bit, count)]
    size = chans // count
    *owned, message = kernel_call(
        functools.partial(columns_kernel, groups, [len(x) for x in xs], kept),
        [shape(size, rows)] * len(kept) + [shape(size * len(kept), rows)],
        2 * rows * chans * chans,
        "columns",
        waits=dys,
    )(*[x for some in xs for x in some])
    blocks = {(offset, 0): (array, 0) for offset, array in zip(kept, owned)}
    sent = [owned[0]]
    dys = [hop(dy, last, last - 1) for dy in dys]
    message = exchange(message, bit)
    blocks.update({(to ^ bit, start ^ bit): (message, at) for at, (to, start) in enumerate(moving)})

    for level in range(last - 1, 0, -1):
        outs = []
        for seq in seqs:
            dy, dpre = kernel_call(
                functools.partial(back_kernel, level, bins),
                [trunk, inside],
                layer_flops,
                "back",
                waits=outs[-1:] or sent,
            )(dys[seq], *slopes[2 * seq : 2 * seq + 2], *back_weights)
            outs.append(dy)
            dpres[level].append(dpre)
        sent = outs
        dys = [hop(dy, level, level - 1, None if level > 1 else last) for dy in outs]
        bit //= 2
        moving = sorted(key for key in blocks if key[0] & bit)
        if moving:
            (message,) = kernel_call(
                functools.partial(message_kernel, [blocks[key][1] for key in moving]),
                [shape(size * len(moving), rows)],
                0,
                "message",
                waits=outs,
            )(*[blocks[key][0] for key in moving])
            sent = [*outs, message]
            message = exchange(message, bit)
            for at, (to, start) in enumerate(moving):
                blocks[to ^ bit, start ^ bit] = (message, at)

    sent = [*sent, message]
    parts = []
    for seq in seqs:
        (part,) = kernel_call(
            functools.partial(head_kernel, sections),
            [inside],
            layer_flops // 4,
            "head",
            waits=parts[-1:] or sent,
        )(
            dys[seq],
            slopes[2 * seq + 1],
            back_weights[1],
            *[dpres[level][seq] for level in range(1, sections)],
        )
        parts.append(part)
    bit = count // 2
    far = [exchange(part, bit) for part in parts]
    received = {
        0: kernel_call(join_kernel, [shape(rows, inner)], 0, "join", waits=far[:1])(*parts),
        bit: far,
    }
    while bit > 1:
        bit //= 2
        received.update(
            {
                offset ^ bit: [exchange(block, bit) for block in some]
                for offset, some in received.items()
            }
        )
    offsets = [*received]
    gathered = [block for offset in offsets for block in received[offset]]
    columns = [blocks[0, offset] for offset in offsets]
    width = size // groups

    def gradient(step, dtype, waits=()):
        places = [at * size + step * width for array, at in columns]
        (part,) = kernel_call(
            functools.partial(grad_kernel, sections, bins, places),
            [shape(3, width, inner, dtype=dtype)],
            2 * 3 * rows * count * width * inner,
            "grad",
            waits=waits,
        )(*[array for array, at in columns], *gathered)
        return part

    others = [gradient(step, jnp.bfloat16) for step in range(1, groups)]
    mine = gradient(0, jnp.float32, waits=others)
    for step, other in enumerate(others, 1):
        route = [(i, (i + step) % groups) for i in range(groups)]
        mine = mine + lax.ppermute(other, "dp", route).astype(jnp.float32)
    return mine[None]


def solution(mesh):
    def shards(inputs, cotangent, dilated_kernel_weight, point_weight):
        bins = inputs.shape[1]
        first_spread = bins // 2 // 2 ** (mesh.shape["pipe"] - 1)
        count = mesh.shape["ctx"]
        residues = (
            first_spread == count
            and mesh.shape["pipe"] > 2
            and bins % (16 * count) == 0
            and 1 < count == 1 << (count.bit_length() - 1) <= 1 << (mesh.shape["pipe"] - 2)
            and inputs.shape[2] % (count * mesh.shape["dp"]) == 0
        )
        plan = residue_shards if residues else edge_shards
        return plan(inputs, cotangent, dilated_kernel_weight, point_weight)

    return jax.shard_map(
        shards,
        mesh=mesh,
        in_specs=(
            P("dp", "ctx", None),
            P("dp", "ctx", None),
            P("pipe", None, None, None),
            P("pipe", None, None),
        ),
        out_specs=P("pipe", None, ("dp", "ctx"), None),
        check_vma=False,
    )
```

```python
import functools
import math

import jax
import jax.numpy as jnp
from jax import lax
from jax.experimental import pallas as pl
from jax.experimental.pallas import tpu as pltpu
from jax.sharding import PartitionSpec as P

root_half = 0.7071067811865476
inv_root_two_pi = 0.3989422804014327

in_vmem = pl.BlockSpec(memory_space=pltpu.VMEM)
anywhere = pl.BlockSpec(memory_space=pl.ANY)
contract_last = (((1,), (1,)), ((), ()))
contract_first = (((0,), (0,)), ((), ()))


def gelu(value):
    return 0.5 * value * (1.0 + lax.erf(value * root_half))


def gelu_slope(value):
    return (
        0.5 * (1.0 + lax.erf(value * root_half))
        + value * jnp.exp(-0.5 * value * value) * inv_root_two_pi
    )


def padded(cells, sides, width):
    for axis, dim in sides:
        count = lax.axis_size(axis)
        ends = count - 1
        head = lax.slice_in_dim(cells, 0, width, axis=dim)
        tail = lax.slice_in_dim(cells, cells.shape[dim] - width, cells.shape[dim], axis=dim)
        cells = jnp.concatenate(
            [
                lax.ppermute(tail, axis, [(i, (i + 1) % count) for i in range(ends)]),
                cells,
                lax.ppermute(head, axis, [((i + 1) % count, i) for i in range(ends)]),
            ],
            axis=dim,
        )
    return cells


def shifted(block, axis, distance):
    devices = range(lax.axis_size(axis))
    route = [(i - distance, i) for i in devices if i - distance in devices]
    return lax.ppermute(block, axis, route)


def edge_shards(inputs, cotangent, dilated_kernel_weight, point_weight):
    sections = lax.axis_size("pipe")
    section = lax.axis_index("pipe")
    seq_count, bins, chans = inputs.shape
    reach = bins // 2
    table = jnp.array(
        [reach // 2 ** (sections - 1 - level) for level in range(sections)], jnp.int32
    )
    spread = table[section]
    dilation_weight = dilated_kernel_weight[0]
    w_point = point_weight[0]
    inner_channel_count = dilation_weight.shape[2]
    scale = 1.0 / math.sqrt(seq_count * lax.axis_size("dp") * bins * lax.axis_size("ctx"))
    ticks = jnp.arange(seq_count + sections - 1, dtype=jnp.int32)

    def conv_fore(extended):
        running_total = jnp.zeros((bins, inner_channel_count), jnp.float32)
        for kernel_offset in range(3):
            receptive_span = lax.dynamic_slice_in_dim(
                extended, reach + (kernel_offset - 1) * spread, bins, 0
            )
            running_total = running_total + jnp.dot(
                receptive_span, dilation_weight[kernel_offset], preferred_element_type=jnp.float32
            )
        return running_total

    def put(store, slot, valid, item):
        current = lax.dynamic_index_in_dim(store, slot, 0, keepdims=False)
        return lax.dynamic_update_index_in_dim(store, jnp.where(valid, item, current), slot, 0)

    kept_x = jnp.zeros(inputs.shape, jnp.bfloat16)
    kept_ext = jnp.zeros((seq_count, bins + 2 * reach, chans), jnp.bfloat16)
    kept_pre = jnp.zeros((seq_count, bins, inner_channel_count), jnp.float32)

    def fore_tick(carry, tick):
        received, store_x, store_ext, store_pre = carry
        micro = tick - section
        valid = (micro >= 0) & (micro < seq_count)
        slot = jnp.clip(micro, 0, seq_count - 1)
        first = lax.dynamic_index_in_dim(inputs, slot, 0, keepdims=False)
        trunk_in = jnp.where(section == 0, first, received)
        act = gelu(trunk_in.astype(jnp.float32)).astype(jnp.bfloat16)
        extended = padded(act, (("ctx", 0),), reach)
        pre = conv_fore(extended)
        inner = gelu(pre).astype(jnp.bfloat16)
        out = (
            trunk_in.astype(jnp.float32)
            + jnp.dot(inner, w_point, preferred_element_type=jnp.float32)
        ).astype(jnp.bfloat16)
        sent = shifted(out, "pipe", 1)
        store_x = put(store_x, slot, valid, trunk_in)
        store_ext = put(store_ext, slot, valid, extended)
        store_pre = put(store_pre, slot, valid, pre)
        return ((sent, store_x, store_ext, store_pre), None)

    start_recv = jnp.zeros((bins, chans), jnp.bfloat16)
    (unused, kept_x, kept_ext, kept_pre), unused_out = lax.scan(
        fore_tick, (start_recv, kept_x, kept_ext, kept_pre), ticks
    )

    def back_tick(carry, tick):
        received, grad = carry
        micro = tick - (sections - 1 - section)
        valid = (micro >= 0) & (micro < seq_count)
        slot = jnp.clip(micro, 0, seq_count - 1)
        last = (
            lax.dynamic_index_in_dim(cotangent, slot, 0, keepdims=False).astype(jnp.float32) * scale
        ).astype(jnp.bfloat16)
        upstream = jnp.where(section == sections - 1, last, received)
        trunk_in = lax.dynamic_index_in_dim(kept_x, slot, 0, keepdims=False)
        extended = lax.dynamic_index_in_dim(kept_ext, slot, 0, keepdims=False)
        pre = lax.dynamic_index_in_dim(kept_pre, slot, 0, keepdims=False)
        inner_grad = lax.dot_general(
            upstream, w_point, contract_last, preferred_element_type=jnp.float32
        )
        dpre = (inner_grad * gelu_slope(pre) * valid.astype(jnp.float32)).astype(jnp.bfloat16)
        dpre_ext = padded(dpre, (("ctx", 0),), reach)
        dact = jnp.zeros((bins, chans), jnp.float32)
        taps = []
        for kernel_offset in range(3):
            receptive_span = lax.dynamic_slice_in_dim(
                dpre_ext, reach - (kernel_offset - 1) * spread, bins, 0
            )
            dact = dact + lax.dot_general(
                receptive_span,
                dilation_weight[kernel_offset],
                contract_last,
                preferred_element_type=jnp.float32,
            )
            source = lax.dynamic_slice_in_dim(
                extended, reach + (kernel_offset - 1) * spread, bins, 0
            )
            taps.append(
                lax.dot_general(source, dpre, contract_first, preferred_element_type=jnp.float32)
            )
        grad = grad + jnp.stack(taps)
        back = (
            upstream.astype(jnp.float32) + dact * gelu_slope(trunk_in.astype(jnp.float32))
        ).astype(jnp.bfloat16)
        sent = shifted(back, "pipe", -1)
        return ((sent, grad), None)

    start_grad = jnp.zeros((3, chans, inner_channel_count), jnp.float32)
    (unused_back, grad), unused_seq = lax.scan(back_tick, (start_recv, start_grad), ticks)
    term = grad[None]
    return lax.psum_scatter(term, ("dp", "ctx"), scatter_dimension=2, tiled=True)


def moved(value, by, bins):
    pieces = []
    for start in range(0, value.shape[0], bins):
        piece = value[start : start + bins]
        place = lax.broadcasted_iota(jnp.int32, piece.shape, 0)
        if by > 0:
            keep = place >= by
        else:
            keep = place < bins + by
        pieces.append(jnp.where(keep, pltpu.roll(piece, by % bins, 0), 0.0))
    return jnp.concatenate(pieces, axis=0)


def fore(x, weight_ref, spread, bins):
    act = gelu(x.astype(jnp.float32)).astype(jnp.bfloat16)
    terms = [
        jnp.dot(act, weight_ref[0, tap], preferred_element_type=jnp.float32) for tap in range(3)
    ]
    return terms[1] + moved(terms[0], spread, bins) + moved(terms[2], -spread, bins)


def back_pre(dy, pre_slope, point_ref):
    inner_grad = jnp.dot(dy, point_ref[0], preferred_element_type=jnp.float32)
    return (inner_grad * pre_slope).astype(jnp.bfloat16)


def back_trunk(dy, dpre, x_slope, weight_ref, spread, bins):
    wide = dpre.astype(jnp.float32)
    spans = (
        moved(wide, -spread, bins).astype(jnp.bfloat16),
        dpre,
        moved(wide, spread, bins).astype(jnp.bfloat16),
    )
    dact = jnp.zeros(dy.shape, jnp.float32)
    for tap in range(3):
        dact = dact + jnp.dot(
            spans[tap], weight_ref[0, tap], preferred_element_type=jnp.float32
        )
    return (dy.astype(jnp.float32) + dact * x_slope).astype(jnp.bfloat16)


def of_seq(ref, seq, bins):
    if ref.shape[0] == bins:
        return ref[...]
    return ref[seq * bins : (seq + 1) * bins, :]


def split_kernel(last, payload_ref, *out_refs):
    count = len(out_refs)
    seq_count, bins, chans = payload_ref.shape
    part = bins // count
    section = lax.axis_index("pipe")
    place = lax.axis_index("ctx")

    @pl.when((section == 0) | (section == last))
    def send():
        source = payload_ref[...].reshape(seq_count * bins, chans)
        row = lax.broadcasted_iota(jnp.int32, (part, seq_count * bins), 0)
        col = lax.broadcasted_iota(jnp.int32, (part, seq_count * bins), 1)
        for hop in range(count):
            residue = lax.rem(place + hop, count)
            rows = [
                (col == seq * bins + count * row + residue).astype(jnp.float32)
                for seq in range(seq_count)
            ]
            pick = jnp.concatenate(rows, axis=0).astype(jnp.bfloat16)
            out_refs[hop][...] = jnp.dot(
                pick, source, preferred_element_type=jnp.float32
            ).astype(jnp.bfloat16)


def hold_kernel(weight_ref, point_ref, weight_out, point_out, sems):
    loads = [
        pltpu.make_async_copy(weight_ref, weight_out, sems.at[0]),
        pltpu.make_async_copy(point_ref, point_out, sems.at[1]),
    ]
    for load in loads:
        load.start()
    for load in loads:
        load.wait()


def first_kernel(last, bins, steps, *refs):
    parts, (weight_ref, point_ref, whole_ref, out_ref, pre_ref) = refs[:-5], refs[-5:]
    count = len(parts)
    section = lax.axis_index("pipe")
    place = lax.axis_index("ctx")
    part = bins // count
    seq_count = whole_ref.shape[0] // bins

    @pl.when((section == 0) | (section == last))
    def gather():
        for step, part_ref in zip(steps, parts):
            source = lax.rem(place + count - step, count)
            for seq in range(seq_count):
                at = pl.multiple_of(seq * bins + source * part, part)
                whole_ref[pl.ds(at, part), :] = part_ref[seq * part : (seq + 1) * part, :]

    @pl.when(section == 0)
    def layer():
        x = whole_ref[:bins, :]
        finish(x, fore(x, weight_ref, 1, bins), point_ref, out_ref, pre_ref)


def finish(x, pre, point_ref, out_ref, pre_ref):
    pre_ref[...] = pre
    branch = jnp.dot(
        gelu(pre).astype(jnp.bfloat16), point_ref[0], preferred_element_type=jnp.float32
    )
    out_ref[...] = (x.astype(jnp.float32) + branch).astype(jnp.bfloat16)


def fore_kernel(level, seq, bins, x_ref, weight_ref, point_ref, out_ref, pre_ref):
    @pl.when(lax.axis_index("pipe") == level)
    def layer():
        x = of_seq(x_ref, seq, bins)
        finish(x, fore(x, weight_ref, 2**level, bins), point_ref, out_ref, pre_ref)


def transpose_kernel(weight_ref, point_ref, weight_out, point_out):
    for tap in range(weight_ref.shape[1]):
        weight_out[0, tap] = weight_ref[0, tap].T
    point_out[0] = point_ref[0].T


def turn_kernel(level, seq, bins, scale, x_ref, cot_ref, weight_ref, weight_t_ref, point_t_ref, dy_ref, dpre_ref):
    @pl.when(lax.axis_index("pipe") == level)
    def layer():
        x = of_seq(x_ref, seq, bins)
        pre = fore(x, weight_ref, 2**level, bins)
        cot = of_seq(cot_ref, seq, bins)
        dy = (cot.astype(jnp.float32) * scale).astype(jnp.bfloat16)
        dpre = back_pre(dy, gelu_slope(pre), point_t_ref)
        dpre_ref[...] = dpre
        x_slope = gelu_slope(x.astype(jnp.float32))
        dy_ref[...] = back_trunk(dy, dpre, x_slope, weight_t_ref, 2**level, bins)


def slope_kernel(levels, seq_count, bins, *refs):
    xs, pres = refs[: levels * seq_count], refs[levels * seq_count : 2 * levels * seq_count]
    outs = refs[2 * levels * seq_count :]
    for level in range(levels):

        @pl.when(lax.axis_index("pipe") == level)
        def layer(level=level):
            for seq in range(seq_count):
                x = of_seq(xs[level * seq_count + seq], seq, bins)
                outs[2 * seq][...] = gelu_slope(x.astype(jnp.float32))
                outs[2 * seq + 1][...] = gelu_slope(pres[level * seq_count + seq][...])


def back_kernel(level, bins, dy_in_ref, x_slope_ref, pre_slope_ref, weight_ref, point_ref, dy_ref, dpre_ref):
    @pl.when(lax.axis_index("pipe") == level)
    def layer():
        dy = dy_in_ref[...]
        dpre = back_pre(dy, pre_slope_ref[...], point_ref)
        dpre_ref[...] = dpre
        dy_ref[...] = back_trunk(dy, dpre, x_slope_ref[...], weight_ref, 2**level, bins)


def message_kernel(places, *refs):
    blocks, message_ref = refs[:-1], refs[-1]
    size = message_ref.shape[0] // len(places)
    for to, (ref, at) in enumerate(zip(blocks, places)):
        message_ref[to * size : (to + 1) * size, :] = ref[at * size : (at + 1) * size, :]


def head_kernel(sections, earlier, dy_in_ref, slope_ref, point_ref, *refs):
    others, before, out_ref = refs[: sections - 1], refs[sections - 1 : -1], refs[-1]
    section = lax.axis_index("pipe")
    bins = dy_in_ref.shape[0]
    for ref in before:
        out_ref[:earlier, :] = ref[...]

    @pl.when(section == 0)
    def layer():
        out_ref[earlier : earlier + bins, :] = back_pre(dy_in_ref[...], slope_ref[...], point_ref)

    for level in range(1, sections):

        @pl.when(section == level)
        def keep(level=level):
            out_ref[earlier : earlier + bins, :] = others[level - 1][...]


def columns_kernel(groups, runs, kept, *refs):
    refs, (sent_ref,) = refs[:-1], refs[-1:]
    kept_refs = refs[sum(runs) :]
    count = 2 * len(kept)
    section = lax.axis_index("pipe")
    core = lax.axis_index("dp")
    place = lax.axis_index("ctx")
    x, start = None, 0
    for level, run in enumerate(runs):
        pieces = [ref[...] for ref in refs[start : start + run]]
        start += run
        whole = jnp.concatenate(pieces, axis=0).astype(jnp.float32)
        x = whole if x is None else jnp.where(section == level, whole, x)
    act = gelu(x).astype(jnp.bfloat16)
    chans = act.shape[1]
    width = chans // (groups * count)
    row = lax.broadcasted_iota(jnp.int32, (width, chans), 0)
    col = lax.broadcasted_iota(jnp.int32, (width, chans), 1)

    def block(offset):
        owner = lax.bitwise_xor(place, offset)
        rows = []
        for step in range(groups):
            first = (lax.rem(core + step, groups) * count + owner) * width
            rows.append((col == first + row).astype(jnp.float32))
        pick = jnp.concatenate(rows, axis=0).astype(jnp.bfloat16)
        return lax.dot_general(
            pick, act, contract_last, preferred_element_type=jnp.float32
        ).astype(jnp.bfloat16)

    size = groups * width
    for at, offset in enumerate(kept):
        kept_refs[at][...] = block(offset)
        sent_ref[at * size : (at + 1) * size, :] = block(offset ^ 1)


def grad_kernel(sections, bins, places, *refs):
    columns, refs = refs[: len(places)], refs[len(places) :]
    grads, out_ref = refs[:-1], refs[-1]
    section = lax.axis_index("pipe")
    width = out_ref.shape[1]

    def taps(spread):
        act = jnp.concatenate(
            [ref[at : at + width, :] for ref, at in zip(columns, places)], axis=1
        )
        dpre = jnp.concatenate([ref[...] for ref in grads], axis=0)
        wide = dpre.astype(jnp.float32)
        spans = (
            moved(wide, -spread, bins).astype(jnp.bfloat16),
            dpre,
            moved(wide, spread, bins).astype(jnp.bfloat16),
        )
        for tap in range(3):
            out_ref[tap] = jnp.dot(
                act, spans[tap], preferred_element_type=jnp.float32
            ).astype(out_ref.dtype)

    for level in range(sections):

        @pl.when(section == level)
        def run(level=level):
            taps(2**level)


def kernel_call(body, outs, flops, name, waits=(), carries=(), in_spec=in_vmem, scratch=()):
    def call(*args):
        used, taken = len(args), len(args) + len(waits) + len(carries)

        def run(*refs):
            made = refs[taken : taken + len(outs)]
            body(*refs[:used], *made, *refs[taken + len(outs) + len(carries) :])

        moved_bytes = sum(math.prod(a.shape) * a.dtype.itemsize for a in (*args, *outs))
        return pl.pallas_call(
            run,
            out_shape=[*outs, *(jax.ShapeDtypeStruct(a.shape, a.dtype) for a in carries)],
            in_specs=[in_spec] * used + [anywhere] * (taken - used),
            out_specs=[in_vmem] * len(outs) + [anywhere] * len(carries),
            input_output_aliases={
                used + len(waits) + at: len(outs) + at for at in range(len(carries))
            },
            scratch_shapes=list(scratch),
            compiler_params=pltpu.CompilerParams(vmem_limit_bytes=24 * 2**20),
            cost_estimate=pl.CostEstimate(
                flops=flops, bytes_accessed=moved_bytes, transcendentals=0
            ),
            name=name,
        )(*args, *waits, *carries)

    return call


def residue_shards(inputs, cotangent, weight, point):
    sections = lax.axis_size("pipe")
    section = lax.axis_index("pipe")
    count = lax.axis_size("ctx")
    groups = lax.axis_size("dp")
    seq_count, bins, chans = inputs.shape
    inner = weight.shape[3]
    rows = seq_count * bins
    scale = 1.0 / math.sqrt(seq_count * groups * bins * count)
    last = sections - 1
    seqs = range(seq_count)
    layer_flops = 2 * bins * chans * inner * 4

    def shape(*dims, dtype=jnp.bfloat16):
        return jax.ShapeDtypeStruct(dims, dtype)

    def hop(value, source, target, third=None):
        sends = {source: target, target: source}
        if third is not None and third not in sends:
            sends.update({target: third, third: source})
        route = []
        for core in range(groups):
            for stage in range(sections):
                taker = core if stage in sends else (core + 1) % groups
                for i in range(count):
                    giver = (core * sections + stage) * count + i
                    route.append((giver, (taker * sections + sends.get(stage, stage)) * count + i))
        return lax.ppermute(value, ("dp", "pipe", "ctx"), route)

    def onward(value, step):
        return lax.ppermute(value, "ctx", [(i, (i + step) % count) for i in range(count)])

    def exchange(value, offset):
        return lax.ppermute(value, "ctx", [(i, i ^ offset) for i in range(count)])

    payload = jnp.where(section == last, cotangent, inputs)
    parts = kernel_call(
        functools.partial(split_kernel, last),
        [shape(rows // count, chans)] * count,
        10 * seq_count * layer_flops,
        "split",
    )(payload)
    weight, point = kernel_call(
        hold_kernel,
        [shape(*weight.shape), shape(*point.shape)],
        0,
        "hold",
        waits=[parts[0]],
        in_spec=anywhere,
        scratch=[pltpu.SemaphoreType.DMA((2,))],
    )(weight, point)
    steps = [1, *range(count - 1, 1, -1)]
    parts = [*(onward(parts[step], step) for step in steps), parts[0]]

    trunk, inside = shape(bins, chans), shape(bins, inner)
    inside_wide = shape(bins, inner, dtype=jnp.float32)
    whole, out, pre = kernel_call(
        functools.partial(first_kernel, last, bins, [*steps, 0]),
        [shape(rows, chans), trunk, inside_wide],
        layer_flops,
        "first",
    )(*parts, weight, point)
    outs, pres, xs, sent = [out], [[pre]], [[whole]], ()
    for level in range(last):
        if level > 0:
            third = last if level > 1 else None
            xs.append([hop(out, level - 1, level, third) for out in outs])
            outs = []
            pres.append([])
        for seq in range(len(outs), seq_count):
            out, pre = kernel_call(
                functools.partial(fore_kernel, level, seq, bins),
                [trunk, inside_wide],
                layer_flops,
                "fore",
                waits=outs[-1:] or sent,
            )(xs[level][seq if level else 0], weight, point)
            outs.append(out)
            pres[level].append(pre)
        sent = outs
        if level == 1:
            back_weights = kernel_call(
                transpose_kernel,
                [shape(1, weight.shape[1], inner, chans), shape(1, chans, inner)],
                0,
                "transpose",
                waits=outs,
            )(weight, point)
            sent = [*outs, *back_weights]
    slopes = kernel_call(
        functools.partial(slope_kernel, last, seq_count, bins),
        [shape(bins, chans, dtype=jnp.float32), inside_wide] * seq_count,
        0,
        "slopes",
        waits=outs,
    )(
        *[xs[level][seq if level else 0] for level in range(last) for seq in seqs],
        *[pre for some in pres for pre in some],
    )
    sent = [*sent, *slopes]
    xs.append([hop(out, last - 1, last, 0) for out in outs])

    dys, dpres = [], [[] for level in range(sections)]
    for seq in seqs:
        dy, dpre = kernel_call(
            functools.partial(turn_kernel, last, seq, bins, scale),
            [trunk, inside],
            2 * layer_flops,
            "turn",
            waits=dys[-1:] or sent,
        )(xs[last][seq], whole, weight, *back_weights)
        dys.append(dy)
        dpres[last].append(dpre)
    kept = list(range(0, count, 2))
    moving = [(offset, 0) for offset in range(1, count, 2)]
    size = chans // count
    *owned, message = kernel_call(
        functools.partial(columns_kernel, groups, [len(x) for x in xs], kept),
        [shape(size, rows)] * len(kept) + [shape(size * len(kept), rows)],
        2 * rows * chans * chans,
        "columns",
        waits=dys,
    )(*[x for some in xs for x in some])
    blocks = {(offset, 0): (array, 0) for offset, array in zip(kept, owned)}
    sent = [owned[0]]
    dys = [hop(dy, last, last - 1) for dy in dys]
    message, bit = exchange(message, 1), 1
    blocks.update({(to ^ 1, start ^ 1): (message, at) for at, (to, start) in enumerate(moving)})

    for level in range(last - 1, 0, -1):
        outs = []
        for seq in seqs:
            dy, dpre = kernel_call(
                functools.partial(back_kernel, level, bins),
                [trunk, inside],
                layer_flops,
                "back",
                waits=outs[-1:] or sent,
            )(dys[seq], *slopes[2 * seq : 2 * seq + 2], *back_weights)
            outs.append(dy)
            dpres[level].append(dpre)
        sent = outs
        dys = [hop(dy, level, level - 1, None if level > 1 else last) for dy in outs]
        bit *= 2
        moving = sorted(key for key in blocks if key[0] & bit)
        if moving:
            (message,) = kernel_call(
                functools.partial(message_kernel, [blocks[key][1] for key in moving]),
                [shape(size * len(moving), rows)],
                0,
                "message",
                waits=outs,
            )(*[blocks[key][0] for key in moving])
            sent = [*outs, message]
            message = exchange(message, bit)
            for at, (to, start) in enumerate(moving):
                blocks[to ^ bit, start ^ bit] = (message, at)

    sent = [*sent, message]
    dpre = []
    for seq in seqs:
        dpre = kernel_call(
            functools.partial(head_kernel, sections, seq * bins),
            [shape((seq + 1) * bins, inner)],
            layer_flops // 4,
            "head",
            waits=dpre or sent,
        )(dys[seq], slopes[2 * seq + 1], back_weights[1], *[dpres[level][seq] for level in range(1, sections)], *dpre)
    (dpre,) = dpre
    received, bit = {0: dpre}, count // 2
    while bit:
        received.update({offset ^ bit: exchange(block, bit) for offset, block in received.items()})
        bit //= 2
    offsets = [*received]
    gathered = [received[offset] for offset in offsets]
    columns = [blocks[0, offset] for offset in offsets]
    width = size // groups

    def gradient(step, dtype, waits=()):
        places = [at * size + step * width for array, at in columns]
        (part,) = kernel_call(
            functools.partial(grad_kernel, sections, bins, places),
            [shape(3, width, inner, dtype=dtype)],
            2 * 3 * rows * count * width * inner,
            "grad",
            waits=waits,
        )(*[array for array, at in columns], *gathered)
        return part

    others = [gradient(step, jnp.bfloat16) for step in range(1, groups)]
    mine = gradient(0, jnp.float32, waits=others)
    for step, other in enumerate(others, 1):
        route = [(i, (i + step) % groups) for i in range(groups)]
        mine = mine + lax.ppermute(other, "dp", route).astype(jnp.float32)
    return mine[None]


def solution(mesh):
    def shards(inputs, cotangent, dilated_kernel_weight, point_weight):
        bins = inputs.shape[1]
        first_spread = bins // 2 // 2 ** (mesh.shape["pipe"] - 1)
        count = mesh.shape["ctx"]
        residues = (
            first_spread == count
            and mesh.shape["pipe"] > 2
            and bins % (16 * count) == 0
            and 1 < count == 1 << (count.bit_length() - 1) <= 1 << (mesh.shape["pipe"] - 2)
            and inputs.shape[2] % (count * mesh.shape["dp"]) == 0
        )
        plan = residue_shards if residues else edge_shards
        return plan(inputs, cotangent, dilated_kernel_weight, point_weight)

    return jax.shard_map(
        shards,
        mesh=mesh,
        in_specs=(
            P("dp", "ctx", None),
            P("dp", "ctx", None),
            P("pipe", None, None, None),
            P("pipe", None, None),
        ),
        out_specs=P("pipe", None, ("dp", "ctx"), None),
        check_vma=False,
    )
```

```python
import functools
import math

import jax
import jax.numpy as jnp
from jax import lax
from jax.experimental import pallas as pl
from jax.experimental.pallas import tpu as pltpu
from jax.sharding import PartitionSpec as P

root_half = 0.7071067811865476
inv_root_two_pi = 0.3989422804014327

in_vmem = pl.BlockSpec(memory_space=pltpu.VMEM)
anywhere = pl.BlockSpec(memory_space=pl.ANY)
contract_last = (((1,), (1,)), ((), ()))
contract_first = (((0,), (0,)), ((), ()))


def gelu(value):
    return 0.5 * value * (1.0 + lax.erf(value * root_half))


def gelu_slope(value):
    return (
        0.5 * (1.0 + lax.erf(value * root_half))
        + value * jnp.exp(-0.5 * value * value) * inv_root_two_pi
    )


def padded(cells, sides, width):
    for axis, dim in sides:
        count = lax.axis_size(axis)
        ends = count - 1
        head = lax.slice_in_dim(cells, 0, width, axis=dim)
        tail = lax.slice_in_dim(cells, cells.shape[dim] - width, cells.shape[dim], axis=dim)
        cells = jnp.concatenate(
            [
                lax.ppermute(tail, axis, [(i, (i + 1) % count) for i in range(ends)]),
                cells,
                lax.ppermute(head, axis, [((i + 1) % count, i) for i in range(ends)]),
            ],
            axis=dim,
        )
    return cells


def shifted(block, axis, distance):
    devices = range(lax.axis_size(axis))
    route = [(i - distance, i) for i in devices if i - distance in devices]
    return lax.ppermute(block, axis, route)


def edge_shards(inputs, cotangent, dilated_kernel_weight, point_weight):
    sections = lax.axis_size("pipe")
    section = lax.axis_index("pipe")
    seq_count, bins, chans = inputs.shape
    reach = bins // 2
    table = jnp.array(
        [reach // 2 ** (sections - 1 - level) for level in range(sections)], jnp.int32
    )
    spread = table[section]
    dilation_weight = dilated_kernel_weight[0]
    w_point = point_weight[0]
    inner_channel_count = dilation_weight.shape[2]
    scale = 1.0 / math.sqrt(seq_count * lax.axis_size("dp") * bins * lax.axis_size("ctx"))
    ticks = jnp.arange(seq_count + sections - 1, dtype=jnp.int32)

    def conv_fore(extended):
        running_total = jnp.zeros((bins, inner_channel_count), jnp.float32)
        for kernel_offset in range(3):
            receptive_span = lax.dynamic_slice_in_dim(
                extended, reach + (kernel_offset - 1) * spread, bins, 0
            )
            running_total = running_total + jnp.dot(
                receptive_span, dilation_weight[kernel_offset], preferred_element_type=jnp.float32
            )
        return running_total

    def put(store, slot, valid, item):
        current = lax.dynamic_index_in_dim(store, slot, 0, keepdims=False)
        return lax.dynamic_update_index_in_dim(store, jnp.where(valid, item, current), slot, 0)

    kept_x = jnp.zeros(inputs.shape, jnp.bfloat16)
    kept_ext = jnp.zeros((seq_count, bins + 2 * reach, chans), jnp.bfloat16)
    kept_pre = jnp.zeros((seq_count, bins, inner_channel_count), jnp.float32)

    def fore_tick(carry, tick):
        received, store_x, store_ext, store_pre = carry
        micro = tick - section
        valid = (micro >= 0) & (micro < seq_count)
        slot = jnp.clip(micro, 0, seq_count - 1)
        first = lax.dynamic_index_in_dim(inputs, slot, 0, keepdims=False)
        trunk_in = jnp.where(section == 0, first, received)
        act = gelu(trunk_in.astype(jnp.float32)).astype(jnp.bfloat16)
        extended = padded(act, (("ctx", 0),), reach)
        pre = conv_fore(extended)
        inner = gelu(pre).astype(jnp.bfloat16)
        out = (
            trunk_in.astype(jnp.float32)
            + jnp.dot(inner, w_point, preferred_element_type=jnp.float32)
        ).astype(jnp.bfloat16)
        sent = shifted(out, "pipe", 1)
        store_x = put(store_x, slot, valid, trunk_in)
        store_ext = put(store_ext, slot, valid, extended)
        store_pre = put(store_pre, slot, valid, pre)
        return ((sent, store_x, store_ext, store_pre), None)

    start_recv = jnp.zeros((bins, chans), jnp.bfloat16)
    (unused, kept_x, kept_ext, kept_pre), unused_out = lax.scan(
        fore_tick, (start_recv, kept_x, kept_ext, kept_pre), ticks
    )

    def back_tick(carry, tick):
        received, grad = carry
        micro = tick - (sections - 1 - section)
        valid = (micro >= 0) & (micro < seq_count)
        slot = jnp.clip(micro, 0, seq_count - 1)
        last = (
            lax.dynamic_index_in_dim(cotangent, slot, 0, keepdims=False).astype(jnp.float32) * scale
        ).astype(jnp.bfloat16)
        upstream = jnp.where(section == sections - 1, last, received)
        trunk_in = lax.dynamic_index_in_dim(kept_x, slot, 0, keepdims=False)
        extended = lax.dynamic_index_in_dim(kept_ext, slot, 0, keepdims=False)
        pre = lax.dynamic_index_in_dim(kept_pre, slot, 0, keepdims=False)
        inner_grad = lax.dot_general(
            upstream, w_point, contract_last, preferred_element_type=jnp.float32
        )
        dpre = (inner_grad * gelu_slope(pre) * valid.astype(jnp.float32)).astype(jnp.bfloat16)
        dpre_ext = padded(dpre, (("ctx", 0),), reach)
        dact = jnp.zeros((bins, chans), jnp.float32)
        taps = []
        for kernel_offset in range(3):
            receptive_span = lax.dynamic_slice_in_dim(
                dpre_ext, reach - (kernel_offset - 1) * spread, bins, 0
            )
            dact = dact + lax.dot_general(
                receptive_span,
                dilation_weight[kernel_offset],
                contract_last,
                preferred_element_type=jnp.float32,
            )
            source = lax.dynamic_slice_in_dim(
                extended, reach + (kernel_offset - 1) * spread, bins, 0
            )
            taps.append(
                lax.dot_general(source, dpre, contract_first, preferred_element_type=jnp.float32)
            )
        grad = grad + jnp.stack(taps)
        back = (
            upstream.astype(jnp.float32) + dact * gelu_slope(trunk_in.astype(jnp.float32))
        ).astype(jnp.bfloat16)
        sent = shifted(back, "pipe", -1)
        return ((sent, grad), None)

    start_grad = jnp.zeros((3, chans, inner_channel_count), jnp.float32)
    (unused_back, grad), unused_seq = lax.scan(back_tick, (start_recv, start_grad), ticks)
    term = grad[None]
    return lax.psum_scatter(term, ("dp", "ctx"), scatter_dimension=2, tiled=True)


def moved(value, by, bins):
    pieces = []
    for start in range(0, value.shape[0], bins):
        piece = value[start : start + bins]
        place = lax.broadcasted_iota(jnp.int32, piece.shape, 0)
        if by > 0:
            keep = place >= by
        else:
            keep = place < bins + by
        pieces.append(jnp.where(keep, pltpu.roll(piece, by % bins, 0), 0.0))
    return jnp.concatenate(pieces, axis=0)


def fore(x, weight_ref, spread, bins):
    act = gelu(x.astype(jnp.float32)).astype(jnp.bfloat16)
    terms = [
        jnp.dot(act, weight_ref[0, tap], preferred_element_type=jnp.float32) for tap in range(3)
    ]
    return terms[1] + moved(terms[0], spread, bins) + moved(terms[2], -spread, bins)


def back_pre(dy, pre_slope, point_ref):
    inner_grad = jnp.dot(dy, point_ref[0], preferred_element_type=jnp.float32)
    return (inner_grad * pre_slope).astype(jnp.bfloat16)


def back_trunk(dy, dpre, x_slope, weight_ref, spread, bins):
    wide = dpre.astype(jnp.float32)
    spans = (
        moved(wide, -spread, bins).astype(jnp.bfloat16),
        dpre,
        moved(wide, spread, bins).astype(jnp.bfloat16),
    )
    dact = jnp.zeros(dy.shape, jnp.float32)
    for tap in range(3):
        dact = dact + jnp.dot(
            spans[tap], weight_ref[0, tap], preferred_element_type=jnp.float32
        )
    return (dy.astype(jnp.float32) + dact * x_slope).astype(jnp.bfloat16)


def of_seq(ref, seq, bins):
    if ref.shape[0] == bins:
        return ref[...]
    return ref[seq * bins : (seq + 1) * bins, :]


def split_kernel(last, payload_ref, *out_refs):
    count = len(out_refs)
    seq_count, bins, chans = payload_ref.shape
    part = bins // count
    section = lax.axis_index("pipe")
    place = lax.axis_index("ctx")

    @pl.when((section == 0) | (section == last))
    def send():
        source = payload_ref[...].reshape(seq_count * bins, chans)
        row = lax.broadcasted_iota(jnp.int32, (part, seq_count * bins), 0)
        col = lax.broadcasted_iota(jnp.int32, (part, seq_count * bins), 1)
        for hop in range(count):
            residue = lax.rem(place + hop, count)
            rows = [
                (col == seq * bins + count * row + residue).astype(jnp.float32)
                for seq in range(seq_count)
            ]
            pick = jnp.concatenate(rows, axis=0).astype(jnp.bfloat16)
            out_refs[hop][...] = jnp.dot(
                pick, source, preferred_element_type=jnp.float32
            ).astype(jnp.bfloat16)


def hold_kernel(weight_ref, point_ref, weight_out, point_out, sems):
    loads = [
        pltpu.make_async_copy(weight_ref, weight_out, sems.at[0]),
        pltpu.make_async_copy(point_ref, point_out, sems.at[1]),
    ]
    for load in loads:
        load.start()
    for load in loads:
        load.wait()


def first_kernel(last, bins, steps, *refs):
    parts, (weight_ref, point_ref, whole_ref, out_ref, pre_ref) = refs[:-5], refs[-5:]
    count = len(parts)
    section = lax.axis_index("pipe")
    place = lax.axis_index("ctx")
    part = bins // count
    seq_count = whole_ref.shape[0] // bins

    @pl.when((section == 0) | (section == last))
    def gather():
        for step, part_ref in zip(steps, parts):
            source = lax.rem(place + count - step, count)
            for seq in range(seq_count):
                at = pl.multiple_of(seq * bins + source * part, part)
                whole_ref[pl.ds(at, part), :] = part_ref[seq * part : (seq + 1) * part, :]

    @pl.when(section == 0)
    def layer():
        x = whole_ref[:bins, :]
        finish(x, fore(x, weight_ref, 1, bins), point_ref, out_ref, pre_ref)


def finish(x, pre, point_ref, out_ref, pre_ref):
    pre_ref[...] = pre
    branch = jnp.dot(
        gelu(pre).astype(jnp.bfloat16), point_ref[0], preferred_element_type=jnp.float32
    )
    out_ref[...] = (x.astype(jnp.float32) + branch).astype(jnp.bfloat16)


def fore_kernel(level, seq, bins, x_ref, weight_ref, point_ref, out_ref, pre_ref):
    @pl.when(lax.axis_index("pipe") == level)
    def layer():
        x = of_seq(x_ref, seq, bins)
        finish(x, fore(x, weight_ref, 2**level, bins), point_ref, out_ref, pre_ref)


def transpose_kernel(weight_ref, point_ref, weight_out, point_out):
    for tap in range(weight_ref.shape[1]):
        weight_out[0, tap] = weight_ref[0, tap].T
    point_out[0] = point_ref[0].T


def turn_kernel(level, seq, bins, scale, x_ref, cot_ref, weight_ref, weight_t_ref, point_t_ref, dy_ref, dpre_ref):
    @pl.when(lax.axis_index("pipe") == level)
    def layer():
        x = of_seq(x_ref, seq, bins)
        pre = fore(x, weight_ref, 2**level, bins)
        cot = of_seq(cot_ref, seq, bins)
        dy = (cot.astype(jnp.float32) * scale).astype(jnp.bfloat16)
        dpre = back_pre(dy, gelu_slope(pre), point_t_ref)
        dpre_ref[...] = dpre
        x_slope = gelu_slope(x.astype(jnp.float32))
        dy_ref[...] = back_trunk(dy, dpre, x_slope, weight_t_ref, 2**level, bins)


def slope_kernel(levels, seq_count, bins, *refs):
    xs, pres = refs[: levels * seq_count], refs[levels * seq_count : 2 * levels * seq_count]
    outs = refs[2 * levels * seq_count :]
    for level in range(levels):

        @pl.when(lax.axis_index("pipe") == level)
        def layer(level=level):
            for seq in range(seq_count):
                x = of_seq(xs[level * seq_count + seq], seq, bins)
                outs[2 * seq][...] = gelu_slope(x.astype(jnp.float32))
                outs[2 * seq + 1][...] = gelu_slope(pres[level * seq_count + seq][...])


def back_kernel(level, bins, dy_in_ref, x_slope_ref, pre_slope_ref, weight_ref, point_ref, dy_ref, dpre_ref):
    @pl.when(lax.axis_index("pipe") == level)
    def layer():
        dy = dy_in_ref[...]
        dpre = back_pre(dy, pre_slope_ref[...], point_ref)
        dpre_ref[...] = dpre
        dy_ref[...] = back_trunk(dy, dpre, x_slope_ref[...], weight_ref, 2**level, bins)


def message_kernel(places, *refs):
    blocks, message_ref = refs[:-1], refs[-1]
    size = message_ref.shape[0] // len(places)
    for to, (ref, at) in enumerate(zip(blocks, places)):
        message_ref[to * size : (to + 1) * size, :] = ref[at * size : (at + 1) * size, :]


def head_kernel(sections, earlier, dy_in_ref, slope_ref, point_ref, *refs):
    others, before, out_ref = refs[: sections - 1], refs[sections - 1 : -1], refs[-1]
    section = lax.axis_index("pipe")
    bins = dy_in_ref.shape[0]
    for ref in before:
        out_ref[:earlier, :] = ref[...]

    @pl.when(section == 0)
    def layer():
        out_ref[earlier : earlier + bins, :] = back_pre(dy_in_ref[...], slope_ref[...], point_ref)

    for level in range(1, sections):

        @pl.when(section == level)
        def keep(level=level):
            out_ref[earlier : earlier + bins, :] = others[level - 1][...]


def columns_kernel(groups, runs, kept, *refs):
    refs, (sent_ref,) = refs[:-1], refs[-1:]
    kept_refs = refs[sum(runs) :]
    count = 2 * len(kept)
    section = lax.axis_index("pipe")
    core = lax.axis_index("dp")
    place = lax.axis_index("ctx")
    x, start = None, 0
    for level, run in enumerate(runs):
        pieces = [ref[...] for ref in refs[start : start + run]]
        start += run
        whole = jnp.concatenate(pieces, axis=0).astype(jnp.float32)
        x = whole if x is None else jnp.where(section == level, whole, x)
    act = gelu(x).astype(jnp.bfloat16)
    chans = act.shape[1]
    width = chans // (groups * count)
    row = lax.broadcasted_iota(jnp.int32, (width, chans), 0)
    col = lax.broadcasted_iota(jnp.int32, (width, chans), 1)

    def block(offset):
        owner = lax.bitwise_xor(place, offset)
        rows = []
        for step in range(groups):
            first = (lax.rem(core + step, groups) * count + owner) * width
            rows.append((col == first + row).astype(jnp.float32))
        pick = jnp.concatenate(rows, axis=0).astype(jnp.bfloat16)
        return lax.dot_general(
            pick, act, contract_last, preferred_element_type=jnp.float32
        ).astype(jnp.bfloat16)

    size = groups * width
    for at, offset in enumerate(kept):
        kept_refs[at][...] = block(offset)
        sent_ref[at * size : (at + 1) * size, :] = block(offset ^ 1)


def grad_kernel(sections, bins, places, *refs):
    columns, refs = refs[: len(places)], refs[len(places) :]
    grads, out_ref = refs[:-1], refs[-1]
    section = lax.axis_index("pipe")
    width = out_ref.shape[1]

    def taps(spread):
        act = jnp.concatenate(
            [ref[at : at + width, :] for ref, at in zip(columns, places)], axis=1
        )
        dpre = jnp.concatenate([ref[...] for ref in grads], axis=0)
        wide = dpre.astype(jnp.float32)
        spans = (
            moved(wide, -spread, bins).astype(jnp.bfloat16),
            dpre,
            moved(wide, spread, bins).astype(jnp.bfloat16),
        )
        for tap in range(3):
            out_ref[tap] = jnp.dot(
                act, spans[tap], preferred_element_type=jnp.float32
            ).astype(out_ref.dtype)

    for level in range(sections):

        @pl.when(section == level)
        def run(level=level):
            taps(2**level)


def kernel_call(body, outs, flops, name, waits=(), carries=(), in_spec=in_vmem, scratch=()):
    def call(*args):
        used, taken = len(args), len(args) + len(waits) + len(carries)

        def run(*refs):
            made = refs[taken : taken + len(outs)]
            body(*refs[:used], *made, *refs[taken + len(outs) + len(carries) :])

        moved_bytes = sum(math.prod(a.shape) * a.dtype.itemsize for a in (*args, *outs))
        return pl.pallas_call(
            run,
            out_shape=[*outs, *(jax.ShapeDtypeStruct(a.shape, a.dtype) for a in carries)],
            in_specs=[in_spec] * used + [anywhere] * (taken - used),
            out_specs=[in_vmem] * len(outs) + [anywhere] * len(carries),
            input_output_aliases={
                used + len(waits) + at: len(outs) + at for at in range(len(carries))
            },
            scratch_shapes=list(scratch),
            compiler_params=pltpu.CompilerParams(vmem_limit_bytes=24 * 2**20),
            cost_estimate=pl.CostEstimate(
                flops=flops, bytes_accessed=moved_bytes, transcendentals=0
            ),
            name=name,
        )(*args, *waits, *carries)

    return call


def residue_shards(inputs, cotangent, weight, point):
    sections = lax.axis_size("pipe")
    section = lax.axis_index("pipe")
    count = lax.axis_size("ctx")
    groups = lax.axis_size("dp")
    seq_count, bins, chans = inputs.shape
    inner = weight.shape[3]
    rows = seq_count * bins
    scale = 1.0 / math.sqrt(seq_count * groups * bins * count)
    last = sections - 1
    seqs = range(seq_count)
    layer_flops = 2 * bins * chans * inner * 4

    def shape(*dims, dtype=jnp.bfloat16):
        return jax.ShapeDtypeStruct(dims, dtype)

    def hop(value, source, target, third=None):
        sends = {source: target, target: source}
        if third is not None and third not in sends:
            sends.update({target: third, third: source})
        route = []
        for core in range(groups):
            for stage in range(sections):
                taker = core if stage in sends else (core + 1) % groups
                for i in range(count):
                    giver = (core * sections + stage) * count + i
                    route.append((giver, (taker * sections + sends.get(stage, stage)) * count + i))
        return lax.ppermute(value, ("dp", "pipe", "ctx"), route)

    def onward(value, step):
        return lax.ppermute(value, "ctx", [(i, (i + step) % count) for i in range(count)])

    def exchange(value, offset):
        return lax.ppermute(value, "ctx", [(i, i ^ offset) for i in range(count)])

    payload = jnp.where(section == last, cotangent, inputs)
    parts = kernel_call(
        functools.partial(split_kernel, last),
        [shape(rows // count, chans)] * count,
        10 * seq_count * layer_flops,
        "split",
    )(payload)
    weight, point = kernel_call(
        hold_kernel,
        [shape(*weight.shape), shape(*point.shape)],
        0,
        "hold",
        waits=[parts[0]],
        in_spec=anywhere,
        scratch=[pltpu.SemaphoreType.DMA((2,))],
    )(weight, point)
    steps = [1, *range(count - 1, 1, -1)]
    parts = [*(onward(parts[step], step) for step in steps), parts[0]]

    trunk, inside = shape(bins, chans), shape(bins, inner)
    inside_wide = shape(bins, inner, dtype=jnp.float32)
    whole, out, pre = kernel_call(
        functools.partial(first_kernel, last, bins, [*steps, 0]),
        [shape(rows, chans), trunk, inside_wide],
        layer_flops,
        "first",
    )(*parts, weight, point)
    outs, pres, xs, sent = [out], [[pre]], [[whole]], ()
    for level in range(last):
        if level > 0:
            third = last if level > 1 else None
            xs.append([hop(out, level - 1, level, third) for out in outs])
            outs = []
            pres.append([])
        for seq in range(len(outs), seq_count):
            out, pre = kernel_call(
                functools.partial(fore_kernel, level, seq, bins),
                [trunk, inside_wide],
                layer_flops,
                "fore",
                waits=outs[-1:] or sent,
            )(xs[level][seq if level else 0], weight, point)
            outs.append(out)
            pres[level].append(pre)
        sent = outs
        if level == 1:
            back_weights = kernel_call(
                transpose_kernel,
                [shape(1, weight.shape[1], inner, chans), shape(1, chans, inner)],
                0,
                "transpose",
                waits=outs,
            )(weight, point)
            sent = [*outs, *back_weights]
    slopes = kernel_call(
        functools.partial(slope_kernel, last, seq_count, bins),
        [shape(bins, chans, dtype=jnp.float32), inside_wide] * seq_count,
        0,
        "slopes",
        waits=outs,
    )(
        *[xs[level][seq if level else 0] for level in range(last) for seq in seqs],
        *[pre for some in pres for pre in some],
    )
    sent = [*sent, *slopes]
    xs.append([hop(out, last - 1, last, 0) for out in outs])

    dys, dpres = [], [[] for level in range(sections)]
    for seq in seqs:
        dy, dpre = kernel_call(
            functools.partial(turn_kernel, last, seq, bins, scale),
            [trunk, inside],
            2 * layer_flops,
            "turn",
            waits=dys[-1:] or sent,
        )(xs[last][seq], whole, weight, *back_weights)
        dys.append(dy)
        dpres[last].append(dpre)
    kept = list(range(0, count, 2))
    moving = [(offset, 0) for offset in range(1, count, 2)]
    size = chans // count
    *owned, message = kernel_call(
        functools.partial(columns_kernel, groups, [len(x) for x in xs], kept),
        [shape(size, rows)] * len(kept) + [shape(size * len(kept), rows)],
        2 * rows * chans * chans,
        "columns",
        waits=dys,
    )(*[x for some in xs for x in some])
    blocks = {(offset, 0): (array, 0) for offset, array in zip(kept, owned)}
    sent = [owned[0]]
    dys = [hop(dy, last, last - 1) for dy in dys]
    message, bit = exchange(message, 1), 1
    blocks.update({(to ^ 1, start ^ 1): (message, at) for at, (to, start) in enumerate(moving)})

    for level in range(last - 1, 0, -1):
        outs = []
        for seq in seqs:
            dy, dpre = kernel_call(
                functools.partial(back_kernel, level, bins),
                [trunk, inside],
                layer_flops,
                "back",
                waits=outs[-1:] or sent,
            )(dys[seq], *slopes[2 * seq : 2 * seq + 2], *back_weights)
            outs.append(dy)
            dpres[level].append(dpre)
        sent = outs
        dys = [hop(dy, level, level - 1, 0 if level > 1 else last) for dy in outs]
        bit *= 2
        moving = sorted(key for key in blocks if key[0] & bit)
        if moving:
            (message,) = kernel_call(
                functools.partial(message_kernel, [blocks[key][1] for key in moving]),
                [shape(size * len(moving), rows)],
                0,
                "message",
                waits=outs,
            )(*[blocks[key][0] for key in moving])
            sent = [*outs, message]
            message = exchange(message, bit)
            for at, (to, start) in enumerate(moving):
                blocks[to ^ bit, start ^ bit] = (message, at)

    sent = [*sent, message]
    dpre = []
    for seq in seqs:
        dpre = kernel_call(
            functools.partial(head_kernel, sections, seq * bins),
            [shape((seq + 1) * bins, inner)],
            layer_flops // 4,
            "head",
            waits=dpre or sent,
        )(dys[seq], slopes[2 * seq + 1], back_weights[1], *[dpres[level][seq] for level in range(1, sections)], *dpre)
    (dpre,) = dpre
    received, bit = {0: dpre}, count // 2
    while bit:
        received.update({offset ^ bit: exchange(block, bit) for offset, block in received.items()})
        bit //= 2
    offsets = [*received]
    gathered = [received[offset] for offset in offsets]
    columns = [blocks[0, offset] for offset in offsets]
    width = size // groups

    def gradient(step, dtype, waits=()):
        places = [at * size + step * width for array, at in columns]
        (part,) = kernel_call(
            functools.partial(grad_kernel, sections, bins, places),
            [shape(3, width, inner, dtype=dtype)],
            2 * 3 * rows * count * width * inner,
            "grad",
            waits=waits,
        )(*[array for array, at in columns], *gathered)
        return part

    others = [gradient(step, jnp.bfloat16) for step in range(1, groups)]
    mine = gradient(0, jnp.float32, waits=others)
    for step, other in enumerate(others, 1):
        route = [(i, (i + step) % groups) for i in range(groups)]
        mine = mine + lax.ppermute(other, "dp", route).astype(jnp.float32)
    return mine[None]


def solution(mesh):
    def shards(inputs, cotangent, dilated_kernel_weight, point_weight):
        bins = inputs.shape[1]
        first_spread = bins // 2 // 2 ** (mesh.shape["pipe"] - 1)
        count = mesh.shape["ctx"]
        residues = (
            first_spread == count
            and mesh.shape["pipe"] > 2
            and bins % (16 * count) == 0
            and 1 < count == 1 << (count.bit_length() - 1) <= 1 << (mesh.shape["pipe"] - 2)
            and inputs.shape[2] % (count * mesh.shape["dp"]) == 0
        )
        plan = residue_shards if residues else edge_shards
        return plan(inputs, cotangent, dilated_kernel_weight, point_weight)

    return jax.shard_map(
        shards,
        mesh=mesh,
        in_specs=(
            P("dp", "ctx", None),
            P("dp", "ctx", None),
            P("pipe", None, None, None),
            P("pipe", None, None),
        ),
        out_specs=P("pipe", None, ("dp", "ctx"), None),
        check_vma=False,
    )
```

```python
import functools
import math

import jax
import jax.numpy as jnp
from jax import lax
from jax.experimental import pallas as pl
from jax.experimental.pallas import tpu as pltpu
from jax.sharding import PartitionSpec as P

root_half = 0.7071067811865476
inv_root_two_pi = 0.3989422804014327

in_vmem = pl.BlockSpec(memory_space=pltpu.VMEM)
anywhere = pl.BlockSpec(memory_space=pl.ANY)
contract_last = (((1,), (1,)), ((), ()))
contract_first = (((0,), (0,)), ((), ()))


def gelu(value):
    return 0.5 * value * (1.0 + lax.erf(value * root_half))


def gelu_slope(value):
    return (
        0.5 * (1.0 + lax.erf(value * root_half))
        + value * jnp.exp(-0.5 * value * value) * inv_root_two_pi
    )


def padded(cells, sides, width):
    for axis, dim in sides:
        count = lax.axis_size(axis)
        ends = count - 1
        head = lax.slice_in_dim(cells, 0, width, axis=dim)
        tail = lax.slice_in_dim(cells, cells.shape[dim] - width, cells.shape[dim], axis=dim)
        cells = jnp.concatenate(
            [
                lax.ppermute(tail, axis, [(i, (i + 1) % count) for i in range(ends)]),
                cells,
                lax.ppermute(head, axis, [((i + 1) % count, i) for i in range(ends)]),
            ],
            axis=dim,
        )
    return cells


def shifted(block, axis, distance):
    devices = range(lax.axis_size(axis))
    route = [(i - distance, i) for i in devices if i - distance in devices]
    return lax.ppermute(block, axis, route)


def edge_shards(inputs, cotangent, dilated_kernel_weight, point_weight):
    sections = lax.axis_size("pipe")
    section = lax.axis_index("pipe")
    seq_count, bins, chans = inputs.shape
    reach = bins // 2
    table = jnp.array(
        [reach // 2 ** (sections - 1 - level) for level in range(sections)], jnp.int32
    )
    spread = table[section]
    dilation_weight = dilated_kernel_weight[0]
    w_point = point_weight[0]
    inner_channel_count = dilation_weight.shape[2]
    scale = 1.0 / math.sqrt(seq_count * lax.axis_size("dp") * bins * lax.axis_size("ctx"))
    ticks = jnp.arange(seq_count + sections - 1, dtype=jnp.int32)

    def conv_fore(extended):
        running_total = jnp.zeros((bins, inner_channel_count), jnp.float32)
        for kernel_offset in range(3):
            receptive_span = lax.dynamic_slice_in_dim(
                extended, reach + (kernel_offset - 1) * spread, bins, 0
            )
            running_total = running_total + jnp.dot(
                receptive_span, dilation_weight[kernel_offset], preferred_element_type=jnp.float32
            )
        return running_total

    def put(store, slot, valid, item):
        current = lax.dynamic_index_in_dim(store, slot, 0, keepdims=False)
        return lax.dynamic_update_index_in_dim(store, jnp.where(valid, item, current), slot, 0)

    kept_x = jnp.zeros(inputs.shape, jnp.bfloat16)
    kept_ext = jnp.zeros((seq_count, bins + 2 * reach, chans), jnp.bfloat16)
    kept_pre = jnp.zeros((seq_count, bins, inner_channel_count), jnp.float32)

    def fore_tick(carry, tick):
        received, store_x, store_ext, store_pre = carry
        micro = tick - section
        valid = (micro >= 0) & (micro < seq_count)
        slot = jnp.clip(micro, 0, seq_count - 1)
        first = lax.dynamic_index_in_dim(inputs, slot, 0, keepdims=False)
        trunk_in = jnp.where(section == 0, first, received)
        act = gelu(trunk_in.astype(jnp.float32)).astype(jnp.bfloat16)
        extended = padded(act, (("ctx", 0),), reach)
        pre = conv_fore(extended)
        inner = gelu(pre).astype(jnp.bfloat16)
        out = (
            trunk_in.astype(jnp.float32)
            + jnp.dot(inner, w_point, preferred_element_type=jnp.float32)
        ).astype(jnp.bfloat16)
        sent = shifted(out, "pipe", 1)
        store_x = put(store_x, slot, valid, trunk_in)
        store_ext = put(store_ext, slot, valid, extended)
        store_pre = put(store_pre, slot, valid, pre)
        return ((sent, store_x, store_ext, store_pre), None)

    start_recv = jnp.zeros((bins, chans), jnp.bfloat16)
    (unused, kept_x, kept_ext, kept_pre), unused_out = lax.scan(
        fore_tick, (start_recv, kept_x, kept_ext, kept_pre), ticks
    )

    def back_tick(carry, tick):
        received, grad = carry
        micro = tick - (sections - 1 - section)
        valid = (micro >= 0) & (micro < seq_count)
        slot = jnp.clip(micro, 0, seq_count - 1)
        last = (
            lax.dynamic_index_in_dim(cotangent, slot, 0, keepdims=False).astype(jnp.float32) * scale
        ).astype(jnp.bfloat16)
        upstream = jnp.where(section == sections - 1, last, received)
        trunk_in = lax.dynamic_index_in_dim(kept_x, slot, 0, keepdims=False)
        extended = lax.dynamic_index_in_dim(kept_ext, slot, 0, keepdims=False)
        pre = lax.dynamic_index_in_dim(kept_pre, slot, 0, keepdims=False)
        inner_grad = lax.dot_general(
            upstream, w_point, contract_last, preferred_element_type=jnp.float32
        )
        dpre = (inner_grad * gelu_slope(pre) * valid.astype(jnp.float32)).astype(jnp.bfloat16)
        dpre_ext = padded(dpre, (("ctx", 0),), reach)
        dact = jnp.zeros((bins, chans), jnp.float32)
        taps = []
        for kernel_offset in range(3):
            receptive_span = lax.dynamic_slice_in_dim(
                dpre_ext, reach - (kernel_offset - 1) * spread, bins, 0
            )
            dact = dact + lax.dot_general(
                receptive_span,
                dilation_weight[kernel_offset],
                contract_last,
                preferred_element_type=jnp.float32,
            )
            source = lax.dynamic_slice_in_dim(
                extended, reach + (kernel_offset - 1) * spread, bins, 0
            )
            taps.append(
                lax.dot_general(source, dpre, contract_first, preferred_element_type=jnp.float32)
            )
        grad = grad + jnp.stack(taps)
        back = (
            upstream.astype(jnp.float32) + dact * gelu_slope(trunk_in.astype(jnp.float32))
        ).astype(jnp.bfloat16)
        sent = shifted(back, "pipe", -1)
        return ((sent, grad), None)

    start_grad = jnp.zeros((3, chans, inner_channel_count), jnp.float32)
    (unused_back, grad), unused_seq = lax.scan(back_tick, (start_recv, start_grad), ticks)
    term = grad[None]
    return lax.psum_scatter(term, ("dp", "ctx"), scatter_dimension=2, tiled=True)


def moved(value, by, bins):
    pieces = []
    for start in range(0, value.shape[0], bins):
        piece = value[start : start + bins]
        place = lax.broadcasted_iota(jnp.int32, piece.shape, 0)
        if by > 0:
            keep = place >= by
        else:
            keep = place < bins + by
        pieces.append(jnp.where(keep, pltpu.roll(piece, by % bins, 0), 0.0))
    return jnp.concatenate(pieces, axis=0)


def fore(x, weight_ref, spread, bins):
    act = gelu(x.astype(jnp.float32)).astype(jnp.bfloat16)
    terms = [
        jnp.dot(act, weight_ref[0, tap], preferred_element_type=jnp.float32) for tap in range(3)
    ]
    return terms[1] + moved(terms[0], spread, bins) + moved(terms[2], -spread, bins)


def back_pre(dy, pre_slope, point_ref):
    inner_grad = jnp.dot(dy, point_ref[0], preferred_element_type=jnp.float32)
    return (inner_grad * pre_slope).astype(jnp.bfloat16)


def back_trunk(dy, dpre, x_slope, weight_ref, spread, bins):
    wide = dpre.astype(jnp.float32)
    spans = (
        moved(wide, -spread, bins).astype(jnp.bfloat16),
        dpre,
        moved(wide, spread, bins).astype(jnp.bfloat16),
    )
    dact = jnp.zeros(dy.shape, jnp.float32)
    for tap in range(3):
        dact = dact + jnp.dot(
            spans[tap], weight_ref[0, tap], preferred_element_type=jnp.float32
        )
    return (dy.astype(jnp.float32) + dact * x_slope).astype(jnp.bfloat16)


def of_seq(ref, seq, bins):
    if ref.shape[0] == bins:
        return ref[...]
    return ref[seq * bins : (seq + 1) * bins, :]


def split_kernel(last, payload_ref, *out_refs):
    count = len(out_refs)
    seq_count, bins, chans = payload_ref.shape
    part = bins // count
    section = lax.axis_index("pipe")
    place = lax.axis_index("ctx")

    @pl.when((section == 0) | (section == last))
    def send():
        source = payload_ref[...].reshape(seq_count * bins, chans)
        row = lax.broadcasted_iota(jnp.int32, (part, seq_count * bins), 0)
        col = lax.broadcasted_iota(jnp.int32, (part, seq_count * bins), 1)
        for hop in range(count):
            residue = lax.rem(place + hop, count)
            rows = [
                (col == seq * bins + count * row + residue).astype(jnp.float32)
                for seq in range(seq_count)
            ]
            pick = jnp.concatenate(rows, axis=0).astype(jnp.bfloat16)
            out_refs[hop][...] = jnp.dot(
                pick, source, preferred_element_type=jnp.float32
            ).astype(jnp.bfloat16)


def hold_kernel(weight_ref, point_ref, weight_out, point_out, sems):
    loads = [
        pltpu.make_async_copy(weight_ref, weight_out, sems.at[0]),
        pltpu.make_async_copy(point_ref, point_out, sems.at[1]),
    ]
    for load in loads:
        load.start()
    for load in loads:
        load.wait()


def first_kernel(last, bins, steps, *refs):
    parts, (weight_ref, point_ref, whole_ref, out_ref, pre_ref) = refs[:-5], refs[-5:]
    count = len(parts)
    section = lax.axis_index("pipe")
    place = lax.axis_index("ctx")
    part = bins // count
    seq_count = whole_ref.shape[0] // bins

    @pl.when((section == 0) | (section == last))
    def gather():
        for step, part_ref in zip(steps, parts):
            source = lax.rem(place + count - step, count)
            for seq in range(seq_count):
                at = pl.multiple_of(seq * bins + source * part, part)
                whole_ref[pl.ds(at, part), :] = part_ref[seq * part : (seq + 1) * part, :]

    @pl.when(section == 0)
    def layer():
        x = whole_ref[:bins, :]
        finish(x, fore(x, weight_ref, 1, bins), point_ref, out_ref, pre_ref)


def finish(x, pre, point_ref, out_ref, pre_ref):
    pre_ref[...] = pre
    branch = jnp.dot(
        gelu(pre).astype(jnp.bfloat16), point_ref[0], preferred_element_type=jnp.float32
    )
    out_ref[...] = (x.astype(jnp.float32) + branch).astype(jnp.bfloat16)


def fore_kernel(level, seq, bins, x_ref, weight_ref, point_ref, out_ref, pre_ref):
    @pl.when(lax.axis_index("pipe") == level)
    def layer():
        x = of_seq(x_ref, seq, bins)
        finish(x, fore(x, weight_ref, 2**level, bins), point_ref, out_ref, pre_ref)


def transpose_kernel(weight_ref, point_ref, weight_out, point_out):
    for tap in range(weight_ref.shape[1]):
        weight_out[0, tap] = weight_ref[0, tap].T
    point_out[0] = point_ref[0].T


def turn_kernel(level, seq, bins, scale, x_ref, cot_ref, weight_ref, weight_t_ref, point_t_ref, dy_ref, dpre_ref):
    @pl.when(lax.axis_index("pipe") == level)
    def layer():
        x = of_seq(x_ref, seq, bins)
        pre = fore(x, weight_ref, 2**level, bins)
        cot = of_seq(cot_ref, seq, bins)
        dy = (cot.astype(jnp.float32) * scale).astype(jnp.bfloat16)
        dpre = back_pre(dy, gelu_slope(pre), point_t_ref)
        dpre_ref[...] = dpre
        x_slope = gelu_slope(x.astype(jnp.float32))
        dy_ref[...] = back_trunk(dy, dpre, x_slope, weight_t_ref, 2**level, bins)


def slope_kernel(levels, seq_count, bins, *refs):
    xs, pres = refs[: levels * seq_count], refs[levels * seq_count : 2 * levels * seq_count]
    outs = refs[2 * levels * seq_count :]
    for level in range(levels):

        @pl.when(lax.axis_index("pipe") == level)
        def layer(level=level):
            for seq in range(seq_count):
                x = of_seq(xs[level * seq_count + seq], seq, bins)
                outs[2 * seq][...] = gelu_slope(x.astype(jnp.float32))
                outs[2 * seq + 1][...] = gelu_slope(pres[level * seq_count + seq][...])


def back_kernel(level, bins, dy_in_ref, x_slope_ref, pre_slope_ref, weight_ref, point_ref, dy_ref, dpre_ref):
    @pl.when(lax.axis_index("pipe") == level)
    def layer():
        dy = dy_in_ref[...]
        dpre = back_pre(dy, pre_slope_ref[...], point_ref)
        dpre_ref[...] = dpre
        dy_ref[...] = back_trunk(dy, dpre, x_slope_ref[...], weight_ref, 2**level, bins)


def message_kernel(places, *refs):
    blocks, message_ref = refs[:-1], refs[-1]
    size = message_ref.shape[0] // len(places)
    for to, (ref, at) in enumerate(zip(blocks, places)):
        message_ref[to * size : (to + 1) * size, :] = ref[at * size : (at + 1) * size, :]


def head_kernel(sections, earlier, dy_in_ref, slope_ref, point_ref, *refs):
    others, before, out_ref = refs[: sections - 1], refs[sections - 1 : -1], refs[-1]
    section = lax.axis_index("pipe")
    bins = dy_in_ref.shape[0]
    for ref in before:
        out_ref[:earlier, :] = ref[...]

    @pl.when(section == 0)
    def layer():
        out_ref[earlier : earlier + bins, :] = back_pre(dy_in_ref[...], slope_ref[...], point_ref)

    for level in range(1, sections):

        @pl.when(section == level)
        def keep(level=level):
            out_ref[earlier : earlier + bins, :] = others[level - 1][...]


def columns_kernel(groups, runs, kept, *refs):
    refs, (sent_ref,) = refs[:-1], refs[-1:]
    kept_refs = refs[sum(runs) :]
    count = 2 * len(kept)
    section = lax.axis_index("pipe")
    core = lax.axis_index("dp")
    place = lax.axis_index("ctx")
    x, start = None, 0
    for level, run in enumerate(runs):
        pieces = [ref[...] for ref in refs[start : start + run]]
        start += run
        whole = jnp.concatenate(pieces, axis=0).astype(jnp.float32)
        x = whole if x is None else jnp.where(section == level, whole, x)
    act = gelu(x).astype(jnp.bfloat16)
    chans = act.shape[1]
    width = chans // (groups * count)
    row = lax.broadcasted_iota(jnp.int32, (width, chans), 0)
    col = lax.broadcasted_iota(jnp.int32, (width, chans), 1)

    def block(offset):
        owner = lax.bitwise_xor(place, offset)
        rows = []
        for step in range(groups):
            first = (lax.rem(core + step, groups) * count + owner) * width
            rows.append((col == first + row).astype(jnp.float32))
        pick = jnp.concatenate(rows, axis=0).astype(jnp.bfloat16)
        return lax.dot_general(
            pick, act, contract_last, preferred_element_type=jnp.float32
        ).astype(jnp.bfloat16)

    size = groups * width
    for at, offset in enumerate(kept):
        kept_refs[at][...] = block(offset)
        sent_ref[at * size : (at + 1) * size, :] = block(offset ^ 1)


def grad_kernel(sections, bins, places, *refs):
    columns, refs = refs[: len(places)], refs[len(places) :]
    grads, out_ref = refs[:-1], refs[-1]
    section = lax.axis_index("pipe")
    width = out_ref.shape[1]

    def taps(spread):
        act = jnp.concatenate(
            [ref[at : at + width, :] for ref, at in zip(columns, places)], axis=1
        )
        dpre = jnp.concatenate([ref[...] for ref in grads], axis=0)
        wide = dpre.astype(jnp.float32)
        spans = (
            moved(wide, -spread, bins).astype(jnp.bfloat16),
            dpre,
            moved(wide, spread, bins).astype(jnp.bfloat16),
        )
        for tap in range(3):
            out_ref[tap] = jnp.dot(
                act, spans[tap], preferred_element_type=jnp.float32
            ).astype(out_ref.dtype)

    for level in range(sections):

        @pl.when(section == level)
        def run(level=level):
            taps(2**level)


def kernel_call(body, outs, flops, name, waits=(), carries=(), in_spec=in_vmem, scratch=()):
    def call(*args):
        used, taken = len(args), len(args) + len(waits) + len(carries)

        def run(*refs):
            made = refs[taken : taken + len(outs)]
            body(*refs[:used], *made, *refs[taken + len(outs) + len(carries) :])

        moved_bytes = sum(math.prod(a.shape) * a.dtype.itemsize for a in (*args, *outs))
        return pl.pallas_call(
            run,
            out_shape=[*outs, *(jax.ShapeDtypeStruct(a.shape, a.dtype) for a in carries)],
            in_specs=[in_spec] * used + [anywhere] * (taken - used),
            out_specs=[in_vmem] * len(outs) + [anywhere] * len(carries),
            input_output_aliases={
                used + len(waits) + at: len(outs) + at for at in range(len(carries))
            },
            scratch_shapes=list(scratch),
            compiler_params=pltpu.CompilerParams(vmem_limit_bytes=24 * 2**20),
            cost_estimate=pl.CostEstimate(
                flops=flops, bytes_accessed=moved_bytes, transcendentals=0
            ),
            name=name,
        )(*args, *waits, *carries)

    return call


def residue_shards(inputs, cotangent, weight, point):
    sections = lax.axis_size("pipe")
    section = lax.axis_index("pipe")
    count = lax.axis_size("ctx")
    groups = lax.axis_size("dp")
    seq_count, bins, chans = inputs.shape
    inner = weight.shape[3]
    rows = seq_count * bins
    scale = 1.0 / math.sqrt(seq_count * groups * bins * count)
    last = sections - 1
    seqs = range(seq_count)
    layer_flops = 2 * bins * chans * inner * 4

    def shape(*dims, dtype=jnp.bfloat16):
        return jax.ShapeDtypeStruct(dims, dtype)

    def hop(value, source, target, third=None):
        sends = {source: target, target: source}
        if third is not None and third not in sends:
            sends.update({target: third, third: source})
        route = []
        for core in range(groups):
            for stage in range(sections):
                taker = core if stage in sends else (core + 1) % groups
                for i in range(count):
                    giver = (core * sections + stage) * count + i
                    route.append((giver, (taker * sections + sends.get(stage, stage)) * count + i))
        return lax.ppermute(value, ("dp", "pipe", "ctx"), route)

    def onward(value, step):
        return lax.ppermute(value, "ctx", [(i, (i + step) % count) for i in range(count)])

    def exchange(value, offset):
        return lax.ppermute(value, "ctx", [(i, i ^ offset) for i in range(count)])

    payload = jnp.where(section == last, cotangent, inputs)
    parts = kernel_call(
        functools.partial(split_kernel, last),
        [shape(rows // count, chans)] * count,
        10 * seq_count * layer_flops,
        "split",
    )(payload)
    weight, point = kernel_call(
        hold_kernel,
        [shape(*weight.shape), shape(*point.shape)],
        0,
        "hold",
        waits=[parts[0]],
        in_spec=anywhere,
        scratch=[pltpu.SemaphoreType.DMA((2,))],
    )(weight, point)
    steps = [1, *range(count - 1, 1, -1)]
    parts = [*(onward(parts[step], step) for step in steps), parts[0]]

    trunk, inside = shape(bins, chans), shape(bins, inner)
    inside_wide = shape(bins, inner, dtype=jnp.float32)
    whole, out, pre = kernel_call(
        functools.partial(first_kernel, last, bins, [*steps, 0]),
        [shape(rows, chans), trunk, inside_wide],
        layer_flops,
        "first",
    )(*parts, weight, point)
    outs, pres, xs, sent = [out], [[pre]], [[whole]], ()
    for level in range(last):
        if level > 0:
            third = last if level > 1 else None
            xs.append([hop(out, level - 1, level, third) for out in outs[:-1]])
            xs[level].append(hop(outs[-1], level - 1, level))
            outs = []
            pres.append([])
        for seq in range(len(outs), seq_count):
            out, pre = kernel_call(
                functools.partial(fore_kernel, level, seq, bins),
                [trunk, inside_wide],
                layer_flops,
                "fore",
                waits=outs[-1:] or sent,
            )(xs[level][seq if level else 0], weight, point)
            outs.append(out)
            pres[level].append(pre)
        sent = outs
        if level == 1:
            back_weights = kernel_call(
                transpose_kernel,
                [shape(1, weight.shape[1], inner, chans), shape(1, chans, inner)],
                0,
                "transpose",
                waits=outs,
            )(weight, point)
            sent = [*outs, *back_weights]
    slopes = kernel_call(
        functools.partial(slope_kernel, last, seq_count, bins),
        [shape(bins, chans, dtype=jnp.float32), inside_wide] * seq_count,
        0,
        "slopes",
        waits=outs,
    )(
        *[xs[level][seq if level else 0] for level in range(last) for seq in seqs],
        *[pre for some in pres for pre in some],
    )
    sent = [*sent, *slopes]
    xs.append([hop(out, last - 1, last, 0) for out in outs])

    dys, dpres = [], [[] for level in range(sections)]
    for seq in seqs:
        dy, dpre = kernel_call(
            functools.partial(turn_kernel, last, seq, bins, scale),
            [trunk, inside],
            2 * layer_flops,
            "turn",
            waits=dys[-1:] or sent,
        )(xs[last][seq], whole, weight, *back_weights)
        dys.append(dy)
        dpres[last].append(dpre)
    kept = list(range(0, count, 2))
    moving = [(offset, 0) for offset in range(1, count, 2)]
    size = chans // count
    *owned, message = kernel_call(
        functools.partial(columns_kernel, groups, [len(x) for x in xs], kept),
        [shape(size, rows)] * len(kept) + [shape(size * len(kept), rows)],
        2 * rows * chans * chans,
        "columns",
        waits=dys,
    )(*[x for some in xs for x in some])
    blocks = {(offset, 0): (array, 0) for offset, array in zip(kept, owned)}
    sent = [owned[0]]
    dys = [hop(dy, last, last - 1) for dy in dys]
    message, bit = exchange(message, 1), 1
    blocks.update({(to ^ 1, start ^ 1): (message, at) for at, (to, start) in enumerate(moving)})

    for level in range(last - 1, 0, -1):
        outs = []
        for seq in seqs:
            dy, dpre = kernel_call(
                functools.partial(back_kernel, level, bins),
                [trunk, inside],
                layer_flops,
                "back",
                waits=outs[-1:] or sent,
            )(dys[seq], *slopes[2 * seq : 2 * seq + 2], *back_weights)
            outs.append(dy)
            dpres[level].append(dpre)
        sent = outs
        third = 0 if level > 1 else last
        dys = [hop(dy, level, level - 1, third) for dy in outs[:-1]]
        dys.append(hop(outs[-1], level, level - 1, None if level > 1 else last))
        bit *= 2
        moving = sorted(key for key in blocks if key[0] & bit)
        if moving:
            (message,) = kernel_call(
                functools.partial(message_kernel, [blocks[key][1] for key in moving]),
                [shape(size * len(moving), rows)],
                0,
                "message",
                waits=outs,
            )(*[blocks[key][0] for key in moving])
            sent = [*outs, message]
            message = exchange(message, bit)
            for at, (to, start) in enumerate(moving):
                blocks[to ^ bit, start ^ bit] = (message, at)

    sent = [*sent, message]
    dpre = []
    for seq in seqs:
        dpre = kernel_call(
            functools.partial(head_kernel, sections, seq * bins),
            [shape((seq + 1) * bins, inner)],
            layer_flops // 4,
            "head",
            waits=dpre or sent,
        )(dys[seq], slopes[2 * seq + 1], back_weights[1], *[dpres[level][seq] for level in range(1, sections)], *dpre)
    (dpre,) = dpre
    received, bit = {0: dpre}, count // 2
    while bit:
        received.update({offset ^ bit: exchange(block, bit) for offset, block in received.items()})
        bit //= 2
    offsets = [*received]
    gathered = [received[offset] for offset in offsets]
    columns = [blocks[0, offset] for offset in offsets]
    width = size // groups

    def gradient(step, dtype, waits=()):
        places = [at * size + step * width for array, at in columns]
        (part,) = kernel_call(
            functools.partial(grad_kernel, sections, bins, places),
            [shape(3, width, inner, dtype=dtype)],
            2 * 3 * rows * count * width * inner,
            "grad",
            waits=waits,
        )(*[array for array, at in columns], *gathered)
        return part

    others = [gradient(step, jnp.bfloat16) for step in range(1, groups)]
    mine = gradient(0, jnp.float32, waits=others)
    for step, other in enumerate(others, 1):
        route = [(i, (i + step) % groups) for i in range(groups)]
        mine = mine + lax.ppermute(other, "dp", route).astype(jnp.float32)
    return mine[None]


def solution(mesh):
    def shards(inputs, cotangent, dilated_kernel_weight, point_weight):
        bins = inputs.shape[1]
        first_spread = bins // 2 // 2 ** (mesh.shape["pipe"] - 1)
        count = mesh.shape["ctx"]
        residues = (
            first_spread == count
            and mesh.shape["pipe"] > 2
            and bins % (16 * count) == 0
            and 1 < count == 1 << (count.bit_length() - 1) <= 1 << (mesh.shape["pipe"] - 2)
            and inputs.shape[2] % (count * mesh.shape["dp"]) == 0
        )
        plan = residue_shards if residues else edge_shards
        return plan(inputs, cotangent, dilated_kernel_weight, point_weight)

    return jax.shard_map(
        shards,
        mesh=mesh,
        in_specs=(
            P("dp", "ctx", None),
            P("dp", "ctx", None),
            P("pipe", None, None, None),
            P("pipe", None, None),
        ),
        out_specs=P("pipe", None, ("dp", "ctx"), None),
        check_vma=False,
    )
```

```python
import functools
import math

import jax
import jax.numpy as jnp
from jax import lax
from jax.experimental import pallas as pl
from jax.experimental.pallas import tpu as pltpu
from jax.sharding import PartitionSpec as P

root_half = 0.7071067811865476
inv_root_two_pi = 0.3989422804014327

in_vmem = pl.BlockSpec(memory_space=pltpu.VMEM)
anywhere = pl.BlockSpec(memory_space=pl.ANY)
contract_last = (((1,), (1,)), ((), ()))
contract_first = (((0,), (0,)), ((), ()))


def gelu(value):
    return 0.5 * value * (1.0 + lax.erf(value * root_half))


def gelu_slope(value):
    return (
        0.5 * (1.0 + lax.erf(value * root_half))
        + value * jnp.exp(-0.5 * value * value) * inv_root_two_pi
    )


def padded(cells, sides, width):
    for axis, dim in sides:
        count = lax.axis_size(axis)
        ends = count - 1
        head = lax.slice_in_dim(cells, 0, width, axis=dim)
        tail = lax.slice_in_dim(cells, cells.shape[dim] - width, cells.shape[dim], axis=dim)
        cells = jnp.concatenate(
            [
                lax.ppermute(tail, axis, [(i, (i + 1) % count) for i in range(ends)]),
                cells,
                lax.ppermute(head, axis, [((i + 1) % count, i) for i in range(ends)]),
            ],
            axis=dim,
        )
    return cells


def shifted(block, axis, distance):
    devices = range(lax.axis_size(axis))
    route = [(i - distance, i) for i in devices if i - distance in devices]
    return lax.ppermute(block, axis, route)


def edge_shards(inputs, cotangent, dilated_kernel_weight, point_weight):
    sections = lax.axis_size("pipe")
    section = lax.axis_index("pipe")
    seq_count, bins, chans = inputs.shape
    reach = bins // 2
    table = jnp.array(
        [reach // 2 ** (sections - 1 - level) for level in range(sections)], jnp.int32
    )
    spread = table[section]
    dilation_weight = dilated_kernel_weight[0]
    w_point = point_weight[0]
    inner_channel_count = dilation_weight.shape[2]
    scale = 1.0 / math.sqrt(seq_count * lax.axis_size("dp") * bins * lax.axis_size("ctx"))
    ticks = jnp.arange(seq_count + sections - 1, dtype=jnp.int32)

    def conv_fore(extended):
        running_total = jnp.zeros((bins, inner_channel_count), jnp.float32)
        for kernel_offset in range(3):
            receptive_span = lax.dynamic_slice_in_dim(
                extended, reach + (kernel_offset - 1) * spread, bins, 0
            )
            running_total = running_total + jnp.dot(
                receptive_span, dilation_weight[kernel_offset], preferred_element_type=jnp.float32
            )
        return running_total

    def put(store, slot, valid, item):
        current = lax.dynamic_index_in_dim(store, slot, 0, keepdims=False)
        return lax.dynamic_update_index_in_dim(store, jnp.where(valid, item, current), slot, 0)

    kept_x = jnp.zeros(inputs.shape, jnp.bfloat16)
    kept_ext = jnp.zeros((seq_count, bins + 2 * reach, chans), jnp.bfloat16)
    kept_pre = jnp.zeros((seq_count, bins, inner_channel_count), jnp.float32)

    def fore_tick(carry, tick):
        received, store_x, store_ext, store_pre = carry
        micro = tick - section
        valid = (micro >= 0) & (micro < seq_count)
        slot = jnp.clip(micro, 0, seq_count - 1)
        first = lax.dynamic_index_in_dim(inputs, slot, 0, keepdims=False)
        trunk_in = jnp.where(section == 0, first, received)
        act = gelu(trunk_in.astype(jnp.float32)).astype(jnp.bfloat16)
        extended = padded(act, (("ctx", 0),), reach)
        pre = conv_fore(extended)
        inner = gelu(pre).astype(jnp.bfloat16)
        out = (
            trunk_in.astype(jnp.float32)
            + jnp.dot(inner, w_point, preferred_element_type=jnp.float32)
        ).astype(jnp.bfloat16)
        sent = shifted(out, "pipe", 1)
        store_x = put(store_x, slot, valid, trunk_in)
        store_ext = put(store_ext, slot, valid, extended)
        store_pre = put(store_pre, slot, valid, pre)
        return ((sent, store_x, store_ext, store_pre), None)

    start_recv = jnp.zeros((bins, chans), jnp.bfloat16)
    (unused, kept_x, kept_ext, kept_pre), unused_out = lax.scan(
        fore_tick, (start_recv, kept_x, kept_ext, kept_pre), ticks
    )

    def back_tick(carry, tick):
        received, grad = carry
        micro = tick - (sections - 1 - section)
        valid = (micro >= 0) & (micro < seq_count)
        slot = jnp.clip(micro, 0, seq_count - 1)
        last = (
            lax.dynamic_index_in_dim(cotangent, slot, 0, keepdims=False).astype(jnp.float32) * scale
        ).astype(jnp.bfloat16)
        upstream = jnp.where(section == sections - 1, last, received)
        trunk_in = lax.dynamic_index_in_dim(kept_x, slot, 0, keepdims=False)
        extended = lax.dynamic_index_in_dim(kept_ext, slot, 0, keepdims=False)
        pre = lax.dynamic_index_in_dim(kept_pre, slot, 0, keepdims=False)
        inner_grad = lax.dot_general(
            upstream, w_point, contract_last, preferred_element_type=jnp.float32
        )
        dpre = (inner_grad * gelu_slope(pre) * valid.astype(jnp.float32)).astype(jnp.bfloat16)
        dpre_ext = padded(dpre, (("ctx", 0),), reach)
        dact = jnp.zeros((bins, chans), jnp.float32)
        taps = []
        for kernel_offset in range(3):
            receptive_span = lax.dynamic_slice_in_dim(
                dpre_ext, reach - (kernel_offset - 1) * spread, bins, 0
            )
            dact = dact + lax.dot_general(
                receptive_span,
                dilation_weight[kernel_offset],
                contract_last,
                preferred_element_type=jnp.float32,
            )
            source = lax.dynamic_slice_in_dim(
                extended, reach + (kernel_offset - 1) * spread, bins, 0
            )
            taps.append(
                lax.dot_general(source, dpre, contract_first, preferred_element_type=jnp.float32)
            )
        grad = grad + jnp.stack(taps)
        back = (
            upstream.astype(jnp.float32) + dact * gelu_slope(trunk_in.astype(jnp.float32))
        ).astype(jnp.bfloat16)
        sent = shifted(back, "pipe", -1)
        return ((sent, grad), None)

    start_grad = jnp.zeros((3, chans, inner_channel_count), jnp.float32)
    (unused_back, grad), unused_seq = lax.scan(back_tick, (start_recv, start_grad), ticks)
    term = grad[None]
    return lax.psum_scatter(term, ("dp", "ctx"), scatter_dimension=2, tiled=True)


def moved(value, by, bins):
    pieces = []
    for start in range(0, value.shape[0], bins):
        piece = value[start : start + bins]
        place = lax.broadcasted_iota(jnp.int32, piece.shape, 0)
        if by > 0:
            keep = place >= by
        else:
            keep = place < bins + by
        pieces.append(jnp.where(keep, pltpu.roll(piece, by % bins, 0), 0.0))
    return jnp.concatenate(pieces, axis=0)


def fore(x, weight_ref, spread, bins):
    act = gelu(x.astype(jnp.float32)).astype(jnp.bfloat16)
    terms = [
        jnp.dot(act, weight_ref[0, tap], preferred_element_type=jnp.float32) for tap in range(3)
    ]
    return terms[1] + moved(terms[0], spread, bins) + moved(terms[2], -spread, bins)


def back_pre(dy, pre_slope, point_ref):
    inner_grad = jnp.dot(dy, point_ref[0], preferred_element_type=jnp.float32)
    return (inner_grad * pre_slope).astype(jnp.bfloat16)


def back_trunk(dy, dpre, x_slope, weight_ref, spread, bins):
    wide = dpre.astype(jnp.float32)
    spans = (
        moved(wide, -spread, bins).astype(jnp.bfloat16),
        dpre,
        moved(wide, spread, bins).astype(jnp.bfloat16),
    )
    dact = jnp.zeros(dy.shape, jnp.float32)
    for tap in range(3):
        dact = dact + jnp.dot(
            spans[tap], weight_ref[0, tap], preferred_element_type=jnp.float32
        )
    return (dy.astype(jnp.float32) + dact * x_slope).astype(jnp.bfloat16)


def of_seq(ref, seq, bins):
    if ref.shape[0] == bins:
        return ref[...]
    return ref[seq * bins : (seq + 1) * bins, :]


def split_kernel(last, payload_ref, *out_refs):
    count = len(out_refs)
    seq_count, bins, chans = payload_ref.shape
    part = bins // count
    section = lax.axis_index("pipe")
    place = lax.axis_index("ctx")

    @pl.when((section == 0) | (section == last))
    def send():
        source = payload_ref[...].reshape(seq_count * bins, chans)
        row = lax.broadcasted_iota(jnp.int32, (part, seq_count * bins), 0)
        col = lax.broadcasted_iota(jnp.int32, (part, seq_count * bins), 1)
        for hop in range(count):
            residue = lax.rem(place + hop, count)
            rows = [
                (col == seq * bins + count * row + residue).astype(jnp.float32)
                for seq in range(seq_count)
            ]
            pick = jnp.concatenate(rows, axis=0).astype(jnp.bfloat16)
            out_refs[hop][...] = jnp.dot(
                pick, source, preferred_element_type=jnp.float32
            ).astype(jnp.bfloat16)


def hold_kernel(weight_ref, point_ref, weight_out, point_out, sems):
    loads = [
        pltpu.make_async_copy(weight_ref, weight_out, sems.at[0]),
        pltpu.make_async_copy(point_ref, point_out, sems.at[1]),
    ]
    for load in loads:
        load.start()
    for load in loads:
        load.wait()


def first_kernel(last, bins, steps, *refs):
    parts, (weight_ref, point_ref, whole_ref, out_ref, pre_ref) = refs[:-5], refs[-5:]
    count = len(parts)
    section = lax.axis_index("pipe")
    place = lax.axis_index("ctx")
    part = bins // count
    seq_count = whole_ref.shape[0] // bins

    @pl.when((section == 0) | (section == last))
    def gather():
        for step, part_ref in zip(steps, parts):
            source = lax.rem(place + count - step, count)
            for seq in range(seq_count):
                at = pl.multiple_of(seq * bins + source * part, part)
                whole_ref[pl.ds(at, part), :] = part_ref[seq * part : (seq + 1) * part, :]

    @pl.when(section == 0)
    def layer():
        x = whole_ref[:bins, :]
        finish(x, fore(x, weight_ref, 1, bins), point_ref, out_ref, pre_ref)


def finish(x, pre, point_ref, out_ref, pre_ref):
    pre_ref[...] = pre
    branch = jnp.dot(
        gelu(pre).astype(jnp.bfloat16), point_ref[0], preferred_element_type=jnp.float32
    )
    out_ref[...] = (x.astype(jnp.float32) + branch).astype(jnp.bfloat16)


def fore_kernel(level, seq, bins, x_ref, weight_ref, point_ref, out_ref, pre_ref):
    @pl.when(lax.axis_index("pipe") == level)
    def layer():
        x = of_seq(x_ref, seq, bins)
        finish(x, fore(x, weight_ref, 2**level, bins), point_ref, out_ref, pre_ref)


def transpose_kernel(weight_ref, point_ref, weight_out, point_out):
    for tap in range(weight_ref.shape[1]):
        weight_out[0, tap] = weight_ref[0, tap].T
    point_out[0] = point_ref[0].T


def turn_kernel(level, seq, bins, scale, x_ref, cot_ref, weight_ref, weight_t_ref, point_t_ref, dy_ref, dpre_ref):
    @pl.when(lax.axis_index("pipe") == level)
    def layer():
        x = of_seq(x_ref, seq, bins)
        pre = fore(x, weight_ref, 2**level, bins)
        cot = of_seq(cot_ref, seq, bins)
        dy = (cot.astype(jnp.float32) * scale).astype(jnp.bfloat16)
        dpre = back_pre(dy, gelu_slope(pre), point_t_ref)
        dpre_ref[...] = dpre
        x_slope = gelu_slope(x.astype(jnp.float32))
        dy_ref[...] = back_trunk(dy, dpre, x_slope, weight_t_ref, 2**level, bins)


def slope_kernel(levels, seq_count, bins, *refs):
    xs, pres = refs[: levels * seq_count], refs[levels * seq_count : 2 * levels * seq_count]
    outs = refs[2 * levels * seq_count :]
    for level in range(levels):

        @pl.when(lax.axis_index("pipe") == level)
        def layer(level=level):
            for seq in range(seq_count):
                x = of_seq(xs[level * seq_count + seq], seq, bins)
                outs[2 * seq][...] = gelu_slope(x.astype(jnp.float32))
                outs[2 * seq + 1][...] = gelu_slope(pres[level * seq_count + seq][...])


def back_kernel(level, bins, dy_in_ref, x_slope_ref, pre_slope_ref, weight_ref, point_ref, dy_ref, dpre_ref):
    @pl.when(lax.axis_index("pipe") == level)
    def layer():
        dy = dy_in_ref[...]
        dpre = back_pre(dy, pre_slope_ref[...], point_ref)
        dpre_ref[...] = dpre
        dy_ref[...] = back_trunk(dy, dpre, x_slope_ref[...], weight_ref, 2**level, bins)


def message_kernel(places, *refs):
    blocks, message_ref = refs[:-1], refs[-1]
    size = message_ref.shape[0] // len(places)
    for to, (ref, at) in enumerate(zip(blocks, places)):
        message_ref[to * size : (to + 1) * size, :] = ref[at * size : (at + 1) * size, :]


def head_kernel(sections, earlier, dy_in_ref, slope_ref, point_ref, *refs):
    others, before, out_ref = refs[: sections - 1], refs[sections - 1 : -1], refs[-1]
    section = lax.axis_index("pipe")
    bins = dy_in_ref.shape[0]
    for ref in before:
        out_ref[:earlier, :] = ref[...]

    @pl.when(section == 0)
    def layer():
        out_ref[earlier : earlier + bins, :] = back_pre(dy_in_ref[...], slope_ref[...], point_ref)

    for level in range(1, sections):

        @pl.when(section == level)
        def keep(level=level):
            out_ref[earlier : earlier + bins, :] = others[level - 1][...]


def columns_kernel(groups, runs, kept, *refs):
    refs, (sent_ref,) = refs[:-1], refs[-1:]
    kept_refs = refs[sum(runs) :]
    count = 2 * len(kept)
    section = lax.axis_index("pipe")
    core = lax.axis_index("dp")
    place = lax.axis_index("ctx")
    x, start = None, 0
    for level, run in enumerate(runs):
        pieces = [ref[...] for ref in refs[start : start + run]]
        start += run
        whole = jnp.concatenate(pieces, axis=0).astype(jnp.float32)
        x = whole if x is None else jnp.where(section == level, whole, x)
    act = gelu(x).astype(jnp.bfloat16)
    chans = act.shape[1]
    width = chans // (groups * count)
    row = lax.broadcasted_iota(jnp.int32, (width, chans), 0)
    col = lax.broadcasted_iota(jnp.int32, (width, chans), 1)

    def block(offset):
        owner = lax.bitwise_xor(place, offset)
        rows = []
        for step in range(groups):
            first = (lax.rem(core + step, groups) * count + owner) * width
            rows.append((col == first + row).astype(jnp.float32))
        pick = jnp.concatenate(rows, axis=0).astype(jnp.bfloat16)
        return lax.dot_general(
            pick, act, contract_last, preferred_element_type=jnp.float32
        ).astype(jnp.bfloat16)

    size = groups * width
    for at, offset in enumerate(kept):
        kept_refs[at][...] = block(offset)
        sent_ref[at * size : (at + 1) * size, :] = block(offset ^ 1)


def grad_kernel(sections, bins, places, *refs):
    columns, refs = refs[: len(places)], refs[len(places) :]
    grads, out_ref = refs[:-1], refs[-1]
    section = lax.axis_index("pipe")
    width = out_ref.shape[1]

    def taps(spread):
        act = jnp.concatenate(
            [ref[at : at + width, :] for ref, at in zip(columns, places)], axis=1
        )
        dpre = jnp.concatenate([ref[...] for ref in grads], axis=0)
        wide = dpre.astype(jnp.float32)
        spans = (
            moved(wide, -spread, bins).astype(jnp.bfloat16),
            dpre,
            moved(wide, spread, bins).astype(jnp.bfloat16),
        )
        for tap in range(3):
            out_ref[tap] = jnp.dot(
                act, spans[tap], preferred_element_type=jnp.float32
            ).astype(out_ref.dtype)

    for level in range(sections):

        @pl.when(section == level)
        def run(level=level):
            taps(2**level)


def kernel_call(body, outs, flops, name, waits=(), carries=(), in_spec=in_vmem, scratch=()):
    def call(*args):
        used, taken = len(args), len(args) + len(waits) + len(carries)

        def run(*refs):
            made = refs[taken : taken + len(outs)]
            body(*refs[:used], *made, *refs[taken + len(outs) + len(carries) :])

        moved_bytes = sum(math.prod(a.shape) * a.dtype.itemsize for a in (*args, *outs))
        return pl.pallas_call(
            run,
            out_shape=[*outs, *(jax.ShapeDtypeStruct(a.shape, a.dtype) for a in carries)],
            in_specs=[in_spec] * used + [anywhere] * (taken - used),
            out_specs=[in_vmem] * len(outs) + [anywhere] * len(carries),
            input_output_aliases={
                used + len(waits) + at: len(outs) + at for at in range(len(carries))
            },
            scratch_shapes=list(scratch),
            compiler_params=pltpu.CompilerParams(vmem_limit_bytes=24 * 2**20),
            cost_estimate=pl.CostEstimate(
                flops=flops, bytes_accessed=moved_bytes, transcendentals=0
            ),
            name=name,
        )(*args, *waits, *carries)

    return call


def residue_shards(inputs, cotangent, weight, point):
    sections = lax.axis_size("pipe")
    section = lax.axis_index("pipe")
    count = lax.axis_size("ctx")
    groups = lax.axis_size("dp")
    seq_count, bins, chans = inputs.shape
    inner = weight.shape[3]
    rows = seq_count * bins
    scale = 1.0 / math.sqrt(seq_count * groups * bins * count)
    last = sections - 1
    seqs = range(seq_count)
    layer_flops = 2 * bins * chans * inner * 4

    def shape(*dims, dtype=jnp.bfloat16):
        return jax.ShapeDtypeStruct(dims, dtype)

    def hop(value, source, target, third=None):
        sends = {source: target, target: source}
        if third is not None and third not in sends:
            sends.update({target: third, third: source})
        route = []
        for core in range(groups):
            for stage in range(sections):
                taker = core if stage in sends else (core + 1) % groups
                for i in range(count):
                    giver = (core * sections + stage) * count + i
                    route.append((giver, (taker * sections + sends.get(stage, stage)) * count + i))
        return lax.ppermute(value, ("dp", "pipe", "ctx"), route)

    def onward(value, step):
        return lax.ppermute(value, "ctx", [(i, (i + step) % count) for i in range(count)])

    def exchange(value, offset):
        return lax.ppermute(value, "ctx", [(i, i ^ offset) for i in range(count)])

    payload = jnp.where(section == last, cotangent, inputs)
    parts = kernel_call(
        functools.partial(split_kernel, last),
        [shape(rows // count, chans)] * count,
        10 * seq_count * layer_flops,
        "split",
    )(payload)
    weight, point = kernel_call(
        hold_kernel,
        [shape(*weight.shape), shape(*point.shape)],
        0,
        "hold",
        waits=[parts[0]],
        in_spec=anywhere,
        scratch=[pltpu.SemaphoreType.DMA((2,))],
    )(weight, point)
    steps = [1, *range(count - 1, 1, -1)]
    parts = [*(onward(parts[step], step) for step in steps), parts[0]]

    trunk, inside = shape(bins, chans), shape(bins, inner)
    inside_wide = shape(bins, inner, dtype=jnp.float32)
    whole, out, pre = kernel_call(
        functools.partial(first_kernel, last, bins, [*steps, 0]),
        [shape(rows, chans), trunk, inside_wide],
        layer_flops,
        "first",
    )(*parts, weight, point)
    outs, pres, xs, sent = [out], [[pre]], [[whole]], ()
    for level in range(last):
        if level > 0:
            third = last if level > 1 else None
            xs.append([hop(out, level - 1, level, third) for out in outs[:-1]])
            xs[level].append(hop(outs[-1], level - 1, level))
            outs = []
            pres.append([])
        for seq in range(len(outs), seq_count):
            out, pre = kernel_call(
                functools.partial(fore_kernel, level, seq, bins),
                [trunk, inside_wide],
                layer_flops,
                "fore",
                waits=outs[-1:] or sent,
            )(xs[level][seq if level else 0], weight, point)
            outs.append(out)
            pres[level].append(pre)
        sent = outs
        if level == 1:
            back_weights = kernel_call(
                transpose_kernel,
                [shape(1, weight.shape[1], inner, chans), shape(1, chans, inner)],
                0,
                "transpose",
                waits=outs,
            )(weight, point)
            sent = [*outs, *back_weights]
    slopes = kernel_call(
        functools.partial(slope_kernel, last, seq_count, bins),
        [shape(bins, chans, dtype=jnp.float32), inside_wide] * seq_count,
        0,
        "slopes",
        waits=outs,
    )(
        *[xs[level][seq if level else 0] for level in range(last) for seq in seqs],
        *[pre for some in pres for pre in some],
    )
    sent = [*sent, *slopes]
    xs.append([hop(out, last - 1, last, 0) for out in outs])

    dys, dpres = [], [[] for level in range(sections)]
    for seq in seqs:
        dy, dpre = kernel_call(
            functools.partial(turn_kernel, last, seq, bins, scale),
            [trunk, inside],
            2 * layer_flops,
            "turn",
            waits=dys[-1:] or sent,
        )(xs[last][seq], whole, weight, *back_weights)
        dys.append(dy)
        dpres[last].append(dpre)
    kept = list(range(0, count, 2))
    moving = [(offset, 0) for offset in range(1, count, 2)]
    size = chans // count
    *owned, message = kernel_call(
        functools.partial(columns_kernel, groups, [len(x) for x in xs], kept),
        [shape(size, rows)] * len(kept) + [shape(size * len(kept), rows)],
        2 * rows * chans * chans,
        "columns",
        waits=dys,
    )(*[x for some in xs for x in some])
    blocks = {(offset, 0): (array, 0) for offset, array in zip(kept, owned)}
    sent = [owned[0]]
    dys = [hop(dy, last, last - 1) for dy in dys]
    message, bit = exchange(message, 1), 1
    blocks.update({(to ^ 1, start ^ 1): (message, at) for at, (to, start) in enumerate(moving)})

    for level in range(last - 1, 0, -1):
        outs = []
        for seq in seqs:
            dy, dpre = kernel_call(
                functools.partial(back_kernel, level, bins),
                [trunk, inside],
                layer_flops,
                "back",
                waits=outs[-1:] or sent,
            )(dys[seq], *slopes[2 * seq : 2 * seq + 2], *back_weights)
            outs.append(dy)
            dpres[level].append(dpre)
        sent = outs
        third = 0 if level > 1 else last
        dys = [hop(dy, level, level - 1, third) for dy in outs[:-1]]
        dys.append(hop(outs[-1], level, level - 1, None if level > 1 else last))
        bit *= 2
        moving = sorted(key for key in blocks if key[0] & bit)
        if moving:
            (message,) = kernel_call(
                functools.partial(message_kernel, [blocks[key][1] for key in moving]),
                [shape(size * len(moving), rows)],
                0,
                "message",
                waits=outs,
            )(*[blocks[key][0] for key in moving])
            sent = [*outs, message]
            message = exchange(message, bit)
            for at, (to, start) in enumerate(moving):
                blocks[to ^ bit, start ^ bit] = (message, at)

    sent = [*sent, message]
    dpre = []
    for seq in seqs:
        dpre = kernel_call(
            functools.partial(head_kernel, sections, seq * bins),
            [shape((seq + 1) * bins, inner)],
            layer_flops // 4,
            "head",
            waits=dpre or sent,
        )(dys[seq], slopes[2 * seq + 1], back_weights[1], *[dpres[level][seq] for level in range(1, sections)], *dpre)
    (dpre,) = dpre
    offsets = range(1, count)
    gathered = [*(exchange(dpre, offset) for offset in offsets), dpre]
    columns = [blocks[0, offset] for offset in [*offsets, 0]]
    width = size // groups

    def gradient(step, dtype, waits=()):
        places = [at * size + step * width for array, at in columns]
        (part,) = kernel_call(
            functools.partial(grad_kernel, sections, bins, places),
            [shape(3, width, inner, dtype=dtype)],
            2 * 3 * rows * count * width * inner,
            "grad",
            waits=waits,
        )(*[array for array, at in columns], *gathered)
        return part

    others = [gradient(step, jnp.bfloat16) for step in range(1, groups)]
    mine = gradient(0, jnp.float32, waits=others)
    for step, other in enumerate(others, 1):
        route = [(i, (i + step) % groups) for i in range(groups)]
        mine = mine + lax.ppermute(other, "dp", route).astype(jnp.float32)
    return mine[None]


def solution(mesh):
    def shards(inputs, cotangent, dilated_kernel_weight, point_weight):
        bins = inputs.shape[1]
        first_spread = bins // 2 // 2 ** (mesh.shape["pipe"] - 1)
        count = mesh.shape["ctx"]
        residues = (
            first_spread == count
            and mesh.shape["pipe"] > 2
            and bins % (16 * count) == 0
            and 1 < count == 1 << (count.bit_length() - 1) <= 1 << (mesh.shape["pipe"] - 2)
            and inputs.shape[2] % (count * mesh.shape["dp"]) == 0
        )
        plan = residue_shards if residues else edge_shards
        return plan(inputs, cotangent, dilated_kernel_weight, point_weight)

    return jax.shard_map(
        shards,
        mesh=mesh,
        in_specs=(
            P("dp", "ctx", None),
            P("dp", "ctx", None),
            P("pipe", None, None, None),
            P("pipe", None, None),
        ),
        out_specs=P("pipe", None, ("dp", "ctx"), None),
        check_vma=False,
    )
```

```python
import functools
import math

import jax
import jax.numpy as jnp
from jax import lax
from jax.experimental import pallas as pl
from jax.experimental.pallas import tpu as pltpu
from jax.sharding import PartitionSpec as P

root_half = 0.7071067811865476
inv_root_two_pi = 0.3989422804014327

in_vmem = pl.BlockSpec(memory_space=pltpu.VMEM)
anywhere = pl.BlockSpec(memory_space=pl.ANY)
contract_last = (((1,), (1,)), ((), ()))
contract_first = (((0,), (0,)), ((), ()))


def gelu(value):
    return 0.5 * value * (1.0 + lax.erf(value * root_half))


def gelu_slope(value):
    return (
        0.5 * (1.0 + lax.erf(value * root_half))
        + value * jnp.exp(-0.5 * value * value) * inv_root_two_pi
    )


def padded(cells, sides, width):
    for axis, dim in sides:
        count = lax.axis_size(axis)
        ends = count - 1
        head = lax.slice_in_dim(cells, 0, width, axis=dim)
        tail = lax.slice_in_dim(cells, cells.shape[dim] - width, cells.shape[dim], axis=dim)
        cells = jnp.concatenate(
            [
                lax.ppermute(tail, axis, [(i, (i + 1) % count) for i in range(ends)]),
                cells,
                lax.ppermute(head, axis, [((i + 1) % count, i) for i in range(ends)]),
            ],
            axis=dim,
        )
    return cells


def shifted(block, axis, distance):
    devices = range(lax.axis_size(axis))
    route = [(i - distance, i) for i in devices if i - distance in devices]
    return lax.ppermute(block, axis, route)


def edge_shards(inputs, cotangent, dilated_kernel_weight, point_weight):
    sections = lax.axis_size("pipe")
    section = lax.axis_index("pipe")
    seq_count, bins, chans = inputs.shape
    reach = bins // 2
    table = jnp.array(
        [reach // 2 ** (sections - 1 - level) for level in range(sections)], jnp.int32
    )
    spread = table[section]
    dilation_weight = dilated_kernel_weight[0]
    w_point = point_weight[0]
    inner_channel_count = dilation_weight.shape[2]
    scale = 1.0 / math.sqrt(seq_count * lax.axis_size("dp") * bins * lax.axis_size("ctx"))
    ticks = jnp.arange(seq_count + sections - 1, dtype=jnp.int32)

    def conv_fore(extended):
        running_total = jnp.zeros((bins, inner_channel_count), jnp.float32)
        for kernel_offset in range(3):
            receptive_span = lax.dynamic_slice_in_dim(
                extended, reach + (kernel_offset - 1) * spread, bins, 0
            )
            running_total = running_total + jnp.dot(
                receptive_span, dilation_weight[kernel_offset], preferred_element_type=jnp.float32
            )
        return running_total

    def put(store, slot, valid, item):
        current = lax.dynamic_index_in_dim(store, slot, 0, keepdims=False)
        return lax.dynamic_update_index_in_dim(store, jnp.where(valid, item, current), slot, 0)

    kept_x = jnp.zeros(inputs.shape, jnp.bfloat16)
    kept_ext = jnp.zeros((seq_count, bins + 2 * reach, chans), jnp.bfloat16)
    kept_pre = jnp.zeros((seq_count, bins, inner_channel_count), jnp.float32)

    def fore_tick(carry, tick):
        received, store_x, store_ext, store_pre = carry
        micro = tick - section
        valid = (micro >= 0) & (micro < seq_count)
        slot = jnp.clip(micro, 0, seq_count - 1)
        first = lax.dynamic_index_in_dim(inputs, slot, 0, keepdims=False)
        trunk_in = jnp.where(section == 0, first, received)
        act = gelu(trunk_in.astype(jnp.float32)).astype(jnp.bfloat16)
        extended = padded(act, (("ctx", 0),), reach)
        pre = conv_fore(extended)
        inner = gelu(pre).astype(jnp.bfloat16)
        out = (
            trunk_in.astype(jnp.float32)
            + jnp.dot(inner, w_point, preferred_element_type=jnp.float32)
        ).astype(jnp.bfloat16)
        sent = shifted(out, "pipe", 1)
        store_x = put(store_x, slot, valid, trunk_in)
        store_ext = put(store_ext, slot, valid, extended)
        store_pre = put(store_pre, slot, valid, pre)
        return ((sent, store_x, store_ext, store_pre), None)

    start_recv = jnp.zeros((bins, chans), jnp.bfloat16)
    (unused, kept_x, kept_ext, kept_pre), unused_out = lax.scan(
        fore_tick, (start_recv, kept_x, kept_ext, kept_pre), ticks
    )

    def back_tick(carry, tick):
        received, grad = carry
        micro = tick - (sections - 1 - section)
        valid = (micro >= 0) & (micro < seq_count)
        slot = jnp.clip(micro, 0, seq_count - 1)
        last = (
            lax.dynamic_index_in_dim(cotangent, slot, 0, keepdims=False).astype(jnp.float32) * scale
        ).astype(jnp.bfloat16)
        upstream = jnp.where(section == sections - 1, last, received)
        trunk_in = lax.dynamic_index_in_dim(kept_x, slot, 0, keepdims=False)
        extended = lax.dynamic_index_in_dim(kept_ext, slot, 0, keepdims=False)
        pre = lax.dynamic_index_in_dim(kept_pre, slot, 0, keepdims=False)
        inner_grad = lax.dot_general(
            upstream, w_point, contract_last, preferred_element_type=jnp.float32
        )
        dpre = (inner_grad * gelu_slope(pre) * valid.astype(jnp.float32)).astype(jnp.bfloat16)
        dpre_ext = padded(dpre, (("ctx", 0),), reach)
        dact = jnp.zeros((bins, chans), jnp.float32)
        taps = []
        for kernel_offset in range(3):
            receptive_span = lax.dynamic_slice_in_dim(
                dpre_ext, reach - (kernel_offset - 1) * spread, bins, 0
            )
            dact = dact + lax.dot_general(
                receptive_span,
                dilation_weight[kernel_offset],
                contract_last,
                preferred_element_type=jnp.float32,
            )
            source = lax.dynamic_slice_in_dim(
                extended, reach + (kernel_offset - 1) * spread, bins, 0
            )
            taps.append(
                lax.dot_general(source, dpre, contract_first, preferred_element_type=jnp.float32)
            )
        grad = grad + jnp.stack(taps)
        back = (
            upstream.astype(jnp.float32) + dact * gelu_slope(trunk_in.astype(jnp.float32))
        ).astype(jnp.bfloat16)
        sent = shifted(back, "pipe", -1)
        return ((sent, grad), None)

    start_grad = jnp.zeros((3, chans, inner_channel_count), jnp.float32)
    (unused_back, grad), unused_seq = lax.scan(back_tick, (start_recv, start_grad), ticks)
    term = grad[None]
    return lax.psum_scatter(term, ("dp", "ctx"), scatter_dimension=2, tiled=True)


def moved(value, by, bins):
    pieces = []
    for start in range(0, value.shape[0], bins):
        piece = value[start : start + bins]
        place = lax.broadcasted_iota(jnp.int32, piece.shape, 0)
        if by > 0:
            keep = place >= by
        else:
            keep = place < bins + by
        pieces.append(jnp.where(keep, pltpu.roll(piece, by % bins, 0), 0.0))
    return jnp.concatenate(pieces, axis=0)


def fore(x, weight_ref, spread, bins):
    act = gelu(x.astype(jnp.float32)).astype(jnp.bfloat16)
    terms = [
        jnp.dot(act, weight_ref[0, tap], preferred_element_type=jnp.float32) for tap in range(3)
    ]
    return terms[1] + moved(terms[0], spread, bins) + moved(terms[2], -spread, bins)


def back_pre(dy, pre_slope, point_ref):
    inner_grad = jnp.dot(dy, point_ref[0], preferred_element_type=jnp.float32)
    return (inner_grad * pre_slope).astype(jnp.bfloat16)


def back_trunk(dy, dpre, x_slope, weight_ref, spread, bins):
    wide = dpre.astype(jnp.float32)
    spans = (
        moved(wide, -spread, bins).astype(jnp.bfloat16),
        dpre,
        moved(wide, spread, bins).astype(jnp.bfloat16),
    )
    dact = jnp.zeros(dy.shape, jnp.float32)
    for tap in range(3):
        dact = dact + jnp.dot(
            spans[tap], weight_ref[0, tap], preferred_element_type=jnp.float32
        )
    return (dy.astype(jnp.float32) + dact * x_slope).astype(jnp.bfloat16)


def of_seq(ref, seq, bins):
    if ref.shape[0] == bins:
        return ref[...]
    return ref[seq * bins : (seq + 1) * bins, :]


def split_kernel(last, payload_ref, *out_refs):
    count = len(out_refs)
    seq_count, bins, chans = payload_ref.shape
    part = bins // count
    section = lax.axis_index("pipe")
    place = lax.axis_index("ctx")

    @pl.when((section == 0) | (section == last))
    def send():
        source = payload_ref[...].reshape(seq_count * bins, chans)
        row = lax.broadcasted_iota(jnp.int32, (part, seq_count * bins), 0)
        col = lax.broadcasted_iota(jnp.int32, (part, seq_count * bins), 1)
        for hop in range(count):
            residue = lax.rem(place + hop, count)
            rows = [
                (col == seq * bins + count * row + residue).astype(jnp.float32)
                for seq in range(seq_count)
            ]
            pick = jnp.concatenate(rows, axis=0).astype(jnp.bfloat16)
            out_refs[hop][...] = jnp.dot(
                pick, source, preferred_element_type=jnp.float32
            ).astype(jnp.bfloat16)


def hold_kernel(weight_ref, point_ref, weight_out, point_out, sems):
    loads = [
        pltpu.make_async_copy(weight_ref, weight_out, sems.at[0]),
        pltpu.make_async_copy(point_ref, point_out, sems.at[1]),
    ]
    for load in loads:
        load.start()
    for load in loads:
        load.wait()


def first_kernel(last, bins, steps, *refs):
    parts, (weight_ref, point_ref, whole_ref, out_ref, pre_ref) = refs[:-5], refs[-5:]
    count = len(parts)
    section = lax.axis_index("pipe")
    place = lax.axis_index("ctx")
    part = bins // count
    seq_count = whole_ref.shape[0] // bins

    @pl.when((section == 0) | (section == last))
    def gather():
        for step, part_ref in zip(steps, parts):
            source = lax.rem(place + count - step, count)
            for seq in range(seq_count):
                at = pl.multiple_of(seq * bins + source * part, part)
                whole_ref[pl.ds(at, part), :] = part_ref[seq * part : (seq + 1) * part, :]

    @pl.when(section == 0)
    def layer():
        x = whole_ref[:bins, :]
        finish(x, fore(x, weight_ref, 1, bins), point_ref, out_ref, pre_ref)


def finish(x, pre, point_ref, out_ref, pre_ref):
    pre_ref[...] = pre
    branch = jnp.dot(
        gelu(pre).astype(jnp.bfloat16), point_ref[0], preferred_element_type=jnp.float32
    )
    out_ref[...] = (x.astype(jnp.float32) + branch).astype(jnp.bfloat16)


def fore_kernel(level, seq, bins, x_ref, weight_ref, point_ref, out_ref, pre_ref):
    @pl.when(lax.axis_index("pipe") == level)
    def layer():
        x = of_seq(x_ref, seq, bins)
        finish(x, fore(x, weight_ref, 2**level, bins), point_ref, out_ref, pre_ref)


def transpose_kernel(weight_ref, point_ref, weight_out, point_out):
    for tap in range(weight_ref.shape[1]):
        weight_out[0, tap] = weight_ref[0, tap].T
    point_out[0] = point_ref[0].T


def turn_kernel(level, seq, bins, scale, x_ref, cot_ref, weight_ref, weight_t_ref, point_t_ref, dy_ref, dpre_ref):
    @pl.when(lax.axis_index("pipe") == level)
    def layer():
        x = of_seq(x_ref, seq, bins)
        pre = fore(x, weight_ref, 2**level, bins)
        cot = of_seq(cot_ref, seq, bins)
        dy = (cot.astype(jnp.float32) * scale).astype(jnp.bfloat16)
        dpre = back_pre(dy, gelu_slope(pre), point_t_ref)
        dpre_ref[...] = dpre
        x_slope = gelu_slope(x.astype(jnp.float32))
        dy_ref[...] = back_trunk(dy, dpre, x_slope, weight_t_ref, 2**level, bins)


def slope_kernel(levels, seq_count, bins, *refs):
    xs, pres = refs[: levels * seq_count], refs[levels * seq_count : 2 * levels * seq_count]
    outs = refs[2 * levels * seq_count :]
    for level in range(levels):

        @pl.when(lax.axis_index("pipe") == level)
        def layer(level=level):
            for seq in range(seq_count):
                x = of_seq(xs[level * seq_count + seq], seq, bins)
                outs[2 * seq][...] = gelu_slope(x.astype(jnp.float32))
                outs[2 * seq + 1][...] = gelu_slope(pres[level * seq_count + seq][...])


def back_kernel(level, bins, dy_in_ref, x_slope_ref, pre_slope_ref, weight_ref, point_ref, dy_ref, dpre_ref):
    @pl.when(lax.axis_index("pipe") == level)
    def layer():
        dy = dy_in_ref[...]
        dpre = back_pre(dy, pre_slope_ref[...], point_ref)
        dpre_ref[...] = dpre
        dy_ref[...] = back_trunk(dy, dpre, x_slope_ref[...], weight_ref, 2**level, bins)


def message_kernel(places, *refs):
    blocks, message_ref = refs[:-1], refs[-1]
    size = message_ref.shape[0] // len(places)
    for to, (ref, at) in enumerate(zip(blocks, places)):
        message_ref[to * size : (to + 1) * size, :] = ref[at * size : (at + 1) * size, :]


def head_kernel(sections, earlier, dy_in_ref, slope_ref, point_ref, *refs):
    others, before, out_ref = refs[: sections - 1], refs[sections - 1 : -1], refs[-1]
    section = lax.axis_index("pipe")
    bins = dy_in_ref.shape[0]
    for ref in before:
        out_ref[:earlier, :] = ref[...]

    @pl.when(section == 0)
    def layer():
        out_ref[earlier : earlier + bins, :] = back_pre(dy_in_ref[...], slope_ref[...], point_ref)

    for level in range(1, sections):

        @pl.when(section == level)
        def keep(level=level):
            out_ref[earlier : earlier + bins, :] = others[level - 1][...]


def columns_kernel(groups, runs, kept, *refs):
    refs, (sent_ref,) = refs[:-1], refs[-1:]
    kept_refs = refs[sum(runs) :]
    count = 2 * len(kept)
    section = lax.axis_index("pipe")
    core = lax.axis_index("dp")
    place = lax.axis_index("ctx")
    x, start = None, 0
    for level, run in enumerate(runs):
        pieces = [ref[...] for ref in refs[start : start + run]]
        start += run
        whole = jnp.concatenate(pieces, axis=0).astype(jnp.float32)
        x = whole if x is None else jnp.where(section == level, whole, x)
    act = gelu(x).astype(jnp.bfloat16)
    chans = act.shape[1]
    width = chans // (groups * count)
    row = lax.broadcasted_iota(jnp.int32, (width, chans), 0)
    col = lax.broadcasted_iota(jnp.int32, (width, chans), 1)

    def block(offset):
        owner = lax.bitwise_xor(place, offset)
        rows = []
        for step in range(groups):
            first = (lax.rem(core + step, groups) * count + owner) * width
            rows.append((col == first + row).astype(jnp.float32))
        pick = jnp.concatenate(rows, axis=0).astype(jnp.bfloat16)
        return lax.dot_general(
            pick, act, contract_last, preferred_element_type=jnp.float32
        ).astype(jnp.bfloat16)

    size = groups * width
    for at, offset in enumerate(kept):
        kept_refs[at][...] = block(offset)
        sent_ref[at * size : (at + 1) * size, :] = block(offset ^ 1)


def grad_kernel(sections, bins, places, *refs):
    columns, refs = refs[: len(places)], refs[len(places) :]
    grads, out_ref = refs[:-1], refs[-1]
    section = lax.axis_index("pipe")
    width = out_ref.shape[1]

    def taps(spread):
        act = jnp.concatenate(
            [ref[at : at + width, :] for ref, at in zip(columns, places)], axis=1
        )
        dpre = jnp.concatenate([ref[...] for ref in grads], axis=0)
        wide = dpre.astype(jnp.float32)
        spans = (
            moved(wide, -spread, bins).astype(jnp.bfloat16),
            dpre,
            moved(wide, spread, bins).astype(jnp.bfloat16),
        )
        for tap in range(3):
            out_ref[tap] = jnp.dot(
                act, spans[tap], preferred_element_type=jnp.float32
            ).astype(out_ref.dtype)

    for level in range(sections):

        @pl.when(section == level)
        def run(level=level):
            taps(2**level)


def kernel_call(body, outs, flops, name, waits=(), carries=(), in_spec=in_vmem, scratch=()):
    def call(*args):
        used, taken = len(args), len(args) + len(waits) + len(carries)

        def run(*refs):
            made = refs[taken : taken + len(outs)]
            body(*refs[:used], *made, *refs[taken + len(outs) + len(carries) :])

        moved_bytes = sum(math.prod(a.shape) * a.dtype.itemsize for a in (*args, *outs))
        return pl.pallas_call(
            run,
            out_shape=[*outs, *(jax.ShapeDtypeStruct(a.shape, a.dtype) for a in carries)],
            in_specs=[in_spec] * used + [anywhere] * (taken - used),
            out_specs=[in_vmem] * len(outs) + [anywhere] * len(carries),
            input_output_aliases={
                used + len(waits) + at: len(outs) + at for at in range(len(carries))
            },
            scratch_shapes=list(scratch),
            compiler_params=pltpu.CompilerParams(vmem_limit_bytes=24 * 2**20),
            cost_estimate=pl.CostEstimate(
                flops=flops, bytes_accessed=moved_bytes, transcendentals=0
            ),
            name=name,
        )(*args, *waits, *carries)

    return call


def residue_shards(inputs, cotangent, weight, point):
    sections = lax.axis_size("pipe")
    section = lax.axis_index("pipe")
    count = lax.axis_size("ctx")
    groups = lax.axis_size("dp")
    seq_count, bins, chans = inputs.shape
    inner = weight.shape[3]
    rows = seq_count * bins
    scale = 1.0 / math.sqrt(seq_count * groups * bins * count)
    last = sections - 1
    seqs = range(seq_count)
    layer_flops = 2 * bins * chans * inner * 4

    def shape(*dims, dtype=jnp.bfloat16):
        return jax.ShapeDtypeStruct(dims, dtype)

    def hop(value, source, target, third=None):
        sends = {source: target, target: source}
        if third is not None and third not in sends:
            sends.update({target: third, third: source})
        route = []
        for core in range(groups):
            for stage in range(sections):
                taker = core if stage in sends else (core + 1) % groups
                for i in range(count):
                    giver = (core * sections + stage) * count + i
                    route.append((giver, (taker * sections + sends.get(stage, stage)) * count + i))
        return lax.ppermute(value, ("dp", "pipe", "ctx"), route)

    def onward(value, step):
        return lax.ppermute(value, "ctx", [(i, (i + step) % count) for i in range(count)])

    def exchange(value, offset):
        return lax.ppermute(value, "ctx", [(i, i ^ offset) for i in range(count)])

    payload = jnp.where(section == last, cotangent, inputs)
    parts = kernel_call(
        functools.partial(split_kernel, last),
        [shape(rows // count, chans)] * count,
        10 * seq_count * layer_flops,
        "split",
    )(payload)
    weight, point = kernel_call(
        hold_kernel,
        [shape(*weight.shape), shape(*point.shape)],
        0,
        "hold",
        waits=[parts[0]],
        in_spec=anywhere,
        scratch=[pltpu.SemaphoreType.DMA((2,))],
    )(weight, point)
    steps = [1, *range(count - 1, 1, -1)]
    parts = [*(onward(parts[step], step) for step in steps), parts[0]]

    trunk, inside = shape(bins, chans), shape(bins, inner)
    inside_wide = shape(bins, inner, dtype=jnp.float32)
    whole, out, pre = kernel_call(
        functools.partial(first_kernel, last, bins, [*steps, 0]),
        [shape(rows, chans), trunk, inside_wide],
        layer_flops,
        "first",
    )(*parts, weight, point)
    outs, pres, xs, sent = [out], [[pre]], [[whole]], ()
    for level in range(last):
        if level > 0:
            third = last if level > 1 else None
            xs.append([hop(out, level - 1, level, third) for out in outs[:-1]])
            xs[level].append(hop(outs[-1], level - 1, level))
            outs = []
            pres.append([])
        for seq in range(len(outs), seq_count):
            out, pre = kernel_call(
                functools.partial(fore_kernel, level, seq, bins),
                [trunk, inside_wide],
                layer_flops,
                "fore",
                waits=outs[-1:] or sent,
            )(xs[level][seq if level else 0], weight, point)
            outs.append(out)
            pres[level].append(pre)
        sent = outs
        if level == 1:
            back_weights = kernel_call(
                transpose_kernel,
                [shape(1, weight.shape[1], inner, chans), shape(1, chans, inner)],
                0,
                "transpose",
                waits=outs,
            )(weight, point)
            sent = [*outs, *back_weights]
    slopes = kernel_call(
        functools.partial(slope_kernel, last, seq_count, bins),
        [shape(bins, chans, dtype=jnp.float32), inside_wide] * seq_count,
        0,
        "slopes",
        waits=outs,
    )(
        *[xs[level][seq if level else 0] for level in range(last) for seq in seqs],
        *[pre for some in pres for pre in some],
    )
    sent = [*sent, *slopes]
    xs.append([hop(out, last - 1, last, 0) for out in outs])

    dys, dpres = [], [[] for level in range(sections)]
    for seq in seqs:
        dy, dpre = kernel_call(
            functools.partial(turn_kernel, last, seq, bins, scale),
            [trunk, inside],
            2 * layer_flops,
            "turn",
            waits=dys[-1:] or sent,
        )(xs[last][seq], whole, weight, *back_weights)
        dys.append(dy)
        dpres[last].append(dpre)
    kept = list(range(0, count, 2))
    moving = [(offset, 0) for offset in range(1, count, 2)]
    size = chans // count
    *owned, message = kernel_call(
        functools.partial(columns_kernel, groups, [len(x) for x in xs], kept),
        [shape(size, rows)] * len(kept) + [shape(size * len(kept), rows)],
        2 * rows * chans * chans,
        "columns",
        waits=dys,
    )(*[x for some in xs for x in some])
    blocks = {(offset, 0): (array, 0) for offset, array in zip(kept, owned)}
    sent = [owned[0]]
    dys = [*(hop(dy, last, last - 1, 0) for dy in dys[:-1]), hop(dys[-1], last, last - 1)]
    message, bit = exchange(message, 1), 1
    blocks.update({(to ^ 1, start ^ 1): (message, at) for at, (to, start) in enumerate(moving)})

    for level in range(last - 1, 0, -1):
        outs = []
        for seq in seqs:
            dy, dpre = kernel_call(
                functools.partial(back_kernel, level, bins),
                [trunk, inside],
                layer_flops,
                "back",
                waits=outs[-1:] or sent,
            )(dys[seq], *slopes[2 * seq : 2 * seq + 2], *back_weights)
            outs.append(dy)
            dpres[level].append(dpre)
        sent = outs
        third = 0 if level > 1 else last
        dys = [hop(dy, level, level - 1, third) for dy in outs[:-1]]
        dys.append(hop(outs[-1], level, level - 1, None if level > 1 else last))
        bit *= 2
        moving = sorted(key for key in blocks if key[0] & bit)
        if moving:
            (message,) = kernel_call(
                functools.partial(message_kernel, [blocks[key][1] for key in moving]),
                [shape(size * len(moving), rows)],
                0,
                "message",
                waits=outs,
            )(*[blocks[key][0] for key in moving])
            sent = [*outs, message]
            message = exchange(message, bit)
            for at, (to, start) in enumerate(moving):
                blocks[to ^ bit, start ^ bit] = (message, at)

    sent = [*sent, message]
    dpre = []
    for seq in seqs:
        dpre = kernel_call(
            functools.partial(head_kernel, sections, seq * bins),
            [shape((seq + 1) * bins, inner)],
            layer_flops // 4,
            "head",
            waits=dpre or sent,
        )(dys[seq], slopes[2 * seq + 1], back_weights[1], *[dpres[level][seq] for level in range(1, sections)], *dpre)
    (dpre,) = dpre
    offsets = range(1, count)
    gathered = [*(exchange(dpre, offset) for offset in offsets), dpre]
    columns = [blocks[0, offset] for offset in [*offsets, 0]]
    width = size // groups

    def gradient(step, dtype, waits=()):
        places = [at * size + step * width for array, at in columns]
        (part,) = kernel_call(
            functools.partial(grad_kernel, sections, bins, places),
            [shape(3, width, inner, dtype=dtype)],
            2 * 3 * rows * count * width * inner,
            "grad",
            waits=waits,
        )(*[array for array, at in columns], *gathered)
        return part

    others = [gradient(step, jnp.bfloat16) for step in range(1, groups)]
    mine = gradient(0, jnp.float32, waits=others)
    for step, other in enumerate(others, 1):
        route = [(i, (i + step) % groups) for i in range(groups)]
        mine = mine + lax.ppermute(other, "dp", route).astype(jnp.float32)
    return mine[None]


def solution(mesh):
    def shards(inputs, cotangent, dilated_kernel_weight, point_weight):
        bins = inputs.shape[1]
        first_spread = bins // 2 // 2 ** (mesh.shape["pipe"] - 1)
        count = mesh.shape["ctx"]
        residues = (
            first_spread == count
            and mesh.shape["pipe"] > 2
            and bins % (16 * count) == 0
            and 1 < count == 1 << (count.bit_length() - 1) <= 1 << (mesh.shape["pipe"] - 2)
            and inputs.shape[2] % (count * mesh.shape["dp"]) == 0
        )
        plan = residue_shards if residues else edge_shards
        return plan(inputs, cotangent, dilated_kernel_weight, point_weight)

    return jax.shard_map(
        shards,
        mesh=mesh,
        in_specs=(
            P("dp", "ctx", None),
            P("dp", "ctx", None),
            P("pipe", None, None, None),
            P("pipe", None, None),
        ),
        out_specs=P("pipe", None, ("dp", "ctx"), None),
        check_vma=False,
    )
```

```python
import functools
import math

import jax
import jax.numpy as jnp
from jax import lax
from jax.experimental import pallas as pl
from jax.experimental.pallas import tpu as pltpu
from jax.sharding import PartitionSpec as P

root_half = 0.7071067811865476
inv_root_two_pi = 0.3989422804014327

in_vmem = pl.BlockSpec(memory_space=pltpu.VMEM)
anywhere = pl.BlockSpec(memory_space=pl.ANY)
contract_last = (((1,), (1,)), ((), ()))
contract_first = (((0,), (0,)), ((), ()))


def gelu(value):
    return 0.5 * value * (1.0 + lax.erf(value * root_half))


def gelu_slope(value):
    return (
        0.5 * (1.0 + lax.erf(value * root_half))
        + value * jnp.exp(-0.5 * value * value) * inv_root_two_pi
    )


def padded(cells, sides, width):
    for axis, dim in sides:
        count = lax.axis_size(axis)
        ends = count - 1
        head = lax.slice_in_dim(cells, 0, width, axis=dim)
        tail = lax.slice_in_dim(cells, cells.shape[dim] - width, cells.shape[dim], axis=dim)
        cells = jnp.concatenate(
            [
                lax.ppermute(tail, axis, [(i, (i + 1) % count) for i in range(ends)]),
                cells,
                lax.ppermute(head, axis, [((i + 1) % count, i) for i in range(ends)]),
            ],
            axis=dim,
        )
    return cells


def shifted(block, axis, distance):
    devices = range(lax.axis_size(axis))
    route = [(i - distance, i) for i in devices if i - distance in devices]
    return lax.ppermute(block, axis, route)


def edge_shards(inputs, cotangent, dilated_kernel_weight, point_weight):
    sections = lax.axis_size("pipe")
    section = lax.axis_index("pipe")
    seq_count, bins, chans = inputs.shape
    reach = bins // 2
    table = jnp.array(
        [reach // 2 ** (sections - 1 - level) for level in range(sections)], jnp.int32
    )
    spread = table[section]
    dilation_weight = dilated_kernel_weight[0]
    w_point = point_weight[0]
    inner_channel_count = dilation_weight.shape[2]
    scale = 1.0 / math.sqrt(seq_count * lax.axis_size("dp") * bins * lax.axis_size("ctx"))
    ticks = jnp.arange(seq_count + sections - 1, dtype=jnp.int32)

    def conv_fore(extended):
        running_total = jnp.zeros((bins, inner_channel_count), jnp.float32)
        for kernel_offset in range(3):
            receptive_span = lax.dynamic_slice_in_dim(
                extended, reach + (kernel_offset - 1) * spread, bins, 0
            )
            running_total = running_total + jnp.dot(
                receptive_span, dilation_weight[kernel_offset], preferred_element_type=jnp.float32
            )
        return running_total

    def put(store, slot, valid, item):
        current = lax.dynamic_index_in_dim(store, slot, 0, keepdims=False)
        return lax.dynamic_update_index_in_dim(store, jnp.where(valid, item, current), slot, 0)

    kept_x = jnp.zeros(inputs.shape, jnp.bfloat16)
    kept_ext = jnp.zeros((seq_count, bins + 2 * reach, chans), jnp.bfloat16)
    kept_pre = jnp.zeros((seq_count, bins, inner_channel_count), jnp.float32)

    def fore_tick(carry, tick):
        received, store_x, store_ext, store_pre = carry
        micro = tick - section
        valid = (micro >= 0) & (micro < seq_count)
        slot = jnp.clip(micro, 0, seq_count - 1)
        first = lax.dynamic_index_in_dim(inputs, slot, 0, keepdims=False)
        trunk_in = jnp.where(section == 0, first, received)
        act = gelu(trunk_in.astype(jnp.float32)).astype(jnp.bfloat16)
        extended = padded(act, (("ctx", 0),), reach)
        pre = conv_fore(extended)
        inner = gelu(pre).astype(jnp.bfloat16)
        out = (
            trunk_in.astype(jnp.float32)
            + jnp.dot(inner, w_point, preferred_element_type=jnp.float32)
        ).astype(jnp.bfloat16)
        sent = shifted(out, "pipe", 1)
        store_x = put(store_x, slot, valid, trunk_in)
        store_ext = put(store_ext, slot, valid, extended)
        store_pre = put(store_pre, slot, valid, pre)
        return ((sent, store_x, store_ext, store_pre), None)

    start_recv = jnp.zeros((bins, chans), jnp.bfloat16)
    (unused, kept_x, kept_ext, kept_pre), unused_out = lax.scan(
        fore_tick, (start_recv, kept_x, kept_ext, kept_pre), ticks
    )

    def back_tick(carry, tick):
        received, grad = carry
        micro = tick - (sections - 1 - section)
        valid = (micro >= 0) & (micro < seq_count)
        slot = jnp.clip(micro, 0, seq_count - 1)
        last = (
            lax.dynamic_index_in_dim(cotangent, slot, 0, keepdims=False).astype(jnp.float32) * scale
        ).astype(jnp.bfloat16)
        upstream = jnp.where(section == sections - 1, last, received)
        trunk_in = lax.dynamic_index_in_dim(kept_x, slot, 0, keepdims=False)
        extended = lax.dynamic_index_in_dim(kept_ext, slot, 0, keepdims=False)
        pre = lax.dynamic_index_in_dim(kept_pre, slot, 0, keepdims=False)
        inner_grad = lax.dot_general(
            upstream, w_point, contract_last, preferred_element_type=jnp.float32
        )
        dpre = (inner_grad * gelu_slope(pre) * valid.astype(jnp.float32)).astype(jnp.bfloat16)
        dpre_ext = padded(dpre, (("ctx", 0),), reach)
        dact = jnp.zeros((bins, chans), jnp.float32)
        taps = []
        for kernel_offset in range(3):
            receptive_span = lax.dynamic_slice_in_dim(
                dpre_ext, reach - (kernel_offset - 1) * spread, bins, 0
            )
            dact = dact + lax.dot_general(
                receptive_span,
                dilation_weight[kernel_offset],
                contract_last,
                preferred_element_type=jnp.float32,
            )
            source = lax.dynamic_slice_in_dim(
                extended, reach + (kernel_offset - 1) * spread, bins, 0
            )
            taps.append(
                lax.dot_general(source, dpre, contract_first, preferred_element_type=jnp.float32)
            )
        grad = grad + jnp.stack(taps)
        back = (
            upstream.astype(jnp.float32) + dact * gelu_slope(trunk_in.astype(jnp.float32))
        ).astype(jnp.bfloat16)
        sent = shifted(back, "pipe", -1)
        return ((sent, grad), None)

    start_grad = jnp.zeros((3, chans, inner_channel_count), jnp.float32)
    (unused_back, grad), unused_seq = lax.scan(back_tick, (start_recv, start_grad), ticks)
    term = grad[None]
    return lax.psum_scatter(term, ("dp", "ctx"), scatter_dimension=2, tiled=True)


def moved(value, by, bins):
    pieces = []
    for start in range(0, value.shape[0], bins):
        piece = value[start : start + bins]
        place = lax.broadcasted_iota(jnp.int32, piece.shape, 0)
        if by > 0:
            keep = place >= by
        else:
            keep = place < bins + by
        pieces.append(jnp.where(keep, pltpu.roll(piece, by % bins, 0), 0.0))
    return jnp.concatenate(pieces, axis=0)


def fore(x, weight_ref, spread, bins):
    act = gelu(x.astype(jnp.float32)).astype(jnp.bfloat16)
    terms = [
        jnp.dot(act, weight_ref[0, tap], preferred_element_type=jnp.float32) for tap in range(3)
    ]
    return terms[1] + moved(terms[0], spread, bins) + moved(terms[2], -spread, bins)


def back_pre(dy, pre_slope, point_ref):
    inner_grad = jnp.dot(dy, point_ref[0], preferred_element_type=jnp.float32)
    return (inner_grad * pre_slope).astype(jnp.bfloat16)


def back_trunk(dy, dpre, x_slope, weight_ref, spread, bins):
    wide = dpre.astype(jnp.float32)
    spans = (
        moved(wide, -spread, bins).astype(jnp.bfloat16),
        dpre,
        moved(wide, spread, bins).astype(jnp.bfloat16),
    )
    dact = jnp.zeros(dy.shape, jnp.float32)
    for tap in range(3):
        dact = dact + jnp.dot(
            spans[tap], weight_ref[0, tap], preferred_element_type=jnp.float32
        )
    return (dy.astype(jnp.float32) + dact * x_slope).astype(jnp.bfloat16)


def of_seq(ref, seq, bins):
    if ref.shape[0] == bins:
        return ref[...]
    return ref[seq * bins : (seq + 1) * bins, :]


def split_kernel(last, payload_ref, *out_refs):
    count = len(out_refs)
    seq_count, bins, chans = payload_ref.shape
    part = bins // count
    section = lax.axis_index("pipe")
    place = lax.axis_index("ctx")

    @pl.when((section == 0) | (section == last))
    def send():
        source = payload_ref[...].reshape(seq_count * bins, chans)
        row = lax.broadcasted_iota(jnp.int32, (part, seq_count * bins), 0)
        col = lax.broadcasted_iota(jnp.int32, (part, seq_count * bins), 1)
        for hop in range(count):
            residue = lax.rem(place + hop, count)
            rows = [
                (col == seq * bins + count * row + residue).astype(jnp.float32)
                for seq in range(seq_count)
            ]
            pick = jnp.concatenate(rows, axis=0).astype(jnp.bfloat16)
            out_refs[hop][...] = jnp.dot(
                pick, source, preferred_element_type=jnp.float32
            ).astype(jnp.bfloat16)


def hold_kernel(weight_ref, point_ref, weight_out, point_out, sems):
    loads = [
        pltpu.make_async_copy(weight_ref, weight_out, sems.at[0]),
        pltpu.make_async_copy(point_ref, point_out, sems.at[1]),
    ]
    for load in loads:
        load.start()
    for load in loads:
        load.wait()


def first_kernel(last, bins, steps, *refs):
    parts, (weight_ref, point_ref, whole_ref, out_ref, pre_ref) = refs[:-5], refs[-5:]
    count = len(parts)
    section = lax.axis_index("pipe")
    place = lax.axis_index("ctx")
    part = bins // count
    seq_count = whole_ref.shape[0] // bins

    @pl.when((section == 0) | (section == last))
    def gather():
        for step, part_ref in zip(steps, parts):
            source = lax.rem(place + count - step, count)
            for seq in range(seq_count):
                at = pl.multiple_of(seq * bins + source * part, part)
                whole_ref[pl.ds(at, part), :] = part_ref[seq * part : (seq + 1) * part, :]

    @pl.when(section == 0)
    def layer():
        x = whole_ref[:bins, :]
        finish(x, fore(x, weight_ref, 1, bins), point_ref, out_ref, pre_ref)


def finish(x, pre, point_ref, out_ref, pre_ref):
    pre_ref[...] = pre
    branch = jnp.dot(
        gelu(pre).astype(jnp.bfloat16), point_ref[0], preferred_element_type=jnp.float32
    )
    out_ref[...] = (x.astype(jnp.float32) + branch).astype(jnp.bfloat16)


def fore_kernel(level, seq, bins, x_ref, weight_ref, point_ref, out_ref, pre_ref):
    @pl.when(lax.axis_index("pipe") == level)
    def layer():
        x = of_seq(x_ref, seq, bins)
        finish(x, fore(x, weight_ref, 2**level, bins), point_ref, out_ref, pre_ref)


def transpose_kernel(weight_ref, point_ref, weight_out, point_out):
    for tap in range(weight_ref.shape[1]):
        weight_out[0, tap] = weight_ref[0, tap].T
    point_out[0] = point_ref[0].T


def turn_kernel(level, seq, bins, scale, x_ref, cot_ref, weight_ref, weight_t_ref, point_t_ref, dy_ref, dpre_ref):
    @pl.when(lax.axis_index("pipe") == level)
    def layer():
        x = of_seq(x_ref, seq, bins)
        pre = fore(x, weight_ref, 2**level, bins)
        cot = of_seq(cot_ref, seq, bins)
        dy = (cot.astype(jnp.float32) * scale).astype(jnp.bfloat16)
        dpre = back_pre(dy, gelu_slope(pre), point_t_ref)
        dpre_ref[...] = dpre
        x_slope = gelu_slope(x.astype(jnp.float32))
        dy_ref[...] = back_trunk(dy, dpre, x_slope, weight_t_ref, 2**level, bins)


def slope_kernel(levels, seq_count, bins, *refs):
    xs, pres = refs[: levels * seq_count], refs[levels * seq_count : 2 * levels * seq_count]
    outs = refs[2 * levels * seq_count :]
    for level in range(levels):

        @pl.when(lax.axis_index("pipe") == level)
        def layer(level=level):
            for seq in range(seq_count):
                x = of_seq(xs[level * seq_count + seq], seq, bins)
                outs[2 * seq][...] = gelu_slope(x.astype(jnp.float32))
                outs[2 * seq + 1][...] = gelu_slope(pres[level * seq_count + seq][...])


def back_kernel(level, bins, dy_in_ref, x_slope_ref, pre_slope_ref, weight_ref, point_ref, dy_ref, dpre_ref):
    @pl.when(lax.axis_index("pipe") == level)
    def layer():
        dy = dy_in_ref[...]
        dpre = back_pre(dy, pre_slope_ref[...], point_ref)
        dpre_ref[...] = dpre
        dy_ref[...] = back_trunk(dy, dpre, x_slope_ref[...], weight_ref, 2**level, bins)


def message_kernel(places, *refs):
    blocks, message_ref = refs[:-1], refs[-1]
    size = message_ref.shape[0] // len(places)
    for to, (ref, at) in enumerate(zip(blocks, places)):
        message_ref[to * size : (to + 1) * size, :] = ref[at * size : (at + 1) * size, :]


def head_kernel(sections, earlier, dy_in_ref, slope_ref, point_ref, *refs):
    others, before, out_ref = refs[: sections - 1], refs[sections - 1 : -1], refs[-1]
    section = lax.axis_index("pipe")
    bins = dy_in_ref.shape[0]
    for ref in before:
        out_ref[:earlier, :] = ref[...]

    @pl.when(section == 0)
    def layer():
        out_ref[earlier : earlier + bins, :] = back_pre(dy_in_ref[...], slope_ref[...], point_ref)

    for level in range(1, sections):

        @pl.when(section == level)
        def keep(level=level):
            out_ref[earlier : earlier + bins, :] = others[level - 1][...]


def columns_kernel(groups, runs, kept, *refs):
    refs, (sent_ref,) = refs[:-1], refs[-1:]
    kept_refs = refs[sum(runs) :]
    count = 2 * len(kept)
    section = lax.axis_index("pipe")
    core = lax.axis_index("dp")
    place = lax.axis_index("ctx")
    x, start = None, 0
    for level, run in enumerate(runs):
        pieces = [ref[...] for ref in refs[start : start + run]]
        start += run
        whole = jnp.concatenate(pieces, axis=0).astype(jnp.float32)
        x = whole if x is None else jnp.where(section == level, whole, x)
    act = gelu(x).astype(jnp.bfloat16)
    chans = act.shape[1]
    width = chans // (groups * count)
    row = lax.broadcasted_iota(jnp.int32, (width, chans), 0)
    col = lax.broadcasted_iota(jnp.int32, (width, chans), 1)

    def block(offset):
        owner = lax.bitwise_xor(place, offset)
        rows = []
        for step in range(groups):
            first = (lax.rem(core + step, groups) * count + owner) * width
            rows.append((col == first + row).astype(jnp.float32))
        pick = jnp.concatenate(rows, axis=0).astype(jnp.bfloat16)
        return lax.dot_general(
            pick, act, contract_last, preferred_element_type=jnp.float32
        ).astype(jnp.bfloat16)

    size = groups * width
    for at, offset in enumerate(kept):
        kept_refs[at][...] = block(offset)
        sent_ref[at * size : (at + 1) * size, :] = block(offset ^ 1)


def grad_kernel(sections, bins, places, *refs):
    columns, refs = refs[: len(places)], refs[len(places) :]
    grads, out_ref = refs[:-1], refs[-1]
    section = lax.axis_index("pipe")
    width = out_ref.shape[1]

    def taps(spread):
        act = jnp.concatenate(
            [ref[at : at + width, :] for ref, at in zip(columns, places)], axis=1
        )
        dpre = jnp.concatenate([ref[...] for ref in grads], axis=0)
        wide = dpre.astype(jnp.float32)
        spans = (
            moved(wide, -spread, bins).astype(jnp.bfloat16),
            dpre,
            moved(wide, spread, bins).astype(jnp.bfloat16),
        )
        for tap in range(3):
            out_ref[tap] = jnp.dot(
                act, spans[tap], preferred_element_type=jnp.float32
            ).astype(out_ref.dtype)

    for level in range(sections):

        @pl.when(section == level)
        def run(level=level):
            taps(2**level)


def kernel_call(body, outs, flops, name, waits=(), carries=(), in_spec=in_vmem, scratch=()):
    def call(*args):
        used, taken = len(args), len(args) + len(waits) + len(carries)

        def run(*refs):
            made = refs[taken : taken + len(outs)]
            body(*refs[:used], *made, *refs[taken + len(outs) + len(carries) :])

        moved_bytes = sum(math.prod(a.shape) * a.dtype.itemsize for a in (*args, *outs))
        return pl.pallas_call(
            run,
            out_shape=[*outs, *(jax.ShapeDtypeStruct(a.shape, a.dtype) for a in carries)],
            in_specs=[in_spec] * used + [anywhere] * (taken - used),
            out_specs=[in_vmem] * len(outs) + [anywhere] * len(carries),
            input_output_aliases={
                used + len(waits) + at: len(outs) + at for at in range(len(carries))
            },
            scratch_shapes=list(scratch),
            compiler_params=pltpu.CompilerParams(vmem_limit_bytes=24 * 2**20),
            cost_estimate=pl.CostEstimate(
                flops=flops, bytes_accessed=moved_bytes, transcendentals=0
            ),
            name=name,
        )(*args, *waits, *carries)

    return call


def residue_shards(inputs, cotangent, weight, point):
    sections = lax.axis_size("pipe")
    section = lax.axis_index("pipe")
    count = lax.axis_size("ctx")
    groups = lax.axis_size("dp")
    seq_count, bins, chans = inputs.shape
    inner = weight.shape[3]
    rows = seq_count * bins
    scale = 1.0 / math.sqrt(seq_count * groups * bins * count)
    last = sections - 1
    seqs = range(seq_count)
    layer_flops = 2 * bins * chans * inner * 4

    def shape(*dims, dtype=jnp.bfloat16):
        return jax.ShapeDtypeStruct(dims, dtype)

    def hop(value, source, target, third=None):
        sends = {source: target, target: source}
        if third is not None and third not in sends:
            sends.update({target: third, third: source})
        route = []
        for core in range(groups):
            for stage in range(sections):
                taker = core if stage in sends else (core + 1) % groups
                for i in range(count):
                    giver = (core * sections + stage) * count + i
                    route.append((giver, (taker * sections + sends.get(stage, stage)) * count + i))
        return lax.ppermute(value, ("dp", "pipe", "ctx"), route)

    def onward(value, step):
        return lax.ppermute(value, "ctx", [(i, (i + step) % count) for i in range(count)])

    def exchange(value, offset):
        return lax.ppermute(value, "ctx", [(i, i ^ offset) for i in range(count)])

    payload = jnp.where(section == last, cotangent, inputs)
    parts = kernel_call(
        functools.partial(split_kernel, last),
        [shape(rows // count, chans)] * count,
        10 * seq_count * layer_flops,
        "split",
    )(payload)
    weight, point = kernel_call(
        hold_kernel,
        [shape(*weight.shape), shape(*point.shape)],
        0,
        "hold",
        waits=[parts[0]],
        in_spec=anywhere,
        scratch=[pltpu.SemaphoreType.DMA((2,))],
    )(weight, point)
    steps = [1, *range(count - 1, 1, -1)]
    parts = [*(onward(parts[step], step) for step in steps), parts[0]]

    trunk, inside = shape(bins, chans), shape(bins, inner)
    inside_wide = shape(bins, inner, dtype=jnp.float32)
    whole, out, pre = kernel_call(
        functools.partial(first_kernel, last, bins, [*steps, 0]),
        [shape(rows, chans), trunk, inside_wide],
        layer_flops,
        "first",
    )(*parts, weight, point)
    outs, pres, xs, sent = [out], [[pre]], [[whole]], ()
    for level in range(last):
        if level > 0:
            third = last if level > 1 else None
            xs.append([hop(out, level - 1, level, third) for out in outs[:-1]])
            xs[level].append(hop(outs[-1], level - 1, level))
            outs = []
            pres.append([])
        for seq in range(len(outs), seq_count):
            out, pre = kernel_call(
                functools.partial(fore_kernel, level, seq, bins),
                [trunk, inside_wide],
                layer_flops,
                "fore",
                waits=outs[-1:] or sent,
            )(xs[level][seq if level else 0], weight, point)
            outs.append(out)
            pres[level].append(pre)
        sent = outs
        if level == 1:
            back_weights = kernel_call(
                transpose_kernel,
                [shape(1, weight.shape[1], inner, chans), shape(1, chans, inner)],
                0,
                "transpose",
                waits=outs,
            )(weight, point)
            sent = [*outs, *back_weights]
    slopes = kernel_call(
        functools.partial(slope_kernel, last, seq_count, bins),
        [shape(bins, chans, dtype=jnp.float32), inside_wide] * seq_count,
        0,
        "slopes",
        waits=outs,
    )(
        *[xs[level][seq if level else 0] for level in range(last) for seq in seqs],
        *[pre for some in pres for pre in some],
    )
    sent = [*sent, *slopes]
    xs.append([*(hop(out, last - 1, last, 0) for out in outs[:-1]), hop(outs[-1], last - 1, last)])

    dys, dpres = [], [[] for level in range(sections)]
    for seq in seqs:
        dy, dpre = kernel_call(
            functools.partial(turn_kernel, last, seq, bins, scale),
            [trunk, inside],
            2 * layer_flops,
            "turn",
            waits=dys[-1:] or sent,
        )(xs[last][seq], whole, weight, *back_weights)
        dys.append(dy)
        dpres[last].append(dpre)
    kept = list(range(0, count, 2))
    moving = [(offset, 0) for offset in range(1, count, 2)]
    size = chans // count
    *owned, message = kernel_call(
        functools.partial(columns_kernel, groups, [len(x) for x in xs], kept),
        [shape(size, rows)] * len(kept) + [shape(size * len(kept), rows)],
        2 * rows * chans * chans,
        "columns",
        waits=dys,
    )(*[x for some in xs for x in some])
    blocks = {(offset, 0): (array, 0) for offset, array in zip(kept, owned)}
    sent = [owned[0]]
    dys = [hop(dy, last, last - 1) for dy in dys]
    message, bit = exchange(message, 1), 1
    blocks.update({(to ^ 1, start ^ 1): (message, at) for at, (to, start) in enumerate(moving)})

    for level in range(last - 1, 0, -1):
        outs = []
        for seq in seqs:
            dy, dpre = kernel_call(
                functools.partial(back_kernel, level, bins),
                [trunk, inside],
                layer_flops,
                "back",
                waits=outs[-1:] or sent,
            )(dys[seq], *slopes[2 * seq : 2 * seq + 2], *back_weights)
            outs.append(dy)
            dpres[level].append(dpre)
        sent = outs
        third = 0 if level > 1 else last
        dys = [hop(dy, level, level - 1, third) for dy in outs[:-1]]
        dys.append(hop(outs[-1], level, level - 1, None if level > 1 else last))
        bit *= 2
        moving = sorted(key for key in blocks if key[0] & bit)
        if moving:
            (message,) = kernel_call(
                functools.partial(message_kernel, [blocks[key][1] for key in moving]),
                [shape(size * len(moving), rows)],
                0,
                "message",
                waits=outs,
            )(*[blocks[key][0] for key in moving])
            sent = [*outs, message]
            message = exchange(message, bit)
            for at, (to, start) in enumerate(moving):
                blocks[to ^ bit, start ^ bit] = (message, at)

    sent = [*sent, message]
    dpre = []
    for seq in seqs:
        dpre = kernel_call(
            functools.partial(head_kernel, sections, seq * bins),
            [shape((seq + 1) * bins, inner)],
            layer_flops // 4,
            "head",
            waits=dpre or sent,
        )(dys[seq], slopes[2 * seq + 1], back_weights[1], *[dpres[level][seq] for level in range(1, sections)], *dpre)
    (dpre,) = dpre
    offsets = range(1, count)
    gathered = [*(exchange(dpre, offset) for offset in offsets), dpre]
    columns = [blocks[0, offset] for offset in [*offsets, 0]]
    width = size // groups

    def gradient(step, dtype, waits=()):
        places = [at * size + step * width for array, at in columns]
        (part,) = kernel_call(
            functools.partial(grad_kernel, sections, bins, places),
            [shape(3, width, inner, dtype=dtype)],
            2 * 3 * rows * count * width * inner,
            "grad",
            waits=waits,
        )(*[array for array, at in columns], *gathered)
        return part

    others = [gradient(step, jnp.bfloat16) for step in range(1, groups)]
    mine = gradient(0, jnp.float32, waits=others)
    for step, other in enumerate(others, 1):
        route = [(i, (i + step) % groups) for i in range(groups)]
        mine = mine + lax.ppermute(other, "dp", route).astype(jnp.float32)
    return mine[None]


def solution(mesh):
    def shards(inputs, cotangent, dilated_kernel_weight, point_weight):
        bins = inputs.shape[1]
        first_spread = bins // 2 // 2 ** (mesh.shape["pipe"] - 1)
        count = mesh.shape["ctx"]
        residues = (
            first_spread == count
            and mesh.shape["pipe"] > 2
            and bins % (16 * count) == 0
            and 1 < count == 1 << (count.bit_length() - 1) <= 1 << (mesh.shape["pipe"] - 2)
            and inputs.shape[2] % (count * mesh.shape["dp"]) == 0
        )
        plan = residue_shards if residues else edge_shards
        return plan(inputs, cotangent, dilated_kernel_weight, point_weight)

    return jax.shard_map(
        shards,
        mesh=mesh,
        in_specs=(
            P("dp", "ctx", None),
            P("dp", "ctx", None),
            P("pipe", None, None, None),
            P("pipe", None, None),
        ),
        out_specs=P("pipe", None, ("dp", "ctx"), None),
        check_vma=False,
    )
```
